32 devices in a mesh: dp: 4 (over y, core), mp: 8 (over z, x).
Axes of the slice: x: 2, y: 2, z: 4, core: 2. Of those that a mesh axis runs over, the one named last changes fastest.
Arguments:
- patches: bfloat16 [8, 24, 24, 1024], P('dp', None, None, 'mp'), may hold values from -6 to 6
- first_reduce: bfloat16 [1024, 1024], P(None, 'mp'), may hold values from -0.1875 to 0.1875
- first_mixer: bfloat16 [3, 3, 1024, 1024], P(None, None, 'mp'), may hold values from -0.0625 to 0.0625
- first_expand: bfloat16 [1024, 1024], P('mp'), may hold values from -0.1875 to 0.1875
- first_gain: float32 [1024], P('mp'), may hold values from 0.1 to 1.9
- first_shift: float32 [1024], P('mp'), may hold values from -3 to 3
- second_reduce: bfloat16 [1024, 1024], P(None, 'mp'), may hold values from -0.1875 to 0.1875
- second_mixer: bfloat16 [3, 3, 1024, 1024], P(None, None, 'mp'), may hold values from -0.0625 to 0.0625
- second_expand: bfloat16 [1024, 1024], P('mp'), may hold values from -0.1875 to 0.1875
- second_gain: float32 [1024], P('mp'), may hold values from 0.1 to 1.9
- second_shift: float32 [1024], P('mp'), may hold values from -3 to 3
- readout_in: bfloat16 [1024, 4096], P(None, 'mp'), may hold values from -0.1875 to 0.1875
- readout_out: bfloat16 [4096, 4096], P('mp'), may hold values from -0.09375 to 0.09375
- cotangent: bfloat16 [1152, 4096], P('dp', 'mp'), may hold values from -6 to 6
- live_counts: int32 [4], P('dp'), may hold values from 1 to 2, as said below
Outputs:
- tokens: bfloat16 [1152, 4096], P('dp', 'mp')
- patch_grads: float32 [8, 24, 24, 1024], P('dp', None, None, 'mp')
- first_reduce_grad: float32 [1024, 1024], P(None, 'mp')
- first_mixer_grad: float32 [3, 3, 1024, 1024], P(None, None, 'mp')
- first_expand_grad: float32 [1024, 1024], P('mp')
- first_gain_grad: float32 [1024], P('mp')
- first_shift_grad: float32 [1024], P('mp')
- second_reduce_grad: float32 [1024, 1024], P(None, 'mp')
- second_mixer_grad: float32 [3, 3, 1024, 1024], P(None, None, 'mp')
- second_expand_grad: float32 [1024, 1024], P('mp')
- second_gain_grad: float32 [1024], P('mp')
- second_shift_grad: float32 [1024], P('mp')
- readout_in_grad: float32 [1024, 4096], P(None, 'mp')
- readout_out_grad: float32 [4096, 4096], P('mp')
The draws below stay inside these ranges and needn't reach their ends.
Inputs may be any that keep to these rules, and one draw needn't show every extreme that they name: `live_counts`: live grid slots of each data group; 2 in at least one group.
All inputs are finite; a program needn't handle non-finite values.
Results may differ from the reference program's by a relative error of at most 0.03.
Values may be sent and summed in bfloat16 or wider, within the bound.
A program may use at most 128 MiB of HBM per device.

```python
import jax
import jax.numpy as jnp
from jax import lax

C = 1024
OUTD = 4096
GRID = 24
SLOTS = 2
POOLED = 12
GRIDS = 8
N_DP = 4


def draw_live_counts(key, part):
    key = jax.random.fold_in(key, 11)
    key_counts, key_chosen = jax.random.split(key)
    counts = jax.random.randint(key_counts, (N_DP,), 1, SLOTS + 1)
    chosen = jax.random.randint(key_chosen, (), 0, N_DP)
    return jnp.where(jnp.arange(N_DP) == chosen, SLOTS, counts).astype(jnp.int32)


def shard_levels(own_key, extent, cuts, least, largest):
    def one(position, parts):
        draws = jax.random.uniform(jax.random.fold_in(jax.random.fold_in(own_key, 6), position), (parts,), jnp.float32, least / len(cuts), largest / len(cuts))
        return jnp.repeat(jnp.exp(draws), extent[position] // parts).reshape((-1,) + (1,) * (len(extent) - position - 1))

    level = one(*cuts[0])
    for cut in cuts[1:]:
        level = level * one(*cut)
    return level


def scatter_about(own_key, extent, deviation, limit, pieces=(), held_as=jnp.bfloat16):
    array = jax.random.normal(own_key, extent, jnp.float32) * deviation
    if len(pieces) > 0:
        array = shard_levels(own_key, extent, pieces, -0.22, 0.18) * array
    return jnp.clip(array, min=-limit, max=limit).astype(held_as)


def setup_inputs(seed: int = 0) -> dict:
    keys = jax.random.split(jax.random.key(seed), 16)
    patches = scatter_about(keys[0], (GRIDS, GRID, GRID, C), 1.0, 6.0, ((0, 4), (3, 8)))
    first_reduce = scatter_about(keys[1], (C, C), C ** -0.5, 0.1875, ((1, 8),))
    first_mixer = scatter_about(keys[2], (3, 3, C, C), (9 * C) ** -0.5, 0.0625, ((2, 8),))
    first_expand = scatter_about(keys[3], (C, C), C ** -0.5, 0.1875, ((0, 8),))
    first_gain = jnp.clip(1.0 + 0.18 * jax.random.normal(keys[4], (C,), jnp.float32), 0.1, 1.9)
    first_shift = scatter_about(keys[5], (C,), 0.5, 3.0, ((0, 8),), jnp.float32)
    second_reduce = scatter_about(keys[6], (C, C), C ** -0.5, 0.1875, ((1, 8),))
    second_mixer = scatter_about(keys[7], (3, 3, C, C), (9 * C) ** -0.5, 0.0625, ((2, 8),))
    second_expand = scatter_about(keys[8], (C, C), C ** -0.5, 0.1875, ((0, 8),))
    second_gain = jnp.clip(1.0 + 0.18 * jax.random.normal(keys[9], (C,), jnp.float32), 0.1, 1.9)
    second_shift = scatter_about(keys[10], (C,), 0.5, 3.0, ((0, 8),), jnp.float32)
    readout_in = scatter_about(keys[11], (C, OUTD), C ** -0.5, 0.1875, ((1, 8),))
    readout_out = scatter_about(keys[12], (OUTD, OUTD), OUTD ** -0.5, 0.09375, ((0, 8),))
    cotangent = scatter_about(keys[13], (GRIDS * POOLED * POOLED, OUTD), 1.0, 6.0, ((0, 4), (1, 8)))
    live_counts = draw_live_counts(jax.random.fold_in(keys[15], 71), 0)
    return {"patches": patches, "first_reduce": first_reduce, "first_mixer": first_mixer, "first_expand": first_expand, "first_gain": first_gain, "first_shift": first_shift, "second_reduce": second_reduce, "second_mixer": second_mixer, "second_expand": second_expand, "second_gain": second_gain, "second_shift": second_shift, "readout_in": readout_in, "readout_out": readout_out, "cotangent": cotangent, "live_counts": live_counts}


norm_eps = 1e-06
highest = lax.Precision.HIGHEST

@jax.custom_vjp
def low(v):
    return lax.optimization_barrier(v.astype(jnp.bfloat16)).astype(jnp.float32)

@jax.custom_vjp
def low_back(v):
    return v

def low_keep(v):
    return (low(v), None)

def low_pass(kept, grad):
    return (grad,)

def back_keep(v):
    return (v, None)

def back_low(kept, grad):
    return (low(grad),)
low.defvjp(low_keep, low_pass)
low_back.defvjp(back_keep, back_low)

def norm_act(mixed, gain, shift):
    center = lax.optimization_barrier(jnp.mean(mixed, axis=-1, keepdims=True))
    spread = lax.optimization_barrier(jnp.mean((mixed - center) ** 2, axis=-1, keepdims=True))
    normed = (mixed - center) * lax.rsqrt(spread + norm_eps)
    return jax.nn.silu(normed * gain + shift)

def bottleneck(inputs, reduce_w, mixer_w, expand_w, gain, shift):
    pre_act = low_back(jnp.einsum('nhwi,io->nhwo', low(inputs), reduce_w, precision=highest))
    hidden = low(jax.nn.silu(pre_act))
    mixed = low_back(lax.conv_general_dilated(hidden, mixer_w, (1, 1), 'SAME', dimension_numbers=('NHWC', 'HWIO', 'NHWC'), precision=highest))
    branch_in = low(norm_act(mixed, gain, shift))
    return inputs + low_back(jnp.einsum('nhwi,io->nhwo', branch_in, expand_w, precision=highest))

def forward(patches, first_reduce, first_mixer, first_expand, first_gain, first_shift, second_reduce, second_mixer, second_expand, second_gain, second_shift, readout_in, readout_out, live_rows):
    first_out = bottleneck(patches, first_reduce, first_mixer, first_expand, first_gain, first_shift)
    pooled = first_out.reshape(GRIDS, POOLED, 2, POOLED, 2, C).mean(axis=(2, 4))
    second_out = bottleneck(pooled, second_reduce, second_mixer, second_expand, second_gain, second_shift)
    flat = low(second_out.reshape(GRIDS * POOLED * POOLED, C))
    lifted = low_back(jnp.dot(flat, readout_in, precision=highest))
    activated = low(jax.nn.gelu(lifted, approximate=False))
    return jnp.dot(activated, readout_out, precision=highest) * live_rows[:, None]

def reference(patches, first_reduce, first_mixer, first_expand, first_gain, first_shift, second_reduce, second_mixer, second_expand, second_gain, second_shift, readout_in, readout_out, cotangent, live_counts):
    slot_ids = jnp.arange(GRIDS).astype(jnp.int32)
    group_ids = (slot_ids // SLOTS).astype(jnp.int32)
    live_slots = (slot_ids % SLOTS < live_counts[group_ids]).astype(jnp.float32)
    live_rows = jnp.repeat(live_slots, POOLED * POOLED)
    params = (patches, first_reduce, first_mixer, first_expand, first_gain, first_shift, second_reduce, second_mixer, second_expand, second_gain, second_shift, readout_in, readout_out)
    params = tuple((item.astype(jnp.float32) for item in params))

    def wrapped(*values):
        return forward(*values, live_rows)
    outputs, pullback = jax.vjp(wrapped, *params)
    grads = pullback(cotangent.astype(jnp.float32))
    return (outputs.astype(jnp.bfloat16), grads[0], grads[1], grads[2], grads[3], grads[4], grads[5], grads[6], grads[7], grads[8], grads[9], grads[10], grads[11], grads[12])
```

```python
import functools

import jax
import jax.numpy as jnp
import numpy as np
from jax import lax
from jax.experimental import pallas as pl
from jax.experimental.pallas import tpu as pltpu
from jax.sharding import PartitionSpec as P

norm_eps = 1e-06


def conv_same(image, kernel):
    return lax.conv_general_dilated(
        image,
        kernel,
        (1, 1),
        "SAME",
        dimension_numbers=("NHWC", "HWIO", "NHWC"),
        preferred_element_type=jnp.float32,
    )


def silu_back(values, grad_values):
    return jax.vjp(jax.nn.silu, values)[1](grad_values)[0]


def gelu_exact(values):
    return jax.nn.gelu(values, approximate=False)


def gelu_back(values, grad_values):
    return jax.vjp(gelu_exact, values)[1](grad_values)[0]


def block_forward(inputs, reduce_w, mixer_w, expand_w, gain, shift):
    num_grids, grid_height, grid_width, local_chans = inputs.shape
    pixel_rows = num_grids * grid_height * grid_width
    low_in = inputs.astype(jnp.bfloat16).reshape(pixel_rows, local_chans)
    full_in = lax.all_gather(low_in, "mp", axis=1, tiled=True)
    total_chans = full_in.shape[1]
    pre_act = jnp.dot(full_in, reduce_w, preferred_element_type=jnp.float32)
    hidden = jax.nn.silu(pre_act).astype(jnp.bfloat16)
    partial_mix = conv_same(
        hidden.reshape(num_grids, grid_height, grid_width, local_chans), mixer_w
    )
    mixed_sum = lax.psum_scatter(
        partial_mix.reshape(pixel_rows, total_chans).astype(jnp.bfloat16),
        "mp",
        scatter_dimension=1,
        tiled=True,
    ).astype(jnp.float32)
    row_total, row_squares = lax.psum(
        (jnp.sum(mixed_sum, axis=1), jnp.sum(mixed_sum * mixed_sum, axis=1)), "mp"
    )
    center = row_total / total_chans
    inv_std = lax.rsqrt(row_squares / total_chans - center * center + norm_eps)
    normed = (mixed_sum - center[:, None]) * inv_std[:, None]
    affine = normed * gain + shift
    branch_in = jax.nn.silu(affine).astype(jnp.bfloat16)
    partial_out = jnp.dot(branch_in, expand_w, preferred_element_type=jnp.float32)
    branch_out = lax.psum_scatter(
        partial_out.astype(jnp.bfloat16), "mp", scatter_dimension=1, tiled=True
    ).astype(jnp.float32)
    outputs = inputs + branch_out.reshape(inputs.shape)
    return (outputs, (full_in, pre_act, hidden, normed, inv_std, affine, branch_in))


def block_backward(grad_out, saved, reduce_w, mixer_w, expand_w, gain):
    full_in, pre_act, hidden, normed, inv_std, affine, branch_in = saved
    num_grids, grid_height, grid_width, local_chans = grad_out.shape
    pixel_rows = num_grids * grid_height * grid_width
    grad_rows = grad_out.reshape(pixel_rows, local_chans)
    grad_branch = lax.all_gather(grad_rows.astype(jnp.bfloat16), "mp", axis=1, tiled=True)
    total_chans = grad_branch.shape[1]
    expand_grad = jnp.einsum(
        "ri,ro->io", branch_in, grad_branch, preferred_element_type=jnp.float32
    )
    grad_act = jnp.einsum("ro,io->ri", grad_branch, expand_w, preferred_element_type=jnp.float32)
    grad_affine = silu_back(affine, grad_act)
    gain_grad = jnp.sum(grad_affine * normed, axis=0)
    shift_grad = jnp.sum(grad_affine, axis=0)
    scaled = grad_affine * gain
    sum_plain, sum_normed = lax.psum(
        (jnp.sum(scaled, axis=1), jnp.sum(scaled * normed, axis=1)), "mp"
    )
    grad_mixed = inv_std[:, None] * (
        scaled - sum_plain[:, None] / total_chans - normed * sum_normed[:, None] / total_chans
    )
    mixed_full = lax.all_gather(grad_mixed.astype(jnp.bfloat16), "mp", axis=1, tiled=True)
    mixed_image = mixed_full.reshape(num_grids, grid_height, grid_width, total_chans)
    flipped = jnp.transpose(mixer_w[::-1, ::-1], (0, 1, 3, 2))
    grad_hidden = conv_same(mixed_image, flipped).reshape(pixel_rows, local_chans)
    padded = jnp.pad(
        hidden.reshape(num_grids, grid_height, grid_width, local_chans),
        ((0, 0), (1, 1), (1, 1), (0, 0)),
    )
    mixer_grad = jnp.stack(
        [
            jnp.stack(
                [
                    jnp.einsum(
                        "nhwi,nhwo->io",
                        padded[
                            :,
                            offset_h : offset_h + grid_height,
                            offset_w : offset_w + grid_width,
                            :,
                        ],
                        mixed_image,
                        preferred_element_type=jnp.float32,
                    )
                    for offset_w in range(3)
                ]
            )
            for offset_h in range(3)
        ]
    )
    grad_pre = silu_back(pre_act, grad_hidden).astype(jnp.bfloat16)
    reduce_grad = jnp.einsum("ri,ro->io", full_in, grad_pre, preferred_element_type=jnp.float32)
    partial_in = jnp.einsum("ro,io->ri", grad_pre, reduce_w, preferred_element_type=jnp.float32)
    grad_in = (
        lax.psum_scatter(
            partial_in.astype(jnp.bfloat16), "mp", scatter_dimension=1, tiled=True
        ).astype(jnp.float32)
        + grad_rows
    )
    return (
        grad_in.reshape(grad_out.shape),
        (reduce_grad, mixer_grad, expand_grad, gain_grad, shift_grad),
    )


def body(
    patches,
    first_reduce,
    first_mixer,
    first_expand,
    first_gain,
    first_shift,
    second_reduce,
    second_mixer,
    second_expand,
    second_gain,
    second_shift,
    readout_in,
    readout_out,
    cotangent,
    live_counts,
):
    num_grids, grid_height, grid_width, local_chans = patches.shape
    pooled_side = grid_height // 2
    patch_values = patches.astype(jnp.float32)
    first_out = block_forward(
        patch_values, first_reduce, first_mixer, first_expand, first_gain, first_shift
    )[0]
    pooled = first_out.reshape(num_grids, pooled_side, 2, pooled_side, 2, local_chans).mean(
        axis=(2, 4)
    )
    second_out = block_forward(
        pooled, second_reduce, second_mixer, second_expand, second_gain, second_shift
    )[0]
    token_count = num_grids * pooled_side * pooled_side
    flat = second_out.astype(jnp.bfloat16).reshape(token_count, local_chans)
    flat_full = lax.all_gather(flat, "mp", axis=1, tiled=True)
    lifted = jnp.dot(flat_full, readout_in, preferred_element_type=jnp.float32)
    activated = gelu_exact(lifted).astype(jnp.bfloat16)
    partial_tokens = jnp.dot(activated, readout_out, preferred_element_type=jnp.float32)
    summed = lax.psum_scatter(
        partial_tokens.astype(jnp.bfloat16), "mp", scatter_dimension=1, tiled=True
    ).astype(jnp.float32)
    live_slots = (jnp.arange(num_grids) < live_counts[0]).astype(jnp.float32)
    live_rows = jnp.repeat(live_slots, pooled_side * pooled_side)
    tokens = (summed * live_rows[:, None]).astype(jnp.bfloat16)
    grad_tokens = cotangent * live_rows[:, None].astype(jnp.bfloat16)
    grad_full = lax.all_gather(grad_tokens, "mp", axis=1, tiled=True)
    readout_out_grad = jnp.einsum(
        "ri,ro->io", activated, grad_full, preferred_element_type=jnp.float32
    )
    grad_act = jnp.einsum("ro,io->ri", grad_full, readout_out, preferred_element_type=jnp.float32)
    grad_lift = gelu_back(lifted, grad_act).astype(jnp.bfloat16)
    readout_in_grad = jnp.einsum(
        "ri,ro->io", flat_full, grad_lift, preferred_element_type=jnp.float32
    )
    partial_flat = jnp.einsum(
        "ro,io->ri", grad_lift, readout_in, preferred_element_type=jnp.float32
    )
    grad_flat = lax.psum_scatter(
        partial_flat.astype(jnp.bfloat16), "mp", scatter_dimension=1, tiled=True
    ).astype(jnp.float32)
    second_saved = block_forward(
        pooled, second_reduce, second_mixer, second_expand, second_gain, second_shift
    )[1]
    grad_pooled, second_grads = block_backward(
        grad_flat.reshape(num_grids, pooled_side, pooled_side, local_chans),
        second_saved,
        second_reduce,
        second_mixer,
        second_expand,
        second_gain,
    )
    spread_back = jnp.broadcast_to(
        0.25 * grad_pooled[:, :, None, :, None, :],
        (num_grids, pooled_side, 2, pooled_side, 2, local_chans),
    ).reshape(patches.shape)
    first_saved = block_forward(
        patch_values, first_reduce, first_mixer, first_expand, first_gain, first_shift
    )[1]
    patch_grads, first_grads = block_backward(
        spread_back, first_saved, first_reduce, first_mixer, first_expand, first_gain
    )
    summed_grads = (
        lax.psum(first_grads[0].astype(jnp.bfloat16), "dp").astype(jnp.float32),
        lax.psum(first_grads[1].astype(jnp.bfloat16), "dp").astype(jnp.float32),
        lax.psum(first_grads[2].astype(jnp.bfloat16), "dp").astype(jnp.float32),
        lax.psum(first_grads[3].astype(jnp.bfloat16), "dp").astype(jnp.float32),
        lax.psum(first_grads[4].astype(jnp.bfloat16), "dp").astype(jnp.float32),
        lax.psum(second_grads[0].astype(jnp.bfloat16), "dp").astype(jnp.float32),
        lax.psum(second_grads[1].astype(jnp.bfloat16), "dp").astype(jnp.float32),
        lax.psum(second_grads[2].astype(jnp.bfloat16), "dp").astype(jnp.float32),
        lax.psum(second_grads[3].astype(jnp.bfloat16), "dp").astype(jnp.float32),
        lax.psum(second_grads[4].astype(jnp.bfloat16), "dp").astype(jnp.float32),
        lax.psum(readout_in_grad.astype(jnp.bfloat16), "dp").astype(jnp.float32),
        lax.psum(readout_out_grad.astype(jnp.bfloat16), "dp").astype(jnp.float32),
    )
    return (
        tokens,
        patch_grads,
        summed_grads[0],
        summed_grads[1],
        summed_grads[2],
        summed_grads[3],
        summed_grads[4],
        summed_grads[5],
        summed_grads[6],
        summed_grads[7],
        summed_grads[8],
        summed_grads[9],
        summed_grads[10],
        summed_grads[11],
    )


MESH = pl.DeviceIdType.MESH
F32 = jnp.float32
BF16 = jnp.bfloat16
DMA = pltpu.SemaphoreType.DMA
VMEM_LIMIT = 60 * 2**20
ROW_PAD = 16


def dot_nn(a, b):
    return lax.dot_general(a, b, (((1,), (0,)), ((), ())), preferred_element_type=F32)


def dot_nt(a, b):
    return lax.dot_general(a, b, (((1,), (1,)), ((), ())), preferred_element_type=F32)


def dot_tn(a, b):
    return lax.dot_general(a, b, (((0,), (0,)), ((), ())), preferred_element_type=F32)


def dot_full(a, b):
    return lax.dot_general(
        a,
        b,
        (((1,), (0,)), ((), ())),
        precision=lax.Precision.HIGHEST,
        preferred_element_type=F32,
    )


def sigmoid(values):
    return 1.0 / (1.0 + jnp.exp(-values))


def silu(values):
    return values * sigmoid(values)


def silu_slope(values):
    gate = sigmoid(values)
    return gate * (1.0 + values * (1.0 - gate))


class Ring:
    def __init__(self, size):
        self.size = size
        self.reach = size // 2
        self.me = lax.axis_index("mp")
        half = self.me // 2
        self.spot = jnp.where(self.me % 2 == 0, half, size - 1 - half)
        self.right = self.index(self.spot + 1)
        self.left = self.index(self.spot - 1)

    def wrap(self, spot):
        return lax.rem(spot + 2 * self.size, self.size)

    def index(self, spot):
        spot = self.wrap(spot)
        return jnp.where(spot < self.reach, 2 * spot, 2 * (self.size - 1 - spot) + 1)

    def greet(self):
        barrier = pltpu.get_barrier_semaphore()
        for peer in (self.left, self.right):
            pl.semaphore_signal(barrier, inc=1, device_id={"mp": peer}, device_id_type=MESH)
        pl.semaphore_wait(barrier, 2)

    def copy(self, side, src, dst, send, recv):
        peer = self.right if side == 0 else self.left
        return pltpu.make_async_remote_copy(
            src_ref=src,
            dst_ref=dst,
            send_sem=send,
            recv_sem=recv,
            device_id={"mp": peer},
            device_id_type=MESH,
        )


class Gather:
    def __init__(self, ring, own, held, slot, halves, send, recv):
        self.ring, self.own, self.held, self.slot = ring, own, held, slot
        self.halves, self.send, self.recv, self.copies = halves, send, recv, {}

    def _start(self, step):
        ring = self.ring
        for side in range(2):
            away = step - 1
            spot = ring.wrap(ring.spot - away if side == 0 else ring.spot + away)
            dst = self.held.at[self.slot(spot)]
            src = self.own if step == 1 else dst
            if step == ring.reach:
                src, dst = (ref.at[self.halves[side]] for ref in (src, dst))
            copy = ring.copy(
                side, src, dst, self.send.at[side, step - 1], self.recv.at[side, step - 1]
            )
            copy.start()
            self.copies[side, step] = copy

    def start(self):
        self._start(1)

    def arrive(self, step):
        for side in range(2):
            self.copies[side, step].wait_recv()

    def forward(self, step):
        self._start(step + 1)

    def drain(self):
        for copy in self.copies.values():
            copy.wait_send()

    def spots(self, step):
        ring = self.ring
        if step == ring.reach:
            return [ring.wrap(ring.spot + step)]
        return [ring.wrap(ring.spot - step), ring.wrap(ring.spot + step)]


class Scatter:
    def __init__(self, ring, term, out, terms, halves, send, recv):
        self.ring, self.term, self.out, self.inbox = ring, term, out[0], out[1]
        self.terms, self.halves, self.send, self.recv, self.copies = terms, halves, send, recv, {}

    def _start(self, side, step):
        src, dst = self.out.at[side, step - 1], self.inbox.at[side, step - 1]
        if step == 1:
            src, dst = (ref.at[self.halves[side]] for ref in (src, dst))
        copy = self.ring.copy(
            side, src, dst, self.send.at[side, step - 1], self.recv.at[side, step - 1]
        )
        copy.start()
        self.copies[side, step] = copy

    def start(self):
        ring = self.ring
        value = self.term(ring.wrap(ring.spot + ring.reach)).astype(BF16)
        for side in range(2):
            self.out[side, 0] = value
            self._start(side, 1)

    def prepare(self, step):
        ring = self.ring
        away = ring.reach + 1 - step
        self.terms[0] = self.term(ring.wrap(ring.spot + away))
        if away > 0:
            self.terms[1] = self.term(ring.wrap(ring.spot - away))

    def step(self, step):
        for side in range(2):
            self.copies[side, step - 1].wait_recv()
            if step == 2:
                mine, other = self.halves[side], self.halves[1 - side]
                got = self.inbox[(side, 0) + mine].astype(F32)
                self.out[(side, 1) + mine] = (self.terms[(side,) + mine] + got).astype(BF16)
                self.out[(side, 1) + other] = self.terms[(side,) + other].astype(BF16)
            else:
                got = self.inbox[side, step - 2].astype(F32)
                self.out[side, step - 1] = (self.terms[side] + got).astype(BF16)
            self._start(side, step)

    def finish(self):
        reach = self.ring.reach
        for side in range(2):
            self.copies[side, reach].wait_recv()
        return (
            self.terms[0]
            + self.inbox[0, reach - 1].astype(F32)
            + self.inbox[1, reach - 1].astype(F32)
        )

    def drain(self):
        for copy in self.copies.values():
            copy.wait_send()

    def run(self):
        reach = self.ring.reach
        self.start()
        for step in range(2, reach + 1):
            self.prepare(step)
            self.step(step)
        self.prepare(reach + 1)
        return self.finish()


def run_gather(gather, each=None):
    reach = gather.ring.reach
    gather.start()
    for step in range(1, reach + 1):
        gather.arrive(step)
        if step < reach:
            gather.forward(step)
        if each is not None:
            for spot in gather.spots(step):
                each(spot)


def row_halves(rows):
    return ((pl.ds(0, rows // 2),), (pl.ds(rows // 2, rows // 2),))


def column_halves(columns):
    every = slice(None)
    return (
        (every, pl.ds(0, columns // 2)),
        (every, pl.ds(columns // 2, columns // 2)),
    )


def pool_places(side):
    small = side // 2
    place = np.zeros((3 * ROW_PAD, 6 * side), np.float32)
    for row in range(6):
        for column in range(side):
            place[(row // 2) * ROW_PAD + column // 2, row * side + column] = 0.25
    assert small <= ROW_PAD
    return place


def token_places(grids, small):
    place = np.zeros((grids * small * small, grids * small * ROW_PAD), np.float32)
    for line in range(grids * small):
        for column in range(small):
            place[line * small + column, line * ROW_PAD + column] = 1.0
    return place


def norm_rows(mixed, gain, shift):
    center = jnp.mean(mixed, axis=1, keepdims=True)
    apart = mixed - center
    inv_std = lax.rsqrt(jnp.mean(apart * apart, axis=1, keepdims=True) + norm_eps)
    normed = apart * inv_std
    return normed, inv_std, normed * gain + shift


def wide_vector(held, row):
    return jnp.concatenate([held[m, row : row + 1, :] for m in range(held.shape[0])], axis=1)


def spread_taps(image, taps, grids, side, width):
    chans = image.shape[-1]
    rows = side * width

    def one(g, carry):
        for kh in range(3):
            for kw in range(3):
                piece = image[g, kh : kh + side, 7 + kw : 7 + kw + width, :]
                at = (kh * 3 + kw) * chans
                taps[pl.ds(pl.multiple_of(g * rows, 16), rows), at : at + chans] = (
                    piece.reshape(rows, chans).astype(BF16)
                )
        return carry

    lax.fori_loop(0, grids, one, 0)


def collect_taps(image, product, grids, side, width):
    chans = image.shape[-1]
    rows = side * width

    def one(g, carry):
        image[g] = jnp.zeros(image.shape[1:], F32)
        for kh in range(3):
            for kw in range(3):
                at = (kh * 3 + kw) * chans
                piece = product[pl.ds(pl.multiple_of(g * rows, 16), rows), at : at + chans]
                image[g, kh : kh + side, 7 + kw : 7 + kw + width, :] += piece.reshape(
                    side, width, chans
                )
        return carry

    lax.fori_loop(0, grids, one, 0)


def first_forward(
    size, grids, side,
    x, reduce_w, mixer_w, expand_w, vectors, pool,
    x_full, pre, taps, normed, inv_std, branch_sum, pooled, expand_full, vec_full,
    image, out, terms, x_rows, send, recv,
):
    ring = Ring(size)
    ring.greet()
    rows, chans = x.shape
    share = rows // size
    x_full[ring.me] = x[...]
    expand_full[ring.me] = expand_w[...]
    vec_full[ring.me] = vectors[...]
    gx = Gather(ring, x, x_full, ring.index, row_halves(rows), send.at[0], recv.at[0])
    ge = Gather(ring, expand_w, expand_full, ring.index, row_halves(chans), send.at[1], recv.at[1])
    gv = Gather(ring, vectors, vec_full, ring.index, row_halves(16), send.at[2], recv.at[2])

    def add(spot):
        m = ring.index(spot)
        weight = reduce_w[pl.ds(pl.multiple_of(m * chans, chans), chans), :]
        pre[...] += dot_nn(x_full[m], weight)

    own = reduce_w[pl.ds(pl.multiple_of(ring.me * chans, chans), chans), :]
    pre[...] = dot_nn(x[...], own)
    image[...] = jnp.zeros(image.shape, F32)
    run_gather(gx, add)
    run_gather(ge)
    run_gather(gv)
    hidden = silu(pre[...])
    image[:, 1 : 1 + side, 8 : 8 + side, :] = hidden.reshape(grids, side, side, chans)
    spread_taps(image, taps, grids, side, side)

    def term(spot):
        return dot_nn(taps[pl.ds(pl.multiple_of(spot * share, 16), share), :], mixer_w[...])

    total = size * chans
    rs = Scatter(
        ring, term, (out.at[0], out.at[1]), terms, column_halves(total), send.at[3], recv.at[3]
    )
    mixed = rs.run()
    gain, shift = wide_vector(vec_full, 0), wide_vector(vec_full, 1)
    value, inverse, affine = norm_rows(mixed, gain, shift)
    normed[...] = value
    inv_std[...] = jnp.broadcast_to(inverse, inv_std.shape)
    branch = silu(affine).astype(BF16)
    result = dot_nn(branch, expand_full[...].reshape(total, total))
    mine = pl.ds(pl.multiple_of(ring.spot * share, 16), share)
    for m in range(size):
        x_rows[:, m * chans : (m + 1) * chans] = x_full[m, mine, :].astype(F32)
    pooled[...] = dot_full(pool[...], x_rows[...] + result)
    branch_sum[...] = (4.0 * dot_full(pool[...], branch.astype(F32))).astype(BF16)
    for item in (gx, ge, gv, rs):
        item.drain()


def second_forward(
    size, grids, small,
    pooled, reduce_w, mixer_w, expand_w, vec_full, readout_in, readout_out, cotangent, live, places,
    x_full, pre, taps, normed, inv_std, branch, expand_full, grad_rows, tokens, out_grad, in_grad,
    image, own, flat_full, cot_full, lifted, act_live, grad_act, grad_lift, out, terms, tok_out, tok_terms, send, recv,
):
    ring = Ring(size)
    ring.greet()
    share, total = pooled.shape
    chans = total // size
    rows = size * share
    part = readout_in.shape[1]
    near = lambda spot: spot
    own[0] = pooled[...].astype(BF16)
    x_full[ring.spot] = own[0]
    expand_full[ring.me] = expand_w[...]
    cot_full[ring.me] = cotangent[...]
    gx = Gather(ring, own.at[0], x_full, near, column_halves(total), send.at[0], recv.at[0])
    ge = Gather(ring, expand_w, expand_full, ring.index, row_halves(chans), send.at[1], recv.at[1])
    gc = Gather(
        ring, cotangent, cot_full, ring.index, row_halves(cotangent.shape[0]), send.at[2], recv.at[2]
    )
    image[...] = jnp.zeros(image.shape, F32)
    run_gather(gx)
    run_gather(ge)
    run_gather(gc)
    pre[...] = dot_nn(x_full[...].reshape(rows, total), reduce_w[...])
    hidden = silu(pre[...])
    image[:, 1 : 1 + small, 8 : 8 + ROW_PAD, :] = hidden.reshape(grids, small, ROW_PAD, chans)
    spread_taps(image, taps, grids, small, ROW_PAD)

    def mix_term(spot):
        return dot_nn(taps[pl.ds(pl.multiple_of(spot * share, 16), share), :], mixer_w[...])

    halves = column_halves(total)
    rs = Scatter(
        ring, mix_term, (out.at[0], out.at[1]), terms, halves, send.at[3], recv.at[3]
    )
    mixed = rs.run()
    gain, shift = wide_vector(vec_full, 2), wide_vector(vec_full, 3)
    value, inverse, affine = norm_rows(mixed, gain, shift)
    normed[...] = value
    inv_std[...] = jnp.broadcast_to(inverse, inv_std.shape)
    branch[...] = silu(affine).astype(BF16)
    result = pooled[...] + dot_nn(branch[...], expand_full[...].reshape(total, total))
    own[1] = result.astype(BF16)
    flat_full[ring.spot] = own[1]
    gf = Gather(ring, own.at[1], flat_full, near, halves, send.at[4], recv.at[4])
    run_gather(gf)
    flat = dot_nn(places[...], flat_full[...].reshape(rows, total)).astype(BF16)
    lifted[...] = dot_nn(flat, readout_in[...])
    cdf = 0.5 * (1.0 + lax.erf(lifted[...] * 0.7071067811865476))
    activated = (lifted[...] * cdf).astype(BF16)
    act_live[0] = activated
    act_live[1] = (activated.astype(F32) * live[...]).astype(BF16)
    grad_act[...] = jnp.zeros(grad_act.shape, F32)

    def back(m, carry):
        at = pl.ds(pl.multiple_of(m * part, 128), part)
        grad_act[...] += dot_nt(cot_full[m], readout_out[:, at])
        out_grad[:, at] = dot_tn(act_live[1], cot_full[m]).astype(BF16)
        return carry

    lax.fori_loop(0, size, back, 0)
    slope = cdf + lifted[...] * jnp.exp(-0.5 * lifted[...] * lifted[...]) * 0.3989422804014327
    lift = (grad_act[...] * live[...] * slope).astype(BF16)
    in_grad[...] = dot_tn(flat, lift).astype(BF16)
    grad_lift[...] = dot_tn(places[...], lift).astype(BF16)

    def flat_term(spot):
        return dot_nt(grad_lift[pl.ds(pl.multiple_of(spot * share, 16), share), :], readout_in[...])

    rf = Scatter(
        ring, flat_term, (out.at[2], out.at[3]), terms, halves, send.at[5], recv.at[5]
    )
    grad_rows[...] = rf.run()

    def token_term(spot):
        at = pl.ds(pl.multiple_of(ring.index(spot) * part, 128), part)
        return dot_nn(act_live[0], readout_out[:, at])

    rt = Scatter(
        ring, token_term, (tok_out.at[0], tok_out.at[1]), tok_terms, column_halves(part), send.at[6], recv.at[6]
    )
    tokens[...] = (rt.run() * live[...]).astype(BF16)
    for item in (gx, ge, gc, rs, gf, rf, rt):
        item.drain()


def norm_back(grad_branch, normed, inv_std, gain, shift):
    affine = normed * gain + shift
    grad_affine = grad_branch * silu_slope(affine)
    gain_grad = jnp.sum(grad_affine * normed, axis=0, keepdims=True)
    shift_grad = jnp.sum(grad_affine, axis=0, keepdims=True)
    scaled = grad_affine * gain
    mean_plain = jnp.mean(scaled, axis=1, keepdims=True)
    mean_normed = jnp.mean(scaled * normed, axis=1, keepdims=True)
    return inv_std * (scaled - mean_plain - normed * mean_normed), gain_grad, shift_grad


def exchange_columns(ring, src, held, send, recv):
    chans = held.shape[-1]
    mine = pl.ds(pl.multiple_of(ring.me * chans, chans), chans)
    held[ring.me] = src[:, mine]
    copies = []
    for away in range(1, ring.size):
        peer = lax.rem(ring.me + away, ring.size)
        copy = pltpu.make_async_remote_copy(
            src_ref=src.at[:, pl.ds(pl.multiple_of(peer * chans, chans), chans)],
            dst_ref=held.at[ring.me],
            send_sem=send.at[away - 1],
            recv_sem=recv.at[away - 1],
            device_id={"mp": peer},
            device_id_type=MESH,
        )
        copy.start()
        copies.append(copy)
    return copies


def greet_all(ring):
    barrier = pltpu.get_barrier_semaphore()
    for away in range(1, ring.size):
        peer = lax.rem(ring.me + away, ring.size)
        pl.semaphore_signal(barrier, inc=1, device_id={"mp": peer}, device_id_type=MESH)
    pl.semaphore_wait(barrier, ring.size - 1)


def block_tail(ring, low, branch, low_full, branch_full, expand_grad, send, recv, asend, arecv):
    total = low.shape[1]
    copies = exchange_columns(ring, branch, branch_full, asend, arecv)
    low_full[ring.spot] = low[...]
    gl = Gather(ring, low, low_full, lambda spot: spot, column_halves(total), send, recv)
    run_gather(gl)
    for copy in copies:
        copy.wait()
    gl.drain()
    expand_grad[...] = jnp.zeros(expand_grad.shape, BF16)
    acc = None
    for spot in range(ring.size):
        m = 2 * spot if spot < ring.reach else 2 * (ring.size - 1 - spot) + 1
        part = dot_tn(branch_full[m], low_full[spot])
        acc = part if acc is None else acc + part
    expand_grad[...] = acc.astype(BF16)


def second_backward(
    size, grids, small,
    grad_rows, normed, inv_std, vec_full, branch, expand_full, taps, x_full, pre, mixer_w, reduce_w,
    grad_in, mixer_grad, reduce_grad, expand_grad, vec_grad,
    image, low, low_full, branch_full, mix_full, product, grad_pre, out, terms, send, recv, asend, arecv,
):
    ring = Ring(size)
    greet_all(ring)
    share, total = grad_rows.shape
    rows = size * share
    halves = column_halves(total)
    gain, shift = wide_vector(vec_full, 2), wide_vector(vec_full, 3)
    low[0] = grad_rows[...].astype(BF16)
    grad_branch = dot_nt(low[0], expand_full[...].reshape(total, total))
    mix, gain_grad, shift_grad = norm_back(
        grad_branch, normed[...], inv_std[:, 0:1], gain, shift
    )
    vec_grad[0:1, :] = gain_grad
    vec_grad[1:2, :] = shift_grad
    low[1] = mix.astype(BF16)
    mix_full[ring.spot] = low[1]
    gm = Gather(ring, low.at[1], mix_full, lambda spot: spot, halves, send.at[0], recv.at[0])
    run_gather(gm)
    flat_mix = mix_full[...].reshape(rows, total)
    product[...] = dot_nt(flat_mix, mixer_w[...])
    collect_taps(image, product, grids, small, ROW_PAD)
    grad_hidden = image[:, 1 : 1 + small, 8 : 8 + ROW_PAD, :].reshape(pre.shape)
    grad_pre[...] = (grad_hidden * silu_slope(pre[...])).astype(BF16)

    def term(spot):
        return dot_nt(grad_pre[pl.ds(pl.multiple_of(spot * share, 16), share), :], reduce_w[...])

    rs = Scatter(ring, term, (out.at[0], out.at[1]), terms, halves, send.at[1], recv.at[1])
    grad_in[...] = rs.run() + grad_rows[...]
    mixer_grad[...] = dot_tn(taps[...], flat_mix).astype(BF16)
    reduce_grad[...] = dot_tn(x_full[...].reshape(rows, total), grad_pre[...]).astype(BF16)
    block_tail(
        ring, low.at[0], branch, low_full, branch_full, expand_grad, send.at[2], recv.at[2], asend, arecv
    )
    gm.drain()
    rs.drain()


def first_backward(
    size, grids, side,
    grad_pooled, spread, normed, inv_std, vec_full, branch_sum, expand_full, taps, x_full, pre, mixer_w, reduce_w,
    patch_grads, mixer_grad, reduce_grad, expand_grad, vec_grad,
    image, low, mix, low_full, branch_full, mix_full, product, grad_pre, grad_out, out, terms, send, recv, asend, arecv,
):
    ring = Ring(size)
    greet_all(ring)
    share, total = normed.shape
    chans = total // size
    rows = size * share
    halves = column_halves(total)
    gain, shift = wide_vector(vec_full, 0), wide_vector(vec_full, 1)
    quarter = 0.25 * grad_pooled[...]
    low[...] = quarter.astype(BF16)
    grad_out[...] = dot_full(spread[...], quarter)
    grad_small = dot_nt(low[...], expand_full[...].reshape(total, total))
    grad_branch = dot_full(spread[...], grad_small)
    value, gain_grad, shift_grad = norm_back(
        grad_branch, normed[...], inv_std[:, 0:1], gain, shift
    )
    vec_grad[0:1, :] = gain_grad
    vec_grad[1:2, :] = shift_grad
    mix[...] = value.astype(BF16)
    mix_full[ring.spot] = mix[...]
    gm = Gather(ring, mix, mix_full, lambda spot: spot, halves, send.at[0], recv.at[0])
    run_gather(gm)

    def shares(q, carry):
        product[pl.ds(pl.multiple_of(q * share, 16), share), :] = dot_nt(mix_full[q], mixer_w[...])
        return carry

    lax.fori_loop(0, size, shares, 0)
    collect_taps(image, product, grids, side, side)
    grad_hidden = image[:, 1 : 1 + side, 8 : 8 + side, :].reshape(pre.shape)
    grad_pre[...] = (grad_hidden * silu_slope(pre[...])).astype(BF16)
    mine = pl.ds(pl.multiple_of(ring.spot * share, 16), share)

    def term(spot):
        at = pl.multiple_of(ring.index(spot) * chans, chans)
        return dot_nt(grad_pre[...], reduce_w[pl.ds(at, chans), :])

    def term_and_rows(spot):
        at = pl.ds(pl.multiple_of(ring.index(spot) * chans, chans), chans)
        product[:, 0:chans] = term(spot)
        product[mine, 0:chans] += grad_out[:, at]
        return product[:, 0:chans]

    rs = Scatter(
        ring, term_and_rows, (out.at[0], out.at[1]), terms, row_halves(rows), send.at[1], recv.at[1]
    )
    patch_grads[...] = rs.run()

    def weights(tap, carry):
        at = pl.ds(pl.multiple_of(tap * chans, chans), chans)
        mixer_grad[at, :] = dot_tn(
            taps[:, at], mix_full[...].reshape(rows, total)
        ).astype(BF16)
        return carry

    lax.fori_loop(0, 9, weights, 0)

    def reduces(m, carry):
        at = pl.ds(pl.multiple_of(m * chans, chans), chans)
        reduce_grad[at, :] = dot_tn(x_full[m], grad_pre[...]).astype(BF16)
        return carry

    lax.fori_loop(0, size, reduces, 0)
    block_tail(
        ring, low, branch_sum, low_full, branch_full, expand_grad, send.at[2], recv.at[2], asend, arecv
    )
    gm.drain()
    rs.drain()


def sum_groups(count, *refs):
    ins, outs = refs[:count], refs[count : 2 * count]
    from_core, half_sum, from_far, final = (refs[(2 + k) * count : (3 + k) * count] for k in range(4))
    send, recv = refs[6 * count :]
    me = lax.axis_index("dp")
    core = lax.rem(me, 2)
    other = 1 - core
    twin, far = me - core + other, lax.rem(me + 2, 4)
    barrier = pltpu.get_barrier_semaphore()
    for peer in (twin, far):
        pl.semaphore_signal(barrier, inc=1, device_id={"dp": peer}, device_id_type=MESH)
    pl.semaphore_wait(barrier, 2)

    def go(step, k, src, dst, peer):
        copy = pltpu.make_async_remote_copy(
            src_ref=src,
            dst_ref=dst,
            send_sem=send.at[step, k],
            recv_sem=recv.at[step, k],
            device_id={"dp": peer},
            device_id_type=MESH,
        )
        copy.start()
        return copy

    copies = {}

    def half(k, which):
        rows = ins[k].shape[0] // 2
        return pl.ds(pl.multiple_of(which * rows, 16), rows)

    for k in range(count):
        copies[0, k] = go(0, k, ins[k].at[half(k, other)], from_core[k], twin)
    for k in range(count):
        copies[0, k].wait_recv()
        mine = ins[k][half(k, core), :]
        half_sum[k][...] = (mine.astype(F32) + from_core[k][...].astype(F32)).astype(BF16)
        copies[1, k] = go(1, k, half_sum[k], from_far[k], far)
    for k in range(count):
        copies[1, k].wait_recv()
        total = (half_sum[k][...].astype(F32) + from_far[k][...].astype(F32)).astype(BF16)
        final[k][0] = total
        copies[2, k] = go(2, k, final[k].at[0], final[k].at[1], twin)
        outs[k][half(k, core), :] = total.astype(F32)
    for k in range(count):
        copies[2, k].wait_recv()
        outs[k][half(k, other), :] = final[k][1].astype(F32)
    for copy in copies.values():
        copy.wait_send()


def sum_vectors(size, vectors, result, held, sums, asend, arecv, bsend, brecv):
    ring = Ring(size)
    barrier = pltpu.get_barrier_semaphore()
    me = lax.axis_index("dp")
    groups = sums.shape[0]
    for away in range(1, ring.size):
        peer = lax.rem(ring.me + away, ring.size)
        pl.semaphore_signal(barrier, inc=1, device_id={"mp": peer}, device_id_type=MESH)
    for away in range(1, groups):
        peer = lax.rem(me + away, groups)
        pl.semaphore_signal(barrier, inc=1, device_id={"dp": peer}, device_id_type=MESH)
    pl.semaphore_wait(barrier, ring.size - 1 + groups - 1)
    for copy in exchange_columns(ring, vectors, held, asend, arecv):
        copy.wait()
    sums[me] = jnp.sum(held[...], axis=0)
    copies = []
    for away in range(1, groups):
        copy = pltpu.make_async_remote_copy(
            src_ref=sums.at[me],
            dst_ref=sums.at[me],
            send_sem=bsend.at[away - 1],
            recv_sem=brecv.at[away - 1],
            device_id={"dp": lax.rem(me + away, groups)},
            device_id_type=MESH,
        )
        copy.start()
        copies.append(copy)
    for copy in copies:
        copy.wait()
    result[...] = jnp.sum(sums[...], axis=0)


def kernel_call(kernel, name, number, outs, scratch, flops=0):
    spec = pl.BlockSpec(memory_space=pltpu.VMEM)

    def run(*args):
        return pl.pallas_call(
            kernel,
            name=name,
            out_shape=outs,
            in_specs=[spec] * len(args),
            out_specs=[spec] * len(outs),
            scratch_shapes=scratch,
            cost_estimate=pl.CostEstimate(flops=flops, bytes_accessed=0, transcendentals=0),
            compiler_params=pltpu.CompilerParams(
                collective_id=number, has_side_effects=True, vmem_limit_bytes=VMEM_LIMIT
            ),
        )(*args)

    return run


def fast_body(
    size,
    patches,
    first_reduce,
    first_mixer,
    first_expand,
    first_gain,
    first_shift,
    second_reduce,
    second_mixer,
    second_expand,
    second_gain,
    second_shift,
    readout_in,
    readout_out,
    cotangent,
    live_counts,
):
    S = jax.ShapeDtypeStruct
    V = pltpu.VMEM
    grids, side, _, chans = patches.shape
    total = first_expand.shape[1]
    rows = grids * side * side
    share = rows // size
    small = side // 2
    few = 3 * ROW_PAD
    few_rows = few * size
    token_rows = grids * small * small
    part = readout_in.shape[1]
    wide = readout_out.shape[1]
    reach = size // 2
    pool = pool_places(side)
    places = token_places(grids, small)
    x = patches.reshape(rows, chans)
    mixer_1 = first_mixer.reshape(9 * chans, total)
    mixer_2 = second_mixer.reshape(9 * chans, total)
    vectors = jnp.stack([first_gain, first_shift, second_gain, second_shift] * 4)
    live_slots = (jnp.arange(grids) < live_counts[0]).astype(F32)
    live = jnp.repeat(live_slots, small * small)[:, None]

    outs = [
        S((size, rows, chans), BF16),
        S((rows, chans), F32),
        S((rows, 9 * chans), BF16),
        S((share, total), F32),
        S((share, 128), F32),
        S((few, total), BF16),
        S((few, total), F32),
        S((size, chans, total), BF16),
        S((size, 16, chans), F32),
    ]

    def boxes(r, c):
        return V((2, 2, reach, r, c), BF16)

    scratch = [
        V((grids, side + 2, side + 16, chans), F32),
        boxes(share, total),
        V((2, share, total), F32),
        V((share, total), F32),
        DMA((4, 2, reach)),
        DMA((4, 2, reach)),
    ]
    x_full1, pre1, taps1, normed1, inv1, branch1, pooled, expand1, vec_full = kernel_call(
        functools.partial(first_forward, size, grids, side), "first_forward", 1, outs, scratch
    )(x, first_reduce, mixer_1, first_expand, vectors, pool)

    outs = [
        S((size, few, total), BF16),
        S((few_rows, chans), F32),
        S((few_rows, 9 * chans), BF16),
        S((few, total), F32),
        S((few, 128), F32),
        S((few, total), BF16),
        S((size, chans, total), BF16),
        S((few, total), F32),
        S((token_rows, part), BF16),
        S((part, wide), BF16),
        S((total, part), BF16),
    ]
    scratch = [
        V((grids, small + 2, ROW_PAD + 16, chans), F32),
        V((2, few, total), BF16),
        V((size, few, total), BF16),
        V((size, token_rows, part), BF16),
        V((token_rows, part), F32),
        V((2, token_rows, part), BF16),
        V((token_rows, part), F32),
        V((few_rows, part), BF16),
        V((4, 2, reach, few, total), BF16),
        V((2, few, total), F32),
        boxes(token_rows, part),
        V((2, token_rows, part), F32),
        DMA((7, 2, reach)),
        DMA((7, 2, reach)),
    ]
    (
        x_full2, pre2, taps2, normed2, inv2, branch2, expand2, grad_rows, tokens, out_grad, in_grad,
    ) = kernel_call(
        functools.partial(second_forward, size, grids, small), "second_forward", 2, outs, scratch
    )(
        pooled, second_reduce, mixer_2, second_expand, vec_full, readout_in, readout_out, cotangent,
        live, places.astype(BF16),
    )

    outs = [
        S((few, total), F32),
        S((9 * chans, total), BF16),
        S((total, chans), BF16),
        S((chans, total), BF16),
        S((2, total), F32),
    ]
    scratch = [
        V((grids, small + 2, ROW_PAD + 16, chans), F32),
        V((2, few, total), BF16),
        V((size, few, total), BF16),
        V((size, few, chans), BF16),
        V((size, few, total), BF16),
        V((few_rows, 9 * chans), F32),
        V((few_rows, chans), BF16),
        boxes(few, total),
        V((2, few, total), F32),
        DMA((3, 2, reach)),
        DMA((3, 2, reach)),
        DMA((size - 1,)),
        DMA((size - 1,)),
    ]
    grad_pooled, mixer_grad2, reduce_grad2, expand_grad2, vec_grad2 = kernel_call(
        functools.partial(second_backward, size, grids, small), "second_backward", 3, outs, scratch
    )(
        grad_rows, normed2, inv2, vec_full, branch2, expand2, taps2, x_full2, pre2, mixer_2,
        second_reduce,
    )

    outs = [
        S((rows, chans), F32),
        S((9 * chans, total), BF16),
        S((total, chans), BF16),
        S((chans, total), BF16),
        S((2, total), F32),
    ]
    scratch = [
        V((grids, side + 2, side + 16, chans), F32),
        V((few, total), BF16),
        V((share, total), BF16),
        V((size, few, total), BF16),
        V((size, few, chans), BF16),
        V((size, share, total), BF16),
        V((rows, 9 * chans), F32),
        V((rows, chans), BF16),
        V((share, total), F32),
        boxes(rows, chans),
        V((2, rows, chans), F32),
        DMA((3, 2, reach)),
        DMA((3, 2, reach)),
        DMA((size - 1,)),
        DMA((size - 1,)),
    ]
    patch_grads, mixer_grad1, reduce_grad1, expand_grad1, vec_grad1 = kernel_call(
        functools.partial(first_backward, size, grids, side), "first_backward", 4, outs, scratch
    )(
        grad_pooled, np.ascontiguousarray(4.0 * pool.T), normed1, inv1, vec_full, branch1, expand1, taps1,
        x_full1, pre1, mixer_1, first_reduce,
    )

    def group_sum(number, name, grads):
        count = len(grads)
        sums = [S(g.shape, F32) for g in grads]
        halves = [(g.shape[0] // 2, g.shape[1]) for g in grads]
        scratch = [V(h, BF16) for h in halves * 3] + [V((2,) + h, BF16) for h in halves]
        scratch += [DMA((3, count)), DMA((3, count))]
        return kernel_call(functools.partial(sum_groups, count), name, number, sums, scratch)(*grads)

    out_sum, in_sum = group_sum(5, "sum_readout", [out_grad, in_grad])
    sums = group_sum(
        6,
        "sum_blocks",
        [mixer_grad2, reduce_grad2, expand_grad2, mixer_grad1, reduce_grad1, expand_grad1],
    )
    mixer2_sum, reduce2_sum, expand2_sum, mixer1_sum, reduce1_sum, expand1_sum = sums
    groups = 4
    vec_sum = kernel_call(
        functools.partial(sum_vectors, size),
        "sum_vectors",
        7,
        [S((8, chans), F32)],
        [
            V((size, 8, chans), F32),
            V((groups, 8, chans), F32),
            DMA((size - 1,)),
            DMA((size - 1,)),
            DMA((groups - 1,)),
            DMA((groups - 1,)),
        ],
    )(jnp.concatenate([vec_grad1, vec_grad2] * 2))[0]
    return (
        tokens,
        patch_grads.reshape(patches.shape),
        reduce1_sum,
        mixer1_sum.reshape(first_mixer.shape),
        expand1_sum,
        vec_sum[0],
        vec_sum[1],
        reduce2_sum,
        mixer2_sum.reshape(second_mixer.shape),
        expand2_sum,
        vec_sum[2],
        vec_sum[3],
        in_sum,
        out_sum,
    )


def fits(mesh, patches, first_reduce, readout_in):
    size, groups = mesh.shape["mp"], mesh.shape["dp"]
    grids, side, _, chans = patches.shape
    return (
        groups == 4
        and size % 2 == 0
        and chans % 128 == 0
        and readout_in.shape[1] % 128 == 0
        and grids * side == 6 * size
        and side % 8 == 0
        and side // 2 <= ROW_PAD
    )


def solution(mesh):
    in_specs = (
        P("dp", None, None, "mp"),
        P(None, "mp"),
        P(None, None, "mp", None),
        P("mp", None),
        P("mp"),
        P("mp"),
        P(None, "mp"),
        P(None, None, "mp", None),
        P("mp", None),
        P("mp"),
        P("mp"),
        P(None, "mp"),
        P("mp", None),
        P("dp", "mp"),
        P("dp"),
    )
    out_specs = (
        P("dp", "mp"),
        P("dp", None, None, "mp"),
        P(None, "mp"),
        P(None, None, "mp", None),
        P("mp", None),
        P("mp"),
        P("mp"),
        P(None, "mp"),
        P(None, None, "mp", None),
        P("mp", None),
        P("mp"),
        P("mp"),
        P(None, "mp"),
        P("mp", None),
    )

    def local(*args):
        if fits(mesh, args[0], args[1], args[11]):
            return fast_body(mesh.shape["mp"], *args)
        return body(*args)

    return jax.shard_map(local, mesh=mesh, in_specs=in_specs, out_specs=out_specs, check_vma=False)
```

```python
import functools

import jax
import jax.numpy as jnp
import numpy as np
from jax import lax
from jax.experimental import pallas as pl
from jax.experimental.pallas import tpu as pltpu
from jax.sharding import PartitionSpec as P

norm_eps = 1e-06


def conv_same(image, kernel):
    return lax.conv_general_dilated(
        image,
        kernel,
        (1, 1),
        "SAME",
        dimension_numbers=("NHWC", "HWIO", "NHWC"),
        preferred_element_type=jnp.float32,
    )


def silu_back(values, grad_values):
    return jax.vjp(jax.nn.silu, values)[1](grad_values)[0]


def gelu_exact(values):
    return jax.nn.gelu(values, approximate=False)


def gelu_back(values, grad_values):
    return jax.vjp(gelu_exact, values)[1](grad_values)[0]


def block_forward(inputs, reduce_w, mixer_w, expand_w, gain, shift):
    num_grids, grid_height, grid_width, local_chans = inputs.shape
    pixel_rows = num_grids * grid_height * grid_width
    low_in = inputs.astype(jnp.bfloat16).reshape(pixel_rows, local_chans)
    full_in = lax.all_gather(low_in, "mp", axis=1, tiled=True)
    total_chans = full_in.shape[1]
    pre_act = jnp.dot(full_in, reduce_w, preferred_element_type=jnp.float32)
    hidden = jax.nn.silu(pre_act).astype(jnp.bfloat16)
    partial_mix = conv_same(
        hidden.reshape(num_grids, grid_height, grid_width, local_chans), mixer_w
    )
    mixed_sum = lax.psum_scatter(
        partial_mix.reshape(pixel_rows, total_chans).astype(jnp.bfloat16),
        "mp",
        scatter_dimension=1,
        tiled=True,
    ).astype(jnp.float32)
    row_total, row_squares = lax.psum(
        (jnp.sum(mixed_sum, axis=1), jnp.sum(mixed_sum * mixed_sum, axis=1)), "mp"
    )
    center = row_total / total_chans
    inv_std = lax.rsqrt(row_squares / total_chans - center * center + norm_eps)
    normed = (mixed_sum - center[:, None]) * inv_std[:, None]
    affine = normed * gain + shift
    branch_in = jax.nn.silu(affine).astype(jnp.bfloat16)
    partial_out = jnp.dot(branch_in, expand_w, preferred_element_type=jnp.float32)
    branch_out = lax.psum_scatter(
        partial_out.astype(jnp.bfloat16), "mp", scatter_dimension=1, tiled=True
    ).astype(jnp.float32)
    outputs = inputs + branch_out.reshape(inputs.shape)
    return (outputs, (full_in, pre_act, hidden, normed, inv_std, affine, branch_in))


def block_backward(grad_out, saved, reduce_w, mixer_w, expand_w, gain):
    full_in, pre_act, hidden, normed, inv_std, affine, branch_in = saved
    num_grids, grid_height, grid_width, local_chans = grad_out.shape
    pixel_rows = num_grids * grid_height * grid_width
    grad_rows = grad_out.reshape(pixel_rows, local_chans)
    grad_branch = lax.all_gather(grad_rows.astype(jnp.bfloat16), "mp", axis=1, tiled=True)
    total_chans = grad_branch.shape[1]
    expand_grad = jnp.einsum(
        "ri,ro->io", branch_in, grad_branch, preferred_element_type=jnp.float32
    )
    grad_act = jnp.einsum("ro,io->ri", grad_branch, expand_w, preferred_element_type=jnp.float32)
    grad_affine = silu_back(affine, grad_act)
    gain_grad = jnp.sum(grad_affine * normed, axis=0)
    shift_grad = jnp.sum(grad_affine, axis=0)
    scaled = grad_affine * gain
    sum_plain, sum_normed = lax.psum(
        (jnp.sum(scaled, axis=1), jnp.sum(scaled * normed, axis=1)), "mp"
    )
    grad_mixed = inv_std[:, None] * (
        scaled - sum_plain[:, None] / total_chans - normed * sum_normed[:, None] / total_chans
    )
    mixed_full = lax.all_gather(grad_mixed.astype(jnp.bfloat16), "mp", axis=1, tiled=True)
    mixed_image = mixed_full.reshape(num_grids, grid_height, grid_width, total_chans)
    flipped = jnp.transpose(mixer_w[::-1, ::-1], (0, 1, 3, 2))
    grad_hidden = conv_same(mixed_image, flipped).reshape(pixel_rows, local_chans)
    padded = jnp.pad(
        hidden.reshape(num_grids, grid_height, grid_width, local_chans),
        ((0, 0), (1, 1), (1, 1), (0, 0)),
    )
    mixer_grad = jnp.stack(
        [
            jnp.stack(
                [
                    jnp.einsum(
                        "nhwi,nhwo->io",
                        padded[
                            :,
                            offset_h : offset_h + grid_height,
                            offset_w : offset_w + grid_width,
                            :,
                        ],
                        mixed_image,
                        preferred_element_type=jnp.float32,
                    )
                    for offset_w in range(3)
                ]
            )
            for offset_h in range(3)
        ]
    )
    grad_pre = silu_back(pre_act, grad_hidden).astype(jnp.bfloat16)
    reduce_grad = jnp.einsum("ri,ro->io", full_in, grad_pre, preferred_element_type=jnp.float32)
    partial_in = jnp.einsum("ro,io->ri", grad_pre, reduce_w, preferred_element_type=jnp.float32)
    grad_in = (
        lax.psum_scatter(
            partial_in.astype(jnp.bfloat16), "mp", scatter_dimension=1, tiled=True
        ).astype(jnp.float32)
        + grad_rows
    )
    return (
        grad_in.reshape(grad_out.shape),
        (reduce_grad, mixer_grad, expand_grad, gain_grad, shift_grad),
    )


def body(
    patches,
    first_reduce,
    first_mixer,
    first_expand,
    first_gain,
    first_shift,
    second_reduce,
    second_mixer,
    second_expand,
    second_gain,
    second_shift,
    readout_in,
    readout_out,
    cotangent,
    live_counts,
):
    num_grids, grid_height, grid_width, local_chans = patches.shape
    pooled_side = grid_height // 2
    patch_values = patches.astype(jnp.float32)
    first_out = block_forward(
        patch_values, first_reduce, first_mixer, first_expand, first_gain, first_shift
    )[0]
    pooled = first_out.reshape(num_grids, pooled_side, 2, pooled_side, 2, local_chans).mean(
        axis=(2, 4)
    )
    second_out = block_forward(
        pooled, second_reduce, second_mixer, second_expand, second_gain, second_shift
    )[0]
    token_count = num_grids * pooled_side * pooled_side
    flat = second_out.astype(jnp.bfloat16).reshape(token_count, local_chans)
    flat_full = lax.all_gather(flat, "mp", axis=1, tiled=True)
    lifted = jnp.dot(flat_full, readout_in, preferred_element_type=jnp.float32)
    activated = gelu_exact(lifted).astype(jnp.bfloat16)
    partial_tokens = jnp.dot(activated, readout_out, preferred_element_type=jnp.float32)
    summed = lax.psum_scatter(
        partial_tokens.astype(jnp.bfloat16), "mp", scatter_dimension=1, tiled=True
    ).astype(jnp.float32)
    live_slots = (jnp.arange(num_grids) < live_counts[0]).astype(jnp.float32)
    live_rows = jnp.repeat(live_slots, pooled_side * pooled_side)
    tokens = (summed * live_rows[:, None]).astype(jnp.bfloat16)
    grad_tokens = cotangent * live_rows[:, None].astype(jnp.bfloat16)
    grad_full = lax.all_gather(grad_tokens, "mp", axis=1, tiled=True)
    readout_out_grad = jnp.einsum(
        "ri,ro->io", activated, grad_full, preferred_element_type=jnp.float32
    )
    grad_act = jnp.einsum("ro,io->ri", grad_full, readout_out, preferred_element_type=jnp.float32)
    grad_lift = gelu_back(lifted, grad_act).astype(jnp.bfloat16)
    readout_in_grad = jnp.einsum(
        "ri,ro->io", flat_full, grad_lift, preferred_element_type=jnp.float32
    )
    partial_flat = jnp.einsum(
        "ro,io->ri", grad_lift, readout_in, preferred_element_type=jnp.float32
    )
    grad_flat = lax.psum_scatter(
        partial_flat.astype(jnp.bfloat16), "mp", scatter_dimension=1, tiled=True
    ).astype(jnp.float32)
    second_saved = block_forward(
        pooled, second_reduce, second_mixer, second_expand, second_gain, second_shift
    )[1]
    grad_pooled, second_grads = block_backward(
        grad_flat.reshape(num_grids, pooled_side, pooled_side, local_chans),
        second_saved,
        second_reduce,
        second_mixer,
        second_expand,
        second_gain,
    )
    spread_back = jnp.broadcast_to(
        0.25 * grad_pooled[:, :, None, :, None, :],
        (num_grids, pooled_side, 2, pooled_side, 2, local_chans),
    ).reshape(patches.shape)
    first_saved = block_forward(
        patch_values, first_reduce, first_mixer, first_expand, first_gain, first_shift
    )[1]
    patch_grads, first_grads = block_backward(
        spread_back, first_saved, first_reduce, first_mixer, first_expand, first_gain
    )
    summed_grads = (
        lax.psum(first_grads[0].astype(jnp.bfloat16), "dp").astype(jnp.float32),
        lax.psum(first_grads[1].astype(jnp.bfloat16), "dp").astype(jnp.float32),
        lax.psum(first_grads[2].astype(jnp.bfloat16), "dp").astype(jnp.float32),
        lax.psum(first_grads[3].astype(jnp.bfloat16), "dp").astype(jnp.float32),
        lax.psum(first_grads[4].astype(jnp.bfloat16), "dp").astype(jnp.float32),
        lax.psum(second_grads[0].astype(jnp.bfloat16), "dp").astype(jnp.float32),
        lax.psum(second_grads[1].astype(jnp.bfloat16), "dp").astype(jnp.float32),
        lax.psum(second_grads[2].astype(jnp.bfloat16), "dp").astype(jnp.float32),
        lax.psum(second_grads[3].astype(jnp.bfloat16), "dp").astype(jnp.float32),
        lax.psum(second_grads[4].astype(jnp.bfloat16), "dp").astype(jnp.float32),
        lax.psum(readout_in_grad.astype(jnp.bfloat16), "dp").astype(jnp.float32),
        lax.psum(readout_out_grad.astype(jnp.bfloat16), "dp").astype(jnp.float32),
    )
    return (
        tokens,
        patch_grads,
        summed_grads[0],
        summed_grads[1],
        summed_grads[2],
        summed_grads[3],
        summed_grads[4],
        summed_grads[5],
        summed_grads[6],
        summed_grads[7],
        summed_grads[8],
        summed_grads[9],
        summed_grads[10],
        summed_grads[11],
    )


MESH = pl.DeviceIdType.MESH
F32 = jnp.float32
BF16 = jnp.bfloat16
DMA = pltpu.SemaphoreType.DMA
VMEM_LIMIT = 60 * 2**20
ROW_PAD = 16


def dot_nn(a, b):
    return lax.dot_general(a, b, (((1,), (0,)), ((), ())), preferred_element_type=F32)


def dot_nt(a, b):
    return lax.dot_general(a, b, (((1,), (1,)), ((), ())), preferred_element_type=F32)


def dot_tn(a, b):
    return lax.dot_general(a, b, (((0,), (0,)), ((), ())), preferred_element_type=F32)


def dot_full(a, b):
    return lax.dot_general(
        a,
        b,
        (((1,), (0,)), ((), ())),
        precision=lax.Precision.HIGHEST,
        preferred_element_type=F32,
    )


def sigmoid(values):
    return 1.0 / (1.0 + jnp.exp(-values))


def silu(values):
    return values * sigmoid(values)


def silu_slope(values):
    gate = sigmoid(values)
    return gate * (1.0 + values * (1.0 - gate))


class Ring:
    def __init__(self, size):
        self.size = size
        self.reach = size // 2
        self.me = lax.axis_index("mp")
        half = self.me // 2
        self.spot = jnp.where(self.me % 2 == 0, half, size - 1 - half)
        self.right = self.index(self.spot + 1)
        self.left = self.index(self.spot - 1)

    def wrap(self, spot):
        return lax.rem(spot + 2 * self.size, self.size)

    def index(self, spot):
        spot = self.wrap(spot)
        return jnp.where(spot < self.reach, 2 * spot, 2 * (self.size - 1 - spot) + 1)

    def greet(self):
        barrier = pltpu.get_barrier_semaphore()
        for peer in (self.left, self.right):
            pl.semaphore_signal(barrier, inc=1, device_id={"mp": peer}, device_id_type=MESH)
        pl.semaphore_wait(barrier, 2)

    def copy(self, side, src, dst, send, recv):
        peer = self.right if side == 0 else self.left
        return pltpu.make_async_remote_copy(
            src_ref=src,
            dst_ref=dst,
            send_sem=send,
            recv_sem=recv,
            device_id={"mp": peer},
            device_id_type=MESH,
        )


class Gather:
    def __init__(self, ring, own, held, slot, halves, send, recv):
        self.ring, self.own, self.held, self.slot = ring, own, held, slot
        self.halves, self.send, self.recv, self.copies = halves, send, recv, {}

    def _start(self, step):
        ring = self.ring
        for side in range(2):
            away = step - 1
            spot = ring.wrap(ring.spot - away if side == 0 else ring.spot + away)
            dst = self.held.at[self.slot(spot)]
            src = self.own if step == 1 else dst
            if step == ring.reach:
                src, dst = (ref.at[self.halves[side]] for ref in (src, dst))
            copy = ring.copy(
                side, src, dst, self.send.at[side, step - 1], self.recv.at[side, step - 1]
            )
            copy.start()
            self.copies[side, step] = copy

    def start(self):
        self._start(1)

    def arrive(self, step):
        for side in range(2):
            self.copies[side, step].wait_recv()

    def forward(self, step):
        self._start(step + 1)

    def drain(self):
        for copy in self.copies.values():
            copy.wait_send()

    def spots(self, step):
        ring = self.ring
        if step == ring.reach:
            return [ring.wrap(ring.spot + step)]
        return [ring.wrap(ring.spot - step), ring.wrap(ring.spot + step)]


class Scatter:
    def __init__(self, ring, term, out, terms, halves, send, recv):
        self.ring, self.term, self.out, self.inbox = ring, term, out[0], out[1]
        self.terms, self.halves, self.send, self.recv, self.copies = terms, halves, send, recv, {}

    def _start(self, side, step):
        src, dst = self.out.at[side, step - 1], self.inbox.at[side, step - 1]
        if step == 1:
            src, dst = (ref.at[self.halves[side]] for ref in (src, dst))
        copy = self.ring.copy(
            side, src, dst, self.send.at[side, step - 1], self.recv.at[side, step - 1]
        )
        copy.start()
        self.copies[side, step] = copy

    def start(self):
        ring = self.ring
        value = self.term(ring.wrap(ring.spot + ring.reach)).astype(BF16)
        for side in range(2):
            self.out[side, 0] = value
            self._start(side, 1)

    def prepare(self, step):
        ring = self.ring
        away = ring.reach + 1 - step
        self.terms[0] = self.term(ring.wrap(ring.spot + away))
        if away > 0:
            self.terms[1] = self.term(ring.wrap(ring.spot - away))

    def step(self, step):
        for side in range(2):
            self.copies[side, step - 1].wait_recv()
            if step == 2:
                mine, other = self.halves[side], self.halves[1 - side]
                got = self.inbox[(side, 0) + mine].astype(F32)
                self.out[(side, 1) + mine] = (self.terms[(side,) + mine] + got).astype(BF16)
                self.out[(side, 1) + other] = self.terms[(side,) + other].astype(BF16)
            else:
                got = self.inbox[side, step - 2].astype(F32)
                self.out[side, step - 1] = (self.terms[side] + got).astype(BF16)
            self._start(side, step)

    def finish(self):
        reach = self.ring.reach
        for side in range(2):
            self.copies[side, reach].wait_recv()
        return (
            self.terms[0]
            + self.inbox[0, reach - 1].astype(F32)
            + self.inbox[1, reach - 1].astype(F32)
        )

    def drain(self):
        for copy in self.copies.values():
            copy.wait_send()

    def run(self):
        reach = self.ring.reach
        self.start()
        for step in range(2, reach + 1):
            self.prepare(step)
            self.step(step)
        self.prepare(reach + 1)
        return self.finish()


def row_halves(rows):
    return ((pl.ds(0, rows // 2),), (pl.ds(rows // 2, rows // 2),))


def column_halves(columns):
    every = slice(None)
    return (
        (every, pl.ds(0, columns // 2)),
        (every, pl.ds(columns // 2, columns // 2)),
    )


def pool_places(side):
    small = side // 2
    place = np.zeros((3 * ROW_PAD, 6 * side), np.float32)
    for row in range(6):
        for column in range(side):
            place[(row // 2) * ROW_PAD + column // 2, row * side + column] = 0.25
    assert small <= ROW_PAD
    return place


def token_places(grids, small):
    place = np.zeros((grids * small * small, grids * small * ROW_PAD), np.float32)
    for line in range(grids * small):
        for column in range(small):
            place[line * small + column, line * ROW_PAD + column] = 1.0
    return place


def norm_rows(mixed, gain, shift):
    center = jnp.mean(mixed, axis=1, keepdims=True)
    apart = mixed - center
    inv_std = lax.rsqrt(jnp.mean(apart * apart, axis=1, keepdims=True) + norm_eps)
    normed = apart * inv_std
    return normed, inv_std, normed * gain + shift


def wide_vector(held, row):
    return jnp.concatenate([held[m, row : row + 1, :] for m in range(held.shape[0])], axis=1)


class Pair:
    def __init__(self):
        self.me = lax.axis_index("dp")
        self.core = lax.rem(self.me, 2)
        self.other = 1 - self.core
        self.twin = self.me - self.core + self.other
        self.far = lax.rem(self.me + 2, 4)

    def copy(self, peer, src, dst, send, recv):
        return pltpu.make_async_remote_copy(
            src_ref=src,
            dst_ref=dst,
            send_sem=send,
            recv_sem=recv,
            device_id={"dp": peer},
            device_id_type=MESH,
        )


def greet_ring_and_pair(ring, pair):
    barrier = pltpu.get_barrier_semaphore()
    for peer in (ring.left, ring.right):
        pl.semaphore_signal(barrier, inc=1, device_id={"mp": peer}, device_id_type=MESH)
    for peer in (pair.twin, pair.far):
        pl.semaphore_signal(barrier, inc=1, device_id={"dp": peer}, device_id_type=MESH)
    pl.semaphore_wait(barrier, 4)


class Expand:
    def __init__(self, ring, pair, own, held, send, recv, psend, precv):
        self.ring, self.pair, self.held = ring, pair, held
        self.psend, self.precv, self.copies = psend, precv, []
        chans, quarter = held.shape[2:]
        columns = own[:, pl.ds(pl.multiple_of(pair.me * quarter, 128), quarter)]
        held[pair.me, ring.me] = columns
        self.gather = Gather(
            ring, held.at[pair.me, ring.me], held.at[pair.me], ring.index, row_halves(chans), send, recv
        )

    def across(self):
        self.gather.arrive(self.ring.reach)
        self._swap(0, self.pair.far, self.pair.me)

    def between(self):
        self.copies[0].wait_recv()
        self._swap(1, self.pair.twin, self.pair.me)
        self._swap(2, self.pair.twin, self.pair.far)

    def _swap(self, k, peer, quarter):
        at = self.held.at[quarter]
        copy = self.pair.copy(peer, at, at, self.psend.at[k], self.precv.at[k])
        copy.start()
        self.copies.append(copy)

    def ready(self):
        for copy in self.copies[1:]:
            copy.wait_recv()

    def drain(self):
        self.gather.drain()
        for copy in self.copies:
            copy.wait_send()


def times_expand(rows, held):
    parts = []
    for k in range(held.shape[0]):
        weight = held[k].reshape(rows.shape[1], held.shape[3])
        parts.append(dot_nn(rows, weight))
    return jnp.concatenate(parts, axis=1)


def times_expand_back(rows, held):
    quarter = held.shape[3]
    total = None
    for k in range(held.shape[0]):
        weight = held[k].reshape(held.shape[1] * held.shape[2], quarter)
        part = dot_nt(rows[:, k * quarter : (k + 1) * quarter], weight)
        total = part if total is None else total + part
    return total


def chunk_taps(image, taps, spot, lines, side, width):
    chans = image.shape[-1]
    per_grid = side // lines
    grid, line = spot // per_grid, lax.rem(spot, per_grid) * lines
    for kh in range(3):
        for kw in range(3):
            piece = image[grid, pl.ds(line + kh, lines), 7 + kw : 7 + kw + width, :]
            at = (kh * 3 + kw) * chans
            taps[spot, :, at : at + chans] = piece.reshape(lines * width, chans).astype(BF16)


def chunk_back(image, product, spot, lines, side, width):
    chans = image.shape[-1]
    per_grid = side // lines
    grid, line = spot // per_grid, lax.rem(spot, per_grid) * lines
    for kh in range(3):
        for kw in range(3):
            at = (kh * 3 + kw) * chans
            piece = product[:, at : at + chans].reshape(lines, width, chans)
            image[grid, pl.ds(line + kh, lines), 7 + kw : 7 + kw + width, :] += piece


def forward_kernel(
    size, grids, side,
    x, reduce_1, expand_1, expand_2, gain_1, shift_1, gain_2, shift_2, pool, places, counts,
    mixer_1_any, reduce_2_any, mixer_2_any, readout_in_any, readout_out_any, cotangent,
    x_full_out, pre_1, taps_1_out, normed_1, inv_1, branch_sum, held_1_out, vec_full,
    x_small_out, pre_2, taps_2_out, normed_2, inv_2, branch_2, held_2_out,
    grad_rows, act, out_grad_out, in_grad_out,
    x_full, mixer_1, taps_1, image_1, boxes_1, terms_1, x_rows, held_1, held_2, vectors,
    pooled, low, x_small, reduce_2, mixer_2, taps_2, image_2, boxes_2, boxes_3, terms_2, flat_full, cot_full,
    readout_in, readout_out, lifted, act_live, grad_act, grad_lift, out_grad, in_grad,
    send, recv, psend, precv, load, store,
):
    ring, pair = Ring(size), Pair()
    rows, chans = x.shape
    share = rows // size
    total = size * chans
    small = side // 2
    few = pooled.shape[0]
    part = readout_in.shape[1]
    tokens = cotangent.shape[0]
    wide = column_halves(total)
    near = lambda spot: spot
    loads = [
        pltpu.make_async_copy(src, dst, load.at[k])
        for k, (src, dst) in enumerate(
            [
                (mixer_1_any, mixer_1),
                (reduce_2_any, reduce_2),
                (mixer_2_any, mixer_2),
                (readout_in_any, readout_in),
                (readout_out_any, readout_out),
                (cotangent, cot_full.at[ring.me]),
            ]
        )
    ]
    stores = []

    def keep(src, dst):
        copy = pltpu.make_async_copy(src, dst, store.at[len(stores)])
        copy.start()
        stores.append(copy)

    for copy in loads:
        copy.start()
    greet_ring_and_pair(ring, pair)
    gx = Gather(ring, x, x_full, ring.index, row_halves(rows), send.at[0], recv.at[0])
    gx.start()
    x_full[ring.me] = x[...]
    for k, vector in enumerate((gain_1, shift_1, gain_2, shift_2)):
        for row in (k, k + 8):
            vectors[row : row + 1, :] = vector[...]
    for k in range(4, 8):
        for row in (k, k + 8):
            vectors[row : row + 1, :] = gain_1[...]
    vec_full[ring.me] = vectors[...]
    gv = Gather(ring, vectors, vec_full, ring.index, row_halves(16), send.at[1], recv.at[1])
    e1 = Expand(ring, pair, expand_1, held_1, send.at[2], recv.at[2], psend.at[0], precv.at[0])
    e2 = Expand(ring, pair, expand_2, held_2, send.at[3], recv.at[3], psend.at[1], precv.at[1])

    def add(spot):
        m = ring.index(spot)
        weight = reduce_1[pl.ds(pl.multiple_of(m * chans, chans), chans), :]
        pre_1[...] += dot_nn(x_full[m], weight)

    own = reduce_1[pl.ds(pl.multiple_of(ring.me * chans, chans), chans), :]
    pre_1[...] = dot_nn(x[...], own)
    image_1[...] = jnp.zeros(image_1.shape, F32)
    image_2[...] = jnp.zeros(image_2.shape, F32)
    for step in range(1, ring.reach + 1):
        gx.arrive(step)
        if step < ring.reach:
            gx.forward(step)
        if step == ring.reach - 1:
            for item in (e1.gather, gv, e2.gather):
                item.start()
        for spot in gx.spots(step):
            add(spot)
    keep(x_full, x_full_out)

    def extras(step):
        for item in (e1.gather, gv, e2.gather):
            item.arrive(step)
            item.forward(step)

    hidden = silu(pre_1[...])
    image_1[:, 1 : 1 + side, 8 : 8 + side, :] = hidden.reshape(grids, side, side, chans)
    loads[0].wait()

    def mix_1(spot):
        chunk_taps(image_1, taps_1, spot, 6, side, side)
        return dot_nn(taps_1[spot], mixer_1[...])

    rs1 = Scatter(
        ring, mix_1, (boxes_1.at[0], boxes_1.at[1]), terms_1, wide, send.at[4], recv.at[4]
    )
    rs1.start()
    extras(1)
    for step in range(2, ring.reach + 1):
        rs1.prepare(step)
        rs1.step(step)
        if step < ring.reach:
            extras(step)
        else:
            gv.arrive(ring.reach)
            e1.across()
            e2.across()
    rs1.prepare(ring.reach + 1)
    keep(taps_1, taps_1_out)
    mine = pl.ds(pl.multiple_of(ring.spot * share, 16), share)
    for m in range(size):
        x_rows[:, m * chans : (m + 1) * chans] = x_full[m, mine, :].astype(F32)
    gain_a, shift_a = wide_vector(vec_full, 0), wide_vector(vec_full, 1)
    e1.between()
    mixed = rs1.finish()
    loads[5].wait()
    gc = Gather(
        ring, cot_full.at[ring.me], cot_full, ring.index, row_halves(tokens), send.at[5], recv.at[5]
    )
    gc.start()
    value, inverse, affine = norm_rows(mixed, gain_a, shift_a)
    normed_1[...] = value
    inv_1[...] = jnp.broadcast_to(inverse, inv_1.shape)
    branch = silu(affine).astype(BF16)
    e1.ready()
    e2.between()
    keep(held_1, held_1_out)
    pooled[...] = dot_full(pool[...], x_rows[...] + times_expand(branch, held_1))
    low[0] = pooled[...].astype(BF16)
    x_small[ring.spot] = low[0]
    g2 = Gather(ring, low.at[0], x_small, near, wide, send.at[6], recv.at[6])
    g2.start()
    branch_sum[...] = (4.0 * dot_full(pool[...], branch.astype(F32))).astype(BF16)
    for step in range(1, ring.reach + 1):
        g2.arrive(step)
        if step < ring.reach:
            g2.forward(step)
        if step == 1:
            gc.arrive(1)
            gc.forward(1)
    loads[1].wait()
    pre_2[...] = dot_nn(x_small[...].reshape(size * few, total), reduce_2[...])
    keep(x_small, x_small_out)
    hidden = silu(pre_2[...])
    image_2[:, 1 : 1 + small, 8 : 8 + ROW_PAD, :] = hidden.reshape(grids, small, ROW_PAD, chans)
    loads[2].wait()

    def mix_2(spot):
        chunk_taps(image_2, taps_2, spot, 3, small, ROW_PAD)
        return dot_nn(taps_2[spot], mixer_2[...])

    rs2 = Scatter(
        ring, mix_2, (boxes_2.at[0], boxes_2.at[1]), terms_2, wide, send.at[7], recv.at[7]
    )
    rs2.start()
    gc.arrive(2)
    gc.forward(2)
    for step in range(2, ring.reach + 1):
        rs2.prepare(step)
        rs2.step(step)
    rs2.prepare(ring.reach + 1)
    keep(taps_2, taps_2_out)
    gain_b, shift_b = wide_vector(vec_full, 2), wide_vector(vec_full, 3)
    mixed = rs2.finish()
    value, inverse, affine = norm_rows(mixed, gain_b, shift_b)
    normed_2[...] = value
    inv_2[...] = jnp.broadcast_to(inverse, inv_2.shape)
    branch_2[...] = silu(affine).astype(BF16)
    e2.ready()
    keep(held_2, held_2_out)
    low[1] = (pooled[...] + times_expand(branch_2[...], held_2)).astype(BF16)
    flat_full[ring.spot] = low[1]
    gf = Gather(ring, low.at[1], flat_full, near, wide, send.at[8], recv.at[8])
    gf.start()
    for step in range(1, ring.reach + 1):
        gf.arrive(step)
        if step < ring.reach:
            gf.forward(step)
        if step == 1:
            gc.arrive(3)
            gc.forward(3)
    loads[3].wait()
    flat = dot_nn(places[...], flat_full[...].reshape(size * few, total)).astype(BF16)
    lifted[...] = dot_nn(flat, readout_in[...])
    cdf = 0.5 * (1.0 + lax.erf(lifted[...] * 0.7071067811865476))
    row_ids = lax.broadcasted_iota(jnp.int32, (tokens, 1), 0)
    live = (row_ids < counts[0] * (tokens // grids)).astype(F32)
    activated = (lifted[...] * cdf).astype(BF16)
    act[...] = activated
    act_live[...] = (activated.astype(F32) * live).astype(BF16)
    slope = cdf + lifted[...] * jnp.exp(-0.5 * lifted[...] * lifted[...]) * 0.3989422804014327
    lifted[...] = slope * live
    grad_act[...] = jnp.zeros(grad_act.shape, F32)
    loads[4].wait()
    gc.arrive(ring.reach)

    def back(m, carry):
        at = pl.ds(pl.multiple_of(m * part, 128), part)
        grad_act[...] += dot_nt(cot_full[m], readout_out[:, at])
        return carry

    lax.fori_loop(0, size, back, 0)
    lift = (grad_act[...] * lifted[...]).astype(BF16)
    grad_lift[...] = dot_tn(places[...], lift).astype(BF16)

    def flat_term(spot):
        return dot_nt(grad_lift[pl.ds(pl.multiple_of(spot * few, 16), few), :], readout_in[...])

    rf = Scatter(
        ring, flat_term, (boxes_3.at[0], boxes_3.at[1]), terms_2, wide, send.at[9], recv.at[9]
    )
    rf.start()

    def weights(m, carry):
        at = pl.ds(pl.multiple_of(m * part, 128), part)
        out_grad[:, at] = dot_tn(act_live[...], cot_full[m]).astype(BF16)
        return carry

    lax.fori_loop(0, size // 2, weights, 0)
    for step in range(2, ring.reach + 1):
        rf.prepare(step)
        rf.step(step)
        if step == 2:
            lax.fori_loop(size // 2, size, weights, 0)
            keep(out_grad, out_grad_out)
        if step == 3:
            in_grad[...] = dot_tn(flat, lift).astype(BF16)
            keep(in_grad, in_grad_out)
    rf.prepare(ring.reach + 1)
    grad_rows[...] = rf.finish()
    for item in (gx, gv, e1, e2, rs1, gc, g2, rs2, gf, rf):
        item.drain()
    for copy in stores:
        copy.wait()


def norm_back(grad_branch, normed, inv_std, gain, shift):
    affine = normed * gain + shift
    grad_affine = grad_branch * silu_slope(affine)
    gain_grad = jnp.sum(grad_affine * normed, axis=0, keepdims=True)
    shift_grad = jnp.sum(grad_affine, axis=0, keepdims=True)
    scaled = grad_affine * gain
    mean_plain = jnp.mean(scaled, axis=1, keepdims=True)
    mean_normed = jnp.mean(scaled * normed, axis=1, keepdims=True)
    return inv_std * (scaled - mean_plain - normed * mean_normed), gain_grad, shift_grad


class GroupSum:
    def __init__(self, pair, mine, other, from_core, from_far, result, half, send, recv, local):
        self.pair, self.mine, self.other = pair, mine, other
        self.from_core, self.from_far = from_core, from_far
        self.result = result.at[half]
        self.send, self.recv, self.local, self.copies = send, recv, local, []

    def _go(self, k, peer, src, dst):
        copy = self.pair.copy(peer, src, dst, self.send.at[k], self.recv.at[k])
        copy.start()
        self.copies.append(copy)

    def core(self):
        self._go(0, self.pair.twin, self.other, self.from_core)

    def far(self):
        self.copies[0].wait_recv()
        self.mine[...] = (self.mine[...].astype(F32) + self.from_core[...].astype(F32)).astype(BF16)
        self._go(1, self.pair.far, self.mine, self.from_far)

    def back(self):
        self.copies[1].wait_recv()
        self.from_far[...] = (self.mine[...].astype(F32) + self.from_far[...].astype(F32)).astype(
            BF16
        )
        self._go(2, self.pair.twin, self.from_far, self.result)
        self.kept = pltpu.make_async_copy(self.from_far, self.result, self.local)
        self.kept.start()

    def done(self):
        self.copies[2].wait_recv()
        self.kept.wait()
        for copy in self.copies:
            copy.wait_send()


def half_of(rows, columns, which, by_rows):
    if by_rows:
        return (pl.ds(pl.multiple_of(which * (rows // 2), 16), rows // 2), slice(None))
    return (slice(None), pl.ds(pl.multiple_of(which * (columns // 2), 128), columns // 2))


def send_columns(ring, src, held, slot, send, recv):
    chans = held.shape[-1]
    held[slot] = src[:, pl.ds(pl.multiple_of(ring.me * chans, chans), chans)]
    copies = []
    for away in range(1, ring.size):
        peer = lax.rem(ring.me + away, ring.size)
        copy = pltpu.make_async_remote_copy(
            src_ref=src.at[:, pl.ds(pl.multiple_of(peer * chans, chans), chans)],
            dst_ref=held.at[slot],
            send_sem=send.at[away - 1],
            recv_sem=recv.at[away - 1],
            device_id={"mp": peer},
            device_id_type=MESH,
        )
        copy.start()
        copies.append(copy)
    return copies


def backward_kernel(
    size, grids, side,
    grad_rows, normed_2, inv_2, vec_full, branch_2, normed_1, inv_1, branch_sum, pre_2, pre_1, spread, act, counts,
    reduce_1, reduce_2,
    held_1_any, held_2_any, x_full_any, taps_1_any, x_small_any, taps_2_any, mixer_1_any, mixer_2_any,
    readout_any, out_grad_any, in_grad_any,
    patch_grads, tokens, vec_sum, out_sum, in_sum, mixer_2_sum, reduce_2_sum, expand_2_sum,
    mixer_1_sum, reduce_1_sum, expand_1_sum,
    held, x_full, taps_1, x_small, taps_2, mixer, readout,
    out_mine, out_core, out_far, in_mine, in_core, in_far,
    mixer_2_grad, mixer_2_core, mixer_2_far, reduce_2_grad, reduce_2_core, reduce_2_far,
    expand_2_grad, expand_2_core, expand_2_far,
    mixer_1_grad, mixer_1_core, mixer_1_far, reduce_1_grad, reduce_1_core, reduce_1_far,
    expand_1_grad, expand_1_core, expand_1_far,
    image_1, image_2, product_1, product_2, low_2, low_1, mix_2, mix_1, mix_2_full, mix_1_full,
    low_2_full, low_1_full, branch_2_full, branch_1_full, grad_pre_2, grad_pre_1, grad_out, wide_term,
    boxes_big, terms_big, boxes_small, terms_small, vec_grad, vec_held, vec_part,
    send, recv, all_send, all_recv, sum_send, sum_recv, sum_local, vec_send, vec_recv, load,
):
    ring, pair = Ring(size), Pair()
    few, total = grad_rows.shape
    share = normed_1.shape[0]
    chans = total // size
    rows = size * share
    small = side // 2
    part = out_grad_any.shape[1] // size
    near = lambda spot: spot
    wide = column_halves(total)
    pairs = [
        (held_2_any, held),
        (mixer_2_any, mixer),
        (readout_any, readout),
        (out_grad_any.at[half_of(*out_grad_any.shape, pair.core, True)], out_mine),
        (in_grad_any.at[half_of(*in_grad_any.shape, pair.core, True)], in_mine),
        (taps_2_any, taps_2),
        (x_small_any, x_small),
        (held_1_any, held),
        (mixer_1_any, mixer),
        (taps_1_any, taps_1),
        (x_full_any, x_full),
    ]
    loads = [
        pltpu.make_async_copy(src, dst, load.at[k]) for k, (src, dst) in enumerate(pairs)
    ]
    for k, copy in enumerate(loads):
        if k not in (7, 8):
            copy.start()
    barrier = pltpu.get_barrier_semaphore()
    for away in range(1, size):
        peer = lax.rem(ring.me + away, size)
        pl.semaphore_signal(barrier, inc=1, device_id={"mp": peer}, device_id_type=MESH)
    for peer in (pair.twin, pair.far):
        pl.semaphore_signal(barrier, inc=1, device_id={"dp": peer}, device_id_type=MESH)
    pl.semaphore_wait(barrier, size + 1)

    def group_sum(k, mine, other, from_core, from_far, result, by_rows):
        half = half_of(*result.shape, pair.core, by_rows)
        return GroupSum(
            pair, mine, other, from_core, from_far, result, half, sum_send.at[k], sum_recv.at[k], sum_local.at[k]
        )

    def grad_sum(k, grad, from_core, from_far, result, by_rows):
        mine, other = (
            grad.at[half_of(*grad.shape, which, by_rows)] for which in (pair.core, pair.other)
        )
        return group_sum(k, mine, other, from_core, from_far, result, by_rows)

    out_other = out_grad_any.at[half_of(*out_grad_any.shape, pair.other, True)]
    in_other = in_grad_any.at[half_of(*in_grad_any.shape, pair.other, True)]
    s_out = group_sum(0, out_mine, out_other, out_core, out_far, out_sum, True)
    s_in = group_sum(1, in_mine, in_other, in_core, in_far, in_sum, True)
    s_m2 = grad_sum(2, mixer_2_grad, mixer_2_core, mixer_2_far, mixer_2_sum, False)
    s_r2 = grad_sum(3, reduce_2_grad, reduce_2_core, reduce_2_far, reduce_2_sum, True)
    s_e2 = grad_sum(4, expand_2_grad, expand_2_core, expand_2_far, expand_2_sum, False)
    s_m1 = grad_sum(5, mixer_1_grad, mixer_1_core, mixer_1_far, mixer_1_sum, False)
    s_r1 = grad_sum(6, reduce_1_grad, reduce_1_core, reduce_1_far, reduce_1_sum, True)
    s_e1 = grad_sum(7, expand_1_grad, expand_1_core, expand_1_far, expand_1_sum, False)
    s_out.core()
    s_in.core()

    low_2[...] = grad_rows[...].astype(BF16)
    loads[0].wait()
    gain_b, shift_b = wide_vector(vec_full, 2), wide_vector(vec_full, 3)
    grad_branch = times_expand_back(low_2[...], held)
    value, gain_grad, shift_grad = norm_back(
        grad_branch, normed_2[...], inv_2[:, 0:1], gain_b, shift_b
    )
    loads[7].start()
    mix_2[...] = value.astype(BF16)
    g_mix2 = Gather(ring, mix_2, mix_2_full, near, wide, send.at[0], recv.at[0])
    g_mix2.start()
    mix_2_full[ring.spot] = mix_2[...]
    vec_grad[...] = jnp.zeros(vec_grad.shape, F32)
    vec_grad[2:3, :] = gain_grad
    vec_grad[3:4, :] = shift_grad
    image_2[...] = jnp.zeros(image_2.shape, F32)
    image_1[...] = jnp.zeros(image_1.shape, F32)

    def token_term(spot):
        at = pl.ds(pl.multiple_of(ring.index(spot) * part, 128), part)
        value = dot_nn(act[...], readout[:, at])
        return jnp.concatenate(
            [value[:, k : k + chans] for k in range(0, part, chans)], axis=0
        )

    tall = row_halves(rows)
    big = (boxes_big.at[0], boxes_big.at[1])
    r_tok = Scatter(ring, token_term, big, terms_big, tall, send.at[1], recv.at[1])
    loads[2].wait()
    r_tok.start()

    def back_2(spot):
        product_2[...] = dot_nt(mix_2_full[spot], mixer[...])
        chunk_back(image_2, product_2, spot, 3, small, ROW_PAD)

    loads[1].wait()
    back_2(ring.spot)
    for step in range(1, ring.reach + 1):
        g_mix2.arrive(step)
        if step < ring.reach:
            g_mix2.forward(step)
        for spot in g_mix2.spots(step):
            back_2(spot)
        if step == 2:
            loads[3].wait()
            s_out.far()
    loads[8].start()
    grad_hidden = image_2[:, 1 : 1 + small, 8 : 8 + ROW_PAD, :].reshape(pre_2.shape)
    grad_pre_2[...] = (grad_hidden * silu_slope(pre_2[...])).astype(BF16)

    def in_term_2(spot):
        return dot_nt(grad_pre_2[pl.ds(pl.multiple_of(spot * few, 16), few), :], reduce_2[...])

    r_in2 = Scatter(
        ring, in_term_2, (boxes_small.at[0], boxes_small.at[1]), terms_small, wide, send.at[2], recv.at[2]
    )
    r_in2.start()
    r_tok.prepare(2)
    r_tok.step(2)
    loads[4].wait()
    s_in.far()

    def mixer_half(grad, taps, mix, which, count):
        columns = pl.ds(pl.multiple_of(which * (total // 2), 128), total // 2)

        def one(k, carry):
            at = pl.ds(pl.multiple_of(k * chans, chans), chans)
            left = taps[:, :, at].reshape(size * count, chans)
            right = mix[:, :, columns].reshape(size * count, total // 2)
            grad[at, columns] = dot_tn(left, right).astype(BF16)
            return carry

        lax.fori_loop(0, 9, one, 0)

    loads[5].wait()
    for step in range(2, ring.reach + 1):
        r_in2.prepare(step)
        r_in2.step(step)
        if step == 2:
            mixer_half(mixer_2_grad, taps_2, mix_2_full, pair.other, few)
            s_m2.core()
        if step == 3:
            mixer_half(mixer_2_grad, taps_2, mix_2_full, pair.core, few)
    r_in2.prepare(ring.reach + 1)
    r_tok.prepare(3)
    loads[7].wait()
    quarter = 0.25 * (r_in2.finish() + grad_rows[...])
    r_tok.step(3)
    low_1[...] = quarter.astype(BF16)
    gain_a, shift_a = wide_vector(vec_full, 0), wide_vector(vec_full, 1)
    grad_branch = dot_full(spread[...], times_expand_back(low_1[...], held))
    value, gain_grad, shift_grad = norm_back(
        grad_branch, normed_1[...], inv_1[:, 0:1], gain_a, shift_a
    )
    mix_1[...] = value.astype(BF16)
    g_mix1 = Gather(ring, mix_1, mix_1_full, near, wide, send.at[3], recv.at[3])
    g_mix1.start()
    mix_1_full[ring.spot] = mix_1[...]
    vec_grad[0:1, :] = gain_grad
    vec_grad[1:2, :] = shift_grad
    grad_out[...] = dot_full(spread[...], quarter)
    s_m2.far()
    loads[6].wait()

    def reduce_part(grad, full, grad_pre):
        grad[...] = dot_tn(full, grad_pre).astype(BF16)

    reduce_part(reduce_2_grad, x_small[...].reshape(size * few, total), grad_pre_2[...])
    s_r2.core()
    r_tok.prepare(4)
    r_tok.step(4)

    def back_1(spot):
        product_1[...] = dot_nt(mix_1_full[spot], mixer[...])
        chunk_back(image_1, product_1, spot, 6, side, side)

    loads[8].wait()
    back_1(ring.spot)
    low_2_full[ring.spot] = low_2[...]
    low_1_full[ring.spot] = low_1[...]
    g_low2 = Gather(ring, low_2, low_2_full, near, wide, send.at[4], recv.at[4])
    g_low1 = Gather(ring, low_1, low_1_full, near, wide, send.at[5], recv.at[5])
    for step in range(1, ring.reach + 1):
        g_mix1.arrive(step)
        if step < ring.reach:
            g_mix1.forward(step)
        if step == 1:
            a_low2 = send_columns(
                ring, branch_2, branch_2_full, ring.spot, all_send.at[0], all_recv.at[0]
            )
            a_low1 = send_columns(
                ring, branch_sum, branch_1_full, ring.spot, all_send.at[1], all_recv.at[1]
            )
            a_vec = send_columns(
                ring, vec_grad, vec_held, ring.me, all_send.at[2], all_recv.at[2]
            )
        if step == 2:
            r_tok.prepare(ring.reach + 1)
            value = r_tok.finish()
            r_tok.drain()
            count = rows * chans // part
            value = jnp.concatenate(
                [value[k * count : (k + 1) * count] for k in range(part // chans)], axis=1
            )
            row_ids = lax.broadcasted_iota(jnp.int32, (count, 1), 0)
            live = (row_ids < counts[0] * (count // grids)).astype(F32)
            tokens[...] = (value * live).astype(BF16)
            s_r2.far()
            g_low2.start()
            g_low1.start()
        for spot in g_mix1.spots(step):
            back_1(spot)

    def lows(step):
        for item in (g_low2, g_low1):
            item.arrive(step)
            if step < ring.reach:
                item.forward(step)

    grad_hidden = image_1[:, 1 : 1 + side, 8 : 8 + side, :].reshape(pre_1.shape)
    grad_pre_1[...] = (grad_hidden * silu_slope(pre_1[...])).astype(BF16)
    mine = pl.ds(pl.multiple_of(ring.spot * share, 16), share)

    def in_term_1(spot):
        at = pl.ds(pl.multiple_of(ring.index(spot) * chans, chans), chans)
        wide_term[...] = dot_nt(grad_pre_1[...], reduce_1[at, :])
        wide_term[mine, :] += grad_out[:, at]
        return wide_term[...]

    r_in1 = Scatter(ring, in_term_1, big, terms_big, tall, send.at[6], recv.at[6])
    r_in1.start()
    loads[9].wait()
    mixer_half(mixer_1_grad, taps_1, mix_1_full, pair.other, share)
    s_m1.core()
    lows(1)
    mixer_half(mixer_1_grad, taps_1, mix_1_full, pair.core, share)
    r_in1.prepare(2)
    r_in1.step(2)
    s_m1.far()
    lows(2)
    loads[10].wait()

    def reduces(m, carry):
        at = pl.ds(pl.multiple_of(m * chans, chans), chans)
        reduce_1_grad[at, :] = dot_tn(x_full[m], grad_pre_1[...]).astype(BF16)
        return carry

    lax.fori_loop(0, size, reduces, 0)
    s_r1.core()
    r_in1.prepare(3)
    r_in1.step(3)
    lows(3)
    s_r1.far()
    s_out.back()
    for copy in a_vec:
        copy.wait()
    vec_part[0] = jnp.sum(vec_held[...], axis=0)
    v_core = pair.copy(pair.twin, vec_part.at[0], vec_part.at[1], vec_send.at[0], vec_recv.at[0])
    v_core.start()
    r_in1.prepare(4)
    r_in1.step(4)
    lows(4)
    for copy in a_low2 + a_low1:
        copy.wait()

    def expand_part(grad, branches, lows):
        grad[...] = dot_tn(
            branches[...].reshape(size * few, chans), lows[...].reshape(size * few, total)
        ).astype(BF16)

    expand_part(expand_2_grad, branch_2_full, low_2_full)
    expand_part(expand_1_grad, branch_1_full, low_1_full)
    s_e2.core()
    s_e1.core()
    v_core.wait()
    vec_part[2] = vec_part[0] + vec_part[1]
    v_far = pair.copy(pair.far, vec_part.at[2], vec_part.at[3], vec_send.at[1], vec_recv.at[1])
    v_far.start()
    r_in1.prepare(ring.reach + 1)
    s_in.back()
    s_e2.far()
    s_e1.far()
    s_m2.back()
    s_r2.back()
    patch_grads[...] = r_in1.finish()
    v_far.wait()
    vec_sum[...] = vec_part[2] + vec_part[3]
    s_m1.back()
    s_r1.back()
    s_e2.back()
    s_e1.back()
    for item in (s_out, s_in, s_m2, s_r2, s_e2, s_m1, s_r1, s_e1):
        item.done()
    for item in (g_mix2, r_in2, g_mix1, g_low2, g_low1, r_in1):
        item.drain()


def kernel_call(kernel, name, number, in_specs, outs, out_specs, scratch, flops=0):
    def run(*args):
        return pl.pallas_call(
            kernel,
            name=name,
            out_shape=outs,
            in_specs=in_specs,
            out_specs=out_specs,
            scratch_shapes=scratch,
            cost_estimate=pl.CostEstimate(flops=flops, bytes_accessed=0, transcendentals=0),
            compiler_params=pltpu.CompilerParams(
                collective_id=number, has_side_effects=True, vmem_limit_bytes=VMEM_LIMIT
            ),
        )(*args)

    return run


def fast_body(
    size,
    patches,
    first_reduce,
    first_mixer,
    first_expand,
    first_gain,
    first_shift,
    second_reduce,
    second_mixer,
    second_expand,
    second_gain,
    second_shift,
    readout_in,
    readout_out,
    cotangent,
    live_counts,
):
    S = jax.ShapeDtypeStruct
    V = pltpu.VMEM
    near = pl.BlockSpec(memory_space=pltpu.VMEM)
    scalar = pl.BlockSpec(memory_space=pltpu.SMEM)
    away = pl.BlockSpec(memory_space=pl.ANY)
    grids, side, _, chans = patches.shape
    total = first_expand.shape[1]
    rows = grids * side * side
    share = rows // size
    small = side // 2
    few = 3 * ROW_PAD
    few_rows = few * size
    token_rows = grids * small * small
    part = readout_in.shape[1]
    wide = readout_out.shape[1]
    reach = size // 2
    pool = pool_places(side)
    places = token_places(grids, small).astype(BF16)
    x = patches.reshape(rows, chans)
    mixer_1 = first_mixer.reshape(9 * chans, total)
    mixer_2 = second_mixer.reshape(9 * chans, total)
    vectors = [v.reshape(1, chans) for v in (first_gain, first_shift, second_gain, second_shift)]

    def boxes(r, c):
        return V((2, 2, reach, r, c), BF16)

    image_1 = V((grids, side + 2, side + 16, chans), F32)
    image_2 = V((grids, small + 2, ROW_PAD + 16, chans), F32)
    held = ((4, size, chans, total // 4), BF16)
    x_full = ((size, rows, chans), BF16)
    taps_1 = ((size, share, 9 * chans), BF16)
    x_small = ((size, few, total), BF16)
    taps_2 = ((size, few, 9 * chans), BF16)
    mixer = ((9 * chans, total), BF16)
    outs = [
        (S(*x_full), away),
        (S((rows, chans), F32), near),
        (S(*taps_1), away),
        (S((share, total), F32), near),
        (S((share, 128), F32), near),
        (S((few, total), BF16), near),
        (S(*held), away),
        (S((size, 16, chans), F32), near),
        (S(*x_small), away),
        (S((few_rows, chans), F32), near),
        (S(*taps_2), away),
        (S((few, total), F32), near),
        (S((few, 128), F32), near),
        (S((few, total), BF16), near),
        (S(*held), away),
        (S((few, total), F32), near),
        (S((token_rows, part), BF16), near),
        (S((part, wide), BF16), away),
        (S((total, part), BF16), away),
    ]
    scratch = [
        V(*x_full),
        V(*mixer),
        V(*taps_1),
        image_1,
        boxes(share, total),
        V((2, share, total), F32),
        V((share, total), F32),
        V(*held),
        V(*held),
        V((16, chans), F32),
        V((few, total), F32),
        V((2, few, total), BF16),
        V(*x_small),
        V((total, chans), BF16),
        V(*mixer),
        V(*taps_2),
        image_2,
        boxes(few, total),
        boxes(few, total),
        V((2, few, total), F32),
        V((size, few, total), BF16),
        V((size, token_rows, part), BF16),
        V((total, part), BF16),
        V((part, wide), BF16),
        V((token_rows, part), F32),
        V((token_rows, part), BF16),
        V((token_rows, part), F32),
        V((few_rows, part), BF16),
        V((part, wide), BF16),
        V((total, part), BF16),
        DMA((10, 2, reach)),
        DMA((10, 2, reach)),
        DMA((2, 3)),
        DMA((2, 3)),
        DMA((6,)),
        DMA((8,)),
    ]
    (
        x_full_k, pre_1, taps_1_k, normed_1, inv_1, branch_sum, held_1_k, vec_full,
        x_small_k, pre_2, taps_2_k, normed_2, inv_2, branch_2, held_2_k, grad_rows, act, out_grad, in_grad,
    ) = kernel_call(
        functools.partial(forward_kernel, size, grids, side),
        "forward",
        1,
        [near] * 10 + [scalar] + [away] * 6,
        [shape for shape, _ in outs],
        [spec for _, spec in outs],
        scratch,
    )(
        x, first_reduce, first_expand, second_expand, *vectors, pool, places, live_counts,
        mixer_1, second_reduce, mixer_2, readout_in, readout_out, cotangent,
    )

    sums = [
        ((part, wide), True),
        ((total, part), True),
        ((9 * chans, total), False),
        ((total, chans), True),
        ((chans, total), False),
        ((9 * chans, total), False),
        ((total, chans), True),
        ((chans, total), False),
    ]
    outs = [
        (S((rows, chans), F32), near),
        (S((token_rows, part), BF16), near),
        (S((8, chans), F32), near),
    ]
    outs += [(S(shape, BF16), away) for shape, _ in sums]

    def half(shape, by_rows):
        return (shape[0] // 2, shape[1]) if by_rows else (shape[0], shape[1] // 2)

    scratch = [
        V(*held),
        V(*x_full),
        V(*taps_1),
        V(*x_small),
        V(*taps_2),
        V(*mixer),
        V((part, wide), BF16),
    ]
    for shape, by_rows in sums[:2]:
        scratch += [V(half(shape, by_rows), BF16)] * 3
    for shape, by_rows in sums[2:]:
        scratch += [V(shape, BF16)] + [V(half(shape, by_rows), BF16)] * 2
    scratch += [
        image_1,
        image_2,
        V((share, 9 * chans), F32),
        V((few, 9 * chans), F32),
        V((few, total), BF16),
        V((few, total), BF16),
        V((few, total), BF16),
        V((share, total), BF16),
        V((size, few, total), BF16),
        V((size, share, total), BF16),
        V((size, few, total), BF16),
        V((size, few, total), BF16),
        V((size, few, chans), BF16),
        V((size, few, chans), BF16),
        V((few_rows, chans), BF16),
        V((rows, chans), BF16),
        V((share, total), F32),
        V((rows, chans), F32),
        boxes(rows, chans),
        V((2, rows, chans), F32),
        boxes(few, total),
        V((2, few, total), F32),
        V((8, total), F32),
        V((size, 8, chans), F32),
        V((4, 8, chans), F32),
        DMA((7, 2, reach)),
        DMA((7, 2, reach)),
        DMA((3, size - 1)),
        DMA((3, size - 1)),
        DMA((8, 3)),
        DMA((8, 3)),
        DMA((8,)),
        DMA((2,)),
        DMA((2,)),
        DMA((11,)),
    ]
    patch_grads, tokens, vec_sum, *grads = kernel_call(
        functools.partial(backward_kernel, size, grids, side),
        "backward",
        2,
        [near] * 12 + [scalar] + [near] * 2 + [away] * 11,
        [shape for shape, _ in outs],
        [spec for _, spec in outs],
        scratch,
    )(
        grad_rows, normed_2, inv_2, vec_full, branch_2, normed_1, inv_1, branch_sum, pre_2, pre_1,
        np.ascontiguousarray(4.0 * pool.T), act, live_counts, first_reduce, second_reduce,
        held_1_k, held_2_k, x_full_k, taps_1_k, x_small_k, taps_2_k, mixer_1, mixer_2, readout_out,
        out_grad, in_grad,
    )
    out_g, in_g, mixer_2_g, reduce_2_g, expand_2_g, mixer_1_g, reduce_1_g, expand_1_g = (
        g.astype(F32) for g in grads
    )
    return (
        tokens,
        patch_grads.reshape(patches.shape),
        reduce_1_g,
        mixer_1_g.reshape(first_mixer.shape),
        expand_1_g,
        vec_sum[0],
        vec_sum[1],
        reduce_2_g,
        mixer_2_g.reshape(second_mixer.shape),
        expand_2_g,
        vec_sum[2],
        vec_sum[3],
        in_g,
        out_g,
    )


def fits(mesh, patches, first_reduce, readout_in):
    size, groups = mesh.shape["mp"], mesh.shape["dp"]
    grids, side, _, chans = patches.shape
    return (
        groups == 4
        and size % 2 == 0
        and chans % 128 == 0
        and readout_in.shape[1] % 128 == 0
        and grids * side == 6 * size
        and side % 8 == 0
        and side // 2 <= ROW_PAD
    )


def solution(mesh):
    in_specs = (
        P("dp", None, None, "mp"),
        P(None, "mp"),
        P(None, None, "mp", None),
        P("mp", None),
        P("mp"),
        P("mp"),
        P(None, "mp"),
        P(None, None, "mp", None),
        P("mp", None),
        P("mp"),
        P("mp"),
        P(None, "mp"),
        P("mp", None),
        P("dp", "mp"),
        P("dp"),
    )
    out_specs = (
        P("dp", "mp"),
        P("dp", None, None, "mp"),
        P(None, "mp"),
        P(None, None, "mp", None),
        P("mp", None),
        P("mp"),
        P("mp"),
        P(None, "mp"),
        P(None, None, "mp", None),
        P("mp", None),
        P("mp"),
        P("mp"),
        P(None, "mp"),
        P("mp", None),
    )

    def local(*args):
        if fits(mesh, args[0], args[1], args[11]):
            return fast_body(mesh.shape["mp"], *args)
        return body(*args)

    return jax.shard_map(local, mesh=mesh, in_specs=in_specs, out_specs=out_specs, check_vma=False)
```

```python
import functools

import jax
import jax.numpy as jnp
import numpy as np
from jax import lax
from jax.experimental import pallas as pl
from jax.experimental.pallas import tpu as pltpu
from jax.sharding import PartitionSpec as P

norm_eps = 1e-06


def conv_same(image, kernel):
    return lax.conv_general_dilated(
        image,
        kernel,
        (1, 1),
        "SAME",
        dimension_numbers=("NHWC", "HWIO", "NHWC"),
        preferred_element_type=jnp.float32,
    )


def silu_back(values, grad_values):
    return jax.vjp(jax.nn.silu, values)[1](grad_values)[0]


def gelu_exact(values):
    return jax.nn.gelu(values, approximate=False)


def gelu_back(values, grad_values):
    return jax.vjp(gelu_exact, values)[1](grad_values)[0]


def block_forward(inputs, reduce_w, mixer_w, expand_w, gain, shift):
    num_grids, grid_height, grid_width, local_chans = inputs.shape
    pixel_rows = num_grids * grid_height * grid_width
    low_in = inputs.astype(jnp.bfloat16).reshape(pixel_rows, local_chans)
    full_in = lax.all_gather(low_in, "mp", axis=1, tiled=True)
    total_chans = full_in.shape[1]
    pre_act = jnp.dot(full_in, reduce_w, preferred_element_type=jnp.float32)
    hidden = jax.nn.silu(pre_act).astype(jnp.bfloat16)
    partial_mix = conv_same(
        hidden.reshape(num_grids, grid_height, grid_width, local_chans), mixer_w
    )
    mixed_sum = lax.psum_scatter(
        partial_mix.reshape(pixel_rows, total_chans).astype(jnp.bfloat16),
        "mp",
        scatter_dimension=1,
        tiled=True,
    ).astype(jnp.float32)
    row_total, row_squares = lax.psum(
        (jnp.sum(mixed_sum, axis=1), jnp.sum(mixed_sum * mixed_sum, axis=1)), "mp"
    )
    center = row_total / total_chans
    inv_std = lax.rsqrt(row_squares / total_chans - center * center + norm_eps)
    normed = (mixed_sum - center[:, None]) * inv_std[:, None]
    affine = normed * gain + shift
    branch_in = jax.nn.silu(affine).astype(jnp.bfloat16)
    partial_out = jnp.dot(branch_in, expand_w, preferred_element_type=jnp.float32)
    branch_out = lax.psum_scatter(
        partial_out.astype(jnp.bfloat16), "mp", scatter_dimension=1, tiled=True
    ).astype(jnp.float32)
    outputs = inputs + branch_out.reshape(inputs.shape)
    return (outputs, (full_in, pre_act, hidden, normed, inv_std, affine, branch_in))


def block_backward(grad_out, saved, reduce_w, mixer_w, expand_w, gain):
    full_in, pre_act, hidden, normed, inv_std, affine, branch_in = saved
    num_grids, grid_height, grid_width, local_chans = grad_out.shape
    pixel_rows = num_grids * grid_height * grid_width
    grad_rows = grad_out.reshape(pixel_rows, local_chans)
    grad_branch = lax.all_gather(grad_rows.astype(jnp.bfloat16), "mp", axis=1, tiled=True)
    total_chans = grad_branch.shape[1]
    expand_grad = jnp.einsum(
        "ri,ro->io", branch_in, grad_branch, preferred_element_type=jnp.float32
    )
    grad_act = jnp.einsum("ro,io->ri", grad_branch, expand_w, preferred_element_type=jnp.float32)
    grad_affine = silu_back(affine, grad_act)
    gain_grad = jnp.sum(grad_affine * normed, axis=0)
    shift_grad = jnp.sum(grad_affine, axis=0)
    scaled = grad_affine * gain
    sum_plain, sum_normed = lax.psum(
        (jnp.sum(scaled, axis=1), jnp.sum(scaled * normed, axis=1)), "mp"
    )
    grad_mixed = inv_std[:, None] * (
        scaled - sum_plain[:, None] / total_chans - normed * sum_normed[:, None] / total_chans
    )
    mixed_full = lax.all_gather(grad_mixed.astype(jnp.bfloat16), "mp", axis=1, tiled=True)
    mixed_image = mixed_full.reshape(num_grids, grid_height, grid_width, total_chans)
    flipped = jnp.transpose(mixer_w[::-1, ::-1], (0, 1, 3, 2))
    grad_hidden = conv_same(mixed_image, flipped).reshape(pixel_rows, local_chans)
    padded = jnp.pad(
        hidden.reshape(num_grids, grid_height, grid_width, local_chans),
        ((0, 0), (1, 1), (1, 1), (0, 0)),
    )
    mixer_grad = jnp.stack(
        [
            jnp.stack(
                [
                    jnp.einsum(
                        "nhwi,nhwo->io",
                        padded[
                            :,
                            offset_h : offset_h + grid_height,
                            offset_w : offset_w + grid_width,
                            :,
                        ],
                        mixed_image,
                        preferred_element_type=jnp.float32,
                    )
                    for offset_w in range(3)
                ]
            )
            for offset_h in range(3)
        ]
    )
    grad_pre = silu_back(pre_act, grad_hidden).astype(jnp.bfloat16)
    reduce_grad = jnp.einsum("ri,ro->io", full_in, grad_pre, preferred_element_type=jnp.float32)
    partial_in = jnp.einsum("ro,io->ri", grad_pre, reduce_w, preferred_element_type=jnp.float32)
    grad_in = (
        lax.psum_scatter(
            partial_in.astype(jnp.bfloat16), "mp", scatter_dimension=1, tiled=True
        ).astype(jnp.float32)
        + grad_rows
    )
    return (
        grad_in.reshape(grad_out.shape),
        (reduce_grad, mixer_grad, expand_grad, gain_grad, shift_grad),
    )


def body(
    patches,
    first_reduce,
    first_mixer,
    first_expand,
    first_gain,
    first_shift,
    second_reduce,
    second_mixer,
    second_expand,
    second_gain,
    second_shift,
    readout_in,
    readout_out,
    cotangent,
    live_counts,
):
    num_grids, grid_height, grid_width, local_chans = patches.shape
    pooled_side = grid_height // 2
    patch_values = patches.astype(jnp.float32)
    first_out = block_forward(
        patch_values, first_reduce, first_mixer, first_expand, first_gain, first_shift
    )[0]
    pooled = first_out.reshape(num_grids, pooled_side, 2, pooled_side, 2, local_chans).mean(
        axis=(2, 4)
    )
    second_out = block_forward(
        pooled, second_reduce, second_mixer, second_expand, second_gain, second_shift
    )[0]
    token_count = num_grids * pooled_side * pooled_side
    flat = second_out.astype(jnp.bfloat16).reshape(token_count, local_chans)
    flat_full = lax.all_gather(flat, "mp", axis=1, tiled=True)
    lifted = jnp.dot(flat_full, readout_in, preferred_element_type=jnp.float32)
    activated = gelu_exact(lifted).astype(jnp.bfloat16)
    partial_tokens = jnp.dot(activated, readout_out, preferred_element_type=jnp.float32)
    summed = lax.psum_scatter(
        partial_tokens.astype(jnp.bfloat16), "mp", scatter_dimension=1, tiled=True
    ).astype(jnp.float32)
    live_slots = (jnp.arange(num_grids) < live_counts[0]).astype(jnp.float32)
    live_rows = jnp.repeat(live_slots, pooled_side * pooled_side)
    tokens = (summed * live_rows[:, None]).astype(jnp.bfloat16)
    grad_tokens = cotangent * live_rows[:, None].astype(jnp.bfloat16)
    grad_full = lax.all_gather(grad_tokens, "mp", axis=1, tiled=True)
    readout_out_grad = jnp.einsum(
        "ri,ro->io", activated, grad_full, preferred_element_type=jnp.float32
    )
    grad_act = jnp.einsum("ro,io->ri", grad_full, readout_out, preferred_element_type=jnp.float32)
    grad_lift = gelu_back(lifted, grad_act).astype(jnp.bfloat16)
    readout_in_grad = jnp.einsum(
        "ri,ro->io", flat_full, grad_lift, preferred_element_type=jnp.float32
    )
    partial_flat = jnp.einsum(
        "ro,io->ri", grad_lift, readout_in, preferred_element_type=jnp.float32
    )
    grad_flat = lax.psum_scatter(
        partial_flat.astype(jnp.bfloat16), "mp", scatter_dimension=1, tiled=True
    ).astype(jnp.float32)
    second_saved = block_forward(
        pooled, second_reduce, second_mixer, second_expand, second_gain, second_shift
    )[1]
    grad_pooled, second_grads = block_backward(
        grad_flat.reshape(num_grids, pooled_side, pooled_side, local_chans),
        second_saved,
        second_reduce,
        second_mixer,
        second_expand,
        second_gain,
    )
    spread_back = jnp.broadcast_to(
        0.25 * grad_pooled[:, :, None, :, None, :],
        (num_grids, pooled_side, 2, pooled_side, 2, local_chans),
    ).reshape(patches.shape)
    first_saved = block_forward(
        patch_values, first_reduce, first_mixer, first_expand, first_gain, first_shift
    )[1]
    patch_grads, first_grads = block_backward(
        spread_back, first_saved, first_reduce, first_mixer, first_expand, first_gain
    )
    summed_grads = (
        lax.psum(first_grads[0].astype(jnp.bfloat16), "dp").astype(jnp.float32),
        lax.psum(first_grads[1].astype(jnp.bfloat16), "dp").astype(jnp.float32),
        lax.psum(first_grads[2].astype(jnp.bfloat16), "dp").astype(jnp.float32),
        lax.psum(first_grads[3].astype(jnp.bfloat16), "dp").astype(jnp.float32),
        lax.psum(first_grads[4].astype(jnp.bfloat16), "dp").astype(jnp.float32),
        lax.psum(second_grads[0].astype(jnp.bfloat16), "dp").astype(jnp.float32),
        lax.psum(second_grads[1].astype(jnp.bfloat16), "dp").astype(jnp.float32),
        lax.psum(second_grads[2].astype(jnp.bfloat16), "dp").astype(jnp.float32),
        lax.psum(second_grads[3].astype(jnp.bfloat16), "dp").astype(jnp.float32),
        lax.psum(second_grads[4].astype(jnp.bfloat16), "dp").astype(jnp.float32),
        lax.psum(readout_in_grad.astype(jnp.bfloat16), "dp").astype(jnp.float32),
        lax.psum(readout_out_grad.astype(jnp.bfloat16), "dp").astype(jnp.float32),
    )
    return (
        tokens,
        patch_grads,
        summed_grads[0],
        summed_grads[1],
        summed_grads[2],
        summed_grads[3],
        summed_grads[4],
        summed_grads[5],
        summed_grads[6],
        summed_grads[7],
        summed_grads[8],
        summed_grads[9],
        summed_grads[10],
        summed_grads[11],
    )


MESH = pl.DeviceIdType.MESH
F32 = jnp.float32
BF16 = jnp.bfloat16
DMA = pltpu.SemaphoreType.DMA
VMEM_LIMIT = 60 * 2**20
ROW_PAD = 16


def dot_nn(a, b):
    return lax.dot_general(a, b, (((1,), (0,)), ((), ())), preferred_element_type=F32)


def dot_nt(a, b):
    return lax.dot_general(a, b, (((1,), (1,)), ((), ())), preferred_element_type=F32)


def dot_tn(a, b):
    return lax.dot_general(a, b, (((0,), (0,)), ((), ())), preferred_element_type=F32)


def dot_full(a, b):
    return lax.dot_general(
        a,
        b,
        (((1,), (0,)), ((), ())),
        precision=lax.Precision.HIGHEST,
        preferred_element_type=F32,
    )


def sigmoid(values):
    return 1.0 / (1.0 + jnp.exp(-values))


def silu(values):
    return values * sigmoid(values)


def silu_slope(values):
    gate = sigmoid(values)
    return gate * (1.0 + values * (1.0 - gate))


class Ring:
    def __init__(self, size):
        self.size = size
        self.reach = size // 2
        self.me = lax.axis_index("mp")
        half = self.me // 2
        self.spot = jnp.where(self.me % 2 == 0, half, size - 1 - half)
        self.right = self.index(self.spot + 1)
        self.left = self.index(self.spot - 1)

    def wrap(self, spot):
        return lax.rem(spot + 2 * self.size, self.size)

    def index(self, spot):
        spot = self.wrap(spot)
        return jnp.where(spot < self.reach, 2 * spot, 2 * (self.size - 1 - spot) + 1)

    def greet(self):
        barrier = pltpu.get_barrier_semaphore()
        for peer in (self.left, self.right):
            pl.semaphore_signal(barrier, inc=1, device_id={"mp": peer}, device_id_type=MESH)
        pl.semaphore_wait(barrier, 2)

    def copy(self, side, src, dst, send, recv):
        peer = self.right if side == 0 else self.left
        return pltpu.make_async_remote_copy(
            src_ref=src,
            dst_ref=dst,
            send_sem=send,
            recv_sem=recv,
            device_id={"mp": peer},
            device_id_type=MESH,
        )


class Gather:
    def __init__(self, ring, own, held, slot, lanes, send, recv):
        self.ring, self.own, self.held, self.slot = ring, own, held, slot
        self.lanes, self.send, self.recv, self.copies = lanes, send, recv, {}

    def _start(self, side, step, lane):
        ring = self.ring
        if step == ring.reach and lane != side:
            return
        away = step - 1
        spot = ring.wrap(ring.spot - away if side == 0 else ring.spot + away)
        dst = self.held.at[self.slot(spot)]
        src = self.own if step == 1 else dst
        sems = (sem.at[side, step - 1, lane] for sem in (self.send, self.recv))
        copy = ring.copy(side, src.at[self.lanes[lane]], dst.at[self.lanes[lane]], *sems)
        copy.start()
        self.copies[side, step, lane] = copy

    def start(self):
        for lane in range(2):
            for side in range(2):
                self._start(side, 1, lane)

    def move(self, step):
        for lane in range(2):
            for side in range(2):
                if (side, step, lane) in self.copies:
                    self.copies[side, step, lane].wait_recv()
                    if step < self.ring.reach:
                        self._start(side, step + 1, lane)

    def drain(self):
        for copy in self.copies.values():
            copy.wait_send()

    def spots(self, step):
        ring = self.ring
        if step == ring.reach:
            return [ring.wrap(ring.spot + step)]
        return [ring.wrap(ring.spot - step), ring.wrap(ring.spot + step)]


class Scatter:
    def __init__(self, ring, term, boxes, terms, lanes, send, recv):
        self.ring, self.term, self.out, self.inbox = ring, term, boxes[0], boxes[1]
        self.terms, self.lanes, self.send, self.recv, self.copies = terms, lanes, send, recv, {}

    def _start(self, side, step, lane):
        at = self.lanes[lane]
        sems = (sem.at[side, step - 1, lane] for sem in (self.send, self.recv))
        src, dst = self.out.at[side, step - 1], self.inbox.at[side, step - 1]
        copy = self.ring.copy(side, src.at[at], dst.at[at], *sems)
        copy.start()
        self.copies[side, step, lane] = copy

    def start(self):
        ring = self.ring
        value = self.term(ring.wrap(ring.spot + ring.reach))
        self.terms[0] = value
        for side in range(2):
            at = self.lanes[side]
            self.out[(side, 0) + at] = self.terms[(0,) + at].astype(BF16)
            self._start(side, 1, side)

    def prepare(self, step):
        ring = self.ring
        away = ring.reach + 1 - step
        self.terms[0] = self.term(ring.wrap(ring.spot + away))
        if away > 0:
            self.terms[1] = self.term(ring.wrap(ring.spot - away))
        if step == 2:
            for side in range(2):
                at = self.lanes[1 - side]
                self.out[(side, 1) + at] = self.terms[(side,) + at].astype(BF16)
                self._start(side, 2, 1 - side)

    def _pass(self, side, step, lane):
        at = self.lanes[lane]
        self.copies[side, step - 1, lane].wait_recv()
        got = self.inbox[(side, step - 2) + at].astype(F32)
        self.out[(side, step - 1) + at] = (self.terms[(side,) + at] + got).astype(BF16)
        self._start(side, step, lane)

    def step(self, step):
        if step > 2:
            for side in range(2):
                self._pass(side, step, 1 - side)
        for side in range(2):
            self._pass(side, step, side)

    def finish(self):
        reach = self.ring.reach
        for lane in range(2):
            for side in range(2):
                self.copies[side, reach, lane].wait_recv()
        return (
            self.terms[0]
            + self.inbox[0, reach - 1].astype(F32)
            + self.inbox[1, reach - 1].astype(F32)
        )

    def drain(self):
        for copy in self.copies.values():
            copy.wait_send()


def row_halves(rows):
    return ((pl.ds(0, rows // 2),), (pl.ds(rows // 2, rows // 2),))


def column_halves(columns):
    every = slice(None)
    return (
        (every, pl.ds(0, columns // 2)),
        (every, pl.ds(columns // 2, columns // 2)),
    )


def pool_places(side):
    small = side // 2
    place = np.zeros((3 * ROW_PAD, 6 * side), np.float32)
    for row in range(6):
        for column in range(side):
            place[(row // 2) * ROW_PAD + column // 2, row * side + column] = 0.25
    assert small <= ROW_PAD
    return place


def token_places(grids, small):
    place = np.zeros((grids * small * small, grids * small * ROW_PAD), np.float32)
    for line in range(grids * small):
        for column in range(small):
            place[line * small + column, line * ROW_PAD + column] = 1.0
    return place


def norm_rows(mixed, gain, shift):
    center = jnp.mean(mixed, axis=1, keepdims=True)
    apart = mixed - center
    inv_std = lax.rsqrt(jnp.mean(apart * apart, axis=1, keepdims=True) + norm_eps)
    normed = apart * inv_std
    return normed, inv_std, normed * gain + shift


def wide_vector(held, row):
    return jnp.concatenate([held[m, row : row + 1, :] for m in range(held.shape[0])], axis=1)


def half_of(rows, columns, which, by_rows):
    if by_rows:
        return (pl.ds(pl.multiple_of(which * (rows // 2), 16), rows // 2), slice(None))
    return (slice(None), pl.ds(pl.multiple_of(which * (columns // 2), 128), columns // 2))


class Pair:
    def __init__(self):
        self.me = lax.axis_index("dp")
        self.core = lax.rem(self.me, 2)
        self.other = 1 - self.core
        self.twin = self.me - self.core + self.other
        self.far = lax.rem(self.me + 2, 4)

    def copy(self, peer, src, dst, send, recv):
        return pltpu.make_async_remote_copy(
            src_ref=src,
            dst_ref=dst,
            send_sem=send,
            recv_sem=recv,
            device_id={"dp": peer},
            device_id_type=MESH,
        )


def greet_ring_and_pair(ring, pair):
    barrier = pltpu.get_barrier_semaphore()
    for peer in (ring.left, ring.right):
        pl.semaphore_signal(barrier, inc=1, device_id={"mp": peer}, device_id_type=MESH)
    for peer in (pair.twin, pair.far):
        pl.semaphore_signal(barrier, inc=1, device_id={"dp": peer}, device_id_type=MESH)
    pl.semaphore_wait(barrier, 4)


class Expand:
    def __init__(self, ring, pair, own, held, send, recv, psend, precv):
        self.ring, self.pair, self.held = ring, pair, held
        self.psend, self.precv, self.copies = psend, precv, []
        chans, quarter = held.shape[2:]
        columns = own[:, pl.ds(pl.multiple_of(pair.me * quarter, 128), quarter)]
        held[pair.me, ring.me] = columns
        self.gather = Gather(
            ring, held.at[pair.me, ring.me], held.at[pair.me], ring.index, row_halves(chans), send, recv
        )

    def across(self):
        self.gather.move(self.ring.reach)
        self._swap(0, self.pair.far, self.pair.me)

    def between(self):
        self.copies[0].wait_recv()
        self._swap(1, self.pair.twin, self.pair.me)
        self._swap(2, self.pair.twin, self.pair.far)

    def _swap(self, k, peer, quarter):
        at = self.held.at[quarter]
        copy = self.pair.copy(peer, at, at, self.psend.at[k], self.precv.at[k])
        copy.start()
        self.copies.append(copy)

    def ready(self):
        for copy in self.copies[1:]:
            copy.wait_recv()

    def drain(self):
        self.gather.drain()
        for copy in self.copies:
            copy.wait_send()


def times_expand(rows, held):
    parts = []
    for k in range(held.shape[0]):
        weight = held[k].reshape(rows.shape[1], held.shape[3])
        parts.append(dot_nn(rows, weight))
    return jnp.concatenate(parts, axis=1)


def times_expand_back(rows, held):
    quarter = held.shape[3]
    total = None
    for k in range(held.shape[0]):
        weight = held[k].reshape(held.shape[1] * held.shape[2], quarter)
        part = dot_nt(rows[:, k * quarter : (k + 1) * quarter], weight)
        total = part if total is None else total + part
    return total


def chunk_taps(image, taps, spot, lines, side, width):
    chans = image.shape[-1]
    per_grid = side // lines
    grid, line = spot // per_grid, lax.rem(spot, per_grid) * lines
    for kh in range(3):
        for kw in range(3):
            piece = image[grid, pl.ds(line + kh, lines), 7 + kw : 7 + kw + width, :]
            at = (kh * 3 + kw) * chans
            taps[spot, :, at : at + chans] = piece.reshape(lines * width, chans).astype(BF16)


def chunk_back(image, product, spot, lines, side, width):
    chans = image.shape[-1]
    per_grid = side // lines
    grid, line = spot // per_grid, lax.rem(spot, per_grid) * lines
    for kh in range(3):
        for kw in range(3):
            at = (kh * 3 + kw) * chans
            piece = product[:, at : at + chans].reshape(lines, width, chans)
            image[grid, pl.ds(line + kh, lines), 7 + kw : 7 + kw + width, :] += piece


def forward_kernel(
    size, grids, side,
    x, reduce_1, expand_1, expand_2, gain_1, shift_1, gain_2, shift_2, pool, places, counts,
    mixer_1_any, reduce_2_any, mixer_2_any, readout_in_any, readout_out_any, cotangent,
    x_full_out, pre_1, taps_1_out, normed_1, inv_1, branch_sum, held_1_out, vec_full,
    x_small_out, pre_2, taps_2_out, normed_2, inv_2, branch_2, held_2_out,
    grad_rows, act, out_half_out, in_half_out,
    x_full, mixer_1, taps_1, image_1, boxes_1, terms_1, x_rows, held_1, held_2, vectors,
    pooled, low, x_small, reduce_2, mixer_2, taps_2, image_2, boxes_2, boxes_3, terms_2, flat_full, cot_full,
    readout_in, readout_out, lifted, act_live, grad_act, grad_lift, out_grad, in_grad, out_core, in_core,
    send, recv, psend, precv, csend, crecv, load, store,
):
    ring, pair = Ring(size), Pair()
    rows, chans = x.shape
    share = rows // size
    total = size * chans
    small = side // 2
    few = pooled.shape[0]
    part = readout_in.shape[1]
    tokens = cotangent.shape[0]
    wide = column_halves(total)
    near = lambda spot: spot
    loads = [
        pltpu.make_async_copy(src, dst, load.at[k])
        for k, (src, dst) in enumerate(
            [
                (mixer_1_any, mixer_1),
                (reduce_2_any, reduce_2),
                (mixer_2_any, mixer_2),
                (readout_in_any, readout_in),
                (readout_out_any, readout_out),
                (cotangent, cot_full.at[ring.me]),
            ]
        )
    ]
    stores = []

    def keep(src, dst):
        copy = pltpu.make_async_copy(src, dst, store.at[len(stores)])
        copy.start()
        stores.append(copy)

    for copy in loads:
        copy.start()
    greet_ring_and_pair(ring, pair)
    gx = Gather(ring, x, x_full, ring.index, row_halves(rows), send.at[0], recv.at[0])
    gx.start()
    e1 = Expand(ring, pair, expand_1, held_1, send.at[2], recv.at[2], psend.at[0], precv.at[0])
    e2 = Expand(ring, pair, expand_2, held_2, send.at[3], recv.at[3], psend.at[1], precv.at[1])
    e1.gather.start()
    e2.gather.start()
    x_full[ring.me] = x[...]
    for k, vector in enumerate((gain_1, shift_1, gain_2, shift_2)):
        for row in (k, k + 8):
            vectors[row : row + 1, :] = vector[...]
    for k in range(4, 8):
        for row in (k, k + 8):
            vectors[row : row + 1, :] = gain_1[...]
    vec_full[ring.me] = vectors[...]
    gv = Gather(ring, vectors, vec_full, ring.index, row_halves(16), send.at[1], recv.at[1])
    gv.start()

    def add(spot):
        m = ring.index(spot)
        weight = reduce_1[pl.ds(pl.multiple_of(m * chans, chans), chans), :]
        pre_1[...] += dot_nn(x_full[m], weight)

    own = reduce_1[pl.ds(pl.multiple_of(ring.me * chans, chans), chans), :]
    pre_1[...] = dot_nn(x[...], own)
    image_1[...] = jnp.zeros(image_1.shape, F32)
    image_2[...] = jnp.zeros(image_2.shape, F32)
    for step in range(1, ring.reach + 1):
        gx.move(step)
        for spot in gx.spots(step):
            add(spot)
        if step < ring.reach:
            for item in (e1.gather, e2.gather, gv):
                item.move(step)
    keep(x_full, x_full_out)
    hidden = silu(pre_1[...])
    image_1[:, 1 : 1 + side, 8 : 8 + side, :] = hidden.reshape(grids, side, side, chans)
    loads[0].wait()

    def mix_1(spot):
        chunk_taps(image_1, taps_1, spot, 6, side, side)
        return dot_nn(taps_1[spot], mixer_1[...])

    rs1 = Scatter(
        ring, mix_1, (boxes_1.at[0], boxes_1.at[1]), terms_1, wide, send.at[4], recv.at[4]
    )
    rs1.start()
    e1.across()
    gv.move(ring.reach)
    for step in range(2, ring.reach + 1):
        rs1.prepare(step)
        rs1.step(step)
        if step == ring.reach - 1:
            e1.between()
            e2.across()
    rs1.prepare(ring.reach + 1)
    keep(taps_1, taps_1_out)
    mine = pl.ds(pl.multiple_of(ring.spot * share, 16), share)
    for m in range(size):
        x_rows[:, m * chans : (m + 1) * chans] = x_full[m, mine, :].astype(F32)
    gain_a, shift_a = wide_vector(vec_full, 0), wide_vector(vec_full, 1)
    mixed = rs1.finish()
    loads[5].wait()
    gc = Gather(
        ring, cot_full.at[ring.me], cot_full, ring.index, row_halves(tokens), send.at[5], recv.at[5]
    )
    gc.start()
    value, inverse, affine = norm_rows(mixed, gain_a, shift_a)
    normed_1[...] = value
    inv_1[...] = jnp.broadcast_to(inverse, inv_1.shape)
    branch = silu(affine).astype(BF16)
    e1.ready()
    keep(held_1, held_1_out)
    pooled[...] = dot_full(pool[...], x_rows[...] + times_expand(branch, held_1))
    low[0] = pooled[...].astype(BF16)
    x_small[ring.spot] = low[0]
    g2 = Gather(ring, low.at[0], x_small, near, wide, send.at[6], recv.at[6])
    g2.start()
    branch_sum[...] = (4.0 * dot_full(pool[...], branch.astype(F32))).astype(BF16)
    for step in range(1, ring.reach + 1):
        g2.move(step)
        if step == 1:
            gc.move(1)
    loads[1].wait()
    e2.between()
    pre_2[...] = dot_nn(x_small[...].reshape(size * few, total), reduce_2[...])
    keep(x_small, x_small_out)
    hidden = silu(pre_2[...])
    image_2[:, 1 : 1 + small, 8 : 8 + ROW_PAD, :] = hidden.reshape(grids, small, ROW_PAD, chans)
    loads[2].wait()

    def mix_2(spot):
        chunk_taps(image_2, taps_2, spot, 3, small, ROW_PAD)
        return dot_nn(taps_2[spot], mixer_2[...])

    rs2 = Scatter(
        ring, mix_2, (boxes_2.at[0], boxes_2.at[1]), terms_2, wide, send.at[7], recv.at[7]
    )
    rs2.start()
    gc.move(2)
    for step in range(2, ring.reach + 1):
        rs2.prepare(step)
        rs2.step(step)
    rs2.prepare(ring.reach + 1)
    keep(taps_2, taps_2_out)
    gain_b, shift_b = wide_vector(vec_full, 2), wide_vector(vec_full, 3)
    mixed = rs2.finish()
    value, inverse, affine = norm_rows(mixed, gain_b, shift_b)
    normed_2[...] = value
    inv_2[...] = jnp.broadcast_to(inverse, inv_2.shape)
    branch_2[...] = silu(affine).astype(BF16)
    e2.ready()
    keep(held_2, held_2_out)
    low[1] = (pooled[...] + times_expand(branch_2[...], held_2)).astype(BF16)
    flat_full[ring.spot] = low[1]
    gf = Gather(ring, low.at[1], flat_full, near, wide, send.at[8], recv.at[8])
    gf.start()
    for step in range(1, ring.reach + 1):
        gf.move(step)
        if step == 1:
            gc.move(3)
    loads[3].wait()
    flat = dot_nn(places[...], flat_full[...].reshape(size * few, total)).astype(BF16)
    lifted[...] = dot_nn(flat, readout_in[...])
    cdf = 0.5 * (1.0 + lax.erf(lifted[...] * 0.7071067811865476))
    row_ids = lax.broadcasted_iota(jnp.int32, (tokens, 1), 0)
    live = (row_ids < counts[0] * (tokens // grids)).astype(F32)
    activated = (lifted[...] * cdf).astype(BF16)
    act[...] = activated
    act_live[...] = (activated.astype(F32) * live).astype(BF16)
    slope = cdf + lifted[...] * jnp.exp(-0.5 * lifted[...] * lifted[...]) * 0.3989422804014327
    lifted[...] = slope * live
    grad_act[...] = jnp.zeros(grad_act.shape, F32)
    loads[4].wait()
    gc.move(ring.reach)

    def back(m, carry):
        at = pl.ds(pl.multiple_of(m * part, 128), part)
        grad_act[...] += dot_nt(cot_full[m], readout_out[:, at])
        return carry

    lax.fori_loop(0, size, back, 0)
    lift = (grad_act[...] * lifted[...]).astype(BF16)
    grad_lift[...] = dot_tn(places[...], lift).astype(BF16)

    def flat_term(spot):
        return dot_nt(grad_lift[pl.ds(pl.multiple_of(spot * few, 16), few), :], readout_in[...])

    rf = Scatter(
        ring, flat_term, (boxes_3.at[0], boxes_3.at[1]), terms_2, wide, send.at[9], recv.at[9]
    )
    rf.start()

    def weights(m, carry):
        at = pl.ds(pl.multiple_of(m * part, 128), part)
        out_grad[:, at] = dot_tn(act_live[...], cot_full[m]).astype(BF16)
        return carry

    def swap(k, grad, box):
        half = half_of(*grad.shape, pair.other, True)
        copy = pair.copy(pair.twin, grad.at[half], box, csend.at[k], crecv.at[k])
        copy.start()
        return copy

    def add_half(copy, grad, box, result):
        copy.wait_recv()
        half = half_of(*grad.shape, pair.core, True)
        box[...] = (grad[half].astype(F32) + box[...].astype(F32)).astype(BF16)
        keep(box, result)

    lax.fori_loop(0, size // 2, weights, 0)
    for step in range(2, ring.reach + 1):
        rf.prepare(step)
        rf.step(step)
        if step == 2:
            lax.fori_loop(size // 2, size, weights, 0)
            out_copy = swap(0, out_grad, out_core)
        if step == 3:
            in_grad[...] = dot_tn(flat, lift).astype(BF16)
            in_copy = swap(1, in_grad, in_core)
    rf.prepare(ring.reach + 1)
    grad_rows[...] = rf.finish()
    add_half(out_copy, out_grad, out_core, out_half_out)
    add_half(in_copy, in_grad, in_core, in_half_out)
    for item in (gx, gv, e1, e2, rs1, gc, g2, rs2, gf, rf):
        item.drain()
    for copy in (out_copy, in_copy):
        copy.wait_send()
    for copy in stores:
        copy.wait()


def norm_back(grad_branch, normed, inv_std, gain, shift):
    affine = normed * gain + shift
    grad_affine = grad_branch * silu_slope(affine)
    gain_grad = jnp.sum(grad_affine * normed, axis=0, keepdims=True)
    shift_grad = jnp.sum(grad_affine, axis=0, keepdims=True)
    scaled = grad_affine * gain
    mean_plain = jnp.mean(scaled, axis=1, keepdims=True)
    mean_normed = jnp.mean(scaled * normed, axis=1, keepdims=True)
    return inv_std * (scaled - mean_plain - normed * mean_normed), gain_grad, shift_grad


class GroupSum:
    def __init__(self, pair, mine, other, from_core, from_far, result, half, send, recv, local):
        self.pair, self.mine, self.other = pair, mine, other
        self.from_core, self.from_far = from_core, from_far
        self.result = result.at[half]
        self.send, self.recv, self.local, self.copies = send, recv, local, []

    def _go(self, k, peer, src, dst):
        copy = self.pair.copy(peer, src, dst, self.send.at[k], self.recv.at[k])
        copy.start()
        self.copies.append(copy)

    def core(self):
        self._go(0, self.pair.twin, self.other, self.from_core)

    def far(self):
        if self.from_core is not None:
            self.copies[0].wait_recv()
            self.mine[...] = (self.mine[...].astype(F32) + self.from_core[...].astype(F32)).astype(
                BF16
            )
        self._go(1, self.pair.far, self.mine, self.from_far)

    def back(self):
        self.copies[-1].wait_recv()
        self.from_far[...] = (self.mine[...].astype(F32) + self.from_far[...].astype(F32)).astype(
            BF16
        )
        self._go(2, self.pair.twin, self.from_far, self.result)
        self.kept = pltpu.make_async_copy(self.from_far, self.result, self.local)
        self.kept.start()

    def done(self):
        self.copies[-1].wait_recv()
        self.kept.wait()
        for copy in self.copies:
            copy.wait_send()


def send_columns(ring, src, held, slot, send, recv):
    chans = held.shape[-1]
    held[slot] = src[:, pl.ds(pl.multiple_of(ring.me * chans, chans), chans)]
    copies = []
    for away in range(1, ring.size):
        peer = lax.rem(ring.me + away, ring.size)
        copy = pltpu.make_async_remote_copy(
            src_ref=src.at[:, pl.ds(pl.multiple_of(peer * chans, chans), chans)],
            dst_ref=held.at[slot],
            send_sem=send.at[away - 1],
            recv_sem=recv.at[away - 1],
            device_id={"mp": peer},
            device_id_type=MESH,
        )
        copy.start()
        copies.append(copy)
    return copies


def backward_kernel(
    size, grids, side,
    grad_rows, normed_2, inv_2, vec_full, branch_2, normed_1, inv_1, branch_sum, pre_2, pre_1, spread, act, counts,
    reduce_1, reduce_2,
    held_1_any, held_2_any, x_full_any, taps_1_any, x_small_any, taps_2_any, mixer_1_any, mixer_2_any,
    readout_any, out_half_any, in_half_any,
    patch_grads, tokens, vec_sum, out_sum, in_sum, mixer_2_sum, reduce_2_sum, expand_2_sum,
    mixer_1_sum, reduce_1_sum, expand_1_sum,
    held, x_full, taps_1, x_small, taps_2, mixer, readout,
    out_mine, out_far, in_mine, in_far,
    mixer_2_grad, mixer_2_core, mixer_2_far, reduce_2_grad, reduce_2_core, reduce_2_far,
    expand_2_grad, expand_2_core, expand_2_far,
    mixer_1_grad, mixer_1_core, mixer_1_far, reduce_1_grad, reduce_1_core, reduce_1_far,
    expand_1_grad, expand_1_core, expand_1_far,
    image_1, image_2, product_1, product_2, low_2, low_1, mix_2, mix_1, mix_2_full, mix_1_full,
    low_2_full, low_1_full, branch_2_full, branch_1_full, grad_pre_2, grad_pre_1, grad_out, wide_term,
    boxes_big, terms_big, boxes_small, terms_small, vec_grad, vec_held, vec_part,
    send, recv, all_send, all_recv, sum_send, sum_recv, sum_local, vec_send, vec_recv, load,
):
    ring, pair = Ring(size), Pair()
    few, total = grad_rows.shape
    share = normed_1.shape[0]
    chans = total // size
    rows = size * share
    small = side // 2
    part = readout_any.shape[1] // size
    near = lambda spot: spot
    wide = column_halves(total)
    pairs = [
        (held_2_any, held),
        (mixer_2_any, mixer),
        (readout_any, readout),
        (out_half_any, out_mine),
        (in_half_any, in_mine),
        (taps_2_any, taps_2),
        (x_small_any, x_small),
        (held_1_any, held),
        (mixer_1_any, mixer),
        (taps_1_any, taps_1),
        (x_full_any, x_full),
    ]
    loads = [
        pltpu.make_async_copy(src, dst, load.at[k]) for k, (src, dst) in enumerate(pairs)
    ]
    for k in (3, 0, 1, 4, 2, 5, 6, 9, 10):
        loads[k].start()
    barrier = pltpu.get_barrier_semaphore()
    for away in range(1, size):
        peer = lax.rem(ring.me + away, size)
        pl.semaphore_signal(barrier, inc=1, device_id={"mp": peer}, device_id_type=MESH)
    for peer in (pair.twin, pair.far):
        pl.semaphore_signal(barrier, inc=1, device_id={"dp": peer}, device_id_type=MESH)
    pl.semaphore_wait(barrier, size + 1)

    def group_sum(k, mine, other, from_core, from_far, result, by_rows):
        half = half_of(*result.shape, pair.core, by_rows)
        return GroupSum(
            pair, mine, other, from_core, from_far, result, half, sum_send.at[k], sum_recv.at[k], sum_local.at[k]
        )

    def grad_sum(k, grad, from_core, from_far, result, by_rows):
        mine, other = (
            grad.at[half_of(*grad.shape, which, by_rows)] for which in (pair.core, pair.other)
        )
        return group_sum(k, mine, other, from_core, from_far, result, by_rows)

    s_out = group_sum(0, out_mine, None, None, out_far, out_sum, True)
    s_in = group_sum(1, in_mine, None, None, in_far, in_sum, True)
    s_m2 = grad_sum(2, mixer_2_grad, mixer_2_core, mixer_2_far, mixer_2_sum, False)
    s_r2 = grad_sum(3, reduce_2_grad, reduce_2_core, reduce_2_far, reduce_2_sum, True)
    s_e2 = grad_sum(4, expand_2_grad, expand_2_core, expand_2_far, expand_2_sum, False)
    s_m1 = grad_sum(5, mixer_1_grad, mixer_1_core, mixer_1_far, mixer_1_sum, False)
    s_r1 = grad_sum(6, reduce_1_grad, reduce_1_core, reduce_1_far, reduce_1_sum, True)
    s_e1 = grad_sum(7, expand_1_grad, expand_1_core, expand_1_far, expand_1_sum, False)
    loads[3].wait()
    s_out.far()
    low_2[...] = grad_rows[...].astype(BF16)
    loads[0].wait()
    gain_b, shift_b = wide_vector(vec_full, 2), wide_vector(vec_full, 3)
    grad_branch = times_expand_back(low_2[...], held)
    value, gain_grad, shift_grad = norm_back(
        grad_branch, normed_2[...], inv_2[:, 0:1], gain_b, shift_b
    )
    loads[7].start()
    mix_2[...] = value.astype(BF16)
    g_mix2 = Gather(ring, mix_2, mix_2_full, near, wide, send.at[0], recv.at[0])
    g_mix2.start()
    mix_2_full[ring.spot] = mix_2[...]
    vec_grad[...] = jnp.zeros(vec_grad.shape, F32)
    vec_grad[2:3, :] = gain_grad
    vec_grad[3:4, :] = shift_grad
    image_2[...] = jnp.zeros(image_2.shape, F32)
    image_1[...] = jnp.zeros(image_1.shape, F32)

    def token_term(spot):
        at = pl.ds(pl.multiple_of(ring.index(spot) * part, 128), part)
        value = dot_nn(act[...], readout[:, at])
        return jnp.concatenate(
            [value[:, k : k + chans] for k in range(0, part, chans)], axis=0
        )

    tall = row_halves(rows)
    big = (boxes_big.at[0], boxes_big.at[1])
    r_tok = Scatter(ring, token_term, big, terms_big, tall, send.at[1], recv.at[1])
    loads[2].wait()
    r_tok.start()
    loads[4].wait()
    s_in.far()

    def back_2(spot):
        product_2[...] = dot_nt(mix_2_full[spot], mixer[...])
        chunk_back(image_2, product_2, spot, 3, small, ROW_PAD)

    loads[1].wait()
    back_2(ring.spot)
    for step in range(1, ring.reach + 1):
        g_mix2.move(step)
        for spot in g_mix2.spots(step):
            back_2(spot)
    loads[8].start()
    grad_hidden = image_2[:, 1 : 1 + small, 8 : 8 + ROW_PAD, :].reshape(pre_2.shape)
    grad_pre_2[...] = (grad_hidden * silu_slope(pre_2[...])).astype(BF16)

    def in_term_2(spot):
        return dot_nt(grad_pre_2[pl.ds(pl.multiple_of(spot * few, 16), few), :], reduce_2[...])

    r_in2 = Scatter(
        ring, in_term_2, (boxes_small.at[0], boxes_small.at[1]), terms_small, wide, send.at[2], recv.at[2]
    )
    r_in2.start()
    r_tok.prepare(2)
    r_tok.step(2)

    def mixer_half(grad, taps, mix, which, count):
        columns = pl.ds(pl.multiple_of(which * (total // 2), 128), total // 2)

        def one(k, carry):
            at = pl.ds(pl.multiple_of(k * chans, chans), chans)
            left = taps[:, :, at].reshape(size * count, chans)
            right = mix[:, :, columns].reshape(size * count, total // 2)
            grad[at, columns] = dot_tn(left, right).astype(BF16)
            return carry

        lax.fori_loop(0, 9, one, 0)

    loads[5].wait()
    for step in range(2, ring.reach + 1):
        r_in2.prepare(step)
        r_in2.step(step)
        if step == 2:
            mixer_half(mixer_2_grad, taps_2, mix_2_full, pair.other, few)
            s_m2.core()
        if step == 3:
            mixer_half(mixer_2_grad, taps_2, mix_2_full, pair.core, few)
    r_in2.prepare(ring.reach + 1)
    r_tok.prepare(3)
    loads[7].wait()
    quarter = 0.25 * (r_in2.finish() + grad_rows[...])
    r_tok.step(3)
    low_1[...] = quarter.astype(BF16)
    gain_a, shift_a = wide_vector(vec_full, 0), wide_vector(vec_full, 1)
    grad_branch = dot_full(spread[...], times_expand_back(low_1[...], held))
    value, gain_grad, shift_grad = norm_back(
        grad_branch, normed_1[...], inv_1[:, 0:1], gain_a, shift_a
    )
    mix_1[...] = value.astype(BF16)
    g_mix1 = Gather(ring, mix_1, mix_1_full, near, wide, send.at[3], recv.at[3])
    g_mix1.start()
    mix_1_full[ring.spot] = mix_1[...]
    vec_grad[0:1, :] = gain_grad
    vec_grad[1:2, :] = shift_grad
    grad_out[...] = dot_full(spread[...], quarter)
    s_m2.far()
    loads[6].wait()

    def reduce_part(grad, full, grad_pre):
        grad[...] = dot_tn(full, grad_pre).astype(BF16)

    reduce_part(reduce_2_grad, x_small[...].reshape(size * few, total), grad_pre_2[...])
    s_r2.core()
    r_tok.prepare(4)

    def back_1(spot):
        product_1[...] = dot_nt(mix_1_full[spot], mixer[...])
        chunk_back(image_1, product_1, spot, 6, side, side)

    loads[8].wait()
    back_1(ring.spot)
    low_2_full[ring.spot] = low_2[...]
    low_1_full[ring.spot] = low_1[...]
    g_low2 = Gather(ring, low_2, low_2_full, near, wide, send.at[4], recv.at[4])
    g_low1 = Gather(ring, low_1, low_1_full, near, wide, send.at[5], recv.at[5])
    for step in range(1, ring.reach + 1):
        g_mix1.move(step)
        if step == 1:
            r_tok.step(4)
            a_low2 = send_columns(
                ring, branch_2, branch_2_full, ring.spot, all_send.at[0], all_recv.at[0]
            )
            a_low1 = send_columns(
                ring, branch_sum, branch_1_full, ring.spot, all_send.at[1], all_recv.at[1]
            )
            a_vec = send_columns(
                ring, vec_grad, vec_held, ring.me, all_send.at[2], all_recv.at[2]
            )
        if step == 2:
            r_tok.prepare(ring.reach + 1)
            value = r_tok.finish()
            r_tok.drain()
            count = rows * chans // part
            value = jnp.concatenate(
                [value[k * count : (k + 1) * count] for k in range(part // chans)], axis=1
            )
            row_ids = lax.broadcasted_iota(jnp.int32, (count, 1), 0)
            live = (row_ids < counts[0] * (count // grids)).astype(F32)
            tokens[...] = (value * live).astype(BF16)
            s_r2.far()
            g_low2.start()
            g_low1.start()
        for spot in g_mix1.spots(step):
            back_1(spot)

    def lows(step):
        for item in (g_low2, g_low1):
            item.move(step)

    grad_hidden = image_1[:, 1 : 1 + side, 8 : 8 + side, :].reshape(pre_1.shape)
    grad_pre_1[...] = (grad_hidden * silu_slope(pre_1[...])).astype(BF16)
    mine = pl.ds(pl.multiple_of(ring.spot * share, 16), share)

    def in_term_1(spot):
        at = pl.ds(pl.multiple_of(ring.index(spot) * chans, chans), chans)
        wide_term[...] = dot_nt(grad_pre_1[...], reduce_1[at, :])
        wide_term[mine, :] += grad_out[:, at]
        return wide_term[...]

    r_in1 = Scatter(ring, in_term_1, big, terms_big, tall, send.at[6], recv.at[6])
    r_in1.start()
    loads[9].wait()
    mixer_half(mixer_1_grad, taps_1, mix_1_full, pair.other, share)
    s_m1.core()
    lows(1)
    r_in1.prepare(2)
    r_in1.step(2)
    mixer_half(mixer_1_grad, taps_1, mix_1_full, pair.core, share)
    s_m1.far()
    lows(2)
    loads[10].wait()

    def reduces(m, carry):
        at = pl.ds(pl.multiple_of(m * chans, chans), chans)
        reduce_1_grad[at, :] = dot_tn(x_full[m], grad_pre_1[...]).astype(BF16)
        return carry

    lax.fori_loop(0, size, reduces, 0)
    s_r1.core()
    r_in1.prepare(3)
    r_in1.step(3)
    lows(3)
    s_r1.far()
    s_out.back()
    for copy in a_vec:
        copy.wait()
    vec_part[0] = jnp.sum(vec_held[...], axis=0)
    v_core = pair.copy(pair.twin, vec_part.at[0], vec_part.at[1], vec_send.at[0], vec_recv.at[0])
    v_core.start()
    r_in1.prepare(4)
    r_in1.step(4)
    lows(4)
    for copy in a_low2 + a_low1:
        copy.wait()

    def expand_part(grad, branches, lows):
        grad[...] = dot_tn(
            branches[...].reshape(size * few, chans), lows[...].reshape(size * few, total)
        ).astype(BF16)

    expand_part(expand_2_grad, branch_2_full, low_2_full)
    expand_part(expand_1_grad, branch_1_full, low_1_full)
    s_e2.core()
    s_e1.core()
    v_core.wait()
    vec_part[2] = vec_part[0] + vec_part[1]
    v_far = pair.copy(pair.far, vec_part.at[2], vec_part.at[3], vec_send.at[1], vec_recv.at[1])
    v_far.start()
    r_in1.prepare(ring.reach + 1)
    s_in.back()
    s_e2.far()
    s_e1.far()
    s_m2.back()
    s_r2.back()
    patch_grads[...] = r_in1.finish()
    v_far.wait()
    vec_sum[...] = vec_part[2] + vec_part[3]
    s_m1.back()
    s_r1.back()
    s_e2.back()
    s_e1.back()
    for item in (s_out, s_in, s_m2, s_r2, s_e2, s_m1, s_r1, s_e1):
        item.done()
    for item in (g_mix2, r_in2, g_mix1, g_low2, g_low1, r_in1):
        item.drain()


def widen_kernel(*refs):
    ins, outs = refs[:11], refs[11:]
    for src, dst in zip(ins[:10], outs[:10]):
        dst[...] = src[...].astype(dst.dtype)
    for k in range(4):
        outs[10 + k][...] = ins[10][k : k + 1, :]


def kernel_call(kernel, name, number, in_specs, outs, out_specs, scratch, flops=0):
    def run(*args):
        return pl.pallas_call(
            kernel,
            name=name,
            out_shape=outs,
            in_specs=in_specs,
            out_specs=out_specs,
            scratch_shapes=scratch,
            cost_estimate=pl.CostEstimate(flops=flops, bytes_accessed=0, transcendentals=0),
            compiler_params=pltpu.CompilerParams(
                collective_id=number, has_side_effects=True, vmem_limit_bytes=VMEM_LIMIT
            ),
        )(*args)

    return run


def fast_body(
    size,
    patches,
    first_reduce,
    first_mixer,
    first_expand,
    first_gain,
    first_shift,
    second_reduce,
    second_mixer,
    second_expand,
    second_gain,
    second_shift,
    readout_in,
    readout_out,
    cotangent,
    live_counts,
):
    S = jax.ShapeDtypeStruct
    V = pltpu.VMEM
    near = pl.BlockSpec(memory_space=pltpu.VMEM)
    scalar = pl.BlockSpec(memory_space=pltpu.SMEM)
    away = pl.BlockSpec(memory_space=pl.ANY)
    grids, side, _, chans = patches.shape
    total = first_expand.shape[1]
    rows = grids * side * side
    share = rows // size
    small = side // 2
    few = 3 * ROW_PAD
    few_rows = few * size
    token_rows = grids * small * small
    part = readout_in.shape[1]
    wide = readout_out.shape[1]
    reach = size // 2
    pool = pool_places(side)
    places = token_places(grids, small).astype(BF16)
    x = patches.reshape(rows, chans)
    mixer_1 = first_mixer.reshape(9 * chans, total)
    mixer_2 = second_mixer.reshape(9 * chans, total)
    vectors = [v.reshape(1, chans) for v in (first_gain, first_shift, second_gain, second_shift)]

    def boxes(r, c):
        return V((2, 2, reach, r, c), BF16)

    image_1 = V((grids, side + 2, side + 16, chans), F32)
    image_2 = V((grids, small + 2, ROW_PAD + 16, chans), F32)
    held = ((4, size, chans, total // 4), BF16)
    x_full = ((size, rows, chans), BF16)
    taps_1 = ((size, share, 9 * chans), BF16)
    x_small = ((size, few, total), BF16)
    taps_2 = ((size, few, 9 * chans), BF16)
    mixer = ((9 * chans, total), BF16)
    outs = [
        (S(*x_full), away),
        (S((rows, chans), F32), near),
        (S(*taps_1), away),
        (S((share, total), F32), near),
        (S((share, 128), F32), near),
        (S((few, total), BF16), near),
        (S(*held), away),
        (S((size, 16, chans), F32), near),
        (S(*x_small), away),
        (S((few_rows, chans), F32), near),
        (S(*taps_2), away),
        (S((few, total), F32), near),
        (S((few, 128), F32), near),
        (S((few, total), BF16), near),
        (S(*held), away),
        (S((few, total), F32), near),
        (S((token_rows, part), BF16), near),
        (S((part // 2, wide), BF16), away),
        (S((total // 2, part), BF16), away),
    ]
    scratch = [
        V(*x_full),
        V(*mixer),
        V(*taps_1),
        image_1,
        boxes(share, total),
        V((2, share, total), F32),
        V((share, total), F32),
        V(*held),
        V(*held),
        V((16, chans), F32),
        V((few, total), F32),
        V((2, few, total), BF16),
        V(*x_small),
        V((total, chans), BF16),
        V(*mixer),
        V(*taps_2),
        image_2,
        boxes(few, total),
        boxes(few, total),
        V((2, few, total), F32),
        V((size, few, total), BF16),
        V((size, token_rows, part), BF16),
        V((total, part), BF16),
        V((part, wide), BF16),
        V((token_rows, part), F32),
        V((token_rows, part), BF16),
        V((token_rows, part), F32),
        V((few_rows, part), BF16),
        V((part, wide), BF16),
        V((total, part), BF16),
        V((part // 2, wide), BF16),
        V((total // 2, part), BF16),
        DMA((10, 2, reach, 2)),
        DMA((10, 2, reach, 2)),
        DMA((2, 3)),
        DMA((2, 3)),
        DMA((2,)),
        DMA((2,)),
        DMA((6,)),
        DMA((8,)),
    ]
    (
        x_full_k, pre_1, taps_1_k, normed_1, inv_1, branch_sum, held_1_k, vec_full,
        x_small_k, pre_2, taps_2_k, normed_2, inv_2, branch_2, held_2_k, grad_rows, act, out_half, in_half,
    ) = kernel_call(
        functools.partial(forward_kernel, size, grids, side),
        "forward",
        1,
        [near] * 10 + [scalar] + [away] * 6,
        [shape for shape, _ in outs],
        [spec for _, spec in outs],
        scratch,
    )(
        x, first_reduce, first_expand, second_expand, *vectors, pool, places, live_counts,
        mixer_1, second_reduce, mixer_2, readout_in, readout_out, cotangent,
    )

    sums = [
        ((part, wide), True),
        ((total, part), True),
        ((9 * chans, total), False),
        ((total, chans), True),
        ((chans, total), False),
        ((9 * chans, total), False),
        ((total, chans), True),
        ((chans, total), False),
    ]
    outs = [
        (S((rows, chans), F32), near),
        (S((token_rows, part), BF16), near),
        (S((8, chans), F32), near),
    ]
    outs += [(S(shape, BF16), away) for shape, _ in sums]

    def half(shape, by_rows):
        return (shape[0] // 2, shape[1]) if by_rows else (shape[0], shape[1] // 2)

    scratch = [
        V(*held),
        V(*x_full),
        V(*taps_1),
        V(*x_small),
        V(*taps_2),
        V(*mixer),
        V((part, wide), BF16),
    ]
    for shape, by_rows in sums[:2]:
        scratch += [V(half(shape, by_rows), BF16)] * 2
    for shape, by_rows in sums[2:]:
        scratch += [V(shape, BF16)] + [V(half(shape, by_rows), BF16)] * 2
    scratch += [
        image_1,
        image_2,
        V((share, 9 * chans), F32),
        V((few, 9 * chans), F32),
        V((few, total), BF16),
        V((few, total), BF16),
        V((few, total), BF16),
        V((share, total), BF16),
        V((size, few, total), BF16),
        V((size, share, total), BF16),
        V((size, few, total), BF16),
        V((size, few, total), BF16),
        V((size, few, chans), BF16),
        V((size, few, chans), BF16),
        V((few_rows, chans), BF16),
        V((rows, chans), BF16),
        V((share, total), F32),
        V((rows, chans), F32),
        boxes(rows, chans),
        V((2, rows, chans), F32),
        boxes(few, total),
        V((2, few, total), F32),
        V((8, total), F32),
        V((size, 8, chans), F32),
        V((4, 8, chans), F32),
        DMA((7, 2, reach, 2)),
        DMA((7, 2, reach, 2)),
        DMA((3, size - 1)),
        DMA((3, size - 1)),
        DMA((8, 3)),
        DMA((8, 3)),
        DMA((8,)),
        DMA((2,)),
        DMA((2,)),
        DMA((11,)),
    ]
    patch_grads, tokens, vec_sum, *grads = kernel_call(
        functools.partial(backward_kernel, size, grids, side),
        "backward",
        2,
        [near] * 12 + [scalar] + [near] * 2 + [away] * 11,
        [shape for shape, _ in outs],
        [spec for _, spec in outs],
        scratch,
    )(
        grad_rows, normed_2, inv_2, vec_full, branch_2, normed_1, inv_1, branch_sum, pre_2, pre_1,
        np.ascontiguousarray(4.0 * pool.T), act, live_counts, first_reduce, second_reduce,
        held_1_k, held_2_k, x_full_k, taps_1_k, x_small_k, taps_2_k, mixer_1, mixer_2, readout_out,
        out_half, in_half,
    )
    tall = [(rows, chans, F32)] + [shape + (BF16,) for shape, _ in sums]
    blocks = [pl.BlockSpec((r // size, c), lambda k: (k, 0)) for r, c, _ in tall]
    blocks += [pl.BlockSpec(tokens.shape, lambda k: (0, 0)), pl.BlockSpec(vec_sum.shape, lambda k: (0, 0))]
    one = pl.BlockSpec((1, chans), lambda k: (0, 0))
    (
        patch_grads, out_g, in_g, mixer_2_g, reduce_2_g, expand_2_g, mixer_1_g, reduce_1_g, expand_1_g, tokens,
        gain_1_g, shift_1_g, gain_2_g, shift_2_g,
    ) = pl.pallas_call(
        widen_kernel,
        name="widen",
        grid=(size,),
        in_specs=blocks,
        out_shape=[S((r, c), F32) for r, c, _ in tall] + [S(tokens.shape, BF16)] + [S((1, chans), F32)] * 4,
        out_specs=blocks[:-1] + [one] * 4,
        compiler_params=pltpu.CompilerParams(vmem_limit_bytes=VMEM_LIMIT),
    )(patch_grads, *grads, tokens, vec_sum)
    return (
        tokens,
        patch_grads.reshape(patches.shape),
        reduce_1_g,
        mixer_1_g.reshape(first_mixer.shape),
        expand_1_g,
        gain_1_g.reshape(chans),
        shift_1_g.reshape(chans),
        reduce_2_g,
        mixer_2_g.reshape(second_mixer.shape),
        expand_2_g,
        gain_2_g.reshape(chans),
        shift_2_g.reshape(chans),
        in_g,
        out_g,
    )


def fits(mesh, patches, first_reduce, readout_in):
    size, groups = mesh.shape["mp"], mesh.shape["dp"]
    grids, side, _, chans = patches.shape
    return (
        groups == 4
        and size % 2 == 0
        and chans % 128 == 0
        and readout_in.shape[1] % 128 == 0
        and grids * side == 6 * size
        and side % 8 == 0
        and side // 2 <= ROW_PAD
    )


def solution(mesh):
    in_specs = (
        P("dp", None, None, "mp"),
        P(None, "mp"),
        P(None, None, "mp", None),
        P("mp", None),
        P("mp"),
        P("mp"),
        P(None, "mp"),
        P(None, None, "mp", None),
        P("mp", None),
        P("mp"),
        P("mp"),
        P(None, "mp"),
        P("mp", None),
        P("dp", "mp"),
        P("dp"),
    )
    out_specs = (
        P("dp", "mp"),
        P("dp", None, None, "mp"),
        P(None, "mp"),
        P(None, None, "mp", None),
        P("mp", None),
        P("mp"),
        P("mp"),
        P(None, "mp"),
        P(None, None, "mp", None),
        P("mp", None),
        P("mp"),
        P("mp"),
        P(None, "mp"),
        P("mp", None),
    )

    def local(*args):
        if fits(mesh, args[0], args[1], args[11]):
            return fast_body(mesh.shape["mp"], *args)
        return body(*args)

    return jax.shard_map(local, mesh=mesh, in_specs=in_specs, out_specs=out_specs, check_vma=False)
```

```python
import functools

import jax
import jax.numpy as jnp
import numpy as np
from jax import lax
from jax.experimental import pallas as pl
from jax.experimental.pallas import tpu as pltpu
from jax.sharding import PartitionSpec as P

norm_eps = 1e-06


def conv_same(image, kernel):
    return lax.conv_general_dilated(
        image,
        kernel,
        (1, 1),
        "SAME",
        dimension_numbers=("NHWC", "HWIO", "NHWC"),
        preferred_element_type=jnp.float32,
    )


def silu_back(values, grad_values):
    return jax.vjp(jax.nn.silu, values)[1](grad_values)[0]


def gelu_exact(values):
    return jax.nn.gelu(values, approximate=False)


def gelu_back(values, grad_values):
    return jax.vjp(gelu_exact, values)[1](grad_values)[0]


def block_forward(inputs, reduce_w, mixer_w, expand_w, gain, shift):
    num_grids, grid_height, grid_width, local_chans = inputs.shape
    pixel_rows = num_grids * grid_height * grid_width
    low_in = inputs.astype(jnp.bfloat16).reshape(pixel_rows, local_chans)
    full_in = lax.all_gather(low_in, "mp", axis=1, tiled=True)
    total_chans = full_in.shape[1]
    pre_act = jnp.dot(full_in, reduce_w, preferred_element_type=jnp.float32)
    hidden = jax.nn.silu(pre_act).astype(jnp.bfloat16)
    partial_mix = conv_same(
        hidden.reshape(num_grids, grid_height, grid_width, local_chans), mixer_w
    )
    mixed_sum = lax.psum_scatter(
        partial_mix.reshape(pixel_rows, total_chans).astype(jnp.bfloat16),
        "mp",
        scatter_dimension=1,
        tiled=True,
    ).astype(jnp.float32)
    row_total, row_squares = lax.psum(
        (jnp.sum(mixed_sum, axis=1), jnp.sum(mixed_sum * mixed_sum, axis=1)), "mp"
    )
    center = row_total / total_chans
    inv_std = lax.rsqrt(row_squares / total_chans - center * center + norm_eps)
    normed = (mixed_sum - center[:, None]) * inv_std[:, None]
    affine = normed * gain + shift
    branch_in = jax.nn.silu(affine).astype(jnp.bfloat16)
    partial_out = jnp.dot(branch_in, expand_w, preferred_element_type=jnp.float32)
    branch_out = lax.psum_scatter(
        partial_out.astype(jnp.bfloat16), "mp", scatter_dimension=1, tiled=True
    ).astype(jnp.float32)
    outputs = inputs + branch_out.reshape(inputs.shape)
    return (outputs, (full_in, pre_act, hidden, normed, inv_std, affine, branch_in))


def block_backward(grad_out, saved, reduce_w, mixer_w, expand_w, gain):
    full_in, pre_act, hidden, normed, inv_std, affine, branch_in = saved
    num_grids, grid_height, grid_width, local_chans = grad_out.shape
    pixel_rows = num_grids * grid_height * grid_width
    grad_rows = grad_out.reshape(pixel_rows, local_chans)
    grad_branch = lax.all_gather(grad_rows.astype(jnp.bfloat16), "mp", axis=1, tiled=True)
    total_chans = grad_branch.shape[1]
    expand_grad = jnp.einsum(
        "ri,ro->io", branch_in, grad_branch, preferred_element_type=jnp.float32
    )
    grad_act = jnp.einsum("ro,io->ri", grad_branch, expand_w, preferred_element_type=jnp.float32)
    grad_affine = silu_back(affine, grad_act)
    gain_grad = jnp.sum(grad_affine * normed, axis=0)
    shift_grad = jnp.sum(grad_affine, axis=0)
    scaled = grad_affine * gain
    sum_plain, sum_normed = lax.psum(
        (jnp.sum(scaled, axis=1), jnp.sum(scaled * normed, axis=1)), "mp"
    )
    grad_mixed = inv_std[:, None] * (
        scaled - sum_plain[:, None] / total_chans - normed * sum_normed[:, None] / total_chans
    )
    mixed_full = lax.all_gather(grad_mixed.astype(jnp.bfloat16), "mp", axis=1, tiled=True)
    mixed_image = mixed_full.reshape(num_grids, grid_height, grid_width, total_chans)
    flipped = jnp.transpose(mixer_w[::-1, ::-1], (0, 1, 3, 2))
    grad_hidden = conv_same(mixed_image, flipped).reshape(pixel_rows, local_chans)
    padded = jnp.pad(
        hidden.reshape(num_grids, grid_height, grid_width, local_chans),
        ((0, 0), (1, 1), (1, 1), (0, 0)),
    )
    mixer_grad = jnp.stack(
        [
            jnp.stack(
                [
                    jnp.einsum(
                        "nhwi,nhwo->io",
                        padded[
                            :,
                            offset_h : offset_h + grid_height,
                            offset_w : offset_w + grid_width,
                            :,
                        ],
                        mixed_image,
                        preferred_element_type=jnp.float32,
                    )
                    for offset_w in range(3)
                ]
            )
            for offset_h in range(3)
        ]
    )
    grad_pre = silu_back(pre_act, grad_hidden).astype(jnp.bfloat16)
    reduce_grad = jnp.einsum("ri,ro->io", full_in, grad_pre, preferred_element_type=jnp.float32)
    partial_in = jnp.einsum("ro,io->ri", grad_pre, reduce_w, preferred_element_type=jnp.float32)
    grad_in = (
        lax.psum_scatter(
            partial_in.astype(jnp.bfloat16), "mp", scatter_dimension=1, tiled=True
        ).astype(jnp.float32)
        + grad_rows
    )
    return (
        grad_in.reshape(grad_out.shape),
        (reduce_grad, mixer_grad, expand_grad, gain_grad, shift_grad),
    )


def body(
    patches,
    first_reduce,
    first_mixer,
    first_expand,
    first_gain,
    first_shift,
    second_reduce,
    second_mixer,
    second_expand,
    second_gain,
    second_shift,
    readout_in,
    readout_out,
    cotangent,
    live_counts,
):
    num_grids, grid_height, grid_width, local_chans = patches.shape
    pooled_side = grid_height // 2
    patch_values = patches.astype(jnp.float32)
    first_out = block_forward(
        patch_values, first_reduce, first_mixer, first_expand, first_gain, first_shift
    )[0]
    pooled = first_out.reshape(num_grids, pooled_side, 2, pooled_side, 2, local_chans).mean(
        axis=(2, 4)
    )
    second_out = block_forward(
        pooled, second_reduce, second_mixer, second_expand, second_gain, second_shift
    )[0]
    token_count = num_grids * pooled_side * pooled_side
    flat = second_out.astype(jnp.bfloat16).reshape(token_count, local_chans)
    flat_full = lax.all_gather(flat, "mp", axis=1, tiled=True)
    lifted = jnp.dot(flat_full, readout_in, preferred_element_type=jnp.float32)
    activated = gelu_exact(lifted).astype(jnp.bfloat16)
    partial_tokens = jnp.dot(activated, readout_out, preferred_element_type=jnp.float32)
    summed = lax.psum_scatter(
        partial_tokens.astype(jnp.bfloat16), "mp", scatter_dimension=1, tiled=True
    ).astype(jnp.float32)
    live_slots = (jnp.arange(num_grids) < live_counts[0]).astype(jnp.float32)
    live_rows = jnp.repeat(live_slots, pooled_side * pooled_side)
    tokens = (summed * live_rows[:, None]).astype(jnp.bfloat16)
    grad_tokens = cotangent * live_rows[:, None].astype(jnp.bfloat16)
    grad_full = lax.all_gather(grad_tokens, "mp", axis=1, tiled=True)
    readout_out_grad = jnp.einsum(
        "ri,ro->io", activated, grad_full, preferred_element_type=jnp.float32
    )
    grad_act = jnp.einsum("ro,io->ri", grad_full, readout_out, preferred_element_type=jnp.float32)
    grad_lift = gelu_back(lifted, grad_act).astype(jnp.bfloat16)
    readout_in_grad = jnp.einsum(
        "ri,ro->io", flat_full, grad_lift, preferred_element_type=jnp.float32
    )
    partial_flat = jnp.einsum(
        "ro,io->ri", grad_lift, readout_in, preferred_element_type=jnp.float32
    )
    grad_flat = lax.psum_scatter(
        partial_flat.astype(jnp.bfloat16), "mp", scatter_dimension=1, tiled=True
    ).astype(jnp.float32)
    second_saved = block_forward(
        pooled, second_reduce, second_mixer, second_expand, second_gain, second_shift
    )[1]
    grad_pooled, second_grads = block_backward(
        grad_flat.reshape(num_grids, pooled_side, pooled_side, local_chans),
        second_saved,
        second_reduce,
        second_mixer,
        second_expand,
        second_gain,
    )
    spread_back = jnp.broadcast_to(
        0.25 * grad_pooled[:, :, None, :, None, :],
        (num_grids, pooled_side, 2, pooled_side, 2, local_chans),
    ).reshape(patches.shape)
    first_saved = block_forward(
        patch_values, first_reduce, first_mixer, first_expand, first_gain, first_shift
    )[1]
    patch_grads, first_grads = block_backward(
        spread_back, first_saved, first_reduce, first_mixer, first_expand, first_gain
    )
    summed_grads = (
        lax.psum(first_grads[0].astype(jnp.bfloat16), "dp").astype(jnp.float32),
        lax.psum(first_grads[1].astype(jnp.bfloat16), "dp").astype(jnp.float32),
        lax.psum(first_grads[2].astype(jnp.bfloat16), "dp").astype(jnp.float32),
        lax.psum(first_grads[3].astype(jnp.bfloat16), "dp").astype(jnp.float32),
        lax.psum(first_grads[4].astype(jnp.bfloat16), "dp").astype(jnp.float32),
        lax.psum(second_grads[0].astype(jnp.bfloat16), "dp").astype(jnp.float32),
        lax.psum(second_grads[1].astype(jnp.bfloat16), "dp").astype(jnp.float32),
        lax.psum(second_grads[2].astype(jnp.bfloat16), "dp").astype(jnp.float32),
        lax.psum(second_grads[3].astype(jnp.bfloat16), "dp").astype(jnp.float32),
        lax.psum(second_grads[4].astype(jnp.bfloat16), "dp").astype(jnp.float32),
        lax.psum(readout_in_grad.astype(jnp.bfloat16), "dp").astype(jnp.float32),
        lax.psum(readout_out_grad.astype(jnp.bfloat16), "dp").astype(jnp.float32),
    )
    return (
        tokens,
        patch_grads,
        summed_grads[0],
        summed_grads[1],
        summed_grads[2],
        summed_grads[3],
        summed_grads[4],
        summed_grads[5],
        summed_grads[6],
        summed_grads[7],
        summed_grads[8],
        summed_grads[9],
        summed_grads[10],
        summed_grads[11],
    )


MESH = pl.DeviceIdType.MESH
F32 = jnp.float32
BF16 = jnp.bfloat16
DMA = pltpu.SemaphoreType.DMA
VMEM_LIMIT = 60 * 2**20
ROW_PAD = 16


def dot_nn(a, b):
    return lax.dot_general(a, b, (((1,), (0,)), ((), ())), preferred_element_type=F32)


def dot_nt(a, b):
    return lax.dot_general(a, b, (((1,), (1,)), ((), ())), preferred_element_type=F32)


def dot_tn(a, b):
    return lax.dot_general(a, b, (((0,), (0,)), ((), ())), preferred_element_type=F32)


def dot_full(a, b):
    return lax.dot_general(
        a,
        b,
        (((1,), (0,)), ((), ())),
        precision=lax.Precision.HIGHEST,
        preferred_element_type=F32,
    )


def sigmoid(values):
    return 1.0 / (1.0 + jnp.exp(-values))


def silu(values):
    return values * sigmoid(values)


def silu_slope(values):
    gate = sigmoid(values)
    return gate * (1.0 + values * (1.0 - gate))


class Ring:
    def __init__(self, size):
        self.size = size
        self.reach = size // 2
        self.me = lax.axis_index("mp")
        half = self.me // 2
        self.spot = jnp.where(self.me % 2 == 0, half, size - 1 - half)
        self.right = self.index(self.spot + 1)
        self.left = self.index(self.spot - 1)

    def wrap(self, spot):
        return lax.rem(spot + 2 * self.size, self.size)

    def index(self, spot):
        spot = self.wrap(spot)
        return jnp.where(spot < self.reach, 2 * spot, 2 * (self.size - 1 - spot) + 1)

    def greet(self):
        barrier = pltpu.get_barrier_semaphore()
        for peer in (self.left, self.right):
            pl.semaphore_signal(barrier, inc=1, device_id={"mp": peer}, device_id_type=MESH)
        pl.semaphore_wait(barrier, 2)

    def copy(self, side, src, dst, send, recv):
        peer = self.right if side == 0 else self.left
        return pltpu.make_async_remote_copy(
            src_ref=src,
            dst_ref=dst,
            send_sem=send,
            recv_sem=recv,
            device_id={"mp": peer},
            device_id_type=MESH,
        )


def wait_bytes(like, sem):
    pltpu.make_async_copy(like, like, sem).wait()


class Gather:
    def __init__(self, ring, own, held, slot, lanes, send, recv):
        self.ring, self.own, self.held, self.slot = ring, own, held, slot
        self.lanes, self.send, self.recv, self.copies = lanes, send, recv, {}

    def _start(self, side, step, lane):
        ring = self.ring
        if step == ring.reach and lane != side:
            return
        away = step - 1
        spot = ring.wrap(ring.spot - away if side == 0 else ring.spot + away)
        dst = self.held.at[self.slot(spot)]
        src = self.own if step == 1 else dst
        at = self.lanes[lane]
        copy = ring.copy(
            side, src.at[at], dst.at[at], self.send, self.recv.at[side, step - 1, lane]
        )
        copy.start()
        self.copies[side, step, lane] = copy

    def start(self):
        for lane in range(2):
            for side in range(2):
                self._start(side, 1, lane)

    def move(self, step):
        for lane in range(2):
            for side in range(2):
                if (side, step, lane) in self.copies:
                    self.copies[side, step, lane].wait_recv()
                    if step < self.ring.reach:
                        self._start(side, step + 1, lane)

    def drain(self):
        wait_bytes(self.held.at[pl.ds(0, self.ring.size - 1)], self.send)

    def spots(self, step):
        ring = self.ring
        if step == ring.reach:
            return [ring.wrap(ring.spot + step)]
        return [ring.wrap(ring.spot - step), ring.wrap(ring.spot + step)]


class Scatter:
    def __init__(self, ring, term, boxes, terms, lanes, send, recv):
        self.ring, self.term, self.out, self.inbox = ring, term, boxes[0], boxes[1]
        self.terms, self.lanes, self.send, self.recv, self.copies = terms, lanes, send, recv, {}

    def place(self, side, step):
        return side * self.ring.reach + step - 1

    def _start(self, side, step, lane):
        at, place = self.lanes[lane], self.place(side, step)
        src, dst = self.out.at[place], self.inbox.at[place]
        copy = self.ring.copy(
            side, src.at[at], dst.at[at], self.send, self.recv.at[side, step - 1, lane]
        )
        copy.start()
        self.copies[side, step, lane] = copy

    def start(self):
        ring = self.ring
        value = self.term(ring.wrap(ring.spot + ring.reach))
        self.terms[0] = value
        for side in range(2):
            at = self.lanes[side]
            self.out[(self.place(side, 1),) + at] = self.terms[(0,) + at].astype(BF16)
            self._start(side, 1, side)

    def prepare(self, step):
        ring = self.ring
        away = ring.reach + 1 - step
        self.terms[0] = self.term(ring.wrap(ring.spot + away))
        if away > 0:
            self.terms[1] = self.term(ring.wrap(ring.spot - away))
        if step == 2:
            for side in range(2):
                at = self.lanes[1 - side]
                self.out[(self.place(side, 2),) + at] = self.terms[(side,) + at].astype(BF16)
                self._start(side, 2, 1 - side)

    def _pass(self, side, step, lane):
        at = self.lanes[lane]
        self.copies[side, step - 1, lane].wait_recv()
        got = self.inbox[(self.place(side, step - 1),) + at].astype(F32)
        self.out[(self.place(side, step),) + at] = (self.terms[(side,) + at] + got).astype(BF16)
        self._start(side, step, lane)

    def step(self, step):
        if step > 2:
            for side in range(2):
                self._pass(side, step, 1 - side)
        for side in range(2):
            self._pass(side, step, side)

    def finish(self):
        reach = self.ring.reach
        for lane in range(2):
            for side in range(2):
                self.copies[side, reach, lane].wait_recv()
        return (
            self.terms[0]
            + self.inbox[self.place(0, reach)].astype(F32)
            + self.inbox[self.place(1, reach)].astype(F32)
        )

    def drain(self):
        wait_bytes(self.out.at[pl.ds(0, self.ring.size - 1)], self.send)


def row_halves(rows):
    return ((pl.ds(0, rows // 2),), (pl.ds(rows // 2, rows // 2),))


def column_halves(columns):
    every = slice(None)
    return (
        (every, pl.ds(0, columns // 2)),
        (every, pl.ds(columns // 2, columns // 2)),
    )


def pool_places(side):
    small = side // 2
    place = np.zeros((3 * ROW_PAD, 6 * side), np.float32)
    for row in range(6):
        for column in range(side):
            place[(row // 2) * ROW_PAD + column // 2, row * side + column] = 0.25
    assert small <= ROW_PAD
    return place


def token_places(grids, small):
    place = np.zeros((grids * small * small, grids * small * ROW_PAD), np.float32)
    for line in range(grids * small):
        for column in range(small):
            place[line * small + column, line * ROW_PAD + column] = 1.0
    return place


def norm_rows(mixed, gain, shift):
    center = jnp.mean(mixed, axis=1, keepdims=True)
    apart = mixed - center
    inv_std = lax.rsqrt(jnp.mean(apart * apart, axis=1, keepdims=True) + norm_eps)
    normed = apart * inv_std
    return normed, inv_std, normed * gain + shift


def wide_vector(held, row):
    return jnp.concatenate([held[m, row : row + 1, :] for m in range(held.shape[0])], axis=1)


def half_of(rows, columns, which, by_rows):
    if by_rows:
        return (pl.ds(pl.multiple_of(which * (rows // 2), 16), rows // 2), slice(None))
    return (slice(None), pl.ds(pl.multiple_of(which * (columns // 2), 128), columns // 2))


class Pair:
    def __init__(self):
        self.me = lax.axis_index("dp")
        self.core = lax.rem(self.me, 2)
        self.other = 1 - self.core
        self.twin = self.me - self.core + self.other
        self.far = lax.rem(self.me + 2, 4)
        self.across = lax.rem(self.twin + 2, 4)

    def copy(self, peer, src, dst, send, recv):
        return pltpu.make_async_remote_copy(
            src_ref=src,
            dst_ref=dst,
            send_sem=send,
            recv_sem=recv,
            device_id={"dp": peer},
            device_id_type=MESH,
        )


def greet_ring_and_pair(ring, pair):
    barrier = pltpu.get_barrier_semaphore()
    for peer in (ring.left, ring.right):
        pl.semaphore_signal(barrier, inc=1, device_id={"mp": peer}, device_id_type=MESH)
    for peer in (pair.twin, pair.far, pair.across):
        pl.semaphore_signal(barrier, inc=1, device_id={"dp": peer}, device_id_type=MESH)
    pl.semaphore_wait(barrier, 5)


class Share:
    def __init__(self, ring, pair, blocks, held, send, recv, twin_send, local):
        self.ring, self.pair, self.blocks, self.held = ring, pair, blocks, held
        self.send, self.recv, self.twin_send, self.local = send, recv, twin_send, local
        self.copies = []

    def go(self, spot):
        pair, half = self.pair, self.ring.size // 2
        m = self.ring.index(spot)
        same = m // half == pair.core
        j = lax.rem(m, half)
        src, dst = self.blocks.at[m], self.held.at[j, pair.me]
        peer = jnp.where(same, pair.far, pair.across)
        sem = self.recv.at[jnp.where(same, 0, 1), j]
        copy = pair.copy(peer, src, dst, self.send.at[len(self.copies)], sem)
        copy.start()
        self.copies.append(copy)

        @pl.when(same)
        def _():
            pltpu.make_async_copy(src, dst, self.local.at[j]).start()

        @pl.when(jnp.logical_not(same))
        def _():
            pair.copy(pair.twin, src, dst, self.twin_send.at[j], self.recv.at[2, j]).start()

    def drain(self):
        pair = self.pair
        for copy in self.copies:
            copy.wait_send()
        for j in range(self.ring.size // 2):
            src, dst = self.blocks.at[j], self.held.at[j, pair.me]
            pltpu.make_async_copy(src, dst, self.local.at[j]).wait()
            pair.copy(pair.twin, src, dst, self.twin_send.at[j], self.recv.at[2, j]).wait()
            for kind, peer in enumerate((pair.far, pair.across)):
                dst = self.held.at[j, peer]
                pair.copy(peer, src, dst, self.send.at[0], self.recv.at[kind, j]).wait_recv()


class Expand:
    def __init__(self, ring, pair, own, held, send, recv, psend, precv, load):
        self.ring, self.pair, self.held = ring, pair, held
        self.psend, self.precv, self.copies = psend, precv, []
        chans, quarter = held.shape[2:]
        columns = own.at[:, pl.ds(pl.multiple_of(pair.me * quarter, 128), quarter)]
        self.load = pltpu.make_async_copy(columns, held.at[pair.me, ring.me], load)
        self.load.start()
        self.gather = Gather(
            ring, held.at[pair.me, ring.me], held.at[pair.me], ring.index, row_halves(chans), send, recv
        )

    def across(self):
        self.gather.move(self.ring.reach)
        self._swap(0, self.pair.far, self.pair.me)

    def between(self):
        self.copies[0].wait_recv()
        self._swap(1, self.pair.twin, self.pair.me)
        self._swap(2, self.pair.twin, self.pair.far)

    def _swap(self, k, peer, quarter):
        at = self.held.at[quarter]
        copy = self.pair.copy(peer, at, at, self.psend.at[k], self.precv.at[k])
        copy.start()
        self.copies.append(copy)

    def ready(self):
        for copy in self.copies[1:]:
            copy.wait_recv()

    def drain(self):
        self.gather.drain()
        for copy in self.copies:
            copy.wait_send()


def times_expand(rows, held):
    parts = []
    for k in range(held.shape[0]):
        weight = held[k].reshape(rows.shape[1], held.shape[3])
        parts.append(dot_nn(rows, weight))
    return jnp.concatenate(parts, axis=1)


def times_expand_back(rows, held):
    quarter = held.shape[3]
    total = None
    for k in range(held.shape[0]):
        weight = held[k].reshape(held.shape[1] * held.shape[2], quarter)
        part = dot_nt(rows[:, k * quarter : (k + 1) * quarter], weight)
        total = part if total is None else total + part
    return total


def chunk_taps(image, taps, spot, lines, side, width):
    chans = image.shape[-1]
    per_grid = side // lines
    grid, line = spot // per_grid, lax.rem(spot, per_grid) * lines
    for kh in range(3):
        for kw in range(3):
            piece = image[grid, pl.ds(line + kh, lines), 7 + kw : 7 + kw + width, :]
            at = (kh * 3 + kw) * chans
            taps[spot, :, at : at + chans] = piece.reshape(lines * width, chans).astype(BF16)


def chunk_back(image, product, spot, lines, side, width):
    chans = image.shape[-1]
    per_grid = side // lines
    grid, line = spot // per_grid, lax.rem(spot, per_grid) * lines
    for kh in range(3):
        for kw in range(3):
            at = (kh * 3 + kw) * chans
            piece = product[:, at : at + chans].reshape(lines, width, chans)
            image[grid, pl.ds(line + kh, lines), 7 + kw : 7 + kw + width, :] += piece


def all_terms(terms, value):
    terms[...] = value.reshape(terms.shape)


def forward_kernel(
    size, grids, side,
    gain_1, shift_1, gain_2, shift_2, pool, places, counts,
    x, reduce_1_any, expand_1, expand_2, mixer_1_any, reduce_2_any, mixer_2_any, readout_in_any, readout_out_any, cotangent,
    x_full_out, pre_1_out, taps_1_out, normed_1_out, inv_1, branch_sum, held_1_out, vec_full,
    x_small_out, pre_2, taps_2_out, normed_2, inv_2, branch_2, held_2_out,
    grad_rows, act_out, cot_wide_out, in_half_out,
    x_full, reduce_1, pre_1, normed_1, act, terms_all, mixer_1, taps_1, image_1, boxes_1, terms_1, x_rows, held_1, held_2, vectors,
    pooled, low, x_small, reduce_2, mixer_2, taps_2, image_2, boxes_2, terms_2, flat_full, cot_full,
    readout_in, readout_out, lifted, grad_act, grad_lift, in_grad, in_core,
    send, recv, psend, precv, csend, crecv, ysend, yrecv, tsend, local, load, store,
):
    ring, pair = Ring(size), Pair()
    rows, chans = x.shape
    share = rows // size
    total = size * chans
    small = side // 2
    few = pooled.shape[0]
    part = readout_in.shape[1]
    tokens = cotangent.shape[0]
    wide = column_halves(total)
    near = lambda spot: spot
    loads = [
        pltpu.make_async_copy(src, dst, load.at[k])
        for k, (src, dst) in enumerate(
            [
                (mixer_1_any, mixer_1),
                (reduce_2_any, reduce_2),
                (mixer_2_any, mixer_2),
                (readout_in_any, readout_in),
                (readout_out_any, readout_out),
                (cotangent, cot_full.at[ring.me]),
                (x, x_full.at[ring.me]),
                (reduce_1_any, reduce_1),
            ]
        )
    ]
    stores = []

    def keep(src, dst):
        copy = pltpu.make_async_copy(src, dst, store.at[len(stores)])
        copy.start()
        stores.append(copy)

    for k in (6, 7):
        loads[k].start()
    e1 = Expand(
        ring, pair, expand_1, held_1, send.at[2], recv.at[2], psend.at[0], precv.at[0], load.at[8]
    )
    e2 = Expand(
        ring, pair, expand_2, held_2, send.at[3], recv.at[3], psend.at[1], precv.at[1], load.at[9]
    )
    greet_ring_and_pair(ring, pair)
    gx = Gather(ring, x, x_full, ring.index, row_halves(rows), send.at[0], recv.at[0])
    gx.start()
    for k in range(6):
        loads[k].start()
    for item in (e1, e2):
        item.load.wait()
        item.gather.start()
    for k, vector in enumerate((gain_1, shift_1, gain_2, shift_2)):
        for row in (k, k + 8):
            vectors[row : row + 1, :] = vector[...]
    for k in range(4, 8):
        for row in (k, k + 8):
            vectors[row : row + 1, :] = gain_1[...]
    vec_full[ring.me] = vectors[...]
    gv = Gather(ring, vectors, vec_full, ring.index, row_halves(16), send.at[1], recv.at[4])
    gv.start()

    def add(spot):
        m = ring.index(spot)
        weight = reduce_1[pl.ds(pl.multiple_of(m * chans, chans), chans), :]
        pre_1[...] += dot_nn(x_full[m], weight)

    loads[6].wait()
    loads[7].wait()
    own = reduce_1[pl.ds(pl.multiple_of(ring.me * chans, chans), chans), :]
    pre_1[...] = dot_nn(x_full[ring.me], own)
    image_1[...] = jnp.zeros(image_1.shape, F32)
    image_2[...] = jnp.zeros(image_2.shape, F32)
    for step in range(1, ring.reach + 1):
        gx.move(step)
        for spot in gx.spots(step):
            add(spot)
        if step < ring.reach:
            for item in (e1.gather, e2.gather, gv):
                item.move(step)
    keep(x_full, x_full_out)
    keep(pre_1, pre_1_out)
    hidden = silu(pre_1[...])
    image_1[:, 1 : 1 + side, 8 : 8 + side, :] = hidden.reshape(grids, side, side, chans)
    loads[0].wait()

    def mix_1(spot):
        chunk_taps(image_1, taps_1, spot, 6, side, side)
        return dot_nn(taps_1[spot], mixer_1[...])

    rs1 = Scatter(
        ring, mix_1, (boxes_1.at[0], boxes_1.at[1]), terms_1, wide, send.at[4], recv.at[1]
    )
    rs1.start()
    e1.across()
    gv.move(ring.reach)
    loads[5].wait()
    share_cot = Share(ring, pair, cot_full, cot_wide_out, ysend, yrecv, tsend, local)
    share_cot.go(ring.spot)
    for step in range(2, ring.reach + 1):
        rs1.prepare(step)
        rs1.step(step)
        if step == ring.reach - 1:
            e1.between()
            e2.across()
    rs1.prepare(ring.reach + 1)
    keep(taps_1, taps_1_out)
    mine = pl.ds(pl.multiple_of(ring.spot * share, 16), share)
    for m in range(size):
        x_rows[:, m * chans : (m + 1) * chans] = x_full[m, mine, :].astype(F32)
    gain_a, shift_a = wide_vector(vec_full, 0), wide_vector(vec_full, 1)
    mixed = rs1.finish()
    gc = Gather(
        ring, cot_full.at[ring.me], cot_full, ring.index, row_halves(tokens), send.at[5], recv.at[5]
    )
    gc.start()

    def move_cot(step):
        gc.move(step)
        for spot in gc.spots(step):
            share_cot.go(spot)

    value, inverse, affine = norm_rows(mixed, gain_a, shift_a)
    normed_1[...] = value
    keep(normed_1, normed_1_out)
    inv_1[...] = jnp.broadcast_to(inverse, inv_1.shape)
    branch = silu(affine).astype(BF16)
    e1.ready()
    keep(held_1, held_1_out)
    pooled[...] = dot_full(pool[...], x_rows[...] + times_expand(branch, held_1))
    low[0] = pooled[...].astype(BF16)
    x_small[ring.spot] = low[0]
    g2 = Gather(ring, low.at[0], x_small, near, wide, send.at[6], recv.at[0])
    g2.start()
    branch_sum[...] = (4.0 * dot_full(pool[...], branch.astype(F32))).astype(BF16)
    for step in range(1, ring.reach + 1):
        g2.move(step)
        if step == 1:
            move_cot(1)
    loads[1].wait()
    e2.between()
    pre_2[...] = dot_nn(x_small[...].reshape(size * few, total), reduce_2[...])
    keep(x_small, x_small_out)
    hidden = silu(pre_2[...])
    image_2[:, 1 : 1 + small, 8 : 8 + ROW_PAD, :] = hidden.reshape(grids, small, ROW_PAD, chans)
    loads[2].wait()

    def taps(spot, carry):
        chunk_taps(image_2, taps_2, spot, 3, small, ROW_PAD)
        return carry

    lax.fori_loop(0, size, taps, 0)
    all_terms(terms_all, dot_nn(taps_2[...].reshape(size * few, 9 * chans), mixer_2[...]))
    rs2 = Scatter(
        ring, terms_all.__getitem__, (boxes_2.at[0], boxes_2.at[1]), terms_2, wide, send.at[7], recv.at[1]
    )
    rs2.start()
    move_cot(2)
    for step in range(2, ring.reach + 1):
        rs2.prepare(step)
        rs2.step(step)
    rs2.prepare(ring.reach + 1)
    keep(taps_2, taps_2_out)
    gain_b, shift_b = wide_vector(vec_full, 2), wide_vector(vec_full, 3)
    mixed = rs2.finish()
    value, inverse, affine = norm_rows(mixed, gain_b, shift_b)
    normed_2[...] = value
    inv_2[...] = jnp.broadcast_to(inverse, inv_2.shape)
    branch_2[...] = silu(affine).astype(BF16)
    e2.ready()
    keep(held_2, held_2_out)
    low[1] = (pooled[...] + times_expand(branch_2[...], held_2)).astype(BF16)
    flat_full[ring.spot] = low[1]
    gf = Gather(ring, low.at[1], flat_full, near, wide, send.at[8], recv.at[0])
    gf.start()
    for step in range(1, ring.reach + 1):
        gf.move(step)
        if step == 1:
            move_cot(3)
    loads[3].wait()
    flat = dot_nn(places[...], flat_full[...].reshape(size * few, total)).astype(BF16)
    lifted[...] = dot_nn(flat, readout_in[...])
    cdf = 0.5 * (1.0 + lax.erf(lifted[...] * 0.7071067811865476))
    row_ids = lax.broadcasted_iota(jnp.int32, (tokens, 1), 0)
    live = (row_ids < counts[0] * (tokens // grids)).astype(F32)
    activated = (lifted[...] * cdf).astype(BF16)
    act[...] = activated
    keep(act, act_out)
    slope = cdf + lifted[...] * jnp.exp(-0.5 * lifted[...] * lifted[...]) * 0.3989422804014327
    lifted[...] = slope * live
    grad_act[...] = jnp.zeros(grad_act.shape, F32)
    loads[4].wait()
    move_cot(ring.reach)

    def back(m, carry):
        at = pl.ds(pl.multiple_of(m * part, 128), part)
        grad_act[...] += dot_nt(cot_full[m], readout_out[:, at])
        return carry

    lax.fori_loop(0, size, back, 0)
    lift = (grad_act[...] * lifted[...]).astype(BF16)
    grad_lift[...] = dot_tn(places[...], lift).astype(BF16)

    rs2.drain()
    all_terms(terms_all, dot_nt(grad_lift[...], readout_in[...]))
    rf = Scatter(
        ring, terms_all.__getitem__, (boxes_2.at[0], boxes_2.at[1]), terms_2, wide, send.at[9], recv.at[1]
    )
    rf.start()

    def swap(k, grad, box):
        half = half_of(*grad.shape, pair.other, True)
        copy = pair.copy(pair.twin, grad.at[half], box, csend.at[k], crecv.at[k])
        copy.start()
        return copy

    def add_half(copy, grad, box, result):
        copy.wait_recv()
        half = half_of(*grad.shape, pair.core, True)
        box[...] = (grad[half].astype(F32) + box[...].astype(F32)).astype(BF16)
        keep(box, result)

    in_grad[...] = dot_tn(flat, lift).astype(BF16)
    in_copy = swap(0, in_grad, in_core)
    for step in range(2, ring.reach + 1):
        rf.prepare(step)
        rf.step(step)
    rf.prepare(ring.reach + 1)
    grad_rows[...] = rf.finish()
    add_half(in_copy, in_grad, in_core, in_half_out)
    for item in (gx, gv, e1, e2, rs1, gc, g2, gf, rf):
        item.drain()
    in_copy.wait_send()
    share_cot.drain()
    for copy in stores:
        copy.wait()


def norm_back(grad_branch, normed, inv_std, gain, shift):
    affine = normed * gain + shift
    grad_affine = grad_branch * silu_slope(affine)
    gain_grad = jnp.sum(grad_affine * normed, axis=0, keepdims=True)
    shift_grad = jnp.sum(grad_affine, axis=0, keepdims=True)
    scaled = grad_affine * gain
    mean_plain = jnp.mean(scaled, axis=1, keepdims=True)
    mean_normed = jnp.mean(scaled * normed, axis=1, keepdims=True)
    return inv_std * (scaled - mean_plain - normed * mean_normed), gain_grad, shift_grad


class GroupSum:
    def __init__(self, pair, mine, other, from_core, from_far, result, half, send, recv, local):
        self.pair, self.mine, self.other = pair, mine, other
        self.from_core, self.from_far = from_core, from_far
        self.result = result.at[half]
        self.send, self.recv, self.local, self.copies = send, recv, local, []

    def _go(self, k, peer, src, dst):
        copy = self.pair.copy(peer, src, dst, self.send.at[k], self.recv.at[k])
        copy.start()
        self.copies.append(copy)

    def core(self):
        self._go(0, self.pair.twin, self.other, self.from_core)

    def far(self):
        if self.from_core is not None:
            self.copies[0].wait_recv()
            self.mine[...] = (self.mine[...].astype(F32) + self.from_core[...].astype(F32)).astype(
                BF16
            )
        self._go(1, self.pair.far, self.mine, self.from_far)

    def back(self):
        self.copies[-1].wait_recv()
        self.from_far[...] = (self.mine[...].astype(F32) + self.from_far[...].astype(F32)).astype(
            BF16
        )
        self._go(2, self.pair.twin, self.from_far, self.result)
        self.kept = pltpu.make_async_copy(self.from_far, self.result, self.local)
        self.kept.start()

    def done(self):
        self.copies[-1].wait_recv()
        self.kept.wait()
        for copy in self.copies:
            copy.wait_send()


def quarter_of(grad, which):
    columns = grad.shape[1] // 4
    return pl.ds(pl.multiple_of(which * columns, 128), columns)


class OutSum:
    def __init__(self, pair, act_all, cot_wide, grad, result, send, recv, local):
        self.pair, self.act_all, self.cot_wide, self.grad = pair, act_all, cot_wide, grad
        half = half_of(*result.shape, pair.core, False)
        self.result = result.at[half]
        self.send, self.recv, self.local = send, recv, local

    def spread(self, act_live):
        pair = self.pair
        self.act_all[pair.me] = act_live
        at = self.act_all.at[pair.me]
        self.copies = []
        for k, peer in enumerate((pair.far, pair.across, pair.twin)):
            copy = pair.copy(peer, at, at, self.send.at[k], self.recv.at[k])
            copy.start()
            self.copies.append(copy)

    def arrive(self):
        for copy in self.copies:
            copy.wait_recv()

    def block(self, j):
        groups, rows, part = self.act_all.shape
        left = self.act_all[...].reshape(groups * rows, part)
        right = self.cot_wide[j].reshape(groups * rows, part)
        self.grad[:, j * part : (j + 1) * part] = dot_tn(left, right).astype(BF16)

    def back(self):
        copy = self.pair.copy(
            self.pair.twin, self.grad, self.result, self.send.at[3], self.recv.at[3]
        )
        copy.start()
        self.copies.append(copy)
        self.kept = pltpu.make_async_copy(self.grad, self.result, self.local)
        self.kept.start()

    def done(self):
        self.copies[3].wait_recv()
        self.kept.wait()
        for copy in self.copies:
            copy.wait_send()


def send_columns(ring, src, held, slot, send, recv):
    chans = held.shape[-1]
    held[slot] = src[:, pl.ds(pl.multiple_of(ring.me * chans, chans), chans)]
    copies = []
    for away in range(1, ring.size):
        peer = lax.rem(ring.me + away, ring.size)
        copy = pltpu.make_async_remote_copy(
            src_ref=src.at[:, pl.ds(pl.multiple_of(peer * chans, chans), chans)],
            dst_ref=held.at[slot],
            send_sem=send.at[away - 1],
            recv_sem=recv.at[away - 1],
            device_id={"mp": peer},
            device_id_type=MESH,
        )
        copy.start()
        copies.append(copy)
    return copies


def backward_kernel(
    size, grids, side,
    grad_rows, normed_2, inv_2, vec_full, branch_2, inv_1, branch_sum, pre_2, spread, counts, reduce_2,
    normed_1_any, pre_1_any, act_any, reduce_1_any, held_1_any, held_2_any, x_full_any, taps_1_any, x_small_any, taps_2_any, mixer_1_any, mixer_2_any,
    readout_any, cot_wide_any, in_half_any,
    patch_grads, tokens, vec_sum, out_sum, in_sum, mixer_2_sum, reduce_2_sum, expand_2_sum,
    mixer_1_sum, reduce_1_sum, expand_1_sum,
    normed_1, pre_1, act, reduce_1, terms_all, held, x_full, taps_1, x_small, taps_2, mixer, readout,
    cot_wide, act_all, out_grad, in_mine, in_far,
    mixer_2_grad, mixer_2_core, mixer_2_far, reduce_2_grad, reduce_2_core, reduce_2_far,
    expand_2_grad, expand_2_core, expand_2_far,
    mixer_1_grad, mixer_1a_core, mixer_1a_far, mixer_1b_core, mixer_1b_far, reduce_1_grad, reduce_1_core, reduce_1_far,
    expand_1_grad, expand_1_core, expand_1_far,
    image_1, image_2, product_1, product_2, low_2, low_1, mix_2, mix_1, mix_2_full, mix_1_full,
    low_2_full, low_1_full, branch_2_full, branch_1_full, grad_pre_2, grad_pre_1, grad_out, wide_term,
    boxes_big, terms_big, boxes_small, terms_small, vec_grad, vec_held, vec_part,
    send, recv, all_send, all_recv, sum_send, sum_recv, sum_local, vec_send, vec_recv, act_send, act_recv, load,
):
    ring, pair = Ring(size), Pair()
    few, total = grad_rows.shape
    share = normed_1.shape[0]
    chans = total // size
    rows = size * share
    small = side // 2
    part = readout_any.shape[1] // size
    near = lambda spot: spot
    wide = column_halves(total)
    pairs = [
        (held_2_any, held),
        (mixer_2_any, mixer),
        (readout_any, readout),
        (cot_wide_any, cot_wide),
        (in_half_any, in_mine),
        (taps_2_any, taps_2),
        (x_small_any, x_small),
        (held_1_any, held),
        (mixer_1_any, mixer),
        (taps_1_any, taps_1),
        (x_full_any, x_full),
        (act_any, act),
        (normed_1_any, normed_1),
        (pre_1_any, pre_1),
        (reduce_1_any, reduce_1),
    ]
    loads = [
        pltpu.make_async_copy(src, dst, load.at[k]) for k, (src, dst) in enumerate(pairs)
    ]
    for k in (0, 1, 11, 4, 2, 5, 6, 12, 3, 13, 14, 9, 10):
        loads[k].start()
    barrier = pltpu.get_barrier_semaphore()
    for away in range(1, size):
        peer = lax.rem(ring.me + away, size)
        pl.semaphore_signal(barrier, inc=1, device_id={"mp": peer}, device_id_type=MESH)
    for peer in (pair.twin, pair.far, pair.across):
        pl.semaphore_signal(barrier, inc=1, device_id={"dp": peer}, device_id_type=MESH)
    pl.semaphore_wait(barrier, size + 2)

    def group_sum(k, mine, other, from_core, from_far, result, by_rows):
        half = half_of(*result.shape, pair.core, by_rows)
        return GroupSum(
            pair, mine, other, from_core, from_far, result, half, sum_send.at[k], sum_recv.at[k], sum_local.at[k]
        )

    def grad_sum(k, grad, from_core, from_far, result, by_rows):
        mine, other = (
            grad.at[half_of(*grad.shape, which, by_rows)] for which in (pair.core, pair.other)
        )
        return group_sum(k, mine, other, from_core, from_far, result, by_rows)

    def quarter_sum(k, which, grad, from_core, from_far, result):
        mine, other = (
            (slice(None), quarter_of(grad, 2 * core + which)) for core in (pair.core, pair.other)
        )
        return GroupSum(
            pair, grad.at[mine], grad.at[other], from_core, from_far, result, mine, sum_send.at[k], sum_recv.at[k],
            sum_local.at[k],
        )

    s_out = OutSum(pair, act_all, cot_wide, out_grad, out_sum, act_send, act_recv, sum_local.at[0])
    s_in = group_sum(1, in_mine, None, None, in_far, in_sum, True)
    s_m2 = grad_sum(2, mixer_2_grad, mixer_2_core, mixer_2_far, mixer_2_sum, False)
    s_r2 = grad_sum(3, reduce_2_grad, reduce_2_core, reduce_2_far, reduce_2_sum, True)
    s_e2 = grad_sum(4, expand_2_grad, expand_2_core, expand_2_far, expand_2_sum, False)
    s_m1a = quarter_sum(5, 0, mixer_1_grad, mixer_1a_core, mixer_1a_far, mixer_1_sum)
    s_m1b = quarter_sum(8, 1, mixer_1_grad, mixer_1b_core, mixer_1b_far, mixer_1_sum)
    s_r1 = grad_sum(6, reduce_1_grad, reduce_1_core, reduce_1_far, reduce_1_sum, True)
    s_e1 = grad_sum(7, expand_1_grad, expand_1_core, expand_1_far, expand_1_sum, False)
    low_2[...] = grad_rows[...].astype(BF16)
    loads[0].wait()
    gain_b, shift_b = wide_vector(vec_full, 2), wide_vector(vec_full, 3)
    grad_branch = times_expand_back(low_2[...], held)
    value, gain_grad, shift_grad = norm_back(
        grad_branch, normed_2[...], inv_2[:, 0:1], gain_b, shift_b
    )
    loads[7].start()
    mix_2[...] = value.astype(BF16)
    g_mix2 = Gather(ring, mix_2, mix_2_full, near, wide, send.at[0], recv.at[0])
    g_mix2.start()
    mix_2_full[ring.spot] = mix_2[...]
    vec_grad[...] = jnp.zeros(vec_grad.shape, F32)
    vec_grad[2:3, :] = gain_grad
    vec_grad[3:4, :] = shift_grad
    image_2[...] = jnp.zeros(image_2.shape, F32)
    image_1[...] = jnp.zeros(image_1.shape, F32)

    def token_term(spot):
        at = pl.ds(pl.multiple_of(ring.index(spot) * part, 128), part)
        value = dot_nn(act[...], readout[:, at])
        return jnp.concatenate(
            [value[:, k : k + chans] for k in range(0, part, chans)], axis=0
        )

    tall = row_halves(rows)
    big = (boxes_big.at[0], boxes_big.at[1])
    r_tok = Scatter(ring, token_term, big, terms_big, tall, send.at[1], recv.at[2])
    loads[4].wait()
    s_in.far()
    loads[11].wait()
    token_ids = lax.broadcasted_iota(jnp.int32, (act.shape[0], 1), 0)
    live = (token_ids < counts[0] * (act.shape[0] // grids)).astype(F32)
    s_out.spread((act[...].astype(F32) * live).astype(BF16))
    low_2_full[ring.spot] = low_2[...]
    g_low2 = Gather(ring, low_2, low_2_full, near, wide, send.at[4], recv.at[3])
    g_low2.start()
    a_low2 = send_columns(
        ring, branch_2, branch_2_full, ring.spot, all_send.at[0], all_recv.at[0]
    )

    def back_2(spot):
        product_2[...] = dot_nt(mix_2_full[spot], mixer[...])
        chunk_back(image_2, product_2, spot, 3, small, ROW_PAD)

    loads[1].wait()
    back_2(ring.spot)
    for step in range(1, ring.reach + 1):
        g_mix2.move(step)
        for spot in g_mix2.spots(step):
            back_2(spot)
        g_low2.move(step)
    loads[8].start()
    grad_hidden = image_2[:, 1 : 1 + small, 8 : 8 + ROW_PAD, :].reshape(pre_2.shape)
    grad_pre_2[...] = (grad_hidden * silu_slope(pre_2[...])).astype(BF16)

    all_terms(terms_all, dot_nt(grad_pre_2[...], reduce_2[...]))
    r_in2 = Scatter(
        ring, terms_all.__getitem__, (boxes_small.at[0], boxes_small.at[1]), terms_small, wide, send.at[2], recv.at[1]
    )
    r_in2.start()
    loads[2].wait()
    r_tok.start()

    def mixer_part(grad, taps, mix, columns, count):
        left = taps[...].reshape(size * count, 9 * chans)
        right = mix[:, :, columns].reshape(size * count, columns.size)
        grad[:, columns] = dot_tn(left, right).astype(BF16)

    for step in range(2, ring.reach + 1):
        r_in2.prepare(step)
        r_in2.step(step)
        if step == 2:
            r_tok.prepare(2)
        if step == 3:
            r_tok.step(2)
    r_in2.prepare(ring.reach + 1)
    r_tok.prepare(3)
    loads[7].wait()
    quarter = 0.25 * (r_in2.finish() + grad_rows[...])
    r_tok.step(3)
    loads[12].wait()
    low_1[...] = quarter.astype(BF16)
    gain_a, shift_a = wide_vector(vec_full, 0), wide_vector(vec_full, 1)
    grad_branch = dot_full(spread[...], times_expand_back(low_1[...], held))
    value, gain_grad, shift_grad = norm_back(
        grad_branch, normed_1[...], inv_1[:, 0:1], gain_a, shift_a
    )
    mix_1[...] = value.astype(BF16)
    g_mix1 = Gather(ring, mix_1, mix_1_full, near, wide, send.at[3], recv.at[0])
    g_mix1.start()
    mix_1_full[ring.spot] = mix_1[...]
    vec_grad[0:1, :] = gain_grad
    vec_grad[1:2, :] = shift_grad
    grad_out[...] = dot_full(spread[...], quarter)
    loads[5].wait()
    mixer_part(mixer_2_grad, taps_2, mix_2_full, half_of(*mixer_2_grad.shape, pair.other, False)[1], few)
    s_m2.core()
    loads[6].wait()

    def reduce_part(grad, full, grad_pre):
        grad[...] = dot_tn(full, grad_pre).astype(BF16)

    reduce_part(reduce_2_grad, x_small[...].reshape(size * few, total), grad_pre_2[...])
    s_r2.core()
    r_tok.prepare(4)

    def expand_part(grad, branches, lows):
        grad[...] = dot_tn(
            branches[...].reshape(size * few, chans), lows[...].reshape(size * few, total)
        ).astype(BF16)

    def back_1(spot):
        product_1[...] = dot_nt(mix_1_full[spot], mixer[...])
        chunk_back(image_1, product_1, spot, 6, side, side)

    loads[8].wait()
    back_1(ring.spot)
    low_1_full[ring.spot] = low_1[...]
    g_low1 = Gather(ring, low_1, low_1_full, near, wide, send.at[5], recv.at[4])
    for step in range(1, ring.reach + 1):
        g_mix1.move(step)
        if step == 1:
            r_tok.step(4)
            a_low1 = send_columns(
                ring, branch_sum, branch_1_full, ring.spot, all_send.at[1], all_recv.at[1]
            )
            a_vec = send_columns(
                ring, vec_grad, vec_held, ring.me, all_send.at[2], all_recv.at[2]
            )
            mixer_part(
                mixer_2_grad, taps_2, mix_2_full, half_of(*mixer_2_grad.shape, pair.core, False)[1], few
            )
            s_m2.far()
        if step == 2:
            r_tok.prepare(ring.reach + 1)
            value = r_tok.finish()
            r_tok.drain()
            count = rows * chans // part
            value = jnp.concatenate(
                [value[k * count : (k + 1) * count] for k in range(part // chans)], axis=1
            )
            row_ids = lax.broadcasted_iota(jnp.int32, (count, 1), 0)
            live = (row_ids < counts[0] * (count // grids)).astype(F32)
            tokens[...] = (value * live).astype(BF16)
            s_r2.far()
            g_low1.start()
        for spot in g_mix1.spots(step):
            back_1(spot)
        if step == 2:
            loads[3].wait()
            s_out.arrive()
            for copy in a_low2:
                copy.wait()
            expand_part(expand_2_grad, branch_2_full, low_2_full)
            s_e2.core()
            s_out.block(0)
            s_out.block(1)
        if step == 3:
            s_out.block(2)
            s_out.block(3)
            s_out.back()
            s_e2.far()

    def lows(step):
        g_low1.move(step)

    loads[13].wait()
    loads[14].wait()
    grad_hidden = image_1[:, 1 : 1 + side, 8 : 8 + side, :].reshape(pre_1.shape)
    grad_pre_1[...] = (grad_hidden * silu_slope(pre_1[...])).astype(BF16)
    mine = pl.ds(pl.multiple_of(ring.spot * share, 16), share)

    def in_term_1(spot):
        at = pl.ds(pl.multiple_of(ring.index(spot) * chans, chans), chans)
        wide_term[...] = dot_nt(grad_pre_1[...], reduce_1[at, :])
        wide_term[mine, :] += grad_out[:, at]
        return wide_term[...]

    r_in1 = Scatter(ring, in_term_1, big, terms_big, tall, send.at[6], recv.at[1])
    r_in1.start()
    loads[9].wait()
    mixer_part(mixer_1_grad, taps_1, mix_1_full, quarter_of(mixer_1_grad, 2 * pair.other), share)
    s_m1a.core()
    r_in1.prepare(2)
    mixer_part(mixer_1_grad, taps_1, mix_1_full, quarter_of(mixer_1_grad, 2 * pair.core), share)
    s_m1a.far()
    r_in1.step(2)
    mixer_part(mixer_1_grad, taps_1, mix_1_full, quarter_of(mixer_1_grad, 2 * pair.other + 1), share)
    s_m1b.core()
    lows(1)
    mixer_part(mixer_1_grad, taps_1, mix_1_full, quarter_of(mixer_1_grad, 2 * pair.core + 1), share)
    s_m1b.far()
    lows(2)
    loads[10].wait()

    def reduces(m, carry):
        at = pl.ds(pl.multiple_of(m * chans, chans), chans)
        reduce_1_grad[at, :] = dot_tn(x_full[m], grad_pre_1[...]).astype(BF16)
        return carry

    lax.fori_loop(0, size, reduces, 0)
    s_r1.core()
    r_in1.prepare(3)
    r_in1.step(3)
    lows(3)
    s_r1.far()
    for copy in a_vec:
        copy.wait()
    vec_part[0] = jnp.sum(vec_held[...], axis=0)
    v_core = pair.copy(pair.twin, vec_part.at[0], vec_part.at[1], vec_send.at[0], vec_recv.at[0])
    v_core.start()
    r_in1.prepare(4)
    r_in1.step(4)
    lows(4)
    for copy in a_low1:
        copy.wait()

    expand_part(expand_1_grad, branch_1_full, low_1_full)
    s_e1.core()
    v_core.wait()
    vec_part[2] = vec_part[0] + vec_part[1]
    v_far = pair.copy(pair.far, vec_part.at[2], vec_part.at[3], vec_send.at[1], vec_recv.at[1])
    v_far.start()
    r_in1.prepare(ring.reach + 1)
    s_in.back()
    s_e1.far()
    s_m2.back()
    s_r2.back()
    patch_grads[...] = r_in1.finish()
    v_far.wait()
    vec_sum[...] = vec_part[2] + vec_part[3]
    s_m1a.back()
    s_m1b.back()
    s_r1.back()
    s_e2.back()
    s_e1.back()
    for item in (s_out, s_in, s_m2, s_r2, s_e2, s_m1a, s_m1b, s_r1, s_e1):
        item.done()
    for item in (g_mix2, r_in2, g_mix1, g_low2, g_low1, r_in1):
        item.drain()


def widen_kernel(*refs):
    ins, outs = refs[:11], refs[11:]
    for src, dst in zip(ins[:10], outs[:10]):
        dst[...] = src[...].astype(dst.dtype)
    for k in range(4):
        outs[10 + k][...] = ins[10][k : k + 1, :]


def kernel_call(kernel, name, number, in_specs, outs, out_specs, scratch, flops=0):
    def run(*args):
        return pl.pallas_call(
            kernel,
            name=name,
            out_shape=outs,
            in_specs=in_specs,
            out_specs=out_specs,
            scratch_shapes=scratch,
            cost_estimate=pl.CostEstimate(flops=flops, bytes_accessed=0, transcendentals=0),
            compiler_params=pltpu.CompilerParams(
                collective_id=number, has_side_effects=True, vmem_limit_bytes=VMEM_LIMIT
            ),
        )(*args)

    return run


def fast_body(
    size,
    patches,
    first_reduce,
    first_mixer,
    first_expand,
    first_gain,
    first_shift,
    second_reduce,
    second_mixer,
    second_expand,
    second_gain,
    second_shift,
    readout_in,
    readout_out,
    cotangent,
    live_counts,
):
    S = jax.ShapeDtypeStruct
    V = pltpu.VMEM
    near = pl.BlockSpec(memory_space=pltpu.VMEM)
    scalar = pl.BlockSpec(memory_space=pltpu.SMEM)
    away = pl.BlockSpec(memory_space=pl.ANY)
    grids, side, _, chans = patches.shape
    total = first_expand.shape[1]
    rows = grids * side * side
    share = rows // size
    small = side // 2
    few = 3 * ROW_PAD
    few_rows = few * size
    token_rows = grids * small * small
    part = readout_in.shape[1]
    wide = readout_out.shape[1]
    reach = size // 2
    pool = pool_places(side)
    places = token_places(grids, small).astype(BF16)
    x = patches.reshape(rows, chans)
    mixer_1 = first_mixer.reshape(9 * chans, total)
    mixer_2 = second_mixer.reshape(9 * chans, total)
    vectors = [v.reshape(1, chans) for v in (first_gain, first_shift, second_gain, second_shift)]

    def boxes(r, c):
        return V((2, size, r, c), BF16)

    image_1 = V((grids, side + 2, side + 16, chans), F32)
    image_2 = V((grids, small + 2, ROW_PAD + 16, chans), F32)
    held = ((4, size, chans, total // 4), BF16)
    x_full = ((size, rows, chans), BF16)
    taps_1 = ((size, share, 9 * chans), BF16)
    x_small = ((size, few, total), BF16)
    taps_2 = ((size, few, 9 * chans), BF16)
    mixer = ((9 * chans, total), BF16)
    outs = [
        (S(*x_full), away),
        (S((rows, chans), F32), away),
        (S(*taps_1), away),
        (S((share, total), F32), away),
        (S((share, 128), F32), near),
        (S((few, total), BF16), near),
        (S(*held), away),
        (S((size, 16, chans), F32), near),
        (S(*x_small), away),
        (S((few_rows, chans), F32), near),
        (S(*taps_2), away),
        (S((few, total), F32), near),
        (S((few, 128), F32), near),
        (S((few, total), BF16), near),
        (S(*held), away),
        (S((few, total), F32), near),
        (S((token_rows, part), BF16), away),
        (S((size // 2, 4, token_rows, part), BF16), away),
        (S((total // 2, part), BF16), away),
    ]
    scratch = [
        V(*x_full),
        V((total, chans), BF16),
        V((rows, chans), F32),
        V((share, total), F32),
        V((token_rows, part), BF16),
        V((size, few, total), F32),
        V(*mixer),
        V(*taps_1),
        image_1,
        boxes(share, total),
        V((2, share, total), F32),
        V((share, total), F32),
        V(*held),
        V(*held),
        V((16, chans), F32),
        V((few, total), F32),
        V((2, few, total), BF16),
        V(*x_small),
        V((total, chans), BF16),
        V(*mixer),
        V(*taps_2),
        image_2,
        boxes(few, total),
        V((2, few, total), F32),
        V((size, few, total), BF16),
        V((size, token_rows, part), BF16),
        V((total, part), BF16),
        V((part, wide), BF16),
        V((token_rows, part), F32),
        V((token_rows, part), F32),
        V((few_rows, part), BF16),
        V((total, part), BF16),
        V((total // 2, part), BF16),
        DMA((10,)),
        DMA((6, 2, reach, 2)),
        DMA((2, 3)),
        DMA((2, 3)),
        DMA((1,)),
        DMA((1,)),
        DMA((size,)),
        DMA((3, size // 2)),
        DMA((size // 2,)),
        DMA((size // 2,)),
        DMA((10,)),
        DMA((10,)),
    ]
    (
        x_full_k, pre_1, taps_1_k, normed_1, inv_1, branch_sum, held_1_k, vec_full,
        x_small_k, pre_2, taps_2_k, normed_2, inv_2, branch_2, held_2_k, grad_rows, act, cot_wide, in_half,
    ) = kernel_call(
        functools.partial(forward_kernel, size, grids, side),
        "forward",
        1,
        [near] * 6 + [scalar] + [away] * 10,
        [shape for shape, _ in outs],
        [spec for _, spec in outs],
        scratch,
    )(
        *vectors, pool, places, live_counts, x, first_reduce, first_expand, second_expand,
        mixer_1, second_reduce, mixer_2, readout_in, readout_out, cotangent,
    )

    sums = [
        ((part, wide), True),
        ((total, part), True),
        ((9 * chans, total), False),
        ((total, chans), True),
        ((chans, total), False),
        ((9 * chans, total), False),
        ((total, chans), True),
        ((chans, total), False),
    ]
    outs = [
        (S((rows, chans), F32), near),
        (S((token_rows, part), BF16), near),
        (S((8, chans), F32), near),
    ]
    outs += [(S(shape, BF16), away) for shape, _ in sums]

    def half(shape, by_rows):
        return (shape[0] // 2, shape[1]) if by_rows else (shape[0], shape[1] // 2)

    scratch = [
        V((share, total), F32),
        V((rows, chans), F32),
        V((token_rows, part), BF16),
        V((total, chans), BF16),
        V((size, few, total), F32),
        V(*held),
        V(*x_full),
        V(*taps_1),
        V(*x_small),
        V(*taps_2),
        V(*mixer),
        V((part, wide), BF16),
    ]
    scratch += [
        V((size // 2, 4, token_rows, part), BF16),
        V((4, token_rows, part), BF16),
        V((part, wide // 2), BF16),
    ]
    scratch += [V(half(*sums[1]), BF16)] * 2
    for k, (shape, by_rows) in enumerate(sums[2:]):
        if k == 3:
            scratch += [V(shape, BF16)] + [V((shape[0], shape[1] // 4), BF16)] * 4
        else:
            scratch += [V(shape, BF16)] + [V(half(shape, by_rows), BF16)] * 2
    scratch += [
        image_1,
        image_2,
        V((share, 9 * chans), F32),
        V((few, 9 * chans), F32),
        V((few, total), BF16),
        V((few, total), BF16),
        V((few, total), BF16),
        V((share, total), BF16),
        V((size, few, total), BF16),
        V((size, share, total), BF16),
        V((size, few, total), BF16),
        V((size, few, total), BF16),
        V((size, few, chans), BF16),
        V((size, few, chans), BF16),
        V((few_rows, chans), BF16),
        V((rows, chans), BF16),
        V((share, total), F32),
        V((rows, chans), F32),
        boxes(rows, chans),
        V((2, rows, chans), F32),
        boxes(few, total),
        V((2, few, total), F32),
        V((8, total), F32),
        V((size, 8, chans), F32),
        V((4, 8, chans), F32),
        DMA((7,)),
        DMA((5, 2, reach, 2)),
        DMA((3, size - 1)),
        DMA((3, size - 1)),
        DMA((9, 3)),
        DMA((9, 3)),
        DMA((9,)),
        DMA((2,)),
        DMA((2,)),
        DMA((4,)),
        DMA((4,)),
        DMA((15,)),
    ]
    patch_grads, tokens, vec_sum, *grads = kernel_call(
        functools.partial(backward_kernel, size, grids, side),
        "backward",
        2,
        [near] * 9 + [scalar] + [near] + [away] * 15,
        [shape for shape, _ in outs],
        [spec for _, spec in outs],
        scratch,
    )(
        grad_rows, normed_2, inv_2, vec_full, branch_2, inv_1, branch_sum, pre_2,
        np.ascontiguousarray(4.0 * pool.T), live_counts, second_reduce, normed_1, pre_1, act, first_reduce,
        held_1_k, held_2_k, x_full_k, taps_1_k, x_small_k, taps_2_k, mixer_1, mixer_2, readout_out,
        cot_wide, in_half,
    )
    tall = [(rows, chans, F32)] + [shape + (BF16,) for shape, _ in sums]
    blocks = [pl.BlockSpec((r // 4, c), lambda k: (k, 0)) for r, c, _ in tall]
    blocks += [pl.BlockSpec(tokens.shape, lambda k: (0, 0)), pl.BlockSpec(vec_sum.shape, lambda k: (0, 0))]
    one = pl.BlockSpec((1, chans), lambda k: (0, 0))
    (
        patch_grads, out_g, in_g, mixer_2_g, reduce_2_g, expand_2_g, mixer_1_g, reduce_1_g, expand_1_g, tokens,
        gain_1_g, shift_1_g, gain_2_g, shift_2_g,
    ) = pl.pallas_call(
        widen_kernel,
        name="widen",
        grid=(4,),
        in_specs=blocks,
        out_shape=[S((r, c), F32) for r, c, _ in tall] + [S(tokens.shape, BF16)] + [S((1, chans), F32)] * 4,
        out_specs=blocks[:-1] + [one] * 4,
        compiler_params=pltpu.CompilerParams(vmem_limit_bytes=VMEM_LIMIT),
    )(patch_grads, *grads, tokens, vec_sum)
    return (
        tokens,
        patch_grads.reshape(patches.shape),
        reduce_1_g,
        mixer_1_g.reshape(first_mixer.shape),
        expand_1_g,
        gain_1_g.reshape(chans),
        shift_1_g.reshape(chans),
        reduce_2_g,
        mixer_2_g.reshape(second_mixer.shape),
        expand_2_g,
        gain_2_g.reshape(chans),
        shift_2_g.reshape(chans),
        in_g,
        out_g,
    )


def fits(mesh, patches, first_reduce, readout_in):
    size, groups = mesh.shape["mp"], mesh.shape["dp"]
    grids, side, _, chans = patches.shape
    return (
        groups == 4
        and size % 2 == 0
        and chans % 128 == 0
        and readout_in.shape[1] % 128 == 0
        and grids * side == 6 * size
        and side % 8 == 0
        and side // 2 <= ROW_PAD
    )


def solution(mesh):
    in_specs = (
        P("dp", None, None, "mp"),
        P(None, "mp"),
        P(None, None, "mp", None),
        P("mp", None),
        P("mp"),
        P("mp"),
        P(None, "mp"),
        P(None, None, "mp", None),
        P("mp", None),
        P("mp"),
        P("mp"),
        P(None, "mp"),
        P("mp", None),
        P("dp", "mp"),
        P("dp"),
    )
    out_specs = (
        P("dp", "mp"),
        P("dp", None, None, "mp"),
        P(None, "mp"),
        P(None, None, "mp", None),
        P("mp", None),
        P("mp"),
        P("mp"),
        P(None, "mp"),
        P(None, None, "mp", None),
        P("mp", None),
        P("mp"),
        P("mp"),
        P(None, "mp"),
        P("mp", None),
    )

    def local(*args):
        if fits(mesh, args[0], args[1], args[11]):
            return fast_body(mesh.shape["mp"], *args)
        return body(*args)

    return jax.shard_map(local, mesh=mesh, in_specs=in_specs, out_specs=out_specs, check_vma=False)
```

```python
import functools

import jax
import jax.numpy as jnp
import numpy as np
from jax import lax
from jax.experimental import pallas as pl
from jax.experimental.pallas import tpu as pltpu
from jax.sharding import PartitionSpec as P

norm_eps = 1e-06


def conv_same(image, kernel):
    return lax.conv_general_dilated(
        image,
        kernel,
        (1, 1),
        "SAME",
        dimension_numbers=("NHWC", "HWIO", "NHWC"),
        preferred_element_type=jnp.float32,
    )


def silu_back(values, grad_values):
    return jax.vjp(jax.nn.silu, values)[1](grad_values)[0]


def gelu_exact(values):
    return jax.nn.gelu(values, approximate=False)


def gelu_back(values, grad_values):
    return jax.vjp(gelu_exact, values)[1](grad_values)[0]


def block_forward(inputs, reduce_w, mixer_w, expand_w, gain, shift):
    num_grids, grid_height, grid_width, local_chans = inputs.shape
    pixel_rows = num_grids * grid_height * grid_width
    low_in = inputs.astype(jnp.bfloat16).reshape(pixel_rows, local_chans)
    full_in = lax.all_gather(low_in, "mp", axis=1, tiled=True)
    total_chans = full_in.shape[1]
    pre_act = jnp.dot(full_in, reduce_w, preferred_element_type=jnp.float32)
    hidden = jax.nn.silu(pre_act).astype(jnp.bfloat16)
    partial_mix = conv_same(
        hidden.reshape(num_grids, grid_height, grid_width, local_chans), mixer_w
    )
    mixed_sum = lax.psum_scatter(
        partial_mix.reshape(pixel_rows, total_chans).astype(jnp.bfloat16),
        "mp",
        scatter_dimension=1,
        tiled=True,
    ).astype(jnp.float32)
    row_total, row_squares = lax.psum(
        (jnp.sum(mixed_sum, axis=1), jnp.sum(mixed_sum * mixed_sum, axis=1)), "mp"
    )
    center = row_total / total_chans
    inv_std = lax.rsqrt(row_squares / total_chans - center * center + norm_eps)
    normed = (mixed_sum - center[:, None]) * inv_std[:, None]
    affine = normed * gain + shift
    branch_in = jax.nn.silu(affine).astype(jnp.bfloat16)
    partial_out = jnp.dot(branch_in, expand_w, preferred_element_type=jnp.float32)
    branch_out = lax.psum_scatter(
        partial_out.astype(jnp.bfloat16), "mp", scatter_dimension=1, tiled=True
    ).astype(jnp.float32)
    outputs = inputs + branch_out.reshape(inputs.shape)
    return (outputs, (full_in, pre_act, hidden, normed, inv_std, affine, branch_in))


def block_backward(grad_out, saved, reduce_w, mixer_w, expand_w, gain):
    full_in, pre_act, hidden, normed, inv_std, affine, branch_in = saved
    num_grids, grid_height, grid_width, local_chans = grad_out.shape
    pixel_rows = num_grids * grid_height * grid_width
    grad_rows = grad_out.reshape(pixel_rows, local_chans)
    grad_branch = lax.all_gather(grad_rows.astype(jnp.bfloat16), "mp", axis=1, tiled=True)
    total_chans = grad_branch.shape[1]
    expand_grad = jnp.einsum(
        "ri,ro->io", branch_in, grad_branch, preferred_element_type=jnp.float32
    )
    grad_act = jnp.einsum("ro,io->ri", grad_branch, expand_w, preferred_element_type=jnp.float32)
    grad_affine = silu_back(affine, grad_act)
    gain_grad = jnp.sum(grad_affine * normed, axis=0)
    shift_grad = jnp.sum(grad_affine, axis=0)
    scaled = grad_affine * gain
    sum_plain, sum_normed = lax.psum(
        (jnp.sum(scaled, axis=1), jnp.sum(scaled * normed, axis=1)), "mp"
    )
    grad_mixed = inv_std[:, None] * (
        scaled - sum_plain[:, None] / total_chans - normed * sum_normed[:, None] / total_chans
    )
    mixed_full = lax.all_gather(grad_mixed.astype(jnp.bfloat16), "mp", axis=1, tiled=True)
    mixed_image = mixed_full.reshape(num_grids, grid_height, grid_width, total_chans)
    flipped = jnp.transpose(mixer_w[::-1, ::-1], (0, 1, 3, 2))
    grad_hidden = conv_same(mixed_image, flipped).reshape(pixel_rows, local_chans)
    padded = jnp.pad(
        hidden.reshape(num_grids, grid_height, grid_width, local_chans),
        ((0, 0), (1, 1), (1, 1), (0, 0)),
    )
    mixer_grad = jnp.stack(
        [
            jnp.stack(
                [
                    jnp.einsum(
                        "nhwi,nhwo->io",
                        padded[
                            :,
                            offset_h : offset_h + grid_height,
                            offset_w : offset_w + grid_width,
                            :,
                        ],
                        mixed_image,
                        preferred_element_type=jnp.float32,
                    )
                    for offset_w in range(3)
                ]
            )
            for offset_h in range(3)
        ]
    )
    grad_pre = silu_back(pre_act, grad_hidden).astype(jnp.bfloat16)
    reduce_grad = jnp.einsum("ri,ro->io", full_in, grad_pre, preferred_element_type=jnp.float32)
    partial_in = jnp.einsum("ro,io->ri", grad_pre, reduce_w, preferred_element_type=jnp.float32)
    grad_in = (
        lax.psum_scatter(
            partial_in.astype(jnp.bfloat16), "mp", scatter_dimension=1, tiled=True
        ).astype(jnp.float32)
        + grad_rows
    )
    return (
        grad_in.reshape(grad_out.shape),
        (reduce_grad, mixer_grad, expand_grad, gain_grad, shift_grad),
    )


def body(
    patches,
    first_reduce,
    first_mixer,
    first_expand,
    first_gain,
    first_shift,
    second_reduce,
    second_mixer,
    second_expand,
    second_gain,
    second_shift,
    readout_in,
    readout_out,
    cotangent,
    live_counts,
):
    num_grids, grid_height, grid_width, local_chans = patches.shape
    pooled_side = grid_height // 2
    patch_values = patches.astype(jnp.float32)
    first_out = block_forward(
        patch_values, first_reduce, first_mixer, first_expand, first_gain, first_shift
    )[0]
    pooled = first_out.reshape(num_grids, pooled_side, 2, pooled_side, 2, local_chans).mean(
        axis=(2, 4)
    )
    second_out = block_forward(
        pooled, second_reduce, second_mixer, second_expand, second_gain, second_shift
    )[0]
    token_count = num_grids * pooled_side * pooled_side
    flat = second_out.astype(jnp.bfloat16).reshape(token_count, local_chans)
    flat_full = lax.all_gather(flat, "mp", axis=1, tiled=True)
    lifted = jnp.dot(flat_full, readout_in, preferred_element_type=jnp.float32)
    activated = gelu_exact(lifted).astype(jnp.bfloat16)
    partial_tokens = jnp.dot(activated, readout_out, preferred_element_type=jnp.float32)
    summed = lax.psum_scatter(
        partial_tokens.astype(jnp.bfloat16), "mp", scatter_dimension=1, tiled=True
    ).astype(jnp.float32)
    live_slots = (jnp.arange(num_grids) < live_counts[0]).astype(jnp.float32)
    live_rows = jnp.repeat(live_slots, pooled_side * pooled_side)
    tokens = (summed * live_rows[:, None]).astype(jnp.bfloat16)
    grad_tokens = cotangent * live_rows[:, None].astype(jnp.bfloat16)
    grad_full = lax.all_gather(grad_tokens, "mp", axis=1, tiled=True)
    readout_out_grad = jnp.einsum(
        "ri,ro->io", activated, grad_full, preferred_element_type=jnp.float32
    )
    grad_act = jnp.einsum("ro,io->ri", grad_full, readout_out, preferred_element_type=jnp.float32)
    grad_lift = gelu_back(lifted, grad_act).astype(jnp.bfloat16)
    readout_in_grad = jnp.einsum(
        "ri,ro->io", flat_full, grad_lift, preferred_element_type=jnp.float32
    )
    partial_flat = jnp.einsum(
        "ro,io->ri", grad_lift, readout_in, preferred_element_type=jnp.float32
    )
    grad_flat = lax.psum_scatter(
        partial_flat.astype(jnp.bfloat16), "mp", scatter_dimension=1, tiled=True
    ).astype(jnp.float32)
    second_saved = block_forward(
        pooled, second_reduce, second_mixer, second_expand, second_gain, second_shift
    )[1]
    grad_pooled, second_grads = block_backward(
        grad_flat.reshape(num_grids, pooled_side, pooled_side, local_chans),
        second_saved,
        second_reduce,
        second_mixer,
        second_expand,
        second_gain,
    )
    spread_back = jnp.broadcast_to(
        0.25 * grad_pooled[:, :, None, :, None, :],
        (num_grids, pooled_side, 2, pooled_side, 2, local_chans),
    ).reshape(patches.shape)
    first_saved = block_forward(
        patch_values, first_reduce, first_mixer, first_expand, first_gain, first_shift
    )[1]
    patch_grads, first_grads = block_backward(
        spread_back, first_saved, first_reduce, first_mixer, first_expand, first_gain
    )
    summed_grads = (
        lax.psum(first_grads[0].astype(jnp.bfloat16), "dp").astype(jnp.float32),
        lax.psum(first_grads[1].astype(jnp.bfloat16), "dp").astype(jnp.float32),
        lax.psum(first_grads[2].astype(jnp.bfloat16), "dp").astype(jnp.float32),
        lax.psum(first_grads[3].astype(jnp.bfloat16), "dp").astype(jnp.float32),
        lax.psum(first_grads[4].astype(jnp.bfloat16), "dp").astype(jnp.float32),
        lax.psum(second_grads[0].astype(jnp.bfloat16), "dp").astype(jnp.float32),
        lax.psum(second_grads[1].astype(jnp.bfloat16), "dp").astype(jnp.float32),
        lax.psum(second_grads[2].astype(jnp.bfloat16), "dp").astype(jnp.float32),
        lax.psum(second_grads[3].astype(jnp.bfloat16), "dp").astype(jnp.float32),
        lax.psum(second_grads[4].astype(jnp.bfloat16), "dp").astype(jnp.float32),
        lax.psum(readout_in_grad.astype(jnp.bfloat16), "dp").astype(jnp.float32),
        lax.psum(readout_out_grad.astype(jnp.bfloat16), "dp").astype(jnp.float32),
    )
    return (
        tokens,
        patch_grads,
        summed_grads[0],
        summed_grads[1],
        summed_grads[2],
        summed_grads[3],
        summed_grads[4],
        summed_grads[5],
        summed_grads[6],
        summed_grads[7],
        summed_grads[8],
        summed_grads[9],
        summed_grads[10],
        summed_grads[11],
    )


MESH = pl.DeviceIdType.MESH
F32 = jnp.float32
BF16 = jnp.bfloat16
DMA = pltpu.SemaphoreType.DMA
VMEM_LIMIT = 63 * 2**20
ROW_PAD = 16


def dot_nn(a, b):
    return lax.dot_general(a, b, (((1,), (0,)), ((), ())), preferred_element_type=F32)


def dot_nt(a, b):
    return lax.dot_general(a, b, (((1,), (1,)), ((), ())), preferred_element_type=F32)


def dot_tn(a, b):
    return lax.dot_general(a, b, (((0,), (0,)), ((), ())), preferred_element_type=F32)


def dot_full(a, b):
    return lax.dot_general(
        a,
        b,
        (((1,), (0,)), ((), ())),
        precision=lax.Precision.HIGHEST,
        preferred_element_type=F32,
    )


def sigmoid(values):
    return 1.0 / (1.0 + jnp.exp(-values))


def silu(values):
    return values * sigmoid(values)


def silu_slope(values):
    gate = sigmoid(values)
    return gate * (1.0 + values * (1.0 - gate))


class Ring:
    def __init__(self, size):
        self.size = size
        self.reach = size // 2
        self.me = lax.axis_index("mp")
        half = self.me // 2
        self.spot = jnp.where(self.me % 2 == 0, half, size - 1 - half)
        self.right = self.index(self.spot + 1)
        self.left = self.index(self.spot - 1)

    def wrap(self, spot):
        return lax.rem(spot + 2 * self.size, self.size)

    def index(self, spot):
        spot = self.wrap(spot)
        return jnp.where(spot < self.reach, 2 * spot, 2 * (self.size - 1 - spot) + 1)

    def greet(self):
        barrier = pltpu.get_barrier_semaphore()
        for peer in (self.left, self.right):
            pl.semaphore_signal(barrier, inc=1, device_id={"mp": peer}, device_id_type=MESH)
        pl.semaphore_wait(barrier, 2)

    def copy(self, side, src, dst, send, recv):
        peer = self.right if side == 0 else self.left
        return pltpu.make_async_remote_copy(
            src_ref=src,
            dst_ref=dst,
            send_sem=send,
            recv_sem=recv,
            device_id={"mp": peer},
            device_id_type=MESH,
        )


def wait_bytes(like, sem):
    pltpu.make_async_copy(like, like, sem).wait()


class Gather:
    def __init__(self, ring, own, held, slot, lanes, send, recv):
        self.ring, self.own, self.held, self.slot = ring, own, held, slot
        self.lanes, self.send, self.recv, self.copies = lanes, send, recv, {}

    def _start(self, side, step, lane):
        ring = self.ring
        if step == ring.reach and lane // (len(self.lanes) // 2) != side:
            return
        away = step - 1
        spot = ring.wrap(ring.spot - away if side == 0 else ring.spot + away)
        dst = self.held.at[self.slot(spot)]
        src = self.own if step == 1 else dst
        at = self.lanes[lane]
        copy = ring.copy(
            side, src.at[at], dst.at[at], self.send, self.recv.at[side, step - 1, lane]
        )
        copy.start()
        self.copies[side, step, lane] = copy

    def move_lane(self, step, lane):
        for side in range(2):
            if step == 0:
                self._start(side, 1, lane)
            elif (side, step, lane) in self.copies:
                self.copies[side, step, lane].wait_recv()
                if step < self.ring.reach:
                    self._start(side, step + 1, lane)

    def start(self):
        self.move(0)

    def move(self, step, after=None):
        for lane in range(len(self.lanes)):
            self.move_lane(step, lane)
            if after is not None:
                after()

    def drain(self):
        wait_bytes(self.held.at[pl.ds(0, self.ring.size - 1)], self.send)

    def spots(self, step):
        ring = self.ring
        if step == ring.reach:
            return [ring.wrap(ring.spot + step)]
        return [ring.wrap(ring.spot - step), ring.wrap(ring.spot + step)]


class Scatter:
    def __init__(self, ring, term, boxes, terms, lanes, send, recv, extra=None):
        self.ring, self.term, self.out, self.inbox = ring, term, boxes[0], boxes[1]
        self.extra = extra
        self.terms, self.lanes, self.send, self.recv, self.copies = terms, lanes, send, recv, {}

    def place(self, side, step):
        return side * self.ring.reach + step - 1

    def _start(self, side, step, lane):
        at, place = self.lanes[lane], self.place(side, step)
        src, dst = self.out.at[place], self.inbox.at[place]
        copy = self.ring.copy(
            side, src.at[at], dst.at[at], self.send, self.recv.at[side, step - 1, lane]
        )
        copy.start()
        self.copies[side, step, lane] = copy

    def _fill(self, k, spot):
        self.terms[k] = self.term(spot)
        if self.extra is not None:
            self.extra(spot, self.terms.at[k])

    def start(self):
        ring, count = self.ring, len(self.lanes)
        self._fill(0, ring.wrap(ring.spot + ring.reach))
        for lane in range(count):
            side = lane // (count // 2)
            at = self.lanes[lane]
            self.out[(self.place(side, 1),) + at] = self.terms[(0,) + at].astype(BF16)
            self._start(side, 1, lane)

    def prepare(self, step, send=True):
        ring = self.ring
        away = ring.reach + 1 - step
        self._fill(0, ring.wrap(ring.spot + away))
        if away > 0:
            self._fill(1, ring.wrap(ring.spot - away))
        if step == 2 and send:
            for k in range(len(self.lanes) // 2):
                self.step_lane(2, k)

    def step_lane(self, step, k):
        count = len(self.lanes)
        for side in range(2):
            lane = (k + count // 2) % count if side == 0 else k
            at = self.lanes[lane]
            value = self.terms[(side,) + at]
            if (side, step - 1, lane) in self.copies:
                self.copies[side, step - 1, lane].wait_recv()
                value = value + self.inbox[(self.place(side, step - 1),) + at].astype(F32)
            self.out[(self.place(side, step),) + at] = value.astype(BF16)
            self._start(side, step, lane)

    def step(self, step, after=None):
        count = len(self.lanes)
        for k in range(count // 2 if step == 2 else 0, count):
            self.step_lane(step, k)
            if after is not None:
                after()

    def finish(self):
        reach = self.ring.reach
        for lane in range(len(self.lanes)):
            for side in range(2):
                self.copies[side, reach, lane].wait_recv()
        return (
            self.terms[0]
            + self.inbox[self.place(0, reach)].astype(F32)
            + self.inbox[self.place(1, reach)].astype(F32)
        )

    def drain(self):
        wait_bytes(self.out.at[pl.ds(0, self.ring.size - 1)], self.send)


class Later:
    def __init__(self):
        self.steps = []

    def add(self, step, *args):
        self.steps.append((step, args))

    def tick(self, count=1):
        for _ in range(min(count, len(self.steps))):
            step, args = self.steps.pop(0)
            step(*args)

    def rest(self):
        self.tick(len(self.steps))


def row_halves(rows):
    return ((pl.ds(0, rows // 2),), (pl.ds(rows // 2, rows // 2),))


def column_halves(columns):
    every = slice(None)
    return (
        (every, pl.ds(0, columns // 2)),
        (every, pl.ds(columns // 2, columns // 2)),
    )


def pool_places(side):
    small = side // 2
    place = np.zeros((3 * ROW_PAD, 6 * side), np.float32)
    for row in range(6):
        for column in range(side):
            place[(row // 2) * ROW_PAD + column // 2, row * side + column] = 0.25
    assert small <= ROW_PAD
    return place


def token_places(grids, small):
    place = np.zeros((grids * small * small, grids * small * ROW_PAD), np.float32)
    for line in range(grids * small):
        for column in range(small):
            place[line * small + column, line * ROW_PAD + column] = 1.0
    return place


def norm_rows(mixed, gain, shift):
    center = jnp.mean(mixed, axis=1, keepdims=True)
    apart = mixed - center
    inv_std = lax.rsqrt(jnp.mean(apart * apart, axis=1, keepdims=True) + norm_eps)
    normed = apart * inv_std
    return normed, inv_std, normed * gain + shift


def wide_vector(held, row):
    return jnp.concatenate([held[m, row : row + 1, :] for m in range(held.shape[0])], axis=1)


def half_of(rows, columns, which, by_rows):
    if by_rows:
        return (pl.ds(pl.multiple_of(which * (rows // 2), 16), rows // 2), slice(None))
    return (slice(None), pl.ds(pl.multiple_of(which * (columns // 2), 128), columns // 2))


class Pair:
    def __init__(self):
        self.me = lax.axis_index("dp")
        self.core = lax.rem(self.me, 2)
        self.other = 1 - self.core
        self.twin = self.me - self.core + self.other
        self.far = lax.rem(self.me + 2, 4)
        self.across = lax.rem(self.twin + 2, 4)

    def copy(self, peer, src, dst, send, recv):
        return pltpu.make_async_remote_copy(
            src_ref=src,
            dst_ref=dst,
            send_sem=send,
            recv_sem=recv,
            device_id={"dp": peer},
            device_id_type=MESH,
        )


class Share:
    def __init__(self, ring, pair, blocks, held, send, recv, twin_send, local):
        self.ring, self.pair, self.blocks, self.held = ring, pair, blocks, held
        self.send, self.recv, self.twin_send, self.local = send, recv, twin_send, local
        self.copies = []

    def go(self, spot):
        pair, half = self.pair, self.ring.size // 2
        m = self.ring.index(spot)
        same = m // half == pair.core
        j = lax.rem(m, half)
        src, dst = self.blocks.at[m], self.held.at[j, pair.me]
        peer = jnp.where(same, pair.far, pair.across)
        sem = self.recv.at[jnp.where(same, 0, 1), j]
        copy = pair.copy(peer, src, dst, self.send.at[len(self.copies)], sem)
        copy.start()
        self.copies.append(copy)

        @pl.when(same)
        def _():
            pltpu.make_async_copy(src, dst, self.local.at[j]).start()

        @pl.when(jnp.logical_not(same))
        def _():
            pair.copy(pair.twin, src, dst, self.twin_send.at[j], self.recv.at[2, j]).start()

    def drain(self):
        pair = self.pair
        for copy in self.copies:
            copy.wait_send()
        for j in range(self.ring.size // 2):
            src, dst = self.blocks.at[j], self.held.at[j, pair.me]
            pltpu.make_async_copy(src, dst, self.local.at[j]).wait()
            pair.copy(pair.twin, src, dst, self.twin_send.at[j], self.recv.at[2, j]).wait()
            for kind, peer in enumerate((pair.far, pair.across)):
                dst = self.held.at[j, peer]
                pair.copy(peer, src, dst, self.send.at[0], self.recv.at[kind, j]).wait_recv()


class Expand:
    def __init__(self, ring, pair, own, held, send, recv, psend, precv, load):
        self.ring, self.pair, self.held = ring, pair, held
        self.psend, self.precv, self.copies = psend, precv, []
        chans, quarter = held.shape[2:]
        columns = own.at[:, pl.ds(pl.multiple_of(pair.me * quarter, 128), quarter)]
        self.load = pltpu.make_async_copy(columns, held.at[pair.me, ring.me], load)
        self.load.start()
        self.gather = Gather(
            ring, held.at[pair.me, ring.me], held.at[pair.me], ring.index, row_halves(chans), send, recv
        )

    def across(self):
        self._swap(0, self.pair.far, self.pair.me)

    def between(self):
        self.copies[0].wait_recv()
        self._swap(1, self.pair.twin, self.pair.me)
        self._swap(2, self.pair.twin, self.pair.far)

    def _swap(self, k, peer, quarter):
        at = self.held.at[quarter]
        copy = self.pair.copy(peer, at, at, self.psend.at[k], self.precv.at[k])
        copy.start()
        self.copies.append(copy)

    def ready(self):
        for copy in self.copies[1:]:
            copy.wait_recv()

    def drain(self):
        self.gather.drain()
        for copy in self.copies:
            copy.wait_send()


def times_expand(rows, held):
    parts = []
    for k in range(held.shape[0]):
        weight = held[k].reshape(rows.shape[1], held.shape[3])
        parts.append(dot_nn(rows, weight))
    return jnp.concatenate(parts, axis=1)


def times_expand_back(rows, held):
    quarter = held.shape[3]
    total = None
    for k in range(held.shape[0]):
        weight = held[k].reshape(held.shape[1] * held.shape[2], quarter)
        part = dot_nt(rows[:, k * quarter : (k + 1) * quarter], weight)
        total = part if total is None else total + part
    return total


def chunk_taps(image, taps, spot, lines, side, width):
    chans = image.shape[-1]
    per_grid = side // lines
    grid, line = spot // per_grid, lax.rem(spot, per_grid) * lines
    for kh in range(3):
        for kw in range(3):
            piece = image[grid, pl.ds(line + kh, lines), 7 + kw : 7 + kw + width, :]
            at = (kh * 3 + kw) * chans
            taps[spot, :, at : at + chans] = piece.reshape(lines * width, chans).astype(BF16)


def chunk_back(image, product, spot, lines, side, width):
    chans = image.shape[-1]
    per_grid = side // lines
    grid, line = spot // per_grid, lax.rem(spot, per_grid) * lines
    for kh in range(3):
        for kw in range(3):
            at = (kh * 3 + kw) * chans
            piece = product[:, at : at + chans].reshape(lines, width, chans)
            image[grid, pl.ds(line + kh, lines), 7 + kw : 7 + kw + width, :] += piece


def all_terms(terms, value):
    terms[...] = value.reshape(terms.shape)


def norm_back(grad_branch, normed, inv_std, gain, shift):
    affine = normed * gain + shift
    grad_affine = grad_branch * silu_slope(affine)
    gain_grad = jnp.sum(grad_affine * normed, axis=0, keepdims=True)
    shift_grad = jnp.sum(grad_affine, axis=0, keepdims=True)
    scaled = grad_affine * gain
    mean_plain = jnp.mean(scaled, axis=1, keepdims=True)
    mean_normed = jnp.mean(scaled * normed, axis=1, keepdims=True)
    return inv_std * (scaled - mean_plain - normed * mean_normed), gain_grad, shift_grad

class GroupSum:
    def __init__(self, pair, mine, other, from_core, from_far, result, half, send, recv, local):
        self.pair, self.mine, self.other = pair, mine, other
        self.from_core, self.from_far = from_core, from_far
        self.result = result.at[half]
        self.send, self.recv, self.local, self.copies = send, recv, local, []

    def _go(self, k, peer, src, dst):
        copy = self.pair.copy(peer, src, dst, self.send.at[k], self.recv.at[k])
        copy.start()
        self.copies.append(copy)

    def core(self):
        self._go(0, self.pair.twin, self.other, self.from_core)

    def far(self):
        if self.from_core is not None:
            self.copies[0].wait_recv()
            self.mine[...] = (self.mine[...].astype(F32) + self.from_core[...].astype(F32)).astype(
                BF16
            )
        self._go(1, self.pair.far, self.mine, self.from_far)

    def back(self):
        self.copies[-1].wait_recv()
        self.from_far[...] = (self.mine[...].astype(F32) + self.from_far[...].astype(F32)).astype(
            BF16
        )
        self._go(2, self.pair.twin, self.from_far, self.result)
        self.kept = pltpu.make_async_copy(self.from_far, self.result, self.local)
        self.kept.start()

    def done(self):
        self.copies[-1].wait_recv()
        self.kept.wait()
        for copy in self.copies:
            copy.wait_send()


def quarter_of(grad, which):
    columns = grad.shape[1] // 4
    return pl.ds(pl.multiple_of(which * columns, 128), columns)


class OutSum:
    def __init__(self, pair, act_all, cot_wide, grad, result, send, recv, local):
        self.pair, self.act_all, self.cot_wide, self.grad = pair, act_all, cot_wide, grad
        half = half_of(*result.shape, pair.core, False)
        self.result = result.at[half]
        self.send, self.recv, self.local = send, recv, local

    def spread(self, act_live):
        pair = self.pair
        self.act_all[pair.me] = act_live
        at = self.act_all.at[pair.me]
        self.copies = []
        for k, peer in enumerate((pair.far, pair.across, pair.twin)):
            copy = pair.copy(peer, at, at, self.send.at[k], self.recv.at[k])
            copy.start()
            self.copies.append(copy)

    def arrive(self):
        for copy in self.copies:
            copy.wait_recv()

    def block(self, j):
        groups, rows, part = self.act_all.shape
        left = self.act_all[...].reshape(groups * rows, part)
        right = self.cot_wide[j % 2].reshape(groups * rows, part)
        self.grad[:, j * part : (j + 1) * part] = dot_tn(left, right).astype(BF16)

    def back(self):
        copy = self.pair.copy(
            self.pair.twin, self.grad, self.result, self.send.at[3], self.recv.at[3]
        )
        copy.start()
        self.copies.append(copy)
        self.kept = pltpu.make_async_copy(self.grad, self.result, self.local)
        self.kept.start()

    def done(self):
        self.copies[3].wait_recv()
        self.kept.wait()
        for copy in self.copies:
            copy.wait_send()


def send_columns(ring, src, held, slot, send, recv):
    chans = held.shape[-1]
    held[slot] = src[:, pl.ds(pl.multiple_of(ring.me * chans, chans), chans)]
    copies = []
    for away in range(1, ring.size):
        peer = lax.rem(ring.me + away, ring.size)
        copy = pltpu.make_async_remote_copy(
            src_ref=src.at[:, pl.ds(pl.multiple_of(peer * chans, chans), chans)],
            dst_ref=held.at[slot],
            send_sem=send.at[away - 1],
            recv_sem=recv.at[away - 1],
            device_id={"mp": peer},
            device_id_type=MESH,
        )
        copy.start()
        copies.append(copy)
    return copies


def stack(value, columns):
    width = value.shape[1]
    return jnp.concatenate([value[:, k : k + columns] for k in range(0, width, columns)], axis=0)


def unstack(value, rows):
    return jnp.concatenate([value[k : k + rows] for k in range(0, value.shape[0], rows)], axis=1)


def layer_kernel(
    size, grids, side,
    gain_1, shift_1, gain_2, shift_2, pool, spread, places, counts,
    x, reduce_1_any, expand_1, expand_2, mixer_1_any, reduce_2_any, mixer_2_any, readout_in_any, readout_out_any,
    cotangent,
    patch_grads, tokens, vec_sum, cot_wide_any, out_sum, in_sum, mixer_2_sum, reduce_2_sum, expand_2_sum,
    mixer_1_sum, reduce_1_sum, expand_1_sum,
    x_full, reduce_1, reduce_2, mixer, readout_in, readout, vectors, vec_full, pre_1, taps_1, image_1, held_1, held_2,
    normed_1, inv_1, branch_1, pooled, low, x_small, pre_2, taps_2, image_2, normed_2, inv_2, branch_2,
    flat_full, cot_full, lifted, act, grad_act, grad_lift, grad_rows, terms_all,
    boxes_big, terms_big, boxes_small, terms_small,
    cot_wide, act_all, out_grad, in_grad, in_core, in_far,
    mixer_2_grad, mixer_2_core, mixer_2_far, reduce_2_grad, reduce_2_core, reduce_2_far,
    expand_2_grad, expand_2_core, expand_2_far,
    mixer_1_grad, mixer_1a_core, mixer_1a_far, mixer_1b_core, mixer_1b_far, reduce_1_grad, reduce_1_core, reduce_1_far,
    expand_1_grad, expand_1_core, expand_1_far,
    product_1, low_1, mix_2, mix_1, mix_2_full, low_1_full, branch_2_full, branch_1_full,
    grad_pre_2, grad_pre_1, grad_out, vec_grad, vec_held, vec_part,
    send, recv, cot_recv, tok_recv, psend, precv, csend, crecv, ysend, yrecv, tsend, local, all_send, all_recv,
    sum_send, sum_recv, sum_local, vec_send, vec_recv, act_send, act_recv, load,
):
    ring, pair = Ring(size), Pair()
    rows, chans = x.shape
    share = rows // size
    total = size * chans
    small = side // 2
    few = pooled.shape[0]
    part = readout_in.shape[1]
    count = cotangent.shape[0]
    wide, tall = column_halves(total), row_halves(rows)
    near = lambda spot: spot
    big, little = (boxes_big.at[0], boxes_big.at[1]), (boxes_small.at[0], boxes_small.at[1])
    low_2_full, mix_1_full = flat_full, cot_full

    def fetch(k, src, dst):
        return pltpu.make_async_copy(src, dst, load.at[k])

    l_x = fetch(0, x, x_full.at[ring.me])
    l_reduce_1 = fetch(1, reduce_1_any, reduce_1)
    l_mixer = [
        fetch(2, mixer_1_any, mixer),
        fetch(2, mixer_2_any, mixer),
        fetch(2, mixer_1_any, mixer),
    ]
    l_reduce_2 = fetch(3, reduce_2_any, reduce_2)
    l_in = fetch(4, readout_in_any, readout_in)
    l_out = fetch(5, readout_out_any, readout)
    l_cot = fetch(6, cotangent, cot_full.at[ring.me])
    l_wide = [
        fetch(7 + j % 2, cot_wide_any.at[j], cot_wide.at[j % 2]) for j in range(size // 2)
    ]
    l_x.start()
    l_reduce_1.start()
    e1 = Expand(
        ring, pair, expand_1, held_1, send.at[0], recv.at[2], psend.at[0], precv.at[0], load.at[9]
    )
    e2 = Expand(
        ring, pair, expand_2, held_2, send.at[1], recv.at[3], psend.at[1], precv.at[1], load.at[10]
    )
    barrier = pltpu.get_barrier_semaphore()
    for peer in (ring.left, ring.right):
        pl.semaphore_signal(barrier, inc=1, device_id={"mp": peer}, device_id_type=MESH)
    for peer in (pair.twin, pair.far, pair.across):
        pl.semaphore_signal(barrier, inc=1, device_id={"dp": peer}, device_id_type=MESH)
    pl.semaphore_wait(barrier, 5)
    gx = Gather(ring, x, x_full, ring.index, tall, send.at[2], recv.at[0])
    gx.start()
    for copy in (l_mixer[0], l_reduce_2, l_in, l_out, l_cot):
        copy.start()
    e1.load.wait()
    e1.gather.start()
    for k, vector in enumerate((gain_1, shift_1, gain_2, shift_2)):
        for row in (k, k + 8):
            vectors[row : row + 1, :] = vector[...]
    for k in range(4, 8):
        for row in (k, k + 8):
            vectors[row : row + 1, :] = gain_1[...]
    vec_full[ring.me] = vectors[...]
    gv = Gather(ring, vectors, vec_full, ring.index, row_halves(16), send.at[3], recv.at[4])
    gv.start()

    def add(spot):
        m = ring.index(spot)
        weight = reduce_1[pl.ds(pl.multiple_of(m * chans, chans), chans), :]
        pre_1[...] += dot_nn(x_full[m], weight)

    l_x.wait()
    l_reduce_1.wait()
    own = reduce_1[pl.ds(pl.multiple_of(ring.me * chans, chans), chans), :]
    pre_1[...] = dot_nn(x_full[ring.me], own)
    image_1[...] = jnp.zeros(image_1.shape, F32)
    image_2[...] = jnp.zeros(image_2.shape, F32)
    for step in range(1, ring.reach + 1):
        gx.move(step)
        for spot in gx.spots(step):
            add(spot)
        if step < ring.reach:
            for item in (e1.gather, gv):
                item.move(step)
    hidden = silu(pre_1[...])
    image_1[:, 1 : 1 + side, 8 : 8 + side, :] = hidden.reshape(grids, side, side, chans)
    l_mixer[0].wait()

    def mix_term(spot):
        chunk_taps(image_1, taps_1, spot, 6, side, side)
        return stack(dot_nn(taps_1[spot], mixer[...]), chans)

    rs1 = Scatter(ring, mix_term, big, terms_big, tall, send.at[4], recv.at[1])
    rs1.start()
    e1.gather.move(ring.reach)
    e1.across()
    gv.move(ring.reach)
    l_cot.wait()
    share_cot = Share(ring, pair, cot_full, cot_wide_any, ysend, yrecv, tsend, local)
    share_cot.go(ring.spot)
    for step in range(2, ring.reach + 1):
        rs1.prepare(step)
        rs1.step(step)
        if step == ring.reach - 1:
            e1.between()
    e2.load.wait()
    e2.gather.start()
    rs1.prepare(ring.reach + 1)
    l_mixer[1].start()
    mine = pl.ds(pl.multiple_of(ring.spot * share, 16), share)
    gain_a, shift_a = wide_vector(vec_full, 0), wide_vector(vec_full, 1)
    mixed = unstack(rs1.finish(), share)
    thin = [(pl.ds(k, count // 6),) for k in range(0, count, count // 6)]
    gc = Gather(
        ring, cot_full.at[ring.me], cot_full, ring.index, thin, send.at[5], cot_recv
    )

    held_back = []

    def move_cot(step, lane):
        gc.move_lane(step, lane)
        if step > 0 and lane == len(thin) - 1:
            held_back.extend(gc.spots(step))

    def share_blocks():
        while held_back:
            share_cot.go(held_back.pop(0))

    cots = Later()
    late = [(step, lane) for step in range(1, ring.reach + 1) for lane in range(2)]
    for step in range(ring.reach + 1):
        for lane in range(len(thin)):
            if len(cots.steps) >= 4 and late:
                cots.add(e2.gather.move_lane, *late.pop(0))
            cots.add(move_cot, step, lane)
    cots.tick(4)
    value, inverse, affine = norm_rows(mixed, gain_a, shift_a)
    normed_1[...] = value
    inv_1[...] = jnp.broadcast_to(inverse, inv_1.shape)
    branch = silu(affine).astype(BF16)
    e1.ready()
    x_rows = jnp.concatenate([x_full[m, mine, :].astype(F32) for m in range(size)], axis=1)
    pooled[...] = dot_full(pool[...], x_rows + times_expand(branch, held_1))
    low[0] = pooled[...].astype(BF16)
    x_small[ring.spot] = low[0]
    g2 = Gather(ring, low.at[0], x_small, near, wide, send.at[6], recv.at[0])
    g2.start()
    branch_1[...] = (4.0 * dot_full(pool[...], branch.astype(F32))).astype(BF16)
    rs1.drain()
    for step in range(1, ring.reach + 1):
        g2.move(step, lambda: cots.tick(2))
    e2.across()
    share_blocks()
    l_reduce_2.wait()
    cots.tick(3)
    pre_2[...] = dot_nn(x_small[...].reshape(size * few, total), reduce_2[...])
    hidden = silu(pre_2[...])
    image_2[:, 1 : 1 + small, 8 : 8 + ROW_PAD, :] = hidden.reshape(grids, small, ROW_PAD, chans)
    l_mixer[1].wait()

    def taps(spot, carry):
        chunk_taps(image_2, taps_2, spot, 3, small, ROW_PAD)
        return carry

    lax.fori_loop(0, size, taps, 0)
    all_terms(terms_all, dot_nn(taps_2[...].reshape(size * few, 9 * chans), mixer[...]))
    rs2 = Scatter(ring, terms_all.__getitem__, little, terms_small, wide, send.at[7], recv.at[1])
    rs2.start()
    for step in range(2, ring.reach + 1):
        rs2.prepare(step)
        rs2.step(step, cots.tick)
        share_blocks()
    rs2.prepare(ring.reach + 1)
    gain_b, shift_b = wide_vector(vec_full, 2), wide_vector(vec_full, 3)
    e2.between()
    mixed = rs2.finish()
    cots.tick(2)
    value, inverse, affine = norm_rows(mixed, gain_b, shift_b)
    normed_2[...] = value
    inv_2[...] = jnp.broadcast_to(inverse, inv_2.shape)
    branch_2[...] = silu(affine).astype(BF16)
    e2.ready()
    low[1] = (pooled[...] + times_expand(branch_2[...], held_2)).astype(BF16)
    flat_full[ring.spot] = low[1]
    gf = Gather(ring, low.at[1], flat_full, near, wide, send.at[8], recv.at[0])
    gf.start()
    rs2.drain()
    for step in range(1, ring.reach + 1):
        gf.move(step, cots.tick)
        share_blocks()
    g2.drain()
    gf.drain()
    l_in.wait()
    flat = dot_nn(places[...], flat_full[...].reshape(size * few, total)).astype(BF16)
    lifted[...] = dot_nn(flat, readout_in[...])
    cdf = 0.5 * (1.0 + lax.erf(lifted[...] * 0.7071067811865476))
    row_ids = lax.broadcasted_iota(jnp.int32, (count, 1), 0)
    live = (row_ids < counts[0] * (count // grids)).astype(F32)
    activated = (lifted[...] * cdf).astype(BF16)
    act[...] = activated
    slope = cdf + lifted[...] * jnp.exp(-0.5 * lifted[...] * lifted[...]) * 0.3989422804014327
    lifted[...] = slope * live
    grad_act[...] = jnp.zeros(grad_act.shape, F32)
    l_out.wait()
    cots.rest()
    share_blocks()

    def back(m, carry):
        at = pl.ds(pl.multiple_of(m * part, 128), part)
        grad_act[...] += dot_nt(cot_full[m], readout[:, at])
        return carry

    lax.fori_loop(0, size, back, 0)
    lift = (grad_act[...] * lifted[...]).astype(BF16)
    grad_lift[...] = dot_tn(places[...], lift).astype(BF16)
    all_terms(terms_all, dot_nt(grad_lift[...], readout_in[...]))
    rf = Scatter(ring, terms_all.__getitem__, little, terms_small, wide, send.at[9], recv.at[1])
    rf.start()

    def token_term(spot):
        at = pl.ds(pl.multiple_of(ring.index(spot) * part, 128), part)
        return stack(dot_nn(act[...], readout[:, at]), chans)

    quarters = [(pl.ds(k, rows // 4),) for k in range(0, rows, rows // 4)]
    r_tok = Scatter(ring, token_term, big, terms_big, quarters, send.at[10], tok_recv)
    toks = Later()
    toks.add(r_tok.prepare, 2, False)
    for step in range(2, ring.reach + 1):
        if step > 2:
            toks.add(r_tok.prepare, step)
        for k in range(4):
            toks.add(r_tok.step_lane, step, k)
    rf.prepare(2)
    r_tok.start()
    in_grad[...] = dot_tn(flat, lift).astype(BF16)
    in_other = half_of(*in_grad.shape, pair.other, True)
    in_copy = pair.copy(pair.twin, in_grad.at[in_other], in_core, csend.at[0], crecv.at[0])
    in_copy.start()
    rf.step(2)
    toks.tick()
    rf.prepare(3)
    rf.step(3)
    toks.tick()
    rf.prepare(4)
    rf.step(4)
    toks.tick()
    rf.prepare(ring.reach + 1)

    def group_sum(k, mine, other, from_core, from_far, result, by_rows):
        half = half_of(*result.shape, pair.core, by_rows)
        return GroupSum(
            pair, mine, other, from_core, from_far, result, half, sum_send.at[k], sum_recv.at[k], sum_local.at[k]
        )

    def grad_sum(k, grad, from_core, from_far, result, by_rows):
        mine, other = (
            grad.at[half_of(*grad.shape, which, by_rows)] for which in (pair.core, pair.other)
        )
        return group_sum(k, mine, other, from_core, from_far, result, by_rows)

    def quarter_sum(k, which, grad, from_core, from_far, result):
        mine, other = (
            (slice(None), quarter_of(grad, 2 * core + which)) for core in (pair.core, pair.other)
        )
        return GroupSum(
            pair, grad.at[mine], grad.at[other], from_core, from_far, result, mine, sum_send.at[k], sum_recv.at[k],
            sum_local.at[k],
        )

    s_out = OutSum(pair, act_all, cot_wide, out_grad, out_sum, act_send, act_recv, sum_local.at[0])
    s_in = group_sum(1, in_core, None, None, in_far, in_sum, True)
    s_m2 = grad_sum(2, mixer_2_grad, mixer_2_core, mixer_2_far, mixer_2_sum, False)
    s_r2 = grad_sum(3, reduce_2_grad, reduce_2_core, reduce_2_far, reduce_2_sum, True)
    s_e2 = grad_sum(4, expand_2_grad, expand_2_core, expand_2_far, expand_2_sum, False)
    s_m1a = quarter_sum(5, 0, mixer_1_grad, mixer_1a_core, mixer_1a_far, mixer_1_sum)
    s_m1b = quarter_sum(8, 1, mixer_1_grad, mixer_1b_core, mixer_1b_far, mixer_1_sum)
    s_r1 = grad_sum(6, reduce_1_grad, reduce_1_core, reduce_1_far, reduce_1_sum, True)
    s_e1 = grad_sum(7, expand_1_grad, expand_1_core, expand_1_far, expand_1_sum, False)
    s_out.spread((act[...].astype(F32) * live).astype(BF16))
    grad_rows[...] = rf.finish()
    low[0] = grad_rows[...].astype(BF16)
    value, gain_grad, shift_grad = norm_back(
        times_expand_back(low[0], held_2), normed_2[...], inv_2[:, 0:1], gain_b, shift_b
    )
    mix_2[...] = value.astype(BF16)
    g_mix2 = Gather(ring, mix_2, mix_2_full, near, wide, send.at[11], recv.at[0])
    g_mix2.start()
    mix_2_full[ring.spot] = mix_2[...]
    toks.tick()
    in_copy.wait_recv()
    in_mine = in_grad[half_of(*in_grad.shape, pair.core, True)]
    in_core[...] = (in_mine.astype(F32) + in_core[...].astype(F32)).astype(BF16)
    s_in.far()
    vec_grad[...] = jnp.zeros(vec_grad.shape, F32)
    vec_grad[2:3, :] = gain_grad
    vec_grad[3:4, :] = shift_grad
    image_2[...] = jnp.zeros(image_2.shape, F32)
    image_1[...] = jnp.zeros(image_1.shape, F32)
    low_2_full[ring.spot] = low[0]
    g_low2 = Gather(ring, low.at[0], low_2_full, near, wide, send.at[12], recv.at[2])
    g_low2.start()
    a_low2 = send_columns(
        ring, branch_2, branch_2_full, ring.spot, all_send.at[0], all_recv.at[0]
    )
    rf.drain()

    def back_2(spot):
        product_1[0:few, :] = dot_nt(mix_2_full[spot], mixer[...])
        chunk_back(image_2, product_1.at[0:few], spot, 3, small, ROW_PAD)

    back_2(ring.spot)
    for step in range(1, ring.reach + 1):
        g_mix2.move(step)
        for spot in g_mix2.spots(step):
            back_2(spot)
        if step > 1:
            g_low2.move(step - 1)
        toks.tick(2 if step < 3 else 1)
    l_mixer[2].start()
    grad_hidden = image_2[:, 1 : 1 + small, 8 : 8 + ROW_PAD, :].reshape(pre_2.shape)
    grad_pre_2[...] = (grad_hidden * silu_slope(pre_2[...])).astype(BF16)
    all_terms(terms_all, dot_nt(grad_pre_2[...], reduce_2[...]))
    gc.drain()
    share_cot.drain()
    r_in2 = Scatter(ring, terms_all.__getitem__, little, terms_small, wide, send.at[13], recv.at[1])
    r_in2.start()
    for k in range(2):
        l_wide[k].start()
    def mixer_part(grad, taps, right, columns):
        left = taps[...].reshape(right.shape[0], 9 * chans)
        grad[:, columns] = dot_tn(left, right).astype(BF16)

    def mixer_2_half(which):
        columns = half_of(*mixer_2_grad.shape, which, False)[1]
        right = mix_2_full[:, :, columns].reshape(size * few, total // 2)
        mixer_part(mixer_2_grad, taps_2, right, columns)

    def mixer_1_quarter(core, which):
        quarter = total // 4
        lines = pl.ds(pl.multiple_of(core * share, 16), share)
        right = mix_1_full[:, lines, which * quarter : (which + 1) * quarter]
        columns = quarter_of(mixer_1_grad, 2 * core + which)
        mixer_part(mixer_1_grad, taps_1, right.reshape(rows, quarter), columns)

    def expand_part(grad, branches, lows):
        grad[...] = dot_tn(
            branches[...].reshape(size * few, chans), lows[...].reshape(size * few, total)
        ).astype(BF16)

    r_in2.prepare(2)
    r_in2.step(2)
    toks.tick(2)
    g_low2.move(ring.reach)
    mixer_2_half(pair.other)
    s_m2.core()
    r_in2.prepare(3)
    r_in2.step(3)
    toks.tick()
    mixer_2_half(pair.core)
    r_in2.prepare(4)
    r_in2.step(4)
    toks.tick()
    s_m2.far()
    reduce_2_grad[...] = dot_tn(x_small[...].reshape(size * few, total), grad_pre_2[...]).astype(BF16)
    s_r2.core()
    r_in2.prepare(ring.reach + 1)
    toks.tick()
    quarter = 0.25 * (r_in2.finish() + grad_rows[...])
    low_1[...] = quarter.astype(BF16)
    grad_branch = dot_full(spread[...], times_expand_back(low_1[...], held_1))
    value, gain_grad, shift_grad = norm_back(
        grad_branch, normed_1[...], inv_1[:, 0:1], gain_a, shift_a
    )
    mix_1[...] = stack(value.astype(BF16), total // 2)
    g_mix1 = Gather(ring, mix_1, mix_1_full, near, row_halves(2 * share), send.at[14], recv.at[0])
    g_mix1.start()
    mix_1_full[ring.spot] = mix_1[...]
    toks.rest()
    s_r2.far()
    vec_grad[0:1, :] = gain_grad
    vec_grad[1:2, :] = shift_grad
    grad_out[...] = dot_full(spread[...], quarter)
    a_low1 = send_columns(
        ring, branch_1, branch_1_full, ring.spot, all_send.at[1], all_recv.at[1]
    )
    a_vec = send_columns(ring, vec_grad, vec_held, ring.me, all_send.at[2], all_recv.at[2])

    def back_1(spot):
        half = total // 2
        product_1[...] = dot_nt(mix_1_full[spot, 0:share], mixer[:, 0:half])
        product_1[...] += dot_nt(mix_1_full[spot, share : 2 * share], mixer[:, half:total])
        chunk_back(image_1, product_1, spot, 6, side, side)

    l_mixer[2].wait()
    back_1(ring.spot)
    low_1_full[ring.spot] = low_1[...]
    g_low1 = Gather(ring, low_1, low_1_full, near, wide, send.at[15], recv.at[3])
    for step in range(1, ring.reach + 1):
        g_mix1.move(step)
        if step == 1:
            r_tok.prepare(ring.reach + 1)
            tokens[...] = (unstack(r_tok.finish(), count) * live).astype(BF16)
            r_tok.drain()
        for spot in g_mix1.spots(step):
            back_1(spot)
        if step == 2:
            for copy in a_low2:
                copy.wait()
            expand_part(expand_2_grad, branch_2_full, low_2_full)
            s_e2.core()
            s_out.arrive()
            for j in range(2):
                l_wide[j].wait()
                s_out.block(j)
                l_wide[j + 2].start()
        if step == 3:
            s_e2.far()
            for j in range(2, 4):
                l_wide[j].wait()
                s_out.block(j)
            s_out.back()
    g_low1.start()
    grad_hidden = image_1[:, 1 : 1 + side, 8 : 8 + side, :].reshape(pre_1.shape)
    grad_pre_1[...] = (grad_hidden * silu_slope(pre_1[...])).astype(BF16)

    def in_term(spot):
        at = pl.ds(pl.multiple_of(ring.index(spot) * chans, chans), chans)
        return dot_nt(grad_pre_1[...], reduce_1[at, :])

    def in_rows(spot, terms):
        at = pl.ds(pl.multiple_of(ring.index(spot) * chans, chans), chans)
        terms[mine, :] += grad_out[:, at]

    r_in1 = Scatter(ring, in_term, big, terms_big, tall, send.at[16], recv.at[1], in_rows)
    r_in1.start()
    r_in1.prepare(2)
    mixer_1_quarter(pair.other, 0)
    s_m1a.core()
    mixer_1_quarter(pair.core, 0)
    s_m1a.far()
    mixer_1_quarter(pair.other, 1)
    s_m1b.core()
    r_in1.step(2)
    mixer_1_quarter(pair.core, 1)
    s_m1b.far()
    g_low1.move(1)
    r_in1.prepare(3)
    r_in1.step(3)
    g_low1.move(2)

    def reduces(m, carry):
        at = pl.ds(pl.multiple_of(m * chans, chans), chans)
        reduce_1_grad[at, :] = dot_tn(x_full[m], grad_pre_1[...]).astype(BF16)
        return carry

    lax.fori_loop(0, size, reduces, 0)
    s_r1.core()
    r_in1.prepare(4)
    r_in1.step(4)
    g_low1.move(3)
    s_r1.far()
    for copy in a_vec:
        copy.wait()
    vec_part[0] = jnp.sum(vec_held[...], axis=0)
    v_core = pair.copy(pair.twin, vec_part.at[0], vec_part.at[1], vec_send.at[0], vec_recv.at[0])
    v_core.start()
    g_low1.move(ring.reach)
    for copy in a_low1:
        copy.wait()
    expand_part(expand_1_grad, branch_1_full, low_1_full)
    s_e1.core()
    v_core.wait()
    vec_part[2] = vec_part[0] + vec_part[1]
    v_far = pair.copy(pair.far, vec_part.at[2], vec_part.at[3], vec_send.at[1], vec_recv.at[1])
    v_far.start()
    r_in1.prepare(ring.reach + 1)
    s_e1.far()
    s_in.back()
    s_m2.back()
    s_r2.back()
    s_e2.back()
    patch_grads[...] = r_in1.finish()
    v_far.wait()
    vec_sum[...] = vec_part[2] + vec_part[3]
    s_m1a.back()
    s_m1b.back()
    s_r1.back()
    s_e1.back()
    for item in (s_out, s_in, s_m2, s_r2, s_e2, s_m1a, s_m1b, s_r1, s_e1):
        item.done()
    for item in (gx, gv, e1, e2, g_mix2, g_low2, r_in2, g_mix1, g_low1, r_in1):
        item.drain()
    in_copy.wait_send()


def widen_kernel(*refs):
    ins, outs = refs[:11], refs[11:]
    for src, dst in zip(ins[:10], outs[:10]):
        dst[...] = src[...].astype(dst.dtype)
    for k in range(4):
        outs[10 + k][...] = ins[10][k : k + 1, :]


def kernel_call(kernel, name, number, in_specs, outs, out_specs, scratch, flops=0):
    def run(*args):
        return pl.pallas_call(
            kernel,
            name=name,
            out_shape=outs,
            in_specs=in_specs,
            out_specs=out_specs,
            scratch_shapes=scratch,
            cost_estimate=pl.CostEstimate(flops=flops, bytes_accessed=0, transcendentals=0),
            compiler_params=pltpu.CompilerParams(
                collective_id=number, has_side_effects=True, vmem_limit_bytes=VMEM_LIMIT
            ),
        )(*args)

    return run


def fast_body(
    size,
    patches,
    first_reduce,
    first_mixer,
    first_expand,
    first_gain,
    first_shift,
    second_reduce,
    second_mixer,
    second_expand,
    second_gain,
    second_shift,
    readout_in,
    readout_out,
    cotangent,
    live_counts,
):
    S = jax.ShapeDtypeStruct
    V = pltpu.VMEM
    near = pl.BlockSpec(memory_space=pltpu.VMEM)
    scalar = pl.BlockSpec(memory_space=pltpu.SMEM)
    away = pl.BlockSpec(memory_space=pl.ANY)
    grids, side, _, chans = patches.shape
    total = first_expand.shape[1]
    rows = grids * side * side
    share = rows // size
    small = side // 2
    few = 3 * ROW_PAD
    few_rows = few * size
    token_rows = grids * small * small
    part = readout_in.shape[1]
    wide = readout_out.shape[1]
    reach = size // 2
    pool = pool_places(side)
    places = token_places(grids, small).astype(BF16)
    x = patches.reshape(rows, chans)
    mixer_1 = first_mixer.reshape(9 * chans, total)
    mixer_2 = second_mixer.reshape(9 * chans, total)
    vectors = [v.reshape(1, chans) for v in (first_gain, first_shift, second_gain, second_shift)]

    held = ((4, size, chans, total // 4), BF16)
    x_small = ((size, few, total), BF16)
    mixer = ((9 * chans, total), BF16)
    sums = [
        ((part, wide), True),
        ((total, part), True),
        ((9 * chans, total), False),
        ((total, chans), True),
        ((chans, total), False),
        ((9 * chans, total), False),
        ((total, chans), True),
        ((chans, total), False),
    ]
    outs = [
        (S((rows, chans), F32), near),
        (S((token_rows, part), BF16), near),
        (S((8, chans), F32), near),
        (S((size // 2, 4, token_rows, part), BF16), away),
    ]
    outs += [(S(shape, BF16), away) for shape, _ in sums]

    def half(shape, by_rows):
        return (shape[0] // 2, shape[1]) if by_rows else (shape[0], shape[1] // 2)

    scratch = [
        V((size, rows, chans), BF16),
        V((total, chans), BF16),
        V((total, chans), BF16),
        V(*mixer),
        V((total, part), BF16),
        V((part, wide), BF16),
        V((16, chans), F32),
        V((size, 16, chans), F32),
        V((rows, chans), F32),
        V((size, share, 9 * chans), BF16),
        V((grids, side + 2, side + 16, chans), F32),
        V(*held),
        V(*held),
        V((share, total), F32),
        V((share, 128), F32),
        V((few, total), BF16),
        V((few, total), F32),
        V((2, few, total), BF16),
        V(*x_small),
        V((few_rows, chans), F32),
        V((size, few, 9 * chans), BF16),
        V((grids, small + 2, ROW_PAD + 16, chans), F32),
        V((few, total), F32),
        V((few, 128), F32),
        V((few, total), BF16),
        V(*x_small),
        V((size, token_rows, part), BF16),
        V((token_rows, part), F32),
        V((token_rows, part), BF16),
        V((token_rows, part), F32),
        V((few_rows, part), BF16),
        V((few, total), F32),
        V((size, few, total), F32),
        V((2, size, rows, chans), BF16),
        V((2, rows, chans), F32),
        V((2, size, few, total), BF16),
        V((2, few, total), F32),
        V((2, 4, token_rows, part), BF16),
        V((4, token_rows, part), BF16),
        V((part, wide // 2), BF16),
        V((total, part), BF16),
        V(half(*sums[1]), BF16),
        V(half(*sums[1]), BF16),
    ]
    for k, (shape, by_rows) in enumerate(sums[2:]):
        if k == 3:
            scratch += [V(shape, BF16)] + [V((shape[0], shape[1] // 4), BF16)] * 4
        else:
            scratch += [V(shape, BF16)] + [V(half(shape, by_rows), BF16)] * 2
    scratch += [
        V((share, 9 * chans), F32),
        V((few, total), BF16),
        V((few, total), BF16),
        V((2 * share, total // 2), BF16),
        V(*x_small),
        V(*x_small),
        V((size, few, chans), BF16),
        V((size, few, chans), BF16),
        V((few_rows, chans), BF16),
        V((rows, chans), BF16),
        V((share, total), F32),
        V((8, total), F32),
        V((size, 8, chans), F32),
        V((4, 8, chans), F32),
        DMA((17,)),
        DMA((5, 2, reach, 2)),
        DMA((2, reach, 6)),
        DMA((2, reach, 4)),
        DMA((2, 3)),
        DMA((2, 3)),
        DMA((1,)),
        DMA((1,)),
        DMA((size,)),
        DMA((3, size // 2)),
        DMA((size // 2,)),
        DMA((size // 2,)),
        DMA((3, size - 1)),
        DMA((3, size - 1)),
        DMA((9, 3)),
        DMA((9, 3)),
        DMA((9,)),
        DMA((2,)),
        DMA((2,)),
        DMA((4,)),
        DMA((4,)),
        DMA((11,)),
    ]
    patch_grads, tokens, vec_sum, _, *grads = kernel_call(
        functools.partial(layer_kernel, size, grids, side),
        "layer",
        1,
        [near] * 7 + [scalar] + [away] * 10,
        [shape for shape, _ in outs],
        [spec for _, spec in outs],
        scratch,
    )(
        *vectors, pool, np.ascontiguousarray(4.0 * pool.T), places, live_counts, x, first_reduce, first_expand,
        second_expand, mixer_1, second_reduce, mixer_2, readout_in, readout_out, cotangent,
    )
    tall = [(rows, chans, F32)] + [shape + (BF16,) for shape, _ in sums]
    blocks = [pl.BlockSpec((r // 4, c), lambda k: (k, 0)) for r, c, _ in tall]
    blocks += [pl.BlockSpec(tokens.shape, lambda k: (0, 0)), pl.BlockSpec(vec_sum.shape, lambda k: (0, 0))]
    one = pl.BlockSpec((1, chans), lambda k: (0, 0))
    (
        patch_grads, out_g, in_g, mixer_2_g, reduce_2_g, expand_2_g, mixer_1_g, reduce_1_g, expand_1_g, tokens,
        gain_1_g, shift_1_g, gain_2_g, shift_2_g,
    ) = pl.pallas_call(
        widen_kernel,
        name="widen",
        grid=(4,),
        in_specs=blocks,
        out_shape=[S((r, c), F32) for r, c, _ in tall] + [S(tokens.shape, BF16)] + [S((1, chans), F32)] * 4,
        out_specs=blocks[:-1] + [one] * 4,
        compiler_params=pltpu.CompilerParams(vmem_limit_bytes=VMEM_LIMIT),
    )(patch_grads, *grads, tokens, vec_sum)
    return (
        tokens,
        patch_grads.reshape(patches.shape),
        reduce_1_g,
        mixer_1_g.reshape(first_mixer.shape),
        expand_1_g,
        gain_1_g.reshape(chans),
        shift_1_g.reshape(chans),
        reduce_2_g,
        mixer_2_g.reshape(second_mixer.shape),
        expand_2_g,
        gain_2_g.reshape(chans),
        shift_2_g.reshape(chans),
        in_g,
        out_g,
    )


def fits(mesh, patches, first_reduce, readout_in):
    size, groups = mesh.shape["mp"], mesh.shape["dp"]
    grids, side, _, chans = patches.shape
    return (
        groups == 4
        and size % 2 == 0
        and chans % 128 == 0
        and readout_in.shape[1] % 128 == 0
        and grids * side == 6 * size
        and side % 8 == 0
        and side // 2 <= ROW_PAD
    )


def solution(mesh):
    in_specs = (
        P("dp", None, None, "mp"),
        P(None, "mp"),
        P(None, None, "mp", None),
        P("mp", None),
        P("mp"),
        P("mp"),
        P(None, "mp"),
        P(None, None, "mp", None),
        P("mp", None),
        P("mp"),
        P("mp"),
        P(None, "mp"),
        P("mp", None),
        P("dp", "mp"),
        P("dp"),
    )
    out_specs = (
        P("dp", "mp"),
        P("dp", None, None, "mp"),
        P(None, "mp"),
        P(None, None, "mp", None),
        P("mp", None),
        P("mp"),
        P("mp"),
        P(None, "mp"),
        P(None, None, "mp", None),
        P("mp", None),
        P("mp"),
        P("mp"),
        P(None, "mp"),
        P("mp", None),
    )

    def local(*args):
        if fits(mesh, args[0], args[1], args[11]):
            return fast_body(mesh.shape["mp"], *args)
        return body(*args)

    return jax.shard_map(local, mesh=mesh, in_specs=in_specs, out_specs=out_specs, check_vma=False)
```

```python
import functools

import jax
import jax.numpy as jnp
import numpy as np
from jax import lax
from jax.experimental import pallas as pl
from jax.experimental.pallas import tpu as pltpu
from jax.sharding import PartitionSpec as P

norm_eps = 1e-06


def conv_same(image, kernel):
    return lax.conv_general_dilated(
        image,
        kernel,
        (1, 1),
        "SAME",
        dimension_numbers=("NHWC", "HWIO", "NHWC"),
        preferred_element_type=jnp.float32,
    )


def silu_back(values, grad_values):
    return jax.vjp(jax.nn.silu, values)[1](grad_values)[0]


def gelu_exact(values):
    return jax.nn.gelu(values, approximate=False)


def gelu_back(values, grad_values):
    return jax.vjp(gelu_exact, values)[1](grad_values)[0]


def block_forward(inputs, reduce_w, mixer_w, expand_w, gain, shift):
    num_grids, grid_height, grid_width, local_chans = inputs.shape
    pixel_rows = num_grids * grid_height * grid_width
    low_in = inputs.astype(jnp.bfloat16).reshape(pixel_rows, local_chans)
    full_in = lax.all_gather(low_in, "mp", axis=1, tiled=True)
    total_chans = full_in.shape[1]
    pre_act = jnp.dot(full_in, reduce_w, preferred_element_type=jnp.float32)
    hidden = jax.nn.silu(pre_act).astype(jnp.bfloat16)
    partial_mix = conv_same(
        hidden.reshape(num_grids, grid_height, grid_width, local_chans), mixer_w
    )
    mixed_sum = lax.psum_scatter(
        partial_mix.reshape(pixel_rows, total_chans).astype(jnp.bfloat16),
        "mp",
        scatter_dimension=1,
        tiled=True,
    ).astype(jnp.float32)
    row_total, row_squares = lax.psum(
        (jnp.sum(mixed_sum, axis=1), jnp.sum(mixed_sum * mixed_sum, axis=1)), "mp"
    )
    center = row_total / total_chans
    inv_std = lax.rsqrt(row_squares / total_chans - center * center + norm_eps)
    normed = (mixed_sum - center[:, None]) * inv_std[:, None]
    affine = normed * gain + shift
    branch_in = jax.nn.silu(affine).astype(jnp.bfloat16)
    partial_out = jnp.dot(branch_in, expand_w, preferred_element_type=jnp.float32)
    branch_out = lax.psum_scatter(
        partial_out.astype(jnp.bfloat16), "mp", scatter_dimension=1, tiled=True
    ).astype(jnp.float32)
    outputs = inputs + branch_out.reshape(inputs.shape)
    return (outputs, (full_in, pre_act, hidden, normed, inv_std, affine, branch_in))


def block_backward(grad_out, saved, reduce_w, mixer_w, expand_w, gain):
    full_in, pre_act, hidden, normed, inv_std, affine, branch_in = saved
    num_grids, grid_height, grid_width, local_chans = grad_out.shape
    pixel_rows = num_grids * grid_height * grid_width
    grad_rows = grad_out.reshape(pixel_rows, local_chans)
    grad_branch = lax.all_gather(grad_rows.astype(jnp.bfloat16), "mp", axis=1, tiled=True)
    total_chans = grad_branch.shape[1]
    expand_grad = jnp.einsum(
        "ri,ro->io", branch_in, grad_branch, preferred_element_type=jnp.float32
    )
    grad_act = jnp.einsum("ro,io->ri", grad_branch, expand_w, preferred_element_type=jnp.float32)
    grad_affine = silu_back(affine, grad_act)
    gain_grad = jnp.sum(grad_affine * normed, axis=0)
    shift_grad = jnp.sum(grad_affine, axis=0)
    scaled = grad_affine * gain
    sum_plain, sum_normed = lax.psum(
        (jnp.sum(scaled, axis=1), jnp.sum(scaled * normed, axis=1)), "mp"
    )
    grad_mixed = inv_std[:, None] * (
        scaled - sum_plain[:, None] / total_chans - normed * sum_normed[:, None] / total_chans
    )
    mixed_full = lax.all_gather(grad_mixed.astype(jnp.bfloat16), "mp", axis=1, tiled=True)
    mixed_image = mixed_full.reshape(num_grids, grid_height, grid_width, total_chans)
    flipped = jnp.transpose(mixer_w[::-1, ::-1], (0, 1, 3, 2))
    grad_hidden = conv_same(mixed_image, flipped).reshape(pixel_rows, local_chans)
    padded = jnp.pad(
        hidden.reshape(num_grids, grid_height, grid_width, local_chans),
        ((0, 0), (1, 1), (1, 1), (0, 0)),
    )
    mixer_grad = jnp.stack(
        [
            jnp.stack(
                [
                    jnp.einsum(
                        "nhwi,nhwo->io",
                        padded[
                            :,
                            offset_h : offset_h + grid_height,
                            offset_w : offset_w + grid_width,
                            :,
                        ],
                        mixed_image,
                        preferred_element_type=jnp.float32,
                    )
                    for offset_w in range(3)
                ]
            )
            for offset_h in range(3)
        ]
    )
    grad_pre = silu_back(pre_act, grad_hidden).astype(jnp.bfloat16)
    reduce_grad = jnp.einsum("ri,ro->io", full_in, grad_pre, preferred_element_type=jnp.float32)
    partial_in = jnp.einsum("ro,io->ri", grad_pre, reduce_w, preferred_element_type=jnp.float32)
    grad_in = (
        lax.psum_scatter(
            partial_in.astype(jnp.bfloat16), "mp", scatter_dimension=1, tiled=True
        ).astype(jnp.float32)
        + grad_rows
    )
    return (
        grad_in.reshape(grad_out.shape),
        (reduce_grad, mixer_grad, expand_grad, gain_grad, shift_grad),
    )


def body(
    patches,
    first_reduce,
    first_mixer,
    first_expand,
    first_gain,
    first_shift,
    second_reduce,
    second_mixer,
    second_expand,
    second_gain,
    second_shift,
    readout_in,
    readout_out,
    cotangent,
    live_counts,
):
    num_grids, grid_height, grid_width, local_chans = patches.shape
    pooled_side = grid_height // 2
    patch_values = patches.astype(jnp.float32)
    first_out = block_forward(
        patch_values, first_reduce, first_mixer, first_expand, first_gain, first_shift
    )[0]
    pooled = first_out.reshape(num_grids, pooled_side, 2, pooled_side, 2, local_chans).mean(
        axis=(2, 4)
    )
    second_out = block_forward(
        pooled, second_reduce, second_mixer, second_expand, second_gain, second_shift
    )[0]
    token_count = num_grids * pooled_side * pooled_side
    flat = second_out.astype(jnp.bfloat16).reshape(token_count, local_chans)
    flat_full = lax.all_gather(flat, "mp", axis=1, tiled=True)
    lifted = jnp.dot(flat_full, readout_in, preferred_element_type=jnp.float32)
    activated = gelu_exact(lifted).astype(jnp.bfloat16)
    partial_tokens = jnp.dot(activated, readout_out, preferred_element_type=jnp.float32)
    summed = lax.psum_scatter(
        partial_tokens.astype(jnp.bfloat16), "mp", scatter_dimension=1, tiled=True
    ).astype(jnp.float32)
    live_slots = (jnp.arange(num_grids) < live_counts[0]).astype(jnp.float32)
    live_rows = jnp.repeat(live_slots, pooled_side * pooled_side)
    tokens = (summed * live_rows[:, None]).astype(jnp.bfloat16)
    grad_tokens = cotangent * live_rows[:, None].astype(jnp.bfloat16)
    grad_full = lax.all_gather(grad_tokens, "mp", axis=1, tiled=True)
    readout_out_grad = jnp.einsum(
        "ri,ro->io", activated, grad_full, preferred_element_type=jnp.float32
    )
    grad_act = jnp.einsum("ro,io->ri", grad_full, readout_out, preferred_element_type=jnp.float32)
    grad_lift = gelu_back(lifted, grad_act).astype(jnp.bfloat16)
    readout_in_grad = jnp.einsum(
        "ri,ro->io", flat_full, grad_lift, preferred_element_type=jnp.float32
    )
    partial_flat = jnp.einsum(
        "ro,io->ri", grad_lift, readout_in, preferred_element_type=jnp.float32
    )
    grad_flat = lax.psum_scatter(
        partial_flat.astype(jnp.bfloat16), "mp", scatter_dimension=1, tiled=True
    ).astype(jnp.float32)
    second_saved = block_forward(
        pooled, second_reduce, second_mixer, second_expand, second_gain, second_shift
    )[1]
    grad_pooled, second_grads = block_backward(
        grad_flat.reshape(num_grids, pooled_side, pooled_side, local_chans),
        second_saved,
        second_reduce,
        second_mixer,
        second_expand,
        second_gain,
    )
    spread_back = jnp.broadcast_to(
        0.25 * grad_pooled[:, :, None, :, None, :],
        (num_grids, pooled_side, 2, pooled_side, 2, local_chans),
    ).reshape(patches.shape)
    first_saved = block_forward(
        patch_values, first_reduce, first_mixer, first_expand, first_gain, first_shift
    )[1]
    patch_grads, first_grads = block_backward(
        spread_back, first_saved, first_reduce, first_mixer, first_expand, first_gain
    )
    summed_grads = (
        lax.psum(first_grads[0].astype(jnp.bfloat16), "dp").astype(jnp.float32),
        lax.psum(first_grads[1].astype(jnp.bfloat16), "dp").astype(jnp.float32),
        lax.psum(first_grads[2].astype(jnp.bfloat16), "dp").astype(jnp.float32),
        lax.psum(first_grads[3].astype(jnp.bfloat16), "dp").astype(jnp.float32),
        lax.psum(first_grads[4].astype(jnp.bfloat16), "dp").astype(jnp.float32),
        lax.psum(second_grads[0].astype(jnp.bfloat16), "dp").astype(jnp.float32),
        lax.psum(second_grads[1].astype(jnp.bfloat16), "dp").astype(jnp.float32),
        lax.psum(second_grads[2].astype(jnp.bfloat16), "dp").astype(jnp.float32),
        lax.psum(second_grads[3].astype(jnp.bfloat16), "dp").astype(jnp.float32),
        lax.psum(second_grads[4].astype(jnp.bfloat16), "dp").astype(jnp.float32),
        lax.psum(readout_in_grad.astype(jnp.bfloat16), "dp").astype(jnp.float32),
        lax.psum(readout_out_grad.astype(jnp.bfloat16), "dp").astype(jnp.float32),
    )
    return (
        tokens,
        patch_grads,
        summed_grads[0],
        summed_grads[1],
        summed_grads[2],
        summed_grads[3],
        summed_grads[4],
        summed_grads[5],
        summed_grads[6],
        summed_grads[7],
        summed_grads[8],
        summed_grads[9],
        summed_grads[10],
        summed_grads[11],
    )


MESH = pl.DeviceIdType.MESH
F32 = jnp.float32
BF16 = jnp.bfloat16
DMA = pltpu.SemaphoreType.DMA
VMEM_LIMIT = 63 * 2**20
ROW_PAD = 16


def dot_nn(a, b):
    return lax.dot_general(a, b, (((1,), (0,)), ((), ())), preferred_element_type=F32)


def dot_nt(a, b):
    return lax.dot_general(a, b, (((1,), (1,)), ((), ())), preferred_element_type=F32)


def dot_tn(a, b):
    return lax.dot_general(a, b, (((0,), (0,)), ((), ())), preferred_element_type=F32)


def dot_full(a, b):
    return lax.dot_general(
        a,
        b,
        (((1,), (0,)), ((), ())),
        precision=lax.Precision.HIGHEST,
        preferred_element_type=F32,
    )


def sigmoid(values):
    return 1.0 / (1.0 + jnp.exp(-values))


def silu(values):
    return values * sigmoid(values)


def silu_slope(values):
    gate = sigmoid(values)
    return gate * (1.0 + values * (1.0 - gate))


class Ring:
    def __init__(self, size):
        self.size = size
        self.reach = size // 2
        self.me = lax.axis_index("mp")
        half = self.me // 2
        self.spot = jnp.where(self.me % 2 == 0, half, size - 1 - half)
        self.right = self.index(self.spot + 1)
        self.left = self.index(self.spot - 1)

    def wrap(self, spot):
        return lax.rem(spot + 2 * self.size, self.size)

    def index(self, spot):
        spot = self.wrap(spot)
        return jnp.where(spot < self.reach, 2 * spot, 2 * (self.size - 1 - spot) + 1)

    def greet(self):
        barrier = pltpu.get_barrier_semaphore()
        for peer in (self.left, self.right):
            pl.semaphore_signal(barrier, inc=1, device_id={"mp": peer}, device_id_type=MESH)
        pl.semaphore_wait(barrier, 2)

    def copy(self, side, src, dst, send, recv):
        peer = self.right if side == 0 else self.left
        return pltpu.make_async_remote_copy(
            src_ref=src,
            dst_ref=dst,
            send_sem=send,
            recv_sem=recv,
            device_id={"mp": peer},
            device_id_type=MESH,
        )


def wait_bytes(like, sem):
    pltpu.make_async_copy(like, like, sem).wait()


class Gather:
    def __init__(self, ring, own, held, slot, lanes, send, recv):
        self.ring, self.own, self.held, self.slot = ring, own, held, slot
        self.lanes, self.send, self.recv, self.copies = lanes, send, recv, {}

    def _start(self, side, step, lane):
        ring = self.ring
        if step == ring.reach and lane // (len(self.lanes) // 2) != side:
            return
        away = step - 1
        spot = ring.wrap(ring.spot - away if side == 0 else ring.spot + away)
        dst = self.held.at[self.slot(spot)]
        src = self.own if step == 1 else dst
        at = self.lanes[lane]
        copy = ring.copy(
            side, src.at[at], dst.at[at], self.send, self.recv.at[side, step - 1, lane]
        )
        copy.start()
        self.copies[side, step, lane] = copy

    def move_lane(self, step, lane):
        for side in range(2):
            if step == 0:
                self._start(side, 1, lane)
            elif (side, step, lane) in self.copies:
                self.copies[side, step, lane].wait_recv()
                if step < self.ring.reach:
                    self._start(side, step + 1, lane)

    def start(self):
        self.move(0)

    def move(self, step, after=None):
        for lane in range(len(self.lanes)):
            self.move_lane(step, lane)
            if after is not None:
                after()

    def drain(self):
        wait_bytes(self.held.at[pl.ds(0, self.ring.size - 1)], self.send)

    def spots(self, step):
        ring = self.ring
        if step == ring.reach:
            return [ring.wrap(ring.spot + step)]
        return [ring.wrap(ring.spot - step), ring.wrap(ring.spot + step)]


class Scatter:
    def __init__(self, ring, term, boxes, terms, lanes, send, recv, extra=None):
        self.ring, self.term, self.out, self.inbox = ring, term, boxes[0], boxes[1]
        self.extra = extra
        self.terms, self.lanes, self.send, self.recv, self.copies = terms, lanes, send, recv, {}

    def place(self, side, step):
        return side * self.ring.reach + step - 1

    def _start(self, side, step, lane):
        at, place = self.lanes[lane], self.place(side, step)
        src, dst = self.out.at[place], self.inbox.at[place]
        copy = self.ring.copy(
            side, src.at[at], dst.at[at], self.send, self.recv.at[side, step - 1, lane]
        )
        copy.start()
        self.copies[side, step, lane] = copy

    def _fill(self, k, spot):
        self.terms[k] = self.term(spot)
        if self.extra is not None:
            self.extra(spot, self.terms.at[k])

    def start(self):
        ring, count = self.ring, len(self.lanes)
        self._fill(0, ring.wrap(ring.spot + ring.reach))
        for lane in range(count):
            side = lane // (count // 2)
            at = self.lanes[lane]
            self.out[(self.place(side, 1),) + at] = self.terms[(0,) + at].astype(BF16)
            self._start(side, 1, lane)

    def prepare(self, step, send=True):
        ring = self.ring
        away = ring.reach + 1 - step
        self._fill(0, ring.wrap(ring.spot + away))
        if away > 0:
            self._fill(1, ring.wrap(ring.spot - away))
        if step == 2 and send:
            for k in range(len(self.lanes) // 2):
                self.step_lane(2, k)

    def step_lane(self, step, k):
        count = len(self.lanes)
        for side in range(2):
            lane = (k + count // 2) % count if side == 0 else k
            at = self.lanes[lane]
            value = self.terms[(side,) + at]
            if (side, step - 1, lane) in self.copies:
                self.copies[side, step - 1, lane].wait_recv()
                value = value + self.inbox[(self.place(side, step - 1),) + at].astype(F32)
            self.out[(self.place(side, step),) + at] = value.astype(BF16)
            self._start(side, step, lane)

    def step(self, step, after=None):
        count = len(self.lanes)
        for k in range(count // 2 if step == 2 else 0, count):
            self.step_lane(step, k)
            if after is not None:
                after()

    def finish(self):
        reach = self.ring.reach
        for lane in range(len(self.lanes)):
            for side in range(2):
                self.copies[side, reach, lane].wait_recv()
        return (
            self.terms[0]
            + self.inbox[self.place(0, reach)].astype(F32)
            + self.inbox[self.place(1, reach)].astype(F32)
        )

    def drain(self):
        wait_bytes(self.out.at[pl.ds(0, self.ring.size - 1)], self.send)


class Later:
    def __init__(self):
        self.steps = []

    def add(self, step, *args):
        self.steps.append((step, args))

    def tick(self, count=1):
        for _ in range(min(count, len(self.steps))):
            step, args = self.steps.pop(0)
            step(*args)

    def rest(self):
        self.tick(len(self.steps))


def row_halves(rows):
    return ((pl.ds(0, rows // 2),), (pl.ds(rows // 2, rows // 2),))


def column_halves(columns):
    every = slice(None)
    return (
        (every, pl.ds(0, columns // 2)),
        (every, pl.ds(columns // 2, columns // 2)),
    )


def pool_places(side):
    small = side // 2
    place = np.zeros((3 * ROW_PAD, 6 * side), np.float32)
    for row in range(6):
        for column in range(side):
            place[(row // 2) * ROW_PAD + column // 2, row * side + column] = 0.25
    assert small <= ROW_PAD
    return place


def token_places(grids, small):
    place = np.zeros((grids * small * small, grids * small * ROW_PAD), np.float32)
    for line in range(grids * small):
        for column in range(small):
            place[line * small + column, line * ROW_PAD + column] = 1.0
    return place


def norm_rows(mixed, gain, shift):
    center = jnp.mean(mixed, axis=1, keepdims=True)
    apart = mixed - center
    inv_std = lax.rsqrt(jnp.mean(apart * apart, axis=1, keepdims=True) + norm_eps)
    normed = apart * inv_std
    return normed, inv_std, normed * gain + shift


def wide_vector(held, row):
    return jnp.concatenate([held[m, row : row + 1, :] for m in range(held.shape[0])], axis=1)


def half_of(rows, columns, which, by_rows):
    if by_rows:
        return (pl.ds(pl.multiple_of(which * (rows // 2), 16), rows // 2), slice(None))
    return (slice(None), pl.ds(pl.multiple_of(which * (columns // 2), 128), columns // 2))


class Pair:
    def __init__(self):
        self.me = lax.axis_index("dp")
        self.core = lax.rem(self.me, 2)
        self.other = 1 - self.core
        self.twin = self.me - self.core + self.other
        self.far = lax.rem(self.me + 2, 4)
        self.across = lax.rem(self.twin + 2, 4)

    def copy(self, peer, src, dst, send, recv):
        return pltpu.make_async_remote_copy(
            src_ref=src,
            dst_ref=dst,
            send_sem=send,
            recv_sem=recv,
            device_id={"dp": peer},
            device_id_type=MESH,
        )


class Share:
    def __init__(self, ring, pair, blocks, held, send, recv, twin_send, local):
        self.ring, self.pair, self.blocks, self.held = ring, pair, blocks, held
        self.send, self.recv, self.twin_send, self.local = send, recv, twin_send, local
        self.copies = []

    def go(self, spot):
        pair, half = self.pair, self.ring.size // 2
        m = self.ring.index(spot)
        same = m // half == pair.core
        j = lax.rem(m, half)
        src, dst = self.blocks.at[m], self.held.at[j, pair.me]
        peer = jnp.where(same, pair.far, pair.across)
        sem = self.recv.at[jnp.where(same, 0, 1), j]
        copy = pair.copy(peer, src, dst, self.send.at[len(self.copies)], sem)
        copy.start()
        self.copies.append(copy)

        @pl.when(same)
        def _():
            pltpu.make_async_copy(src, dst, self.local.at[j]).start()

        @pl.when(jnp.logical_not(same))
        def _():
            pair.copy(pair.twin, src, dst, self.twin_send.at[j], self.recv.at[2, j]).start()

    def drain(self):
        pair = self.pair
        for copy in self.copies:
            copy.wait_send()
        for j in range(self.ring.size // 2):
            src, dst = self.blocks.at[j], self.held.at[j, pair.me]
            pltpu.make_async_copy(src, dst, self.local.at[j]).wait()
            pair.copy(pair.twin, src, dst, self.twin_send.at[j], self.recv.at[2, j]).wait()
            for kind, peer in enumerate((pair.far, pair.across)):
                dst = self.held.at[j, peer]
                pair.copy(peer, src, dst, self.send.at[0], self.recv.at[kind, j]).wait_recv()


class Expand:
    def __init__(self, ring, pair, own, held, send, recv, psend, precv, load):
        self.ring, self.pair, self.held = ring, pair, held
        self.psend, self.precv, self.copies = psend, precv, []
        chans, quarter = held.shape[2:]
        columns = own.at[:, pl.ds(pl.multiple_of(pair.me * quarter, 128), quarter)]
        self.load = pltpu.make_async_copy(columns, held.at[pair.me, ring.me], load)
        self.load.start()
        self.gather = Gather(
            ring, held.at[pair.me, ring.me], held.at[pair.me], ring.index, row_halves(chans), send, recv
        )

    def across(self):
        self._swap(0, self.pair.far, self.pair.me)

    def between(self):
        self.copies[0].wait_recv()
        self._swap(1, self.pair.twin, self.pair.me)
        self._swap(2, self.pair.twin, self.pair.far)

    def _swap(self, k, peer, quarter):
        at = self.held.at[quarter]
        copy = self.pair.copy(peer, at, at, self.psend.at[k], self.precv.at[k])
        copy.start()
        self.copies.append(copy)

    def ready(self):
        for copy in self.copies[1:]:
            copy.wait_recv()

    def drain(self):
        self.gather.drain()
        for copy in self.copies:
            copy.wait_send()


def times_expand(rows, held):
    parts = []
    for k in range(held.shape[0]):
        weight = held[k].reshape(rows.shape[1], held.shape[3])
        parts.append(dot_nn(rows, weight))
    return jnp.concatenate(parts, axis=1)


def times_expand_back(rows, held):
    quarter = held.shape[3]
    total = None
    for k in range(held.shape[0]):
        weight = held[k].reshape(held.shape[1] * held.shape[2], quarter)
        part = dot_nt(rows[:, k * quarter : (k + 1) * quarter], weight)
        total = part if total is None else total + part
    return total


def chunk_taps(image, taps, spot, lines, side, width):
    chans = image.shape[-1]
    per_grid = side // lines
    grid, line = spot // per_grid, lax.rem(spot, per_grid) * lines
    for kh in range(3):
        for kw in range(3):
            piece = image[grid, pl.ds(line + kh, lines), 7 + kw : 7 + kw + width, :]
            at = (kh * 3 + kw) * chans
            taps[spot, :, at : at + chans] = piece.reshape(lines * width, chans).astype(BF16)


def chunk_back(image, product, spot, lines, side, width):
    chans = image.shape[-1]
    per_grid = side // lines
    grid, line = spot // per_grid, lax.rem(spot, per_grid) * lines
    for kh in range(3):
        for kw in range(3):
            at = (kh * 3 + kw) * chans
            piece = product[:, at : at + chans].reshape(lines, width, chans)
            image[grid, pl.ds(line + kh, lines), 7 + kw : 7 + kw + width, :] += piece


def pack_rows(dst, src):
    columns, width = src.shape[1], dst.shape[1]
    piece = columns - width
    pad = ROW_PAD * piece // columns
    dst[...] = src[:, 0:width]
    for line in range(0, src.shape[0], ROW_PAD):
        for k in range(width // piece):
            dst[line + ROW_PAD - pad : line + ROW_PAD, k * piece : (k + 1) * piece] = src[
                line + k * pad : line + (k + 1) * pad, width:columns
            ]


def unpack_rows(dst, src):
    columns, width = dst.shape[1], src.shape[1]
    piece = columns - width
    pad = ROW_PAD * piece // columns
    dst[:, 0:width] = src[...]
    for line in range(0, src.shape[0], ROW_PAD):
        for k in range(width // piece):
            dst[line + k * pad : line + (k + 1) * pad, width:columns] = src[
                line + ROW_PAD - pad : line + ROW_PAD, k * piece : (k + 1) * piece
            ]
        dst[line + ROW_PAD - pad : line + ROW_PAD, :] = jnp.zeros((pad, columns), F32)


def all_terms(terms, value):
    terms[...] = value.reshape(terms.shape)


def norm_back(grad_branch, normed, inv_std, gain, shift):
    affine = normed * gain + shift
    grad_affine = grad_branch * silu_slope(affine)
    gain_grad = jnp.sum(grad_affine * normed, axis=0, keepdims=True)
    shift_grad = jnp.sum(grad_affine, axis=0, keepdims=True)
    scaled = grad_affine * gain
    mean_plain = jnp.mean(scaled, axis=1, keepdims=True)
    mean_normed = jnp.mean(scaled * normed, axis=1, keepdims=True)
    return inv_std * (scaled - mean_plain - normed * mean_normed), gain_grad, shift_grad

class GroupSum:
    def __init__(self, pair, mine, other, from_core, from_far, result, half, send, recv, local):
        self.pair, self.mine, self.other = pair, mine, other
        self.from_core, self.from_far = from_core, from_far
        self.result = result.at[half]
        self.send, self.recv, self.local, self.copies = send, recv, local, []

    def _go(self, k, peer, src, dst):
        copy = self.pair.copy(peer, src, dst, self.send.at[k], self.recv.at[k])
        copy.start()
        self.copies.append(copy)

    def core(self):
        self._go(0, self.pair.twin, self.other, self.from_core)

    def far(self):
        if self.from_core is not None:
            self.copies[0].wait_recv()
            self.mine[...] = (self.mine[...].astype(F32) + self.from_core[...].astype(F32)).astype(
                BF16
            )
        self._go(1, self.pair.far, self.mine, self.from_far)

    def back(self):
        self.copies[-1].wait_recv()
        self.from_far[...] = (self.mine[...].astype(F32) + self.from_far[...].astype(F32)).astype(
            BF16
        )
        self._go(2, self.pair.twin, self.from_far, self.result)
        self.kept = pltpu.make_async_copy(self.from_far, self.result, self.local)
        self.kept.start()

    def done(self):
        self.copies[-1].wait_recv()
        self.kept.wait()
        for copy in self.copies:
            copy.wait_send()


def quarter_of(grad, which):
    columns = grad.shape[1] // 4
    return pl.ds(pl.multiple_of(which * columns, 128), columns)


class OutSum:
    def __init__(self, pair, act_all, cot_wide, grad, result, send, recv, local):
        self.pair, self.act_all, self.cot_wide, self.grad = pair, act_all, cot_wide, grad
        half = half_of(*result.shape, pair.core, False)
        self.result = result.at[half]
        self.send, self.recv, self.local = send, recv, local

    def spread(self, act_live):
        pair = self.pair
        self.act_all[pair.me] = act_live
        at = self.act_all.at[pair.me]
        self.copies = []
        for k, peer in enumerate((pair.far, pair.across, pair.twin)):
            copy = pair.copy(peer, at, at, self.send.at[k], self.recv.at[k])
            copy.start()
            self.copies.append(copy)

    def arrive(self):
        for copy in self.copies:
            copy.wait_recv()

    def block(self, j):
        groups, rows, part = self.act_all.shape
        left = self.act_all[...].reshape(groups * rows, part)
        right = self.cot_wide[j % 2].reshape(groups * rows, part)
        self.grad[:, j * part : (j + 1) * part] = dot_tn(left, right).astype(BF16)

    def back(self):
        copy = self.pair.copy(
            self.pair.twin, self.grad, self.result, self.send.at[3], self.recv.at[3]
        )
        copy.start()
        self.copies.append(copy)
        self.kept = pltpu.make_async_copy(self.grad, self.result, self.local)
        self.kept.start()

    def done(self):
        self.copies[3].wait_recv()
        self.kept.wait()
        for copy in self.copies:
            copy.wait_send()


def send_columns(ring, src, held, slot, send, recv):
    chans = held.shape[-1]
    held[slot] = src[:, pl.ds(pl.multiple_of(ring.me * chans, chans), chans)]
    copies = []
    for away in range(1, ring.size):
        peer = lax.rem(ring.me + away, ring.size)
        copy = pltpu.make_async_remote_copy(
            src_ref=src.at[:, pl.ds(pl.multiple_of(peer * chans, chans), chans)],
            dst_ref=held.at[slot],
            send_sem=send.at[away - 1],
            recv_sem=recv.at[away - 1],
            device_id={"mp": peer},
            device_id_type=MESH,
        )
        copy.start()
        copies.append(copy)
    return copies


def stack(value, columns):
    width = value.shape[1]
    return jnp.concatenate([value[:, k : k + columns] for k in range(0, width, columns)], axis=0)


def unstack(value, rows):
    return jnp.concatenate([value[k : k + rows] for k in range(0, value.shape[0], rows)], axis=1)


def layer_kernel(
    size, grids, side,
    gain_1, shift_1, gain_2, shift_2, pool, spread, places, counts,
    x, reduce_1_any, expand_1, expand_2, mixer_1_any, reduce_2_any, mixer_2_any, readout_in_any, readout_out_any,
    cotangent,
    patch_grads, tokens, vec_sum, cot_wide_any, out_sum, in_sum, mixer_2_sum, reduce_2_sum, expand_2_sum,
    mixer_1_sum, reduce_1_sum, expand_1_sum,
    x_full, reduce_1, reduce_2, mixer, readout_in, readout, vectors, vec_full, pre_1, taps_1, image_1, held_1, held_2,
    normed_1, inv_1, branch_1, pooled, low, x_small, pre_2, taps_2, image_2, normed_2, inv_2, branch_2,
    flat_full, cot_full, lifted, act, grad_lift, terms_all,
    boxes_big, terms_big, boxes_small, terms_small,
    cot_wide, act_all, out_grad, in_grad, in_core, in_far,
    mixer_2_grad, mixer_2_core, mixer_2_far, reduce_2_grad, reduce_2_core, reduce_2_far,
    expand_2_grad, expand_2_core, expand_2_far,
    mixer_1_grad, mixer_1a_core, mixer_1a_far, mixer_1b_core, mixer_1b_far, reduce_1_grad, reduce_1_core, reduce_1_far,
    expand_1_grad, expand_1_core, expand_1_far,
    product_1, low_1, packed, mix_1, mix_2_full, low_1_full, branch_2_full, branch_1_full,
    grad_pre_2, grad_pre_1, grad_out, vec_grad, vec_held, vec_part,
    send, recv, cot_recv, tok_recv, psend, precv, csend, crecv, ysend, yrecv, tsend, local, all_send, all_recv,
    sum_send, sum_recv, sum_local, vec_send, vec_recv, act_send, act_recv, load,
):
    ring, pair = Ring(size), Pair()
    rows, chans = x.shape
    share = rows // size
    total = size * chans
    small = side // 2
    few = pooled.shape[0]
    part = readout_in.shape[1]
    count = cotangent.shape[0]
    wide, tall = column_halves(total), row_halves(rows)
    near = lambda spot: spot
    big, little = (boxes_big.at[0], boxes_big.at[1]), (boxes_small.at[0], boxes_small.at[1])
    low_2_full, mix_1_full, grad_rows = flat_full, cot_full, pooled
    narrow = column_halves(packed.shape[2])
    loose = product_1.at[few : 2 * few, 0:total]
    tight = product_1.at[2 * few : 3 * few, 0 : packed.shape[2]]

    def gather_packed(value, full, send, recv):
        loose[...] = value
        pack_rows(tight, loose)
        packed[ring.spot] = tight[...].astype(BF16)
        gather = Gather(ring, packed.at[ring.spot], packed, near, narrow, send, recv)
        gather.start()
        full[ring.spot] = value.astype(BF16)
        return gather

    def unpack(full, spot):
        tight[...] = packed[spot].astype(F32)
        unpack_rows(loose, tight)
        full[spot] = loose[...].astype(BF16)

    def packed_term(spot):
        pack_rows(tight, terms_all.at[spot])
        return tight[...]

    def unpacked(value):
        tight[...] = value
        unpack_rows(loose, tight)
        return loose[...]

    def fetch(k, src, dst):
        return pltpu.make_async_copy(src, dst, load.at[k])

    l_x = fetch(0, x, x_full.at[ring.me])
    l_reduce_1 = fetch(1, reduce_1_any, reduce_1)
    l_mixer = [
        fetch(2, mixer_1_any, mixer),
        fetch(2, mixer_2_any, mixer),
        fetch(2, mixer_1_any, mixer),
    ]
    l_reduce_2 = fetch(3, reduce_2_any, reduce_2)
    l_in = fetch(4, readout_in_any, readout_in)
    l_out = fetch(5, readout_out_any, readout)
    l_cot = fetch(6, cotangent, cot_full.at[ring.me])
    l_wide = [
        fetch(7 + j % 2, cot_wide_any.at[j], cot_wide.at[j % 2]) for j in range(size // 2)
    ]
    l_x.start()
    l_reduce_1.start()
    e1 = Expand(
        ring, pair, expand_1, held_1, send.at[0], recv.at[2], psend.at[0], precv.at[0], load.at[9]
    )
    e2 = Expand(
        ring, pair, expand_2, held_2, send.at[1], recv.at[3], psend.at[1], precv.at[1], load.at[10]
    )
    barrier = pltpu.get_barrier_semaphore()
    for peer in (ring.left, ring.right):
        pl.semaphore_signal(barrier, inc=1, device_id={"mp": peer}, device_id_type=MESH)
    for peer in (pair.twin, pair.far, pair.across):
        pl.semaphore_signal(barrier, inc=1, device_id={"dp": peer}, device_id_type=MESH)
    pl.semaphore_wait(barrier, 5)
    gx = Gather(ring, x, x_full, ring.index, tall, send.at[2], recv.at[0])
    gx.start()
    for copy in (l_mixer[0], l_reduce_2, l_in, l_out, l_cot):
        copy.start()
    e1.load.wait()
    e1.gather.start()
    for k, vector in enumerate((gain_1, shift_1, gain_2, shift_2)):
        for row in (k, k + 8):
            vectors[row : row + 1, :] = vector[...]
    for k in range(4, 8):
        for row in (k, k + 8):
            vectors[row : row + 1, :] = gain_1[...]
    vec_full[ring.me] = vectors[...]
    gv = Gather(ring, vectors, vec_full, ring.index, row_halves(16), send.at[3], recv.at[4])
    gv.start()

    def add(spot):
        m = ring.index(spot)
        weight = reduce_1[pl.ds(pl.multiple_of(m * chans, chans), chans), :]
        pre_1[...] += dot_nn(x_full[m], weight)

    l_x.wait()
    l_reduce_1.wait()
    own = reduce_1[pl.ds(pl.multiple_of(ring.me * chans, chans), chans), :]
    pre_1[...] = dot_nn(x_full[ring.me], own)
    image_1[...] = jnp.zeros(image_1.shape, F32)
    image_2[...] = jnp.zeros(image_2.shape, F32)
    for step in range(1, ring.reach + 1):
        gx.move(step)
        for spot in gx.spots(step):
            add(spot)
        if step < ring.reach:
            for item in (e1.gather, gv):
                item.move(step)
    hidden = silu(pre_1[...])
    image_1[:, 1 : 1 + side, 8 : 8 + side, :] = hidden.reshape(grids, side, side, chans)
    l_mixer[0].wait()

    def mix_term(spot):
        chunk_taps(image_1, taps_1, spot, 6, side, side)
        return stack(dot_nn(taps_1[spot], mixer[...]), chans)

    rs1 = Scatter(ring, mix_term, big, terms_big, tall, send.at[4], recv.at[1])
    rs1.start()
    e1.gather.move(ring.reach)
    e1.across()
    gv.move(ring.reach)
    l_cot.wait()
    share_cot = Share(ring, pair, cot_full, cot_wide_any, ysend, yrecv, tsend, local)
    share_cot.go(ring.spot)
    for step in range(2, ring.reach + 1):
        rs1.prepare(step)
        rs1.step(step)
        if step == ring.reach - 1:
            e1.between()
    e2.load.wait()
    e2.gather.start()
    rs1.prepare(ring.reach + 1)
    l_mixer[1].start()
    mine = pl.ds(pl.multiple_of(ring.spot * share, 16), share)
    gain_a, shift_a = wide_vector(vec_full, 0), wide_vector(vec_full, 1)
    mixed = unstack(rs1.finish(), share)
    thin = [(pl.ds(k, count // 6),) for k in range(0, count, count // 6)]
    gc = Gather(
        ring, cot_full.at[ring.me], cot_full, ring.index, thin, send.at[5], cot_recv
    )

    held_back = []

    def move_cot(step, lane):
        gc.move_lane(step, lane)
        if step > 0 and lane == len(thin) - 1:
            held_back.extend(gc.spots(step))

    def share_blocks():
        while held_back:
            share_cot.go(held_back.pop(0))

    cots = Later()
    late = [(step, lane) for step in range(1, ring.reach + 1) for lane in range(2)]
    for step in range(ring.reach + 1):
        for lane in range(len(thin)):
            if len(cots.steps) >= 4 and late:
                cots.add(e2.gather.move_lane, *late.pop(0))
            cots.add(move_cot, step, lane)
    cots.tick(4)
    value, inverse, affine = norm_rows(mixed, gain_a, shift_a)
    normed_1[...] = value
    inv_1[...] = jnp.broadcast_to(inverse, inv_1.shape)
    branch = silu(affine).astype(BF16)
    e1.ready()
    x_rows = jnp.concatenate([x_full[m, mine, :].astype(F32) for m in range(size)], axis=1)
    pooled[...] = dot_full(pool[...], x_rows + times_expand(branch, held_1))
    g2 = gather_packed(pooled[...], x_small, send.at[6], recv.at[0])
    branch_1[...] = (4.0 * dot_full(pool[...], branch.astype(F32))).astype(BF16)
    rs1.drain()
    for step in range(1, ring.reach + 1):
        g2.move(step, lambda: cots.tick(2))
        for spot in g2.spots(step):
            unpack(x_small, spot)
    g2.drain()
    e2.across()
    share_blocks()
    l_reduce_2.wait()
    cots.tick(3)
    pre_2[...] = dot_nn(x_small[...].reshape(size * few, total), reduce_2[...])
    hidden = silu(pre_2[...])
    image_2[:, 1 : 1 + small, 8 : 8 + ROW_PAD, :] = hidden.reshape(grids, small, ROW_PAD, chans)
    l_mixer[1].wait()

    def taps(spot, carry):
        chunk_taps(image_2, taps_2, spot, 3, small, ROW_PAD)
        return carry

    lax.fori_loop(0, size, taps, 0)
    all_terms(terms_all, dot_nn(taps_2[...].reshape(size * few, 9 * chans), mixer[...]))
    rs2 = Scatter(ring, packed_term, little, terms_small, narrow, send.at[7], recv.at[1])
    rs2.start()
    for step in range(2, ring.reach + 1):
        rs2.prepare(step)
        rs2.step(step, cots.tick)
        share_blocks()
    rs2.prepare(ring.reach + 1)
    gain_b, shift_b = wide_vector(vec_full, 2), wide_vector(vec_full, 3)
    e2.between()
    mixed = unpacked(rs2.finish())
    cots.tick(2)
    value, inverse, affine = norm_rows(mixed, gain_b, shift_b)
    normed_2[...] = value
    inv_2[...] = jnp.broadcast_to(inverse, inv_2.shape)
    branch_2[...] = silu(affine).astype(BF16)
    e2.ready()
    value = pooled[...] + times_expand(branch_2[...], held_2)
    gf = gather_packed(value, flat_full, send.at[8], recv.at[0])
    rs2.drain()
    for step in range(1, ring.reach + 1):
        gf.move(step, cots.tick)
        share_blocks()
        for spot in gf.spots(step):
            unpack(flat_full, spot)
    gf.drain()
    l_in.wait()
    flat = dot_nn(places[...], flat_full[...].reshape(size * few, total)).astype(BF16)
    lifted[...] = dot_nn(flat, readout_in[...])
    cdf = 0.5 * (1.0 + lax.erf(lifted[...] * 0.7071067811865476))
    row_ids = lax.broadcasted_iota(jnp.int32, (count, 1), 0)
    live = (row_ids < counts[0] * (count // grids)).astype(F32)
    activated = (lifted[...] * cdf).astype(BF16)
    act[...] = activated
    slope = cdf + lifted[...] * jnp.exp(-0.5 * lifted[...] * lifted[...]) * 0.3989422804014327
    lifted[...] = slope * live
    terms_big[0] = jnp.zeros(terms_big.shape[1:], F32)
    l_out.wait()
    cots.rest()
    share_blocks()

    def back(m, carry):
        at = pl.ds(pl.multiple_of(m * part, 128), part)
        terms_big[0] += stack(dot_nt(cot_full[m], readout[:, at]), chans)
        return carry

    lax.fori_loop(0, size, back, 0)
    lift = (unstack(terms_big[0], count) * lifted[...]).astype(BF16)
    grad_lift[...] = dot_tn(places[...], lift).astype(BF16)
    all_terms(terms_all, dot_nt(grad_lift[...], readout_in[...]))
    rf = Scatter(ring, packed_term, little, terms_small, narrow, send.at[9], recv.at[1])
    rf.start()

    def token_term(spot):
        at = pl.ds(pl.multiple_of(ring.index(spot) * part, 128), part)
        return stack(dot_nn(act[...], readout[:, at]), chans)

    quarters = [(pl.ds(k, rows // 4),) for k in range(0, rows, rows // 4)]
    r_tok = Scatter(ring, token_term, big, terms_big, quarters, send.at[10], tok_recv)
    toks = Later()
    toks.add(r_tok.prepare, 2, False)
    for step in range(2, ring.reach + 1):
        if step > 2:
            toks.add(r_tok.prepare, step)
        for k in range(4):
            toks.add(r_tok.step_lane, step, k)
    rf.prepare(2)
    r_tok.start()
    in_grad[...] = dot_tn(flat, lift).astype(BF16)
    in_other = half_of(*in_grad.shape, pair.other, True)
    in_copy = pair.copy(pair.twin, in_grad.at[in_other], in_core, csend.at[0], crecv.at[0])
    in_copy.start()
    rf.step(2)
    toks.tick()
    rf.prepare(3)
    rf.step(3)
    toks.tick()
    rf.prepare(4)
    rf.step(4)
    toks.tick()
    rf.prepare(ring.reach + 1)

    def group_sum(k, mine, other, from_core, from_far, result, by_rows):
        half = half_of(*result.shape, pair.core, by_rows)
        return GroupSum(
            pair, mine, other, from_core, from_far, result, half, sum_send.at[k], sum_recv.at[k], sum_local.at[k]
        )

    def grad_sum(k, grad, from_core, from_far, result, by_rows):
        mine, other = (
            grad.at[half_of(*grad.shape, which, by_rows)] for which in (pair.core, pair.other)
        )
        return group_sum(k, mine, other, from_core, from_far, result, by_rows)

    def quarter_sum(k, which, grad, from_core, from_far, result):
        mine, other = (
            (slice(None), quarter_of(grad, 2 * core + which)) for core in (pair.core, pair.other)
        )
        return GroupSum(
            pair, grad.at[mine], grad.at[other], from_core, from_far, result, mine, sum_send.at[k], sum_recv.at[k],
            sum_local.at[k],
        )

    s_out = OutSum(pair, act_all, cot_wide, out_grad, out_sum, act_send, act_recv, sum_local.at[0])
    s_in = group_sum(1, in_core, None, None, in_far, in_sum, True)
    s_m2 = grad_sum(2, mixer_2_grad, mixer_2_core, mixer_2_far, mixer_2_sum, False)
    s_r2 = grad_sum(3, reduce_2_grad, reduce_2_core, reduce_2_far, reduce_2_sum, True)
    s_e2 = grad_sum(4, expand_2_grad, expand_2_core, expand_2_far, expand_2_sum, False)
    s_m1a = quarter_sum(5, 0, mixer_1_grad, mixer_1a_core, mixer_1a_far, mixer_1_sum)
    s_m1b = quarter_sum(8, 1, mixer_1_grad, mixer_1b_core, mixer_1b_far, mixer_1_sum)
    s_r1 = grad_sum(6, reduce_1_grad, reduce_1_core, reduce_1_far, reduce_1_sum, True)
    s_e1 = grad_sum(7, expand_1_grad, expand_1_core, expand_1_far, expand_1_sum, False)
    s_out.spread((act[...].astype(F32) * live).astype(BF16))
    grad_rows[...] = unpacked(rf.finish())
    low[...] = grad_rows[...].astype(BF16)
    value, gain_grad, shift_grad = norm_back(
        times_expand_back(low[...], held_2), normed_2[...], inv_2[:, 0:1], gain_b, shift_b
    )
    g_mix2 = gather_packed(value, mix_2_full, send.at[11], recv.at[0])
    toks.tick()
    in_copy.wait_recv()
    in_mine = in_grad[half_of(*in_grad.shape, pair.core, True)]
    in_core[...] = (in_mine.astype(F32) + in_core[...].astype(F32)).astype(BF16)
    s_in.far()
    vec_grad[...] = jnp.zeros(vec_grad.shape, F32)
    vec_grad[2:3, :] = gain_grad
    vec_grad[3:4, :] = shift_grad
    image_2[...] = jnp.zeros(image_2.shape, F32)
    image_1[...] = jnp.zeros(image_1.shape, F32)
    low_2_full[ring.spot] = low[...]
    g_low2 = Gather(ring, low, low_2_full, near, wide, send.at[12], recv.at[2])
    g_low2.start()
    a_low2 = send_columns(
        ring, branch_2, branch_2_full, ring.spot, all_send.at[0], all_recv.at[0]
    )
    rf.drain()

    def back_2(spot):
        product_1[0:few, :] = dot_nt(mix_2_full[spot], mixer[...])
        chunk_back(image_2, product_1.at[0:few], spot, 3, small, ROW_PAD)

    back_2(ring.spot)
    for step in range(1, ring.reach + 1):
        g_mix2.move(step)
        for spot in g_mix2.spots(step):
            unpack(mix_2_full, spot)
            back_2(spot)
        if step > 1:
            g_low2.move(step - 1)
        toks.tick(2 if step < 3 else 1)
    l_mixer[2].start()
    grad_hidden = image_2[:, 1 : 1 + small, 8 : 8 + ROW_PAD, :].reshape(pre_2.shape)
    grad_pre_2[...] = (grad_hidden * silu_slope(pre_2[...])).astype(BF16)
    all_terms(terms_all, dot_nt(grad_pre_2[...], reduce_2[...]))
    gc.drain()
    share_cot.drain()
    r_in2 = Scatter(ring, packed_term, little, terms_small, narrow, send.at[13], recv.at[1])
    r_in2.start()
    for k in range(2):
        l_wide[k].start()
    def mixer_part(grad, taps, right, columns):
        left = taps[...].reshape(right.shape[0], 9 * chans)
        grad[:, columns] = dot_tn(left, right).astype(BF16)

    def mixer_2_half(which):
        columns = half_of(*mixer_2_grad.shape, which, False)[1]
        right = mix_2_full[:, :, columns].reshape(size * few, total // 2)
        mixer_part(mixer_2_grad, taps_2, right, columns)

    def mixer_1_quarter(core, which):
        quarter = total // 4
        lines = pl.ds(pl.multiple_of(core * share, 16), share)
        right = mix_1_full[:, lines, which * quarter : (which + 1) * quarter]
        columns = quarter_of(mixer_1_grad, 2 * core + which)
        mixer_part(mixer_1_grad, taps_1, right.reshape(rows, quarter), columns)

    def expand_part(grad, branches, lows):
        grad[...] = dot_tn(
            branches[...].reshape(size * few, chans), lows[...].reshape(size * few, total)
        ).astype(BF16)

    r_in2.prepare(2)
    r_in2.step(2)
    toks.tick(2)
    g_low2.move(ring.reach)
    mixer_2_half(pair.other)
    s_m2.core()
    r_in2.prepare(3)
    r_in2.step(3)
    toks.tick()
    mixer_2_half(pair.core)
    r_in2.prepare(4)
    r_in2.step(4)
    toks.tick()
    s_m2.far()
    reduce_2_grad[...] = dot_tn(x_small[...].reshape(size * few, total), grad_pre_2[...]).astype(BF16)
    s_r2.core()
    r_in2.prepare(ring.reach + 1)
    toks.tick()
    quarter = 0.25 * (unpacked(r_in2.finish()) + grad_rows[...])
    low_1[...] = quarter.astype(BF16)
    grad_branch = dot_full(spread[...], times_expand_back(low_1[...], held_1))
    value, gain_grad, shift_grad = norm_back(
        grad_branch, normed_1[...], inv_1[:, 0:1], gain_a, shift_a
    )
    mix_1[...] = stack(value.astype(BF16), total // 2)
    g_mix1 = Gather(ring, mix_1, mix_1_full, near, row_halves(2 * share), send.at[14], recv.at[0])
    g_mix1.start()
    mix_1_full[ring.spot] = mix_1[...]
    toks.rest()
    s_r2.far()
    vec_grad[0:1, :] = gain_grad
    vec_grad[1:2, :] = shift_grad
    grad_out[...] = dot_full(spread[...], quarter)
    a_low1 = send_columns(
        ring, branch_1, branch_1_full, ring.spot, all_send.at[1], all_recv.at[1]
    )
    a_vec = send_columns(ring, vec_grad, vec_held, ring.me, all_send.at[2], all_recv.at[2])

    def back_1(spot):
        half = total // 2
        product_1[...] = dot_nt(mix_1_full[spot, 0:share], mixer[:, 0:half])
        product_1[...] += dot_nt(mix_1_full[spot, share : 2 * share], mixer[:, half:total])
        chunk_back(image_1, product_1, spot, 6, side, side)

    l_mixer[2].wait()
    back_1(ring.spot)
    low_1_full[ring.spot] = low_1[...]
    g_low1 = Gather(ring, low_1, low_1_full, near, wide, send.at[15], recv.at[3])
    for step in range(1, ring.reach + 1):
        g_mix1.move(step)
        if step == 1:
            r_tok.prepare(ring.reach + 1)
            tokens[...] = (unstack(r_tok.finish(), count) * live).astype(BF16)
            r_tok.drain()
        for spot in g_mix1.spots(step):
            back_1(spot)
        if step == 2:
            for copy in a_low2:
                copy.wait()
            expand_part(expand_2_grad, branch_2_full, low_2_full)
            s_e2.core()
            s_out.arrive()
            for j in range(2):
                l_wide[j].wait()
                s_out.block(j)
                l_wide[j + 2].start()
        if step == 3:
            s_e2.far()
            for j in range(2, 4):
                l_wide[j].wait()
                s_out.block(j)
            s_out.back()
    g_low1.start()
    grad_hidden = image_1[:, 1 : 1 + side, 8 : 8 + side, :].reshape(pre_1.shape)
    grad_pre_1[...] = (grad_hidden * silu_slope(pre_1[...])).astype(BF16)

    def in_term(spot):
        at = pl.ds(pl.multiple_of(ring.index(spot) * chans, chans), chans)
        return dot_nt(grad_pre_1[...], reduce_1[at, :])

    def in_rows(spot, terms):
        at = pl.ds(pl.multiple_of(ring.index(spot) * chans, chans), chans)
        terms[mine, :] += grad_out[:, at]

    r_in1 = Scatter(ring, in_term, big, terms_big, tall, send.at[16], recv.at[1], in_rows)
    r_in1.start()
    r_in1.prepare(2)
    mixer_1_quarter(pair.other, 0)
    s_m1a.core()
    mixer_1_quarter(pair.core, 0)
    s_m1a.far()
    mixer_1_quarter(pair.other, 1)
    s_m1b.core()
    r_in1.step(2)
    mixer_1_quarter(pair.core, 1)
    s_m1b.far()
    g_low1.move(1)
    r_in1.prepare(3)
    r_in1.step(3)
    g_low1.move(2)

    def reduces(m, carry):
        at = pl.ds(pl.multiple_of(m * chans, chans), chans)
        reduce_1_grad[at, :] = dot_tn(x_full[m], grad_pre_1[...]).astype(BF16)
        return carry

    lax.fori_loop(0, size, reduces, 0)
    s_r1.core()
    r_in1.prepare(4)
    r_in1.step(4)
    g_low1.move(3)
    s_r1.far()
    for copy in a_vec:
        copy.wait()
    vec_part[0] = jnp.sum(vec_held[...], axis=0)
    v_core = pair.copy(pair.twin, vec_part.at[0], vec_part.at[1], vec_send.at[0], vec_recv.at[0])
    v_core.start()
    g_low1.move(ring.reach)
    for copy in a_low1:
        copy.wait()
    expand_part(expand_1_grad, branch_1_full, low_1_full)
    s_e1.core()
    v_core.wait()
    vec_part[2] = vec_part[0] + vec_part[1]
    v_far = pair.copy(pair.far, vec_part.at[2], vec_part.at[3], vec_send.at[1], vec_recv.at[1])
    v_far.start()
    r_in1.prepare(ring.reach + 1)
    s_e1.far()
    s_in.back()
    s_m2.back()
    s_r2.back()
    s_e2.back()
    patch_grads[...] = r_in1.finish()
    v_far.wait()
    vec_sum[...] = vec_part[2] + vec_part[3]
    s_m1a.back()
    s_m1b.back()
    s_r1.back()
    s_e1.back()
    for item in (s_out, s_in, s_m2, s_r2, s_e2, s_m1a, s_m1b, s_r1, s_e1):
        item.done()
    for item in (gx, gv, e1, e2, g_mix2, g_low2, r_in2, g_mix1, g_low1, r_in1):
        item.drain()
    in_copy.wait_send()


def widen_kernel(*refs):
    ins, outs = refs[:11], refs[11:]
    for src, dst in zip(ins[:10], outs[:10]):
        dst[...] = src[...].astype(dst.dtype)
    for k in range(4):
        outs[10 + k][...] = ins[10][k : k + 1, :]


def kernel_call(kernel, name, number, in_specs, outs, out_specs, scratch, flops=0):
    def run(*args):
        return pl.pallas_call(
            kernel,
            name=name,
            out_shape=outs,
            in_specs=in_specs,
            out_specs=out_specs,
            scratch_shapes=scratch,
            cost_estimate=pl.CostEstimate(flops=flops, bytes_accessed=0, transcendentals=0),
            compiler_params=pltpu.CompilerParams(
                collective_id=number, has_side_effects=True, vmem_limit_bytes=VMEM_LIMIT
            ),
        )(*args)

    return run


def fast_body(
    size,
    patches,
    first_reduce,
    first_mixer,
    first_expand,
    first_gain,
    first_shift,
    second_reduce,
    second_mixer,
    second_expand,
    second_gain,
    second_shift,
    readout_in,
    readout_out,
    cotangent,
    live_counts,
):
    S = jax.ShapeDtypeStruct
    V = pltpu.VMEM
    near = pl.BlockSpec(memory_space=pltpu.VMEM)
    scalar = pl.BlockSpec(memory_space=pltpu.SMEM)
    away = pl.BlockSpec(memory_space=pl.ANY)
    grids, side, _, chans = patches.shape
    total = first_expand.shape[1]
    rows = grids * side * side
    share = rows // size
    small = side // 2
    few = 3 * ROW_PAD
    few_rows = few * size
    tight = total * small // ROW_PAD
    token_rows = grids * small * small
    part = readout_in.shape[1]
    wide = readout_out.shape[1]
    reach = size // 2
    pool = pool_places(side)
    places = token_places(grids, small).astype(BF16)
    x = patches.reshape(rows, chans)
    mixer_1 = first_mixer.reshape(9 * chans, total)
    mixer_2 = second_mixer.reshape(9 * chans, total)
    vectors = [v.reshape(1, chans) for v in (first_gain, first_shift, second_gain, second_shift)]

    held = ((4, size, chans, total // 4), BF16)
    x_small = ((size, few, total), BF16)
    mixer = ((9 * chans, total), BF16)
    sums = [
        ((part, wide), True),
        ((total, part), True),
        ((9 * chans, total), False),
        ((total, chans), True),
        ((chans, total), False),
        ((9 * chans, total), False),
        ((total, chans), True),
        ((chans, total), False),
    ]
    outs = [
        (S((rows, chans), F32), near),
        (S((token_rows, part), BF16), near),
        (S((8, chans), F32), near),
        (S((size // 2, 4, token_rows, part), BF16), away),
    ]
    outs += [(S(shape, BF16), away) for shape, _ in sums]

    def half(shape, by_rows):
        return (shape[0] // 2, shape[1]) if by_rows else (shape[0], shape[1] // 2)

    scratch = [
        V((size, rows, chans), BF16),
        V((total, chans), BF16),
        V((total, chans), BF16),
        V(*mixer),
        V((total, part), BF16),
        V((part, wide), BF16),
        V((16, chans), F32),
        V((size, 16, chans), F32),
        V((rows, chans), F32),
        V((size, share, 9 * chans), BF16),
        V((grids, side + 2, side + 16, chans), F32),
        V(*held),
        V(*held),
        V((share, total), F32),
        V((share, 128), F32),
        V((few, total), BF16),
        V((few, total), F32),
        V((few, total), BF16),
        V(*x_small),
        V((few_rows, chans), F32),
        V((size, few, 9 * chans), BF16),
        V((grids, small + 2, ROW_PAD + 16, chans), F32),
        V((few, total), F32),
        V((few, 128), F32),
        V((few, total), BF16),
        V(*x_small),
        V((size, token_rows, part), BF16),
        V((token_rows, part), F32),
        V((token_rows, part), BF16),
        V((few_rows, part), BF16),
        V((size, few, total), F32),
        V((2, size, rows, chans), BF16),
        V((2, rows, chans), F32),
        V((2, size, few, tight), BF16),
        V((2, few, tight), F32),
        V((2, 4, token_rows, part), BF16),
        V((4, token_rows, part), BF16),
        V((part, wide // 2), BF16),
        V((total, part), BF16),
        V(half(*sums[1]), BF16),
        V(half(*sums[1]), BF16),
    ]
    for k, (shape, by_rows) in enumerate(sums[2:]):
        if k == 3:
            scratch += [V(shape, BF16)] + [V((shape[0], shape[1] // 4), BF16)] * 4
        else:
            scratch += [V(shape, BF16)] + [V(half(shape, by_rows), BF16)] * 2
    scratch += [
        V((share, 9 * chans), F32),
        V((few, total), BF16),
        V((size, few, tight), BF16),
        V((2 * share, total // 2), BF16),
        V(*x_small),
        V(*x_small),
        V((size, few, chans), BF16),
        V((size, few, chans), BF16),
        V((few_rows, chans), BF16),
        V((rows, chans), BF16),
        V((share, total), F32),
        V((8, total), F32),
        V((size, 8, chans), F32),
        V((4, 8, chans), F32),
        DMA((17,)),
        DMA((5, 2, reach, 2)),
        DMA((2, reach, 6)),
        DMA((2, reach, 4)),
        DMA((2, 3)),
        DMA((2, 3)),
        DMA((1,)),
        DMA((1,)),
        DMA((size,)),
        DMA((3, size // 2)),
        DMA((size // 2,)),
        DMA((size // 2,)),
        DMA((3, size - 1)),
        DMA((3, size - 1)),
        DMA((9, 3)),
        DMA((9, 3)),
        DMA((9,)),
        DMA((2,)),
        DMA((2,)),
        DMA((4,)),
        DMA((4,)),
        DMA((11,)),
    ]
    patch_grads, tokens, vec_sum, _, *grads = kernel_call(
        functools.partial(layer_kernel, size, grids, side),
        "layer",
        1,
        [near] * 7 + [scalar] + [away] * 10,
        [shape for shape, _ in outs],
        [spec for _, spec in outs],
        scratch,
    )(
        *vectors, pool, np.ascontiguousarray(4.0 * pool.T), places, live_counts, x, first_reduce, first_expand,
        second_expand, mixer_1, second_reduce, mixer_2, readout_in, readout_out, cotangent,
    )
    tall = [(rows, chans, F32)] + [shape + (BF16,) for shape, _ in sums]
    blocks = [pl.BlockSpec((r // 4, c), lambda k: (k, 0)) for r, c, _ in tall]
    blocks += [pl.BlockSpec(tokens.shape, lambda k: (0, 0)), pl.BlockSpec(vec_sum.shape, lambda k: (0, 0))]
    one = pl.BlockSpec((1, chans), lambda k: (0, 0))
    (
        patch_grads, out_g, in_g, mixer_2_g, reduce_2_g, expand_2_g, mixer_1_g, reduce_1_g, expand_1_g, tokens,
        gain_1_g, shift_1_g, gain_2_g, shift_2_g,
    ) = pl.pallas_call(
        widen_kernel,
        name="widen",
        grid=(4,),
        in_specs=blocks,
        out_shape=[S((r, c), F32) for r, c, _ in tall] + [S(tokens.shape, BF16)] + [S((1, chans), F32)] * 4,
        out_specs=blocks[:-1] + [one] * 4,
        compiler_params=pltpu.CompilerParams(vmem_limit_bytes=VMEM_LIMIT),
    )(patch_grads, *grads, tokens, vec_sum)
    return (
        tokens,
        patch_grads.reshape(patches.shape),
        reduce_1_g,
        mixer_1_g.reshape(first_mixer.shape),
        expand_1_g,
        gain_1_g.reshape(chans),
        shift_1_g.reshape(chans),
        reduce_2_g,
        mixer_2_g.reshape(second_mixer.shape),
        expand_2_g,
        gain_2_g.reshape(chans),
        shift_2_g.reshape(chans),
        in_g,
        out_g,
    )


def fits(mesh, patches, first_reduce, readout_in):
    size, groups = mesh.shape["mp"], mesh.shape["dp"]
    grids, side, _, chans = patches.shape
    return (
        groups == 4
        and size % 2 == 0
        and chans % 128 == 0
        and readout_in.shape[1] % 128 == 0
        and grids * side == 6 * size
        and side % 8 == 0
        and ROW_PAD * 3 == 2 * side
        and size * chans % 512 == 0
    )


def solution(mesh):
    in_specs = (
        P("dp", None, None, "mp"),
        P(None, "mp"),
        P(None, None, "mp", None),
        P("mp", None),
        P("mp"),
        P("mp"),
        P(None, "mp"),
        P(None, None, "mp", None),
        P("mp", None),
        P("mp"),
        P("mp"),
        P(None, "mp"),
        P("mp", None),
        P("dp", "mp"),
        P("dp"),
    )
    out_specs = (
        P("dp", "mp"),
        P("dp", None, None, "mp"),
        P(None, "mp"),
        P(None, None, "mp", None),
        P("mp", None),
        P("mp"),
        P("mp"),
        P(None, "mp"),
        P(None, None, "mp", None),
        P("mp", None),
        P("mp"),
        P("mp"),
        P(None, "mp"),
        P("mp", None),
    )

    def local(*args):
        if fits(mesh, args[0], args[1], args[11]):
            return fast_body(mesh.shape["mp"], *args)
        return body(*args)

    return jax.shard_map(local, mesh=mesh, in_specs=in_specs, out_specs=out_specs, check_vma=False)
```

```python
import functools

import jax
import jax.numpy as jnp
import numpy as np
from jax import lax
from jax.experimental import pallas as pl
from jax.experimental.pallas import tpu as pltpu
from jax.sharding import PartitionSpec as P

norm_eps = 1e-06


def conv_same(image, kernel):
    return lax.conv_general_dilated(
        image,
        kernel,
        (1, 1),
        "SAME",
        dimension_numbers=("NHWC", "HWIO", "NHWC"),
        preferred_element_type=jnp.float32,
    )


def silu_back(values, grad_values):
    return jax.vjp(jax.nn.silu, values)[1](grad_values)[0]


def gelu_exact(values):
    return jax.nn.gelu(values, approximate=False)


def gelu_back(values, grad_values):
    return jax.vjp(gelu_exact, values)[1](grad_values)[0]


def block_forward(inputs, reduce_w, mixer_w, expand_w, gain, shift):
    num_grids, grid_height, grid_width, local_chans = inputs.shape
    pixel_rows = num_grids * grid_height * grid_width
    low_in = inputs.astype(jnp.bfloat16).reshape(pixel_rows, local_chans)
    full_in = lax.all_gather(low_in, "mp", axis=1, tiled=True)
    total_chans = full_in.shape[1]
    pre_act = jnp.dot(full_in, reduce_w, preferred_element_type=jnp.float32)
    hidden = jax.nn.silu(pre_act).astype(jnp.bfloat16)
    partial_mix = conv_same(
        hidden.reshape(num_grids, grid_height, grid_width, local_chans), mixer_w
    )
    mixed_sum = lax.psum_scatter(
        partial_mix.reshape(pixel_rows, total_chans).astype(jnp.bfloat16),
        "mp",
        scatter_dimension=1,
        tiled=True,
    ).astype(jnp.float32)
    row_total, row_squares = lax.psum(
        (jnp.sum(mixed_sum, axis=1), jnp.sum(mixed_sum * mixed_sum, axis=1)), "mp"
    )
    center = row_total / total_chans
    inv_std = lax.rsqrt(row_squares / total_chans - center * center + norm_eps)
    normed = (mixed_sum - center[:, None]) * inv_std[:, None]
    affine = normed * gain + shift
    branch_in = jax.nn.silu(affine).astype(jnp.bfloat16)
    partial_out = jnp.dot(branch_in, expand_w, preferred_element_type=jnp.float32)
    branch_out = lax.psum_scatter(
        partial_out.astype(jnp.bfloat16), "mp", scatter_dimension=1, tiled=True
    ).astype(jnp.float32)
    outputs = inputs + branch_out.reshape(inputs.shape)
    return (outputs, (full_in, pre_act, hidden, normed, inv_std, affine, branch_in))


def block_backward(grad_out, saved, reduce_w, mixer_w, expand_w, gain):
    full_in, pre_act, hidden, normed, inv_std, affine, branch_in = saved
    num_grids, grid_height, grid_width, local_chans = grad_out.shape
    pixel_rows = num_grids * grid_height * grid_width
    grad_rows = grad_out.reshape(pixel_rows, local_chans)
    grad_branch = lax.all_gather(grad_rows.astype(jnp.bfloat16), "mp", axis=1, tiled=True)
    total_chans = grad_branch.shape[1]
    expand_grad = jnp.einsum(
        "ri,ro->io", branch_in, grad_branch, preferred_element_type=jnp.float32
    )
    grad_act = jnp.einsum("ro,io->ri", grad_branch, expand_w, preferred_element_type=jnp.float32)
    grad_affine = silu_back(affine, grad_act)
    gain_grad = jnp.sum(grad_affine * normed, axis=0)
    shift_grad = jnp.sum(grad_affine, axis=0)
    scaled = grad_affine * gain
    sum_plain, sum_normed = lax.psum(
        (jnp.sum(scaled, axis=1), jnp.sum(scaled * normed, axis=1)), "mp"
    )
    grad_mixed = inv_std[:, None] * (
        scaled - sum_plain[:, None] / total_chans - normed * sum_normed[:, None] / total_chans
    )
    mixed_full = lax.all_gather(grad_mixed.astype(jnp.bfloat16), "mp", axis=1, tiled=True)
    mixed_image = mixed_full.reshape(num_grids, grid_height, grid_width, total_chans)
    flipped = jnp.transpose(mixer_w[::-1, ::-1], (0, 1, 3, 2))
    grad_hidden = conv_same(mixed_image, flipped).reshape(pixel_rows, local_chans)
    padded = jnp.pad(
        hidden.reshape(num_grids, grid_height, grid_width, local_chans),
        ((0, 0), (1, 1), (1, 1), (0, 0)),
    )
    mixer_grad = jnp.stack(
        [
            jnp.stack(
                [
                    jnp.einsum(
                        "nhwi,nhwo->io",
                        padded[
                            :,
                            offset_h : offset_h + grid_height,
                            offset_w : offset_w + grid_width,
                            :,
                        ],
                        mixed_image,
                        preferred_element_type=jnp.float32,
                    )
                    for offset_w in range(3)
                ]
            )
            for offset_h in range(3)
        ]
    )
    grad_pre = silu_back(pre_act, grad_hidden).astype(jnp.bfloat16)
    reduce_grad = jnp.einsum("ri,ro->io", full_in, grad_pre, preferred_element_type=jnp.float32)
    partial_in = jnp.einsum("ro,io->ri", grad_pre, reduce_w, preferred_element_type=jnp.float32)
    grad_in = (
        lax.psum_scatter(
            partial_in.astype(jnp.bfloat16), "mp", scatter_dimension=1, tiled=True
        ).astype(jnp.float32)
        + grad_rows
    )
    return (
        grad_in.reshape(grad_out.shape),
        (reduce_grad, mixer_grad, expand_grad, gain_grad, shift_grad),
    )


def body(
    patches,
    first_reduce,
    first_mixer,
    first_expand,
    first_gain,
    first_shift,
    second_reduce,
    second_mixer,
    second_expand,
    second_gain,
    second_shift,
    readout_in,
    readout_out,
    cotangent,
    live_counts,
):
    num_grids, grid_height, grid_width, local_chans = patches.shape
    pooled_side = grid_height // 2
    patch_values = patches.astype(jnp.float32)
    first_out = block_forward(
        patch_values, first_reduce, first_mixer, first_expand, first_gain, first_shift
    )[0]
    pooled = first_out.reshape(num_grids, pooled_side, 2, pooled_side, 2, local_chans).mean(
        axis=(2, 4)
    )
    second_out = block_forward(
        pooled, second_reduce, second_mixer, second_expand, second_gain, second_shift
    )[0]
    token_count = num_grids * pooled_side * pooled_side
    flat = second_out.astype(jnp.bfloat16).reshape(token_count, local_chans)
    flat_full = lax.all_gather(flat, "mp", axis=1, tiled=True)
    lifted = jnp.dot(flat_full, readout_in, preferred_element_type=jnp.float32)
    activated = gelu_exact(lifted).astype(jnp.bfloat16)
    partial_tokens = jnp.dot(activated, readout_out, preferred_element_type=jnp.float32)
    summed = lax.psum_scatter(
        partial_tokens.astype(jnp.bfloat16), "mp", scatter_dimension=1, tiled=True
    ).astype(jnp.float32)
    live_slots = (jnp.arange(num_grids) < live_counts[0]).astype(jnp.float32)
    live_rows = jnp.repeat(live_slots, pooled_side * pooled_side)
    tokens = (summed * live_rows[:, None]).astype(jnp.bfloat16)
    grad_tokens = cotangent * live_rows[:, None].astype(jnp.bfloat16)
    grad_full = lax.all_gather(grad_tokens, "mp", axis=1, tiled=True)
    readout_out_grad = jnp.einsum(
        "ri,ro->io", activated, grad_full, preferred_element_type=jnp.float32
    )
    grad_act = jnp.einsum("ro,io->ri", grad_full, readout_out, preferred_element_type=jnp.float32)
    grad_lift = gelu_back(lifted, grad_act).astype(jnp.bfloat16)
    readout_in_grad = jnp.einsum(
        "ri,ro->io", flat_full, grad_lift, preferred_element_type=jnp.float32
    )
    partial_flat = jnp.einsum(
        "ro,io->ri", grad_lift, readout_in, preferred_element_type=jnp.float32
    )
    grad_flat = lax.psum_scatter(
        partial_flat.astype(jnp.bfloat16), "mp", scatter_dimension=1, tiled=True
    ).astype(jnp.float32)
    second_saved = block_forward(
        pooled, second_reduce, second_mixer, second_expand, second_gain, second_shift
    )[1]
    grad_pooled, second_grads = block_backward(
        grad_flat.reshape(num_grids, pooled_side, pooled_side, local_chans),
        second_saved,
        second_reduce,
        second_mixer,
        second_expand,
        second_gain,
    )
    spread_back = jnp.broadcast_to(
        0.25 * grad_pooled[:, :, None, :, None, :],
        (num_grids, pooled_side, 2, pooled_side, 2, local_chans),
    ).reshape(patches.shape)
    first_saved = block_forward(
        patch_values, first_reduce, first_mixer, first_expand, first_gain, first_shift
    )[1]
    patch_grads, first_grads = block_backward(
        spread_back, first_saved, first_reduce, first_mixer, first_expand, first_gain
    )
    summed_grads = (
        lax.psum(first_grads[0].astype(jnp.bfloat16), "dp").astype(jnp.float32),
        lax.psum(first_grads[1].astype(jnp.bfloat16), "dp").astype(jnp.float32),
        lax.psum(first_grads[2].astype(jnp.bfloat16), "dp").astype(jnp.float32),
        lax.psum(first_grads[3].astype(jnp.bfloat16), "dp").astype(jnp.float32),
        lax.psum(first_grads[4].astype(jnp.bfloat16), "dp").astype(jnp.float32),
        lax.psum(second_grads[0].astype(jnp.bfloat16), "dp").astype(jnp.float32),
        lax.psum(second_grads[1].astype(jnp.bfloat16), "dp").astype(jnp.float32),
        lax.psum(second_grads[2].astype(jnp.bfloat16), "dp").astype(jnp.float32),
        lax.psum(second_grads[3].astype(jnp.bfloat16), "dp").astype(jnp.float32),
        lax.psum(second_grads[4].astype(jnp.bfloat16), "dp").astype(jnp.float32),
        lax.psum(readout_in_grad.astype(jnp.bfloat16), "dp").astype(jnp.float32),
        lax.psum(readout_out_grad.astype(jnp.bfloat16), "dp").astype(jnp.float32),
    )
    return (
        tokens,
        patch_grads,
        summed_grads[0],
        summed_grads[1],
        summed_grads[2],
        summed_grads[3],
        summed_grads[4],
        summed_grads[5],
        summed_grads[6],
        summed_grads[7],
        summed_grads[8],
        summed_grads[9],
        summed_grads[10],
        summed_grads[11],
    )


MESH = pl.DeviceIdType.MESH
F32 = jnp.float32
BF16 = jnp.bfloat16
DMA = pltpu.SemaphoreType.DMA
VMEM_LIMIT = 63 * 2**20
ROW_PAD = 16


def dot_nn(a, b):
    return lax.dot_general(a, b, (((1,), (0,)), ((), ())), preferred_element_type=F32)


def dot_nt(a, b):
    return lax.dot_general(a, b, (((1,), (1,)), ((), ())), preferred_element_type=F32)


def dot_tn(a, b):
    return lax.dot_general(a, b, (((0,), (0,)), ((), ())), preferred_element_type=F32)


def dot_full(a, b):
    return lax.dot_general(
        a,
        b,
        (((1,), (0,)), ((), ())),
        precision=lax.Precision.HIGHEST,
        preferred_element_type=F32,
    )


def sigmoid(values):
    return 1.0 / (1.0 + jnp.exp(-values))


def silu(values):
    return values * sigmoid(values)


def silu_slope(values):
    gate = sigmoid(values)
    return gate * (1.0 + values * (1.0 - gate))


class Ring:
    def __init__(self, size):
        self.size = size
        self.reach = size // 2
        self.me = lax.axis_index("mp")
        half = self.me // 2
        self.spot = jnp.where(self.me % 2 == 0, half, size - 1 - half)
        self.right = self.index(self.spot + 1)
        self.left = self.index(self.spot - 1)

    def wrap(self, spot):
        return lax.rem(spot + 2 * self.size, self.size)

    def index(self, spot):
        spot = self.wrap(spot)
        return jnp.where(spot < self.reach, 2 * spot, 2 * (self.size - 1 - spot) + 1)

    def greet(self):
        barrier = pltpu.get_barrier_semaphore()
        for peer in (self.left, self.right):
            pl.semaphore_signal(barrier, inc=1, device_id={"mp": peer}, device_id_type=MESH)
        pl.semaphore_wait(barrier, 2)

    def copy(self, side, src, dst, send, recv):
        peer = self.right if side == 0 else self.left
        return pltpu.make_async_remote_copy(
            src_ref=src,
            dst_ref=dst,
            send_sem=send,
            recv_sem=recv,
            device_id={"mp": peer},
            device_id_type=MESH,
        )


def wait_bytes(like, sem):
    pltpu.make_async_copy(like, like, sem).wait()


class Gather:
    def __init__(self, ring, own, held, slot, lanes, send, recv):
        self.ring, self.own, self.held, self.slot = ring, own, held, slot
        self.lanes, self.send, self.recv, self.copies = lanes, send, recv, {}

    def _start(self, side, step, lane):
        ring = self.ring
        if step == ring.reach and lane // (len(self.lanes) // 2) != side:
            return
        away = step - 1
        spot = ring.wrap(ring.spot - away if side == 0 else ring.spot + away)
        dst = self.held.at[self.slot(spot)]
        src = self.own if step == 1 else dst
        at = self.lanes[lane]
        copy = ring.copy(
            side, src.at[at], dst.at[at], self.send, self.recv.at[side, step - 1, lane]
        )
        copy.start()
        self.copies[side, step, lane] = copy

    def move_lane(self, step, lane):
        for side in range(2):
            if step == 0:
                self._start(side, 1, lane)
            elif (side, step, lane) in self.copies:
                self.copies[side, step, lane].wait_recv()
                if step < self.ring.reach:
                    self._start(side, step + 1, lane)

    def start(self):
        self.move(0)

    def move(self, step, after=None):
        for lane in range(len(self.lanes)):
            self.move_lane(step, lane)
            if after is not None:
                after()

    def drain(self):
        wait_bytes(self.held.at[pl.ds(0, self.ring.size - 1)], self.send)

    def spots(self, step):
        ring = self.ring
        if step == ring.reach:
            return [ring.wrap(ring.spot + step)]
        return [ring.wrap(ring.spot - step), ring.wrap(ring.spot + step)]


class Scatter:
    def __init__(self, ring, term, boxes, terms, lanes, send, recv, extra=None):
        self.ring, self.term, self.out, self.inbox = ring, term, boxes[0], boxes[1]
        self.extra = extra
        self.terms, self.lanes, self.send, self.recv, self.copies = terms, lanes, send, recv, {}

    def place(self, side, step):
        return side * self.ring.reach + step - 1

    def _start(self, side, step, lane):
        at, place = self.lanes[lane], self.place(side, step)
        src, dst = self.out.at[place], self.inbox.at[place]
        copy = self.ring.copy(
            side, src.at[at], dst.at[at], self.send, self.recv.at[side, step - 1, lane]
        )
        copy.start()
        self.copies[side, step, lane] = copy

    def _fill(self, k, spot):
        self.terms[k] = self.term(spot)
        if self.extra is not None:
            self.extra(spot, self.terms.at[k])

    def start(self):
        ring, count = self.ring, len(self.lanes)
        self._fill(0, ring.wrap(ring.spot + ring.reach))
        for lane in range(count):
            side = lane // (count // 2)
            at = self.lanes[lane]
            self.out[(self.place(side, 1),) + at] = self.terms[(0,) + at].astype(BF16)
            self._start(side, 1, lane)

    def prepare(self, step, send=True):
        ring = self.ring
        away = ring.reach + 1 - step
        self._fill(0, ring.wrap(ring.spot + away))
        if away > 0:
            self._fill(1, ring.wrap(ring.spot - away))
        if step == 2 and send:
            for k in range(len(self.lanes) // 2):
                self.step_lane(2, k)

    def step_lane(self, step, k):
        count = len(self.lanes)
        for side in range(2):
            lane = (k + count // 2) % count if side == 0 else k
            at = self.lanes[lane]
            value = self.terms[(side,) + at]
            if (side, step - 1, lane) in self.copies:
                self.copies[side, step - 1, lane].wait_recv()
                value = value + self.inbox[(self.place(side, step - 1),) + at].astype(F32)
            self.out[(self.place(side, step),) + at] = value.astype(BF16)
            self._start(side, step, lane)

    def step(self, step, after=None):
        count = len(self.lanes)
        for k in range(count // 2 if step == 2 else 0, count):
            self.step_lane(step, k)
            if after is not None:
                after()

    def finish(self):
        reach = self.ring.reach
        for lane in range(len(self.lanes)):
            for side in range(2):
                self.copies[side, reach, lane].wait_recv()
        return (
            self.terms[0]
            + self.inbox[self.place(0, reach)].astype(F32)
            + self.inbox[self.place(1, reach)].astype(F32)
        )

    def drain(self):
        wait_bytes(self.out.at[pl.ds(0, self.ring.size - 1)], self.send)


class Later:
    def __init__(self):
        self.steps = []

    def add(self, step, *args):
        self.steps.append((step, args))

    def tick(self, count=1):
        for _ in range(min(count, len(self.steps))):
            step, args = self.steps.pop(0)
            step(*args)

    def rest(self):
        self.tick(len(self.steps))


def row_halves(rows):
    return ((pl.ds(0, rows // 2),), (pl.ds(rows // 2, rows // 2),))


def column_halves(columns):
    every = slice(None)
    return (
        (every, pl.ds(0, columns // 2)),
        (every, pl.ds(columns // 2, columns // 2)),
    )


def pool_places(side):
    small = side // 2
    place = np.zeros((3 * ROW_PAD, 6 * side), np.float32)
    for row in range(6):
        for column in range(side):
            place[(row // 2) * ROW_PAD + column // 2, row * side + column] = 0.25
    assert small <= ROW_PAD
    return place


def token_places(grids, small):
    place = np.zeros((grids * small * small, grids * small * ROW_PAD), np.float32)
    for line in range(grids * small):
        for column in range(small):
            place[line * small + column, line * ROW_PAD + column] = 1.0
    return place


def norm_rows(mixed, gain, shift):
    center = jnp.mean(mixed, axis=1, keepdims=True)
    apart = mixed - center
    inv_std = lax.rsqrt(jnp.mean(apart * apart, axis=1, keepdims=True) + norm_eps)
    normed = apart * inv_std
    return normed, inv_std, normed * gain + shift


def wide_vector(held, row):
    return jnp.concatenate([held[m, row : row + 1, :] for m in range(held.shape[0])], axis=1)


def half_of(rows, columns, which, by_rows):
    if by_rows:
        return (pl.ds(pl.multiple_of(which * (rows // 2), 16), rows // 2), slice(None))
    return (slice(None), pl.ds(pl.multiple_of(which * (columns // 2), 128), columns // 2))


class Pair:
    def __init__(self):
        self.me = lax.axis_index("dp")
        self.core = lax.rem(self.me, 2)
        self.other = 1 - self.core
        self.twin = self.me - self.core + self.other
        self.far = lax.rem(self.me + 2, 4)
        self.across = lax.rem(self.twin + 2, 4)

    def copy(self, peer, src, dst, send, recv):
        return pltpu.make_async_remote_copy(
            src_ref=src,
            dst_ref=dst,
            send_sem=send,
            recv_sem=recv,
            device_id={"dp": peer},
            device_id_type=MESH,
        )


class Share:
    def __init__(self, ring, pair, blocks, held, send, recv, twin_send, local):
        self.ring, self.pair, self.blocks, self.held = ring, pair, blocks, held
        self.send, self.recv, self.twin_send, self.local = send, recv, twin_send, local
        self.copies = []

    def go(self, spot):
        pair, half = self.pair, self.ring.size // 2
        m = self.ring.index(spot)
        same = m // half == pair.core
        j = lax.rem(m, half)
        src, dst = self.blocks.at[m], self.held.at[j, pair.me]
        peer = jnp.where(same, pair.far, pair.across)
        sem = self.recv.at[jnp.where(same, 0, 1), j]
        copy = pair.copy(peer, src, dst, self.send.at[len(self.copies)], sem)
        copy.start()
        self.copies.append(copy)

        @pl.when(same)
        def _():
            pltpu.make_async_copy(src, dst, self.local.at[j]).start()

        @pl.when(jnp.logical_not(same))
        def _():
            pair.copy(pair.twin, src, dst, self.twin_send.at[j], self.recv.at[2, j]).start()

    def drain(self):
        pair = self.pair
        for copy in self.copies:
            copy.wait_send()
        for j in range(self.ring.size // 2):
            src, dst = self.blocks.at[j], self.held.at[j, pair.me]
            pltpu.make_async_copy(src, dst, self.local.at[j]).wait()
            pair.copy(pair.twin, src, dst, self.twin_send.at[j], self.recv.at[2, j]).wait()
            for kind, peer in enumerate((pair.far, pair.across)):
                dst = self.held.at[j, peer]
                pair.copy(peer, src, dst, self.send.at[0], self.recv.at[kind, j]).wait_recv()


class Expand:
    def __init__(self, ring, pair, own, held, send, recv, psend, precv, load):
        self.ring, self.pair, self.held = ring, pair, held
        self.psend, self.precv, self.copies = psend, precv, []
        chans, quarter = held.shape[2:]
        columns = own.at[:, pl.ds(pl.multiple_of(pair.me * quarter, 128), quarter)]
        self.load = pltpu.make_async_copy(columns, held.at[pair.me, ring.me], load)
        self.load.start()
        self.gather = Gather(
            ring, held.at[pair.me, ring.me], held.at[pair.me], ring.index, row_halves(chans), send, recv
        )

    def across(self):
        self._swap(0, self.pair.far, self.pair.me)

    def between(self):
        self.copies[0].wait_recv()
        self._swap(1, self.pair.twin, self.pair.me)
        self._swap(2, self.pair.twin, self.pair.far)

    def _swap(self, k, peer, quarter):
        at = self.held.at[quarter]
        copy = self.pair.copy(peer, at, at, self.psend.at[k], self.precv.at[k])
        copy.start()
        self.copies.append(copy)

    def ready(self):
        for copy in self.copies[1:]:
            copy.wait_recv()

    def drain(self):
        self.gather.drain()
        for copy in self.copies:
            copy.wait_send()


def times_expand(rows, held):
    parts = []
    for k in range(held.shape[0]):
        weight = held[k].reshape(rows.shape[1], held.shape[3])
        parts.append(dot_nn(rows, weight))
    return jnp.concatenate(parts, axis=1)


def times_expand_back(rows, held):
    quarter = held.shape[3]
    total = None
    for k in range(held.shape[0]):
        weight = held[k].reshape(held.shape[1] * held.shape[2], quarter)
        part = dot_nt(rows[:, k * quarter : (k + 1) * quarter], weight)
        total = part if total is None else total + part
    return total


def chunk_taps(image, taps, spot, lines, side, width):
    chans = image.shape[-1]
    per_grid = side // lines
    grid, line = spot // per_grid, lax.rem(spot, per_grid) * lines
    for kh in range(3):
        for kw in range(3):
            piece = image[grid, pl.ds(line + kh, lines), 7 + kw : 7 + kw + width, :]
            at = (kh * 3 + kw) * chans
            taps[spot, :, at : at + chans] = piece.reshape(lines * width, chans).astype(BF16)


def chunk_back(image, product, spot, lines, side, width):
    chans = image.shape[-1]
    per_grid = side // lines
    grid, line = spot // per_grid, lax.rem(spot, per_grid) * lines
    for kh in range(3):
        for kw in range(3):
            at = (kh * 3 + kw) * chans
            piece = product[:, at : at + chans].reshape(lines, width, chans)
            image[grid, pl.ds(line + kh, lines), 7 + kw : 7 + kw + width, :] += piece


def pack_rows(dst, src):
    columns, width = src.shape[1], dst.shape[1]
    piece = columns - width
    pad = ROW_PAD * piece // columns
    dst[...] = src[:, 0:width]
    for line in range(0, src.shape[0], ROW_PAD):
        for k in range(width // piece):
            dst[line + ROW_PAD - pad : line + ROW_PAD, k * piece : (k + 1) * piece] = src[
                line + k * pad : line + (k + 1) * pad, width:columns
            ]


def unpack_rows(dst, src):
    columns, width = dst.shape[1], src.shape[1]
    piece = columns - width
    pad = ROW_PAD * piece // columns
    dst[:, 0:width] = src[...]
    for line in range(0, src.shape[0], ROW_PAD):
        for k in range(width // piece):
            dst[line + k * pad : line + (k + 1) * pad, width:columns] = src[
                line + ROW_PAD - pad : line + ROW_PAD, k * piece : (k + 1) * piece
            ]
        dst[line + ROW_PAD - pad : line + ROW_PAD, :] = jnp.zeros((pad, columns), F32)


def all_terms(terms, value):
    terms[...] = value.reshape(terms.shape)


def norm_back(grad_branch, normed, inv_std, gain, shift):
    affine = normed * gain + shift
    grad_affine = grad_branch * silu_slope(affine)
    gain_grad = jnp.sum(grad_affine * normed, axis=0, keepdims=True)
    shift_grad = jnp.sum(grad_affine, axis=0, keepdims=True)
    scaled = grad_affine * gain
    mean_plain = jnp.mean(scaled, axis=1, keepdims=True)
    mean_normed = jnp.mean(scaled * normed, axis=1, keepdims=True)
    return inv_std * (scaled - mean_plain - normed * mean_normed), gain_grad, shift_grad

class GroupSum:
    def __init__(self, pair, mine, other, from_core, from_far, result, half, send, recv, local):
        self.pair, self.mine, self.other = pair, mine, other
        self.from_core, self.from_far = from_core, from_far
        self.result = result.at[half]
        self.send, self.recv, self.local, self.copies = send, recv, local, []

    def _go(self, k, peer, src, dst):
        copy = self.pair.copy(peer, src, dst, self.send.at[k], self.recv.at[k])
        copy.start()
        self.copies.append(copy)

    def core(self):
        self._go(0, self.pair.twin, self.other, self.from_core)

    def far(self):
        if self.from_core is not None:
            self.copies[0].wait_recv()
            self.mine[...] = (self.mine[...].astype(F32) + self.from_core[...].astype(F32)).astype(
                BF16
            )
        self._go(1, self.pair.far, self.mine, self.from_far)

    def back(self):
        self.copies[-1].wait_recv()
        self.from_far[...] = (self.mine[...].astype(F32) + self.from_far[...].astype(F32)).astype(
            BF16
        )
        self._go(2, self.pair.twin, self.from_far, self.result)
        self.kept = pltpu.make_async_copy(self.from_far, self.result, self.local)
        self.kept.start()

    def done(self):
        self.copies[-1].wait_recv()
        self.kept.wait()
        for copy in self.copies:
            copy.wait_send()


def quarter_of(grad, which):
    columns = grad.shape[1] // 4
    return pl.ds(pl.multiple_of(which * columns, 128), columns)


class OutSum:
    def __init__(self, pair, act_all, cot_wide, grad, result, send, recv, local):
        self.pair, self.act_all, self.cot_wide, self.grad = pair, act_all, cot_wide, grad
        half = half_of(*result.shape, pair.core, False)
        self.result = result.at[half]
        self.send, self.recv, self.local = send, recv, local

    def spread(self, act_live):
        pair = self.pair
        self.act_all[pair.me] = act_live
        at = self.act_all.at[pair.me]
        self.copies = []
        for k, peer in enumerate((pair.far, pair.across, pair.twin)):
            copy = pair.copy(peer, at, at, self.send.at[k], self.recv.at[k])
            copy.start()
            self.copies.append(copy)

    def arrive(self):
        for copy in self.copies:
            copy.wait_recv()

    def block(self, j):
        groups, rows, part = self.act_all.shape
        left = self.act_all[...].reshape(groups * rows, part)
        right = self.cot_wide[j % 2].reshape(groups * rows, part)
        self.grad[:, j * part : (j + 1) * part] = dot_tn(left, right).astype(BF16)

    def back(self):
        copy = self.pair.copy(
            self.pair.twin, self.grad, self.result, self.send.at[3], self.recv.at[3]
        )
        copy.start()
        self.copies.append(copy)
        self.kept = pltpu.make_async_copy(self.grad, self.result, self.local)
        self.kept.start()

    def done(self):
        self.copies[3].wait_recv()
        self.kept.wait()
        for copy in self.copies:
            copy.wait_send()


def send_columns(ring, src, held, slot, send, recv):
    chans = held.shape[-1]
    held[slot] = src[:, pl.ds(pl.multiple_of(ring.me * chans, chans), chans)]
    copies = []
    for away in range(1, ring.size):
        peer = lax.rem(ring.me + away, ring.size)
        copy = pltpu.make_async_remote_copy(
            src_ref=src.at[:, pl.ds(pl.multiple_of(peer * chans, chans), chans)],
            dst_ref=held.at[slot],
            send_sem=send.at[away - 1],
            recv_sem=recv.at[away - 1],
            device_id={"mp": peer},
            device_id_type=MESH,
        )
        copy.start()
        copies.append(copy)
    return copies


def stack(value, columns):
    width = value.shape[1]
    return jnp.concatenate([value[:, k : k + columns] for k in range(0, width, columns)], axis=0)


def unstack(value, rows):
    return jnp.concatenate([value[k : k + rows] for k in range(0, value.shape[0], rows)], axis=1)


def layer_kernel(
    size, grids, side,
    gain_1, shift_1, gain_2, shift_2, pool, spread, places, counts,
    x, reduce_1_any, expand_1, expand_2, mixer_1_any, reduce_2_any, mixer_2_any, readout_in_any, readout_out_any,
    cotangent,
    patch_grads, tokens, vec_sum, cot_wide_any, out_sum, in_sum, mixer_2_sum, reduce_2_sum, expand_2_sum,
    mixer_1_sum, reduce_1_sum, expand_1_sum,
    x_full, reduce_1, reduce_2, mixer, readout_in, readout, vectors, vec_full, pre_1, taps_1, image_1, held_1, held_2,
    normed_1, inv_1, branch_1, pooled, low, x_small, pre_2, taps_2, image_2, normed_2, inv_2, branch_2,
    flat_full, cot_full, lifted, act, grad_lift, terms_all,
    boxes_big, terms_big, boxes_small, terms_small,
    cot_wide, act_all, out_grad, in_grad, in_core, in_far,
    mixer_2_grad, mixer_2_core, mixer_2_far, reduce_2_grad, reduce_2_core, reduce_2_far,
    expand_2_grad, expand_2_core, expand_2_far,
    mixer_1_grad, mixer_1a_core, mixer_1a_far, mixer_1b_core, mixer_1b_far, reduce_1_grad, reduce_1_core, reduce_1_far,
    expand_1_grad, expand_1_core, expand_1_far,
    product_1, low_1, packed, mix_1, mix_2_full, low_1_full, branch_2_full, branch_1_full,
    grad_pre_2, grad_pre_1, grad_out, vec_grad, vec_held, vec_part,
    send, recv, cot_recv, tok_recv, psend, precv, csend, crecv, ysend, yrecv, tsend, local, all_send, all_recv,
    sum_send, sum_recv, sum_local, vec_send, vec_recv, act_send, act_recv, load,
):
    ring, pair = Ring(size), Pair()
    rows, chans = x.shape
    share = rows // size
    total = size * chans
    small = side // 2
    few = pooled.shape[0]
    part = readout_in.shape[1]
    count = cotangent.shape[0]
    wide, tall = column_halves(total), row_halves(rows)
    near = lambda spot: spot
    big, little = (boxes_big.at[0], boxes_big.at[1]), (boxes_small.at[0], boxes_small.at[1])
    low_2_full, mix_1_full, grad_rows = flat_full, cot_full, pooled
    narrow = column_halves(packed.shape[2])
    loose = product_1.at[few : 2 * few, 0:total]
    tight = product_1.at[2 * few : 3 * few, 0 : packed.shape[2]]

    def gather_packed(value, full, send, recv):
        loose[...] = value
        pack_rows(tight, loose)
        packed[ring.spot] = tight[...].astype(BF16)
        gather = Gather(ring, packed.at[ring.spot], packed, near, narrow, send, recv)
        gather.start()
        full[ring.spot] = value.astype(BF16)
        return gather

    def unpack(full, spot):
        tight[...] = packed[spot].astype(F32)
        unpack_rows(loose, tight)
        full[spot] = loose[...].astype(BF16)

    def packed_term(spot):
        pack_rows(tight, terms_all.at[spot])
        return tight[...]

    def unpacked(value):
        tight[...] = value
        unpack_rows(loose, tight)
        return loose[...]

    def fetch(k, src, dst):
        return pltpu.make_async_copy(src, dst, load.at[k])

    l_x = fetch(0, x, x_full.at[ring.me])
    l_reduce_1 = fetch(1, reduce_1_any, reduce_1)
    l_mixer = [
        fetch(2, mixer_1_any, mixer),
        fetch(2, mixer_2_any, mixer),
        fetch(2, mixer_1_any, mixer),
    ]
    l_reduce_2 = fetch(3, reduce_2_any, reduce_2)
    l_in = fetch(4, readout_in_any, readout_in)
    l_out = fetch(5, readout_out_any, readout)
    l_cot = fetch(6, cotangent, cot_full.at[ring.me])
    l_wide = [
        fetch(7 + j % 2, cot_wide_any.at[j], cot_wide.at[j % 2]) for j in range(size // 2)
    ]
    l_x.start()
    l_reduce_1.start()
    e1 = Expand(
        ring, pair, expand_1, held_1, send.at[0], recv.at[2], psend.at[0], precv.at[0], load.at[9]
    )
    e2 = Expand(
        ring, pair, expand_2, held_2, send.at[1], recv.at[3], psend.at[1], precv.at[1], load.at[10]
    )
    barrier = pltpu.get_barrier_semaphore()
    for peer in (ring.left, ring.right):
        pl.semaphore_signal(barrier, inc=1, device_id={"mp": peer}, device_id_type=MESH)
    for peer in (pair.twin, pair.far, pair.across):
        pl.semaphore_signal(barrier, inc=1, device_id={"dp": peer}, device_id_type=MESH)
    pl.semaphore_wait(barrier, 5)
    gx = Gather(ring, x, x_full, ring.index, tall, send.at[2], recv.at[0])
    gx.start()
    for copy in (l_mixer[0], l_reduce_2, l_in, l_out, l_cot):
        copy.start()
    e1.load.wait()
    e1.gather.start()
    for k, vector in enumerate((gain_1, shift_1, gain_2, shift_2)):
        for row in (k, k + 8):
            vectors[row : row + 1, :] = vector[...]
    for k in range(4, 8):
        for row in (k, k + 8):
            vectors[row : row + 1, :] = gain_1[...]
    vec_full[ring.me] = vectors[...]
    gv = Gather(ring, vectors, vec_full, ring.index, row_halves(16), send.at[3], recv.at[4])
    gv.start()

    def add(spot):
        m = ring.index(spot)
        weight = reduce_1[pl.ds(pl.multiple_of(m * chans, chans), chans), :]
        pre_1[...] += dot_nn(x_full[m], weight)

    l_x.wait()
    l_reduce_1.wait()
    own = reduce_1[pl.ds(pl.multiple_of(ring.me * chans, chans), chans), :]
    pre_1[...] = dot_nn(x_full[ring.me], own)
    image_1[...] = jnp.zeros(image_1.shape, F32)
    image_2[...] = jnp.zeros(image_2.shape, F32)
    for step in range(1, ring.reach + 1):
        gx.move(step)
        for spot in gx.spots(step):
            add(spot)
        if step < ring.reach:
            for item in (e1.gather, gv):
                item.move(step)
    hidden = silu(pre_1[...])
    image_1[:, 1 : 1 + side, 8 : 8 + side, :] = hidden.reshape(grids, side, side, chans)
    l_mixer[0].wait()

    def mix_term(spot):
        chunk_taps(image_1, taps_1, spot, 6, side, side)
        return stack(dot_nn(taps_1[spot], mixer[...]), chans)

    rs1 = Scatter(ring, mix_term, big, terms_big, tall, send.at[4], recv.at[1])
    rs1.start()
    e1.gather.move(ring.reach)
    e1.across()
    gv.move(ring.reach)
    l_cot.wait()
    share_cot = Share(ring, pair, cot_full, cot_wide_any, ysend, yrecv, tsend, local)
    share_cot.go(ring.spot)
    for step in range(2, ring.reach + 1):
        rs1.prepare(step)
        rs1.step(step)
        if step == ring.reach - 1:
            e1.between()
    e2.load.wait()
    e2.gather.start()
    rs1.prepare(ring.reach + 1)
    l_mixer[1].start()
    mine = pl.ds(pl.multiple_of(ring.spot * share, 16), share)
    gain_a, shift_a = wide_vector(vec_full, 0), wide_vector(vec_full, 1)
    mixed = unstack(rs1.finish(), share)
    thin = [(pl.ds(k, count // 6),) for k in range(0, count, count // 6)]
    gc = Gather(
        ring, cot_full.at[ring.me], cot_full, ring.index, thin, send.at[5], cot_recv
    )

    held_back = []

    def move_cot(step, lane):
        gc.move_lane(step, lane)
        if step > 0 and lane == len(thin) - 1:
            held_back.extend(gc.spots(step))

    def share_blocks():
        while held_back:
            share_cot.go(held_back.pop(0))

    cots = Later()
    late = [(step, lane) for step in range(1, ring.reach + 1) for lane in range(2)]
    for step in range(ring.reach + 1):
        for lane in range(len(thin)):
            if len(cots.steps) >= 4 and late:
                cots.add(e2.gather.move_lane, *late.pop(0))
            cots.add(move_cot, step, lane)
    cots.tick(4)
    value, inverse, affine = norm_rows(mixed, gain_a, shift_a)
    normed_1[...] = value
    inv_1[...] = jnp.broadcast_to(inverse, inv_1.shape)
    branch = silu(affine).astype(BF16)
    e1.ready()
    x_rows = jnp.concatenate([x_full[m, mine, :].astype(F32) for m in range(size)], axis=1)
    pooled[...] = dot_full(pool[...], x_rows + times_expand(branch, held_1))
    g2 = gather_packed(pooled[...], x_small, send.at[6], recv.at[0])
    branch_1[...] = (4.0 * dot_full(pool[...], branch.astype(F32))).astype(BF16)
    rs1.drain()
    for step in range(1, ring.reach + 1):
        g2.move(step, lambda: cots.tick(2))
        for spot in g2.spots(step):
            unpack(x_small, spot)
    g2.drain()
    e2.across()
    share_blocks()
    l_reduce_2.wait()
    cots.tick(3)
    pre_2[...] = dot_nn(x_small[...].reshape(size * few, total), reduce_2[...])
    hidden = silu(pre_2[...])
    image_2[:, 1 : 1 + small, 8 : 8 + ROW_PAD, :] = hidden.reshape(grids, small, ROW_PAD, chans)
    l_mixer[1].wait()

    def taps(spot, carry):
        chunk_taps(image_2, taps_2, spot, 3, small, ROW_PAD)
        return carry

    lax.fori_loop(0, size, taps, 0)
    all_terms(terms_all, dot_nn(taps_2[...].reshape(size * few, 9 * chans), mixer[...]))
    rs2 = Scatter(ring, packed_term, little, terms_small, narrow, send.at[7], recv.at[1])
    rs2.start()
    for step in range(2, ring.reach + 1):
        rs2.prepare(step)
        rs2.step(step, cots.tick)
        share_blocks()
    rs2.prepare(ring.reach + 1)
    gain_b, shift_b = wide_vector(vec_full, 2), wide_vector(vec_full, 3)
    e2.between()
    mixed = unpacked(rs2.finish())
    cots.tick(2)
    value, inverse, affine = norm_rows(mixed, gain_b, shift_b)
    normed_2[...] = value
    inv_2[...] = jnp.broadcast_to(inverse, inv_2.shape)
    branch_2[...] = silu(affine).astype(BF16)
    e2.ready()
    value = pooled[...] + times_expand(branch_2[...], held_2)
    gf = gather_packed(value, flat_full, send.at[8], recv.at[0])
    rs2.drain()
    for step in range(1, ring.reach + 1):
        gf.move(step, cots.tick)
        share_blocks()
        for spot in gf.spots(step):
            unpack(flat_full, spot)
    gf.drain()
    l_in.wait()
    flat = dot_nn(places[...], flat_full[...].reshape(size * few, total)).astype(BF16)
    lifted[...] = dot_nn(flat, readout_in[...])
    cdf = 0.5 * (1.0 + lax.erf(lifted[...] * 0.7071067811865476))
    row_ids = lax.broadcasted_iota(jnp.int32, (count, 1), 0)
    live = (row_ids < counts[0] * (count // grids)).astype(F32)
    activated = (lifted[...] * cdf).astype(BF16)
    act[...] = activated
    slope = cdf + lifted[...] * jnp.exp(-0.5 * lifted[...] * lifted[...]) * 0.3989422804014327
    lifted[...] = slope * live
    terms_big[0] = jnp.zeros(terms_big.shape[1:], F32)
    l_out.wait()
    cots.rest()
    share_blocks()

    def back(m, carry):
        at = pl.ds(pl.multiple_of(m * part, 128), part)
        terms_big[0] += stack(dot_nt(cot_full[m], readout[:, at]), chans)
        return carry

    lax.fori_loop(0, size, back, 0)
    lift = (unstack(terms_big[0], count) * lifted[...]).astype(BF16)
    grad_lift[...] = dot_tn(places[...], lift).astype(BF16)
    all_terms(terms_all, dot_nt(grad_lift[...], readout_in[...]))
    rf = Scatter(ring, packed_term, little, terms_small, narrow, send.at[9], recv.at[1])
    rf.start()

    def token_term(spot):
        at = pl.ds(pl.multiple_of(ring.index(spot) * part, 128), part)
        return stack(dot_nn(act[...], readout[:, at]), chans)

    quarters = [(pl.ds(k, rows // 4),) for k in range(0, rows, rows // 4)]
    r_tok = Scatter(ring, token_term, big, terms_big, quarters, send.at[10], tok_recv)
    toks = Later()
    toks.add(r_tok.prepare, 2, False)
    for step in range(2, ring.reach + 1):
        if step > 2:
            toks.add(r_tok.prepare, step)
        for k in range(4):
            toks.add(r_tok.step_lane, step, k)
    rf.prepare(2)
    r_tok.start()
    in_grad[...] = dot_tn(flat, lift).astype(BF16)
    in_other = half_of(*in_grad.shape, pair.other, True)
    in_copy = pair.copy(pair.twin, in_grad.at[in_other], in_core, csend.at[0], crecv.at[0])
    in_copy.start()
    rf.step(2)
    toks.tick()
    rf.prepare(3)
    rf.step(3)
    toks.tick()
    rf.prepare(4)
    rf.step(4)
    toks.tick()
    rf.prepare(ring.reach + 1)

    def group_sum(k, mine, other, from_core, from_far, result, by_rows):
        half = half_of(*result.shape, pair.core, by_rows)
        return GroupSum(
            pair, mine, other, from_core, from_far, result, half, sum_send.at[k], sum_recv.at[k], sum_local.at[k]
        )

    def grad_sum(k, grad, from_core, from_far, result, by_rows):
        mine, other = (
            grad.at[half_of(*grad.shape, which, by_rows)] for which in (pair.core, pair.other)
        )
        return group_sum(k, mine, other, from_core, from_far, result, by_rows)

    def quarter_sum(k, which, grad, from_core, from_far, result):
        mine, other = (
            (slice(None), quarter_of(grad, 2 * core + which)) for core in (pair.core, pair.other)
        )
        return GroupSum(
            pair, grad.at[mine], grad.at[other], from_core, from_far, result, mine, sum_send.at[k], sum_recv.at[k],
            sum_local.at[k],
        )

    s_out = OutSum(pair, act_all, cot_wide, out_grad, out_sum, act_send, act_recv, sum_local.at[0])
    s_in = group_sum(1, in_core, None, None, in_far, in_sum, True)
    s_m2 = grad_sum(2, mixer_2_grad, mixer_2_core, mixer_2_far, mixer_2_sum, False)
    s_r2 = grad_sum(3, reduce_2_grad, reduce_2_core, reduce_2_far, reduce_2_sum, True)
    s_e2 = grad_sum(4, expand_2_grad, expand_2_core, expand_2_far, expand_2_sum, False)
    s_m1a = quarter_sum(5, 0, mixer_1_grad, mixer_1a_core, mixer_1a_far, mixer_1_sum)
    s_m1b = quarter_sum(8, 1, mixer_1_grad, mixer_1b_core, mixer_1b_far, mixer_1_sum)
    s_r1 = grad_sum(6, reduce_1_grad, reduce_1_core, reduce_1_far, reduce_1_sum, True)
    s_e1 = grad_sum(7, expand_1_grad, expand_1_core, expand_1_far, expand_1_sum, False)
    s_out.spread((act[...].astype(F32) * live).astype(BF16))
    grad_rows[...] = unpacked(rf.finish())
    low[...] = grad_rows[...].astype(BF16)
    value, gain_grad, shift_grad = norm_back(
        times_expand_back(low[...], held_2), normed_2[...], inv_2[:, 0:1], gain_b, shift_b
    )
    g_mix2 = gather_packed(value, mix_2_full, send.at[11], recv.at[0])
    toks.tick()
    in_copy.wait_recv()
    in_mine = in_grad[half_of(*in_grad.shape, pair.core, True)]
    in_core[...] = (in_mine.astype(F32) + in_core[...].astype(F32)).astype(BF16)
    s_in.far()
    vec_grad[...] = jnp.zeros(vec_grad.shape, F32)
    vec_grad[2:3, :] = gain_grad
    vec_grad[3:4, :] = shift_grad
    image_2[...] = jnp.zeros(image_2.shape, F32)
    image_1[...] = jnp.zeros(image_1.shape, F32)
    low_2_full[ring.spot] = low[...]
    g_low2 = Gather(ring, low, low_2_full, near, wide, send.at[12], recv.at[2])
    g_low2.start()
    a_low2 = send_columns(
        ring, branch_2, branch_2_full, ring.spot, all_send.at[0], all_recv.at[0]
    )
    rf.drain()

    def back_2(spot):
        product_1[0:few, :] = dot_nt(mix_2_full[spot], mixer[...])
        chunk_back(image_2, product_1.at[0:few], spot, 3, small, ROW_PAD)

    back_2(ring.spot)
    for step in range(1, ring.reach + 1):
        g_mix2.move(step)
        for spot in g_mix2.spots(step):
            unpack(mix_2_full, spot)
            back_2(spot)
        if step > 1:
            g_low2.move(step - 1)
        toks.tick(2 if step < 3 else 1)
    l_mixer[2].start()
    grad_hidden = image_2[:, 1 : 1 + small, 8 : 8 + ROW_PAD, :].reshape(pre_2.shape)
    grad_pre_2[...] = (grad_hidden * silu_slope(pre_2[...])).astype(BF16)
    all_terms(terms_all, dot_nt(grad_pre_2[...], reduce_2[...]))
    gc.drain()
    share_cot.drain()
    r_in2 = Scatter(ring, packed_term, little, terms_small, narrow, send.at[13], recv.at[1])
    r_in2.start()
    for k in range(2):
        l_wide[k].start()
    def mixer_part(grad, taps, right, columns):
        left = taps[...].reshape(right.shape[0], 9 * chans)
        grad[:, columns] = dot_tn(left, right).astype(BF16)

    def mixer_2_half(which):
        columns = half_of(*mixer_2_grad.shape, which, False)[1]
        right = mix_2_full[:, :, columns].reshape(size * few, total // 2)
        mixer_part(mixer_2_grad, taps_2, right, columns)

    def mixer_1_quarter(core, which):
        quarter = total // 4
        lines = pl.ds(pl.multiple_of(core * share, 16), share)
        right = mix_1_full[:, lines, which * quarter : (which + 1) * quarter]
        columns = quarter_of(mixer_1_grad, 2 * core + which)
        mixer_part(mixer_1_grad, taps_1, right.reshape(rows, quarter), columns)

    def expand_part(grad, branches, lows):
        grad[...] = dot_tn(
            branches[...].reshape(size * few, chans), lows[...].reshape(size * few, total)
        ).astype(BF16)

    r_in2.prepare(2)
    r_in2.step(2)
    toks.tick(2)
    g_low2.move(ring.reach)
    mixer_2_half(pair.other)
    s_m2.core()
    r_in2.prepare(3)
    r_in2.step(3)
    toks.tick()
    mixer_2_half(pair.core)
    r_in2.prepare(4)
    r_in2.step(4)
    toks.tick()
    s_m2.far()
    reduce_2_grad[...] = dot_tn(x_small[...].reshape(size * few, total), grad_pre_2[...]).astype(BF16)
    s_r2.core()
    r_in2.prepare(ring.reach + 1)
    toks.tick()
    quarter = 0.25 * (unpacked(r_in2.finish()) + grad_rows[...])
    low_1[...] = quarter.astype(BF16)
    grad_branch = dot_full(spread[...], times_expand_back(low_1[...], held_1))
    value, gain_grad, shift_grad = norm_back(
        grad_branch, normed_1[...], inv_1[:, 0:1], gain_a, shift_a
    )
    mix_1[...] = stack(value.astype(BF16), total // 2)
    g_mix1 = Gather(ring, mix_1, mix_1_full, near, row_halves(2 * share), send.at[14], recv.at[0])
    g_mix1.start()
    mix_1_full[ring.spot] = mix_1[...]
    toks.rest()
    s_r2.far()
    vec_grad[0:1, :] = gain_grad
    vec_grad[1:2, :] = shift_grad
    grad_out[...] = dot_full(spread[...], quarter)
    a_low1 = send_columns(
        ring, branch_1, branch_1_full, ring.spot, all_send.at[1], all_recv.at[1]
    )
    a_vec = send_columns(ring, vec_grad, vec_held, ring.me, all_send.at[2], all_recv.at[2])

    def back_1(spot):
        half = total // 2
        product_1[...] = dot_nt(mix_1_full[spot, 0:share], mixer[:, 0:half])
        product_1[...] += dot_nt(mix_1_full[spot, share : 2 * share], mixer[:, half:total])
        chunk_back(image_1, product_1, spot, 6, side, side)

    l_mixer[2].wait()
    back_1(ring.spot)
    low_1_full[ring.spot] = low_1[...]
    g_low1 = Gather(ring, low_1, low_1_full, near, wide, send.at[15], recv.at[3])
    for step in range(1, ring.reach + 1):
        g_mix1.move(step)
        if step == 1:
            r_tok.prepare(ring.reach + 1)
            tokens[...] = (unstack(r_tok.finish(), count) * live).astype(BF16)
            r_tok.drain()
        for spot in g_mix1.spots(step):
            back_1(spot)
        if step == 2:
            for copy in a_low2:
                copy.wait()
            expand_part(expand_2_grad, branch_2_full, low_2_full)
            s_e2.core()
            s_out.arrive()
            for j in range(2):
                l_wide[j].wait()
                s_out.block(j)
                l_wide[j + 2].start()
        if step == 3:
            g_low1.start()
            s_e2.far()
            for j in range(2, 4):
                l_wide[j].wait()
                s_out.block(j)
            s_out.back()
    grad_hidden = image_1[:, 1 : 1 + side, 8 : 8 + side, :].reshape(pre_1.shape)
    grad_pre_1[...] = (grad_hidden * silu_slope(pre_1[...])).astype(BF16)

    def in_term(spot):
        at = pl.ds(pl.multiple_of(ring.index(spot) * chans, chans), chans)
        return dot_nt(grad_pre_1[...], reduce_1[at, :])

    def in_rows(spot, terms):
        at = pl.ds(pl.multiple_of(ring.index(spot) * chans, chans), chans)
        terms[mine, :] += grad_out[:, at]

    r_in1 = Scatter(ring, in_term, big, terms_big, tall, send.at[16], recv.at[1], in_rows)
    r_in1.start()
    r_in1.prepare(2)
    mixer_1_quarter(pair.other, 0)
    s_m1a.core()
    mixer_1_quarter(pair.core, 0)
    s_m1a.far()
    mixer_1_quarter(pair.other, 1)
    s_m1b.core()
    r_in1.step(2)
    mixer_1_quarter(pair.core, 1)
    s_m1b.far()
    g_low1.move(1)
    r_in1.prepare(3)
    r_in1.step(3)
    g_low1.move(2)

    def reduces(m, carry):
        at = pl.ds(pl.multiple_of(m * chans, chans), chans)
        reduce_1_grad[at, :] = dot_tn(x_full[m], grad_pre_1[...]).astype(BF16)
        return carry

    lax.fori_loop(0, size, reduces, 0)
    s_r1.core()
    r_in1.prepare(4)
    g_low1.move(3)
    r_in1.step(4)
    s_r1.far()
    for copy in a_vec:
        copy.wait()
    vec_part[0] = jnp.sum(vec_held[...], axis=0)
    v_core = pair.copy(pair.twin, vec_part.at[0], vec_part.at[1], vec_send.at[0], vec_recv.at[0])
    v_core.start()
    g_low1.move(ring.reach)
    for copy in a_low1:
        copy.wait()
    expand_part(expand_1_grad, branch_1_full, low_1_full)
    s_e1.core()
    v_core.wait()
    vec_part[2] = vec_part[0] + vec_part[1]
    v_far = pair.copy(pair.far, vec_part.at[2], vec_part.at[3], vec_send.at[1], vec_recv.at[1])
    v_far.start()
    r_in1.prepare(ring.reach + 1)
    s_e1.far()
    s_in.back()
    s_m2.back()
    s_r2.back()
    s_e2.back()
    patch_grads[...] = r_in1.finish()
    v_far.wait()
    vec_sum[...] = vec_part[2] + vec_part[3]
    s_m1a.back()
    s_m1b.back()
    s_r1.back()
    s_e1.back()
    for item in (s_out, s_in, s_m2, s_r2, s_e2, s_m1a, s_m1b, s_r1, s_e1):
        item.done()
    for item in (gx, gv, e1, e2, g_mix2, g_low2, r_in2, g_mix1, g_low1, r_in1):
        item.drain()
    in_copy.wait_send()


def widen_kernel(*refs):
    ins, outs = refs[:11], refs[11:]
    for src, dst in zip(ins[:10], outs[:10]):
        dst[...] = src[...].astype(dst.dtype)
    for k in range(4):
        outs[10 + k][...] = ins[10][k : k + 1, :]


def kernel_call(kernel, name, number, in_specs, outs, out_specs, scratch, flops=0):
    def run(*args):
        return pl.pallas_call(
            kernel,
            name=name,
            out_shape=outs,
            in_specs=in_specs,
            out_specs=out_specs,
            scratch_shapes=scratch,
            cost_estimate=pl.CostEstimate(flops=flops, bytes_accessed=0, transcendentals=0),
            compiler_params=pltpu.CompilerParams(
                collective_id=number, has_side_effects=True, vmem_limit_bytes=VMEM_LIMIT
            ),
        )(*args)

    return run


def fast_body(
    size,
    patches,
    first_reduce,
    first_mixer,
    first_expand,
    first_gain,
    first_shift,
    second_reduce,
    second_mixer,
    second_expand,
    second_gain,
    second_shift,
    readout_in,
    readout_out,
    cotangent,
    live_counts,
):
    S = jax.ShapeDtypeStruct
    V = pltpu.VMEM
    near = pl.BlockSpec(memory_space=pltpu.VMEM)
    scalar = pl.BlockSpec(memory_space=pltpu.SMEM)
    away = pl.BlockSpec(memory_space=pl.ANY)
    grids, side, _, chans = patches.shape
    total = first_expand.shape[1]
    rows = grids * side * side
    share = rows // size
    small = side // 2
    few = 3 * ROW_PAD
    few_rows = few * size
    tight = total * small // ROW_PAD
    token_rows = grids * small * small
    part = readout_in.shape[1]
    wide = readout_out.shape[1]
    reach = size // 2
    pool = pool_places(side)
    places = token_places(grids, small).astype(BF16)
    x = patches.reshape(rows, chans)
    mixer_1 = first_mixer.reshape(9 * chans, total)
    mixer_2 = second_mixer.reshape(9 * chans, total)
    vectors = [v.reshape(1, chans) for v in (first_gain, first_shift, second_gain, second_shift)]

    held = ((4, size, chans, total // 4), BF16)
    x_small = ((size, few, total), BF16)
    mixer = ((9 * chans, total), BF16)
    sums = [
        ((part, wide), True),
        ((total, part), True),
        ((9 * chans, total), False),
        ((total, chans), True),
        ((chans, total), False),
        ((9 * chans, total), False),
        ((total, chans), True),
        ((chans, total), False),
    ]
    outs = [
        (S((rows, chans), F32), near),
        (S((token_rows, part), BF16), near),
        (S((8, chans), F32), near),
        (S((size // 2, 4, token_rows, part), BF16), away),
    ]
    outs += [(S(shape, BF16), away) for shape, _ in sums]

    def half(shape, by_rows):
        return (shape[0] // 2, shape[1]) if by_rows else (shape[0], shape[1] // 2)

    scratch = [
        V((size, rows, chans), BF16),
        V((total, chans), BF16),
        V((total, chans), BF16),
        V(*mixer),
        V((total, part), BF16),
        V((part, wide), BF16),
        V((16, chans), F32),
        V((size, 16, chans), F32),
        V((rows, chans), F32),
        V((size, share, 9 * chans), BF16),
        V((grids, side + 2, side + 16, chans), F32),
        V(*held),
        V(*held),
        V((share, total), F32),
        V((share, 128), F32),
        V((few, total), BF16),
        V((few, total), F32),
        V((few, total), BF16),
        V(*x_small),
        V((few_rows, chans), F32),
        V((size, few, 9 * chans), BF16),
        V((grids, small + 2, ROW_PAD + 16, chans), F32),
        V((few, total), F32),
        V((few, 128), F32),
        V((few, total), BF16),
        V(*x_small),
        V((size, token_rows, part), BF16),
        V((token_rows, part), F32),
        V((token_rows, part), BF16),
        V((few_rows, part), BF16),
        V((size, few, total), F32),
        V((2, size, rows, chans), BF16),
        V((2, rows, chans), F32),
        V((2, size, few, tight), BF16),
        V((2, few, tight), F32),
        V((2, 4, token_rows, part), BF16),
        V((4, token_rows, part), BF16),
        V((part, wide // 2), BF16),
        V((total, part), BF16),
        V(half(*sums[1]), BF16),
        V(half(*sums[1]), BF16),
    ]
    for k, (shape, by_rows) in enumerate(sums[2:]):
        if k == 3:
            scratch += [V(shape, BF16)] + [V((shape[0], shape[1] // 4), BF16)] * 4
        else:
            scratch += [V(shape, BF16)] + [V(half(shape, by_rows), BF16)] * 2
    scratch += [
        V((share, 9 * chans), F32),
        V((few, total), BF16),
        V((size, few, tight), BF16),
        V((2 * share, total // 2), BF16),
        V(*x_small),
        V(*x_small),
        V((size, few, chans), BF16),
        V((size, few, chans), BF16),
        V((few_rows, chans), BF16),
        V((rows, chans), BF16),
        V((share, total), F32),
        V((8, total), F32),
        V((size, 8, chans), F32),
        V((4, 8, chans), F32),
        DMA((17,)),
        DMA((5, 2, reach, 2)),
        DMA((2, reach, 6)),
        DMA((2, reach, 4)),
        DMA((2, 3)),
        DMA((2, 3)),
        DMA((1,)),
        DMA((1,)),
        DMA((size,)),
        DMA((3, size // 2)),
        DMA((size // 2,)),
        DMA((size // 2,)),
        DMA((3, size - 1)),
        DMA((3, size - 1)),
        DMA((9, 3)),
        DMA((9, 3)),
        DMA((9,)),
        DMA((2,)),
        DMA((2,)),
        DMA((4,)),
        DMA((4,)),
        DMA((11,)),
    ]
    patch_grads, tokens, vec_sum, _, *grads = kernel_call(
        functools.partial(layer_kernel, size, grids, side),
        "layer",
        1,
        [near] * 7 + [scalar] + [away] * 10,
        [shape for shape, _ in outs],
        [spec for _, spec in outs],
        scratch,
    )(
        *vectors, pool, np.ascontiguousarray(4.0 * pool.T), places, live_counts, x, first_reduce, first_expand,
        second_expand, mixer_1, second_reduce, mixer_2, readout_in, readout_out, cotangent,
    )
    tall = [(rows, chans, F32)] + [shape + (BF16,) for shape, _ in sums]
    blocks = [pl.BlockSpec((r // 4, c), lambda k: (k, 0)) for r, c, _ in tall]
    blocks += [pl.BlockSpec(tokens.shape, lambda k: (0, 0)), pl.BlockSpec(vec_sum.shape, lambda k: (0, 0))]
    one = pl.BlockSpec((1, chans), lambda k: (0, 0))
    (
        patch_grads, out_g, in_g, mixer_2_g, reduce_2_g, expand_2_g, mixer_1_g, reduce_1_g, expand_1_g, tokens,
        gain_1_g, shift_1_g, gain_2_g, shift_2_g,
    ) = pl.pallas_call(
        widen_kernel,
        name="widen",
        grid=(4,),
        in_specs=blocks,
        out_shape=[S((r, c), F32) for r, c, _ in tall] + [S(tokens.shape, BF16)] + [S((1, chans), F32)] * 4,
        out_specs=blocks[:-1] + [one] * 4,
        compiler_params=pltpu.CompilerParams(vmem_limit_bytes=VMEM_LIMIT),
    )(patch_grads, *grads, tokens, vec_sum)
    return (
        tokens,
        patch_grads.reshape(patches.shape),
        reduce_1_g,
        mixer_1_g.reshape(first_mixer.shape),
        expand_1_g,
        gain_1_g.reshape(chans),
        shift_1_g.reshape(chans),
        reduce_2_g,
        mixer_2_g.reshape(second_mixer.shape),
        expand_2_g,
        gain_2_g.reshape(chans),
        shift_2_g.reshape(chans),
        in_g,
        out_g,
    )


def fits(mesh, patches, first_reduce, readout_in):
    size, groups = mesh.shape["mp"], mesh.shape["dp"]
    grids, side, _, chans = patches.shape
    return (
        groups == 4
        and size % 2 == 0
        and chans % 128 == 0
        and readout_in.shape[1] % 128 == 0
        and grids * side == 6 * size
        and side % 8 == 0
        and ROW_PAD * 3 == 2 * side
        and size * chans % 512 == 0
    )


def solution(mesh):
    in_specs = (
        P("dp", None, None, "mp"),
        P(None, "mp"),
        P(None, None, "mp", None),
        P("mp", None),
        P("mp"),
        P("mp"),
        P(None, "mp"),
        P(None, None, "mp", None),
        P("mp", None),
        P("mp"),
        P("mp"),
        P(None, "mp"),
        P("mp", None),
        P("dp", "mp"),
        P("dp"),
    )
    out_specs = (
        P("dp", "mp"),
        P("dp", None, None, "mp"),
        P(None, "mp"),
        P(None, None, "mp", None),
        P("mp", None),
        P("mp"),
        P("mp"),
        P(None, "mp"),
        P(None, None, "mp", None),
        P("mp", None),
        P("mp"),
        P("mp"),
        P(None, "mp"),
        P("mp", None),
    )

    def local(*args):
        if fits(mesh, args[0], args[1], args[11]):
            return fast_body(mesh.shape["mp"], *args)
        return body(*args)

    return jax.shard_map(local, mesh=mesh, in_specs=in_specs, out_specs=out_specs, check_vma=False)
```
